32 devices in a mesh: grid: 4 (over x, core), wide: 8 (over z, y).
Axes of the slice: x: 2, y: 2, z: 4, core: 2. Of those that a mesh axis runs over, the one named last changes fastest.
Arguments:
- mesh_feat: float32 [4, 4, 1024], P('grid', None, 'wide'), may hold values from -6 to 6
- mesh_pos: float32 [4, 3, 1024], P('grid', None, 'wide'), may hold values from 0 to 1
- query_pos: float32 [4, 3, 1024], P('grid', None, 'wide'), may hold values from 0 to 1
- enc_cell: int32 [4, 2048, 128], P('grid', 'wide'), may hold values from 0 to 3839, as said below
- enc_point: int32 [4, 2048, 128], P('grid', 'wide'), may hold values from 0 to 1023
- enc_count: int32 [4, 2048], P('grid', 'wide'), may hold values from 64 to 128, as said below
- dec_cell: int32 [4, 1024, 128], P('grid', 'wide'), may hold values from 0 to 4095, as said below
- dec_query: int32 [4, 1024, 128], P('grid', 'wide'), may hold values from 0 to 895
- dec_count: int32 [4, 1024], P('grid', 'wide'), may hold values from 64 to 128, as said below
- enc_w1: float32 [6, 64], replicated, may hold values from -2.5 to 2.5
- enc_b1: float32 [64], replicated, may hold values from -3 to 3
- enc_w2: float32 [64, 64], replicated, may hold values from -0.75 to 0.75
- enc_b2: float32 [64], replicated, may hold values from -3 to 3
- lift_w: float32 [4, 64], replicated, may hold values from -3 to 3
- lift_b: float32 [64], replicated, may hold values from -3 to 3
- spec_w: float32 [4096, 64, 128], P('wide'), may hold values from -3 to 3
- skip_w: float32 [64, 64], replicated, may hold values from -0.75 to 0.75
- skip_b: float32 [64], replicated, may hold values from -3 to 3
- dec_w1: float32 [6, 64], replicated, may hold values from -2.5 to 2.5
- dec_b1: float32 [64], replicated, may hold values from -3 to 3
- dec_w2: float32 [64, 64], replicated, may hold values from -0.75 to 0.75
- dec_b2: float32 [64], replicated, may hold values from -3 to 3
- proj_w: float32 [64], replicated, may hold values from -0.75 to 0.75
- proj_b: float32 [1], replicated, may hold values from -3 to 3
- pred_bar: float32 [4, 1024], P('grid', 'wide'), may hold values from -6 to 6
Outputs:
- pred: float32 [4, 1024], P('grid', 'wide')
- mesh_feat_grad: float32 [4, 4, 1024], P('grid', None, 'wide')
- enc_w1_grad: float32 [6, 64], replicated
- enc_b1_grad: float32 [64], replicated
- enc_w2_grad: float32 [64, 64], replicated
- enc_b2_grad: float32 [64], replicated
- lift_w_grad: float32 [4, 64], replicated
- lift_b_grad: float32 [64], replicated
- spec_w_grad: float32 [4096, 64, 128], P('wide')
- skip_w_grad: float32 [64, 64], replicated
- skip_b_grad: float32 [64], replicated
- dec_w1_grad: float32 [6, 64], replicated
- dec_b1_grad: float32 [64], replicated
- dec_w2_grad: float32 [64, 64], replicated
- dec_b2_grad: float32 [64], replicated
- proj_w_grad: float32 [64], replicated
- proj_b_grad: float32 [1], replicated
The draws below stay inside these ranges and needn't reach their ends.
Inputs may be any that keep to these rules, and one draw needn't show every extreme that they name: `enc_cell`: every slot, padding slots too, names a cell of its block's 4 rows whose index y is below 24. `dec_cell`: every slot, padding slots too, names a cell of its block's 4 rows. `enc_count`: block b is full where b % 256 == 0; the last block of each shape holds 64. `dec_count`: block b is full where b % 128 == 0; the last block of each shape holds 64.
All inputs are finite; a program needn't handle non-finite values.
Results may differ from the reference program's by a relative error of at most 0.0003.
Values sent between devices are 32-bit elements; how exact they have to be, the bound alone decides.
No kernel may reach another device: no remote copies, remote signals or barrier semaphores. Data moves between devices by JAX's collectives and lax.ppermute only.
A program may use at most 256 MiB of HBM per device.

```python
import math
from functools import partial
import jax
import jax.numpy as jnp
from jax import lax

WIDTH = 64
KHID = 64
MODES = 16
RES = 32
FEATS = 4
ENC_BLK = 256
DEC_BLK = 128
SHAPES = 4
PTS = 1024
QUERIES = 1024
ROWS_DEV = 4
CELLS = 32768
KMODES = 4096
N_WIDE = 8


def cells_in_rows(key, blocks, column_count):
    keys = jax.random.split(key, 3)
    extent = (SHAPES, blocks, 128)
    layer = jax.random.randint(keys[0], extent, 0, ROWS_DEV)
    column = jax.random.randint(keys[1], extent, 0, column_count)
    depth = jax.random.randint(keys[2], extent, 0, RES)
    return ((layer * RES + column) * RES + depth).astype(jnp.int32)


def filled_counts(key, blocks, per_device):
    drawn = jax.random.randint(key, (SHAPES, blocks), 64, 129)
    index = jnp.arange(blocks, dtype=jnp.int32)
    first = (index % per_device == 0)[None, :]
    last = (index == blocks - 1)[None, :]
    return jnp.where(first, 128, jnp.where(last, 64, drawn)).astype(jnp.int32)


def draw_enc_cell(key, part):
    key = jax.random.fold_in(key, 11)
    return cells_in_rows(key, N_WIDE * ENC_BLK, RES - RES // 4)


def draw_dec_cell(key, part):
    key = jax.random.fold_in(key, 13)
    return cells_in_rows(key, N_WIDE * DEC_BLK, RES)


def draw_enc_count(key, part):
    key = jax.random.fold_in(key, 17)
    return filled_counts(key, N_WIDE * ENC_BLK, ENC_BLK)


def draw_dec_count(key, part):
    key = jax.random.fold_in(key, 19)
    return filled_counts(key, N_WIDE * DEC_BLK, DEC_BLK)


def set_ends(entries, stream_key, smallest, largest):
    longest = entries.shape.index(max(entries.shape))
    spots = []
    for shift in (0, 1):
        where = [jax.random.randint(jax.random.fold_in(stream_key, axis), (), 0, length) for axis, length in enumerate(entries.shape)]
        where[longest] = (where[longest] + shift) % entries.shape[longest]
        spots.append(tuple(where))
    return entries.at[spots[0]].set(smallest).at[spots[1]].set(largest)


def block_scale(key, shape, cuts, least, largest):
    factor_of, own = 1.0, jax.random.fold_in(key, 6)
    for position, shards_of in cuts:
        steps = jnp.exp(jax.random.uniform(jax.random.fold_in(own, position), (shards_of,), jnp.float32, least / len(cuts), largest / len(cuts)))
        factor_of = factor_of * jnp.repeat(steps, shape[position] // shards_of).reshape([-1 if axis == position else 1 for axis in range(len(shape))])
    return factor_of


def scatter_about(key, dims, width, limit, shards=(), kind=jnp.bfloat16):
    array = jax.random.normal(key, dims, jnp.float32) * width
    if len(shards) > 0:
        array = block_scale(key, dims, shards, -0.22, 0.18) * array
    return jnp.clip(array, min=-limit, max=limit).astype(kind)


def setup_inputs(seed: int = 0) -> dict:
    arg_keys = jax.random.split(jax.random.key(seed), 26)
    return {
        "mesh_feat": scatter_about(arg_keys[0], (SHAPES, FEATS, PTS), 1.0, 6.0, ((0, 4), (2, 8)), jnp.float32),
        "mesh_pos": jnp.clip(1.0 * jax.random.uniform(arg_keys[1], (SHAPES, 3, PTS), jnp.float32) ** block_scale(arg_keys[1], (SHAPES, 3, PTS), ((0, 4), (2, 8)), -0.2, 0.2), 0.0, 1.0),
        "query_pos": jnp.clip(1.0 * jax.random.uniform(arg_keys[2], (SHAPES, 3, QUERIES), jnp.float32) ** block_scale(arg_keys[2], (SHAPES, 3, QUERIES), ((0, 4), (2, 8)), -0.2, 0.2), 0.0, 1.0),
        "enc_cell": draw_enc_cell(jax.random.fold_in(arg_keys[25], 71), 0),
        "enc_point": set_ends(jax.random.randint(arg_keys[4], (SHAPES, N_WIDE * ENC_BLK, 128), 0, PTS), jax.random.fold_in(arg_keys[4], 1), 0, PTS - 1).astype(jnp.int32),
        "enc_count": draw_enc_count(jax.random.fold_in(arg_keys[25], 71), 0),
        "dec_cell": draw_dec_cell(jax.random.fold_in(arg_keys[25], 71), 0),
        "dec_query": set_ends(jax.random.randint(arg_keys[7], (SHAPES, N_WIDE * DEC_BLK, 128), 0, QUERIES - QUERIES // 8), jax.random.fold_in(arg_keys[7], 1), 0, (QUERIES - QUERIES // 8) - 1).astype(jnp.int32),
        "dec_count": draw_dec_count(jax.random.fold_in(arg_keys[25], 71), 0),
        "enc_w1": scatter_about(arg_keys[9], (6, KHID), 6 ** -0.5, 2.5, (), jnp.float32),
        "enc_b1": scatter_about(arg_keys[10], (KHID,), 0.5, 3.0, (), jnp.float32),
        "enc_w2": scatter_about(arg_keys[11], (KHID, WIDTH), KHID ** -0.5, 0.75, (), jnp.float32),
        "enc_b2": scatter_about(arg_keys[12], (WIDTH,), 0.5, 3.0, (), jnp.float32),
        "lift_w": scatter_about(arg_keys[13], (FEATS, WIDTH), FEATS ** -0.5, 3.0, (), jnp.float32),
        "lift_b": scatter_about(arg_keys[14], (WIDTH,), 0.5, 3.0, (), jnp.float32),
        "spec_w": scatter_about(arg_keys[15], (KMODES, WIDTH, 2 * WIDTH), 0.35, 3.0, ((0, 8),), jnp.float32),
        "skip_w": scatter_about(arg_keys[16], (WIDTH, WIDTH), WIDTH ** -0.5, 0.75, (), jnp.float32),
        "skip_b": scatter_about(arg_keys[17], (WIDTH,), 0.5, 3.0, (), jnp.float32),
        "dec_w1": scatter_about(arg_keys[18], (6, KHID), 6 ** -0.5, 2.5, (), jnp.float32),
        "dec_b1": scatter_about(arg_keys[19], (KHID,), 0.5, 3.0, (), jnp.float32),
        "dec_w2": scatter_about(arg_keys[20], (KHID, WIDTH), KHID ** -0.5, 0.75, (), jnp.float32),
        "dec_b2": scatter_about(arg_keys[21], (WIDTH,), 0.5, 3.0, (), jnp.float32),
        "proj_w": scatter_about(arg_keys[22], (WIDTH,), WIDTH ** -0.5, 0.75, (), jnp.float32),
        "proj_b": scatter_about(arg_keys[23], (1,), 0.5, 3.0, (), jnp.float32),
        "pred_bar": scatter_about(arg_keys[24], (SHAPES, QUERIES), 1.0, 6.0, ((0, 4), (1, 8)), jnp.float32),
    }


highest = lax.Precision.HIGHEST

@jax.custom_vjp
def low(v):
    return lax.optimization_barrier(v.astype(jnp.bfloat16)).astype(jnp.float32)

@jax.custom_vjp
def low_back(v):
    return v

def low_keep(v):
    return (low(v), None)

def low_pass(kept, grad):
    return (grad,)

def back_keep(v):
    return (v, None)

def back_low(kept, grad):
    return (low(grad),)
low.defvjp(low_keep, low_pass)
low_back.defvjp(back_keep, back_low)

def smooth(value):
    return jax.nn.gelu(value, approximate=True)

def kept_freqs(count):
    half = count // 2
    lower = jnp.arange(half, dtype=jnp.int32)
    return jnp.concatenate([lower, lower + RES - half])

def angle_table(freqs, places):
    turns = freqs[:, None] * places[None, :] % RES
    return turns.astype(jnp.float32) * (2.0 * math.pi / RES)

def cell_places(cells):
    layer = cells // (RES * RES)
    column = cells // RES % RES
    depth = cells % RES
    return jnp.stack([layer, column, depth]).astype(jnp.float32) / (RES - 1.0)

def global_cells(cells):
    blocks = cells.shape[0]
    owner = (jnp.arange(blocks, dtype=jnp.int32) // (blocks // N_WIDE)).astype(jnp.int32)
    return (cells + owner[:, None] * (CELLS // N_WIDE)).astype(jnp.int32)

def kernel_values(inputs, w_one, b_one, w_two, b_two):
    hidden = smooth(jnp.dot(inputs, w_one, precision=highest) + b_one)
    return jnp.dot(hidden, w_two, precision=highest) + b_two

def encode(weights, lifted, places, cells, points, counts):
    slots = cells.shape[-1]
    lane = jnp.arange(slots, dtype=jnp.int32)

    def group_sum(group):
        cell_group, point_group, count_group = group
        valid = (lane[None, :] < count_group[:, None]).astype(jnp.float32).reshape(-1)
        cell_group = cell_group.reshape(-1)
        point_group = point_group.reshape(-1)
        inputs = jnp.concatenate([cell_places(cell_group).T, places[point_group]], axis=1)
        kernel = kernel_values(inputs, weights[0], weights[1], weights[2], weights[3])
        message = kernel * lifted[point_group] * valid[:, None]
        return jax.ops.segment_sum(message, cell_group, num_segments=CELLS)

    def step(total, group):
        return (total + jax.checkpoint(group_sum)(group), None)
    groups = (cells.reshape(N_WIDE, -1, slots), points.reshape(N_WIDE, -1, slots), counts.reshape(N_WIDE, -1))
    summed, _ = lax.scan(step, jnp.zeros((CELLS, WIDTH), jnp.float32), groups)
    valid_all = (lane[None, :] < counts[:, None]).astype(jnp.float32).reshape(-1)
    degree = jax.ops.segment_sum(valid_all, cells.reshape(-1), num_segments=CELLS)
    return summed / jnp.maximum(degree, 1.0)[:, None]

def decode(weights, latent, places, cells, queries, counts):
    slots = cells.shape[-1]
    lane = jnp.arange(slots, dtype=jnp.int32)

    def group_sum(group):
        cell_group, query_group, count_group = group
        valid = (lane[None, :] < count_group[:, None]).astype(jnp.float32).reshape(-1)
        cell_group = cell_group.reshape(-1)
        query_group = query_group.reshape(-1)
        inputs = jnp.concatenate([places[query_group], cell_places(cell_group).T], axis=1)
        kernel = kernel_values(inputs, weights[0], weights[1], weights[2], weights[3])
        message = kernel * latent[cell_group] * valid[:, None]
        return jax.ops.segment_sum(message, query_group, num_segments=QUERIES)

    def step(total, group):
        return (total + jax.checkpoint(group_sum)(group), None)
    groups = (cells.reshape(N_WIDE, -1, slots), queries.reshape(N_WIDE, -1, slots), counts.reshape(N_WIDE, -1))
    summed, _ = lax.scan(step, jnp.zeros((QUERIES, WIDTH), jnp.float32), groups)
    valid_all = (lane[None, :] < counts[:, None]).astype(jnp.float32).reshape(-1)
    degree = jax.ops.segment_sum(valid_all, queries.reshape(-1), num_segments=QUERIES)
    return summed / jnp.maximum(degree, 1.0)[:, None]

def spectral(field, spec_w):
    product = partial(jnp.einsum, precision=highest)
    places = jnp.arange(RES, dtype=jnp.int32)
    plane_angle = angle_table(kept_freqs(MODES), places)
    depth_angle = angle_table(jnp.arange(MODES, dtype=jnp.int32), places)
    cos_plane, sin_plane = (jnp.cos(plane_angle), jnp.sin(plane_angle))
    cos_depth, sin_depth = (jnp.cos(depth_angle), jnp.sin(depth_angle))
    z_real = product('xyzc,kz->xykc', field, cos_depth)
    z_imag = -product('xyzc,kz->xykc', field, sin_depth)
    y_real = product('xykc,jy->xjkc', z_real, cos_plane) + product('xykc,jy->xjkc', z_imag, sin_plane)
    y_imag = product('xykc,jy->xjkc', z_imag, cos_plane) - product('xykc,jy->xjkc', z_real, sin_plane)
    m_real = product('xjkc,ix->jkic', y_real, cos_plane) + product('xjkc,ix->jkic', y_imag, sin_plane)
    m_imag = product('xjkc,ix->jkic', y_imag, cos_plane) - product('xjkc,ix->jkic', y_real, sin_plane)
    count = MODES ** 3
    u_real = m_real.reshape(count, WIDTH)
    u_imag = m_imag.reshape(count, WIDTH)
    w_real = spec_w[:, :, :WIDTH]
    w_imag = spec_w[:, :, WIDTH:]
    factor = jnp.where(jnp.arange(MODES, dtype=jnp.int32) == 0, 1.0, 2.0) / float(RES ** 3)
    scale = jnp.broadcast_to(factor[None, :, None], (MODES, MODES, MODES)).reshape(count, 1)
    g_real = (product('mi,mio->mo', u_real, w_real) - product('mi,mio->mo', u_imag, w_imag)) * scale
    g_imag = (product('mi,mio->mo', u_real, w_imag) + product('mi,mio->mo', u_imag, w_real)) * scale
    g_real = g_real.reshape(MODES, MODES, MODES, WIDTH)
    g_imag = g_imag.reshape(MODES, MODES, MODES, WIDTH)
    h_real = product('jkic,ix->xjkc', g_real, cos_plane) - product('jkic,ix->xjkc', g_imag, sin_plane)
    h_imag = product('jkic,ix->xjkc', g_real, sin_plane) + product('jkic,ix->xjkc', g_imag, cos_plane)
    p_real = product('xjkc,jy->xykc', h_real, cos_plane) - product('xjkc,jy->xykc', h_imag, sin_plane)
    p_imag = product('xjkc,jy->xykc', h_real, sin_plane) + product('xjkc,jy->xykc', h_imag, cos_plane)
    return product('xykc,kz->xyzc', p_real, cos_depth) - product('xykc,kz->xyzc', p_imag, sin_depth)

def forward_one(params, feat, point_places, query_places, enc_cells, enc_points, enc_counts, dec_cells, dec_queries, dec_counts):
    enc_w1, enc_b1, enc_w2, enc_b2, lift_w, lift_b, spec_w, skip_w, skip_b, dec_w1, dec_b1, dec_w2, dec_b2, proj_w, proj_b = params
    lifted = jnp.dot(feat.T, lift_w, precision=highest) + lift_b
    lat_in = encode((enc_w1, enc_b1, enc_w2, enc_b2), lifted, point_places.T, global_cells(enc_cells), enc_points, enc_counts)
    spectral_part = spectral(lat_in.reshape(RES, RES, RES, WIDTH), spec_w).reshape(CELLS, WIDTH)
    latent = smooth(spectral_part + jnp.dot(lat_in, skip_w, precision=highest) + skip_b)
    aggregated = decode((dec_w1, dec_b1, dec_w2, dec_b2), latent, query_places.T, global_cells(dec_cells), dec_queries, dec_counts)
    return jnp.dot(aggregated, proj_w, precision=highest) + proj_b[0]

def reference(mesh_feat, mesh_pos, query_pos, enc_cell, enc_point, enc_count, dec_cell, dec_query, dec_count, enc_w1, enc_b1, enc_w2, enc_b2, lift_w, lift_b, spec_w, skip_w, skip_b, dec_w1, dec_b1, dec_w2, dec_b2, proj_w, proj_b, pred_bar):
    params = (enc_w1, enc_b1, enc_w2, enc_b2, lift_w, lift_b, spec_w, skip_w, skip_b, dec_w1, dec_b1, dec_w2, dec_b2, proj_w, proj_b)

    def per_shape(totals, items):
        feat, point_places, query_places, enc_cells, enc_points, enc_counts, dec_cells, dec_queries, dec_counts, cotangent = items

        def wrapped(feat_in, params_in):
            return forward_one(params_in, feat_in, point_places, query_places, enc_cells, enc_points, enc_counts, dec_cells, dec_queries, dec_counts)
        prediction, back = jax.vjp(wrapped, feat, params)
        feat_grad, params_grad = back(cotangent)
        return (jax.tree.map(jnp.add, totals, params_grad), (prediction, feat_grad))
    zeros = jax.tree.map(jnp.zeros_like, params)
    totals, outputs = lax.scan(per_shape, zeros, (mesh_feat, mesh_pos, query_pos, enc_cell, enc_point, enc_count, dec_cell, dec_query, dec_count, pred_bar))
    return (outputs[0], outputs[1], totals[0], totals[1], totals[2], totals[3], totals[4], totals[5], totals[6], totals[7], totals[8], totals[9], totals[10], totals[11], totals[12], totals[13], totals[14])
```

```python
from functools import partial
import math

import jax
import jax.numpy as jnp
import ml_dtypes
import numpy as np
from jax import lax
from jax.experimental import pallas as pl
from jax.experimental.pallas import tpu as pltpu
from jax.sharding import PartitionSpec as P

MODES = 16
RES = 32
PLANE = RES * RES
CHUNK = 256
LANES = 128
GROUP = 4
FEAT_ROWS = 8
ENC_WINDOW = 64
DEC_WINDOW = 128
PAD = 256
STEP_MODES = 32
F32 = jnp.float32
BF16 = jnp.bfloat16
GELU_A = 0.7978845608028654
GELU_B = 0.044715

NN = (((1,), (0,)), ((), ()))
NT = (((1,), (1,)), ((), ()))
TN = (((0,), (0,)), ((), ()))

VMEM = pl.BlockSpec(memory_space=pltpu.VMEM)
SMEM = pl.BlockSpec(memory_space=pltpu.SMEM)


def kept_freqs():
    half = MODES // 2
    return np.concatenate([np.arange(half), np.arange(RES - half, RES)])


def plane_matrix(owners):
    lines = MODES * MODES // owners
    line = np.arange(MODES * MODES)
    freq_y, freq_z = kept_freqs()[line // MODES], line % MODES
    cell = np.arange(PLANE)
    turns = (freq_y[:, None] * (cell // RES) + freq_z[:, None] * (cell % RES)) % RES
    angle = turns * (2.0 * math.pi / RES)
    both = np.stack([np.cos(angle), -np.sin(angle)]).reshape(2, owners, lines, PLANE)
    matrix = both.transpose(1, 0, 2, 3).reshape(2 * MODES * MODES, PLANE)
    return matrix.astype(np.float32)


def halves_np(matrix):
    high = matrix.astype(ml_dtypes.bfloat16)
    low = (matrix - high.astype(np.float32)).astype(ml_dtypes.bfloat16)
    return high, low


def line_angles():
    turns = (kept_freqs()[:, None] * np.arange(RES)[None, :]) % RES
    return turns * (2.0 * math.pi / RES)


def x_tables(rows_here, width):
    angle = line_angles().reshape(MODES, RES // rows_here, rows_here, 1)
    angle = np.broadcast_to(angle, (MODES, RES // rows_here, rows_here, width))
    angle = angle.reshape(MODES, RES // rows_here, rows_here * width)
    return np.cos(angle).astype(np.float32), np.sin(angle).astype(np.float32)


def log2(number):
    return number.bit_length() - 1


def iota(shape, axis):
    return lax.broadcasted_iota(jnp.int32, shape, axis)


def halves(value):
    high = value.astype(BF16)
    low = (value - high.astype(F32)).astype(BF16)
    return high, low


def dot(a, b, dims=NN):
    return lax.dot_general(a, b, dims, preferred_element_type=F32)


def dot3(a, b, dims=NN):
    a_high, a_low = halves(a)
    b_high, b_low = halves(b)
    return dot(a_high, b_high, dims) + dot(a_low, b_high, dims) + dot(a_high, b_low, dims)


def one_hot(index, first, rows):
    places = iota((rows, index.shape[1]), 0) + first
    return jnp.where(places == index, 1.0, 0.0).astype(BF16)


def gelu_both(value):
    square = value * value
    turn = jnp.tanh(value * (GELU_A + (GELU_A * GELU_B) * square))
    half = 0.5 * (1.0 + turn)
    slope = half + (0.5 * value) * (1.0 - turn * turn) * (
        GELU_A + (3.0 * GELU_A * GELU_B) * square
    )
    return value * half, slope


def sort_columns(values):
    rows = values.shape[0]
    regs = rows // 8
    low = log2(regs)
    total = low + 3 + 7
    sub = iota((8, LANES), 0)
    lane = iota((8, LANES), 1)
    x = values.reshape(regs, 8, LANES)

    def flip(x, bit):
        if bit >= total:
            return x
        if bit < low:
            y = x.reshape(regs >> (bit + 1), 2, 1 << bit, 8, LANES)
            return jnp.stack([y[:, 0], ~y[:, 1]], axis=1).reshape(regs, 8, LANES)
        if bit < low + 3:
            mask = -((sub >> (bit - low)) & 1)
        else:
            mask = -((lane >> (bit - low - 3)) & 1)
        return x ^ mask[None]

    def exchange(x, bit):
        if bit < low:
            y = x.reshape(regs >> (bit + 1), 2, 1 << bit, 8, LANES)
            one, two = y[:, 0], y[:, 1]
            pair = [jnp.minimum(one, two), jnp.maximum(one, two)]
            return jnp.stack(pair, axis=1).reshape(regs, 8, LANES)
        if bit < low + 3:
            axis, dist, size, place = 1, 1 << (bit - low), 8, sub
        else:
            axis, dist, size, place = 2, 1 << (bit - low - 3), LANES, lane
        after = pltpu.roll(x, size - dist, axis)
        before = after if 2 * dist == size else pltpu.roll(x, dist, axis)
        first = ((place & dist) == 0)[None]
        return jnp.where(first, jnp.minimum(x, after), jnp.maximum(x, before))

    for phase in range(1, total + 1):
        x = flip(x, phase)
        for bit in reversed(range(phase)):
            x = exchange(x, bit)
        x = flip(x, phase)
    return x.reshape(rows, LANES)


def layer_matrix(feat_rows, cell_rows, owners):
    feat_high, feat_low = halves(feat_rows)
    cell_high, cell_low = halves(cell_rows)
    parts = [feat_high] * owners + [feat_high] * owners + [feat_low] * owners
    parts += [cell_high, cell_low]
    stacked = jnp.concatenate([part.astype(F32) for part in parts], axis=0)
    depth = stacked.shape[0]
    more = -depth % LANES
    if more:
        stacked = jnp.concatenate([stacked, jnp.zeros((more, stacked.shape[1]), F32)], axis=0)
    return stacked.T[:, :depth].astype(BF16)


def edge_inputs(key, table, first_row, owners):
    shift = log2(owners * LANES)
    cell = key >> shift
    point = key & (owners * LANES - 1)
    low_hot = one_hot(point & (LANES - 1), 0, LANES)
    found = dot(table, low_hot)
    owner = (iota(found.shape, 0) >> 3) & (owners - 1)
    found = jnp.where(owner == (point >> 7), found, 0.0)
    row = iota((8, key.shape[1]), 0)
    shifts = jnp.where(row == 0, 2 * log2(RES), jnp.where(row == 1, log2(RES), 0))
    place = (cell >> shifts) & jnp.where(row < 3, RES - 1, 0)
    place = (place + jnp.where(row == 0, first_row, 0)).astype(F32)
    return cell, point, low_hot, found, place


def stack_inputs(found, place, owners):
    exact = found.astype(BF16)
    places = jnp.concatenate([place, place], axis=0).astype(BF16)
    return jnp.concatenate([exact, exact[: owners * FEAT_ROWS], places], axis=0)


def fold_feats(found, owners):
    return jnp.sum(found.reshape(2 * owners, FEAT_ROWS, found.shape[1]), axis=0)


def stack3(value):
    high, low = halves(value)
    return jnp.concatenate([high, low, high], axis=0)


def weights3(matrix):
    high, low = halves(matrix)
    return jnp.concatenate([high, high, low], axis=1)


def key_row(keys_ref, chunk):
    per = CHUNK // keys_ref.shape[1]
    rows = [keys_ref[pl.ds(chunk * per + i, 1), :] for i in range(per)]
    return rows[0] if per == 1 else jnp.concatenate(rows, axis=1)


def cell_range(bounds_ref, line, chunk, per):
    return bounds_ref[line, chunk * per], bounds_ref[line + 1, chunk * per + per - 1]


def spread(block, copies):
    rows, columns = block.shape
    tiled = jnp.concatenate([jnp.concatenate([block] * copies, axis=1)] * copies, axis=0)
    return jnp.where(
        iota(tiled.shape, 0) // rows == iota(tiled.shape, 1) // columns, tiled, 0.0
    )


def gather_blocks(product, copies, rows, columns):
    total = product[:rows, :columns]
    for i in range(1, copies):
        total = total + product[i * rows : (i + 1) * rows, i * columns : (i + 1) * columns]
    return total


def tile_lanes(row, copies):
    return row if copies == 1 else jnp.concatenate([row] * copies, axis=1)


def fold_lanes(row, copies, width):
    total = row[:, :width]
    for i in range(1, copies):
        total = total + row[:, i * width : (i + 1) * width]
    return total


def sort_kernel(
    enc_cell, enc_point, enc_count, dec_cell, dec_query, dec_count, feat, pos, query_pos, pred_bar,
    enc_keys, dec_keys, bounds, payload, *, owners, cells,
):
    shift = log2(owners * LANES)

    def column(counts):
        return jnp.broadcast_to(counts, (8, counts.shape[1])).T[:, :1]

    def keys(cell, point, count):
        lane = iota(cell.shape, 1)
        key = jnp.where(lane < column(count), (cell << shift) | point, cells << shift)
        return sort_columns(key)

    enc = keys(enc_cell[...], enc_point[...], enc_count[...])
    dec = keys(dec_cell[...], dec_query[...], dec_count[...])
    enc_keys[...] = enc.T
    dec_keys[...] = dec.T
    ends = [enc[:1], enc[-1:], dec[:1], dec[-1:]]
    bounds[...] = jnp.concatenate(ends + [jnp.zeros((4, LANES), jnp.int32)], axis=0) >> shift

    blocks = dec_cell.shape[0]
    lane_valid = jnp.where(
        iota((blocks, LANES), 1) < column(dec_count[...]), dec_query[...], owners * LANES
    )
    ones = jnp.zeros((max(owners, 16), LANES), F32)
    degree = ones
    for block in range(0, blocks, 2):
        row = jnp.concatenate([lane_valid[block : block + 1], lane_valid[block + 1 : block + 2]], axis=1)
        high = one_hot(row >> 7, 0, ones.shape[0])
        low = one_hot(row & (LANES - 1), 0, LANES)
        degree = degree + dot(high, low, NT)
    degree = degree[:owners]
    filled = jnp.ones((1, LANES), F32)
    empty = jnp.zeros((3, LANES), F32)
    rows = [pos[...], filled, feat[...], query_pos[...], filled, pred_bar[...], empty, degree]
    mine = jnp.concatenate(rows, axis=0)
    for owner in range(owners):
        payload[owner] = mine


def enc_forward_kernel(
    place_ref, bounds, keys, shared, w1, b1, w2, b2, lift_w, lift_b, plane_high, plane_low,
    saved, lat, scale, plane_out,
    total, table, first, second, message, *, owners, cells, width,
):
    step = pl.program_id(0)
    rows_here = cells // PLANE
    per = CHUNK // keys.shape[1]
    first_row = place_ref[0] * rows_here

    @pl.when(step == 0)
    def _():
        total[...] = jnp.zeros_like(total)
        feats = jnp.concatenate([shared[i, :FEAT_ROWS] for i in range(owners)], axis=0)
        table[...] = jnp.concatenate(halves(feats), axis=0)
        empty = jnp.zeros((3, width), F32)
        pre_rows = jnp.concatenate([w1[3:6], b1[...], jnp.zeros((4, width), F32)], axis=0)
        lift_rows = jnp.concatenate([empty, lift_b[...], lift_w[...]], axis=0)
        cell_rows = jnp.concatenate([w1[0:3] / (RES - 1.0), jnp.zeros((5, width), F32)], axis=0)
        first[...] = layer_matrix(
            jnp.concatenate([pre_rows, lift_rows], axis=1),
            jnp.concatenate([cell_rows, jnp.zeros((8, width), F32)], axis=1),
            owners,
        )
        second[...] = weights3(w2[...].T)

    low_cell, _ = cell_range(bounds, 0, step * GROUP, per)

    @pl.when(low_cell < cells)
    def _():
        bias = jnp.broadcast_to(b2[...], (8, width)).T[:, :1]
        windows = []
        for i in range(GROUP):
            chunk = step * GROUP + i
            lanes = slice(i * CHUNK, (i + 1) * CHUNK)
            key = key_row(keys, chunk)
            cell, _, _, found, place = edge_inputs(key, table[...], first_row, owners)
            both = dot(first[...], stack_inputs(found, place, owners))
            lifted = both[width:]
            hidden, slope = gelu_both(both[:width])
            kernel = dot(second[...], stack3(hidden)) + bias
            saved[0 * width : 1 * width, lanes] = hidden
            saved[1 * width : 2 * width, lanes] = slope
            saved[2 * width : 3 * width, lanes] = lifted
            saved[3 * width : 4 * width, lanes] = kernel
            saved[4 * width :, lanes] = fold_feats(found, owners)
            high, low = halves(kernel * lifted)
            ones = jnp.ones((16, CHUNK), BF16)
            rows = jnp.concatenate([high, low, ones], axis=0)
            message[:, lanes] = rows
            begin, end = cell_range(bounds, 0, chunk, per)
            begin = pl.multiple_of(begin & -8, 8)
            hot = one_hot(cell, begin, ENC_WINDOW)
            where = pl.ds(begin, ENC_WINDOW)
            total[where, : 2 * width + 16] += dot(hot, rows, NT)
            windows.append((key, begin, (end - begin) // ENC_WINDOW + 1))

        most = windows[0][2]
        for _, _, count in windows[1:]:
            most = jnp.maximum(most, count)

        @pl.when(most > 1)
        def _():
            for i, (key, begin, count) in enumerate(windows):
                cell = key >> log2(owners * LANES)

                def more(j, carry):
                    start = pl.multiple_of(begin + j * ENC_WINDOW, 8)
                    hot = one_hot(cell, start, ENC_WINDOW)
                    part = dot(hot, message[:, i * CHUNK : (i + 1) * CHUNK], NT)
                    total[pl.ds(start, ENC_WINDOW), : 2 * width + 16] += part
                    return carry

                lax.fori_loop(1, count, more, 0)

    @pl.when(step == pl.num_programs(0) - 1)
    def _():
        fields, scales = [], []
        for row in range(rows_here):
            slab = total[row * PLANE : (row + 1) * PLANE]
            inverse = 1.0 / jnp.maximum(slab[:, 2 * width : 2 * width + 1], 1.0)
            fields.append((slab[:, :width] + slab[:, width : 2 * width]) * inverse)
            scales.append(jnp.broadcast_to(inverse, (PLANE, width)))
        field = jnp.concatenate(fields, axis=1)
        lat[...] = field
        scale[...] = jnp.concatenate(scales, axis=1)
        high, low = halves(field)
        plane_out[...] = (
            dot(plane_high[...], high) + dot(plane_low[...], high) + dot(plane_high[...], low)
        )


def dec_sums_kernel(
    place_ref, bounds, keys, shared, w1, b1, saved, sums,
    total, table, first, message, *, owners, cells, width,
):
    step = pl.program_id(0)
    rows_here = cells // PLANE
    per = CHUNK // keys.shape[1]
    first_row = place_ref[0] * rows_here

    @pl.when(step == 0)
    def _():
        total[...] = jnp.zeros_like(total)
        degree = shared[0, 2 * FEAT_ROWS :]
        for i in range(1, owners):
            degree = degree + shared[i, 2 * FEAT_ROWS :]
        inverse = 1.0 / jnp.maximum(degree, 1.0)
        feats = []
        for i in range(owners):
            rows = shared[i, FEAT_ROWS : 2 * FEAT_ROWS]
            weighted = rows * inverse[i : i + 1]
            feats.append(jnp.where(iota(rows.shape, 0) == 4, weighted, rows))
        table[...] = jnp.concatenate(halves(jnp.concatenate(feats, axis=0)), axis=0)
        feat_rows = jnp.concatenate([w1[0:3], b1[...], jnp.zeros((4, width), F32)], axis=0)
        cell_rows = jnp.concatenate([w1[3:6] / (RES - 1.0), jnp.zeros((5, width), F32)], axis=0)
        first[...] = layer_matrix(feat_rows, cell_rows, owners)

    low_cell, _ = cell_range(bounds, 2, step * GROUP, per)

    @pl.when(low_cell < cells)
    def _():
        windows = []
        for i in range(GROUP):
            chunk = step * GROUP + i
            lanes = slice(i * CHUNK, (i + 1) * CHUNK)
            key = key_row(keys, chunk)
            cell, _, _, found, place = edge_inputs(key, table[...], first_row, owners)
            hidden, slope = gelu_both(dot(first[...], stack_inputs(found, place, owners)))
            feats = fold_feats(found, owners)
            weight = feats[4:5]
            saved[0 * width : 1 * width, lanes] = hidden
            saved[1 * width : 2 * width, lanes] = slope * weight
            saved[2 * width :, lanes] = feats
            high, low = halves(hidden * weight)
            w_high, w_low = halves(feats)
            tail = jnp.concatenate([w_high.astype(F32), w_low.astype(F32)], axis=0).astype(BF16)
            rows = jnp.concatenate([high, low, tail], axis=0)
            message[:, lanes] = rows
            begin, end = cell_range(bounds, 2, chunk, per)
            begin = pl.multiple_of(begin & -8, 8)
            hot = one_hot(cell, begin, DEC_WINDOW)
            where = pl.ds(begin, DEC_WINDOW)
            total[where, : 2 * width + 16] += dot(hot, rows, NT)
            windows.append((key, begin, (end - begin) // DEC_WINDOW + 1))

        most = windows[0][2]
        for _, _, count in windows[1:]:
            most = jnp.maximum(most, count)

        @pl.when(most > 1)
        def _():
            for i, (key, begin, count) in enumerate(windows):
                cell = key >> log2(owners * LANES)

                def more(j, carry):
                    start = pl.multiple_of(begin + j * DEC_WINDOW, 8)
                    hot = one_hot(cell, start, DEC_WINDOW)
                    part = dot(hot, message[:, i * CHUNK : (i + 1) * CHUNK], NT)
                    total[pl.ds(start, DEC_WINDOW), : 2 * width + 16] += part
                    return carry

                lax.fori_loop(1, count, more, 0)

    @pl.when(step == pl.num_programs(0) - 1)
    def _():
        hidden_sums, weight_sums = [], []
        for row in range(rows_here):
            slab = total[row * PLANE : (row + 1) * PLANE]
            hidden_sums.append(slab[:, :width] + slab[:, width : 2 * width])
            weight = slab[:, 2 * width + 4 : 2 * width + 5] + slab[:, 2 * width + 12 : 2 * width + 13]
            weight_sums.append(jnp.broadcast_to(weight, (PLANE, width)))
        sums[0] = jnp.concatenate(hidden_sums, axis=1)
        sums[1] = jnp.concatenate(weight_sums, axis=1)


def x_forward(lines_ref, cos_ref, sin_ref, put, owners, lines, width):
    lanes = lines_ref.shape[2]
    for kx in range(MODES):
        real = jnp.zeros((lines, lanes), F32)
        imag = jnp.zeros((lines, lanes), F32)
        for owner in range(owners):
            cos, sin = cos_ref[kx, owner : owner + 1], sin_ref[kx, owner : owner + 1]
            line_real, line_imag = lines_ref[owner, :lines], lines_ref[owner, lines:]
            real = real + cos * line_real + sin * line_imag
            imag = imag + cos * line_imag - sin * line_real
        if lanes == width:
            put(kx, jnp.concatenate([real, imag], axis=1))
        else:
            pair = 2 * width
            while real.shape[1] > pair:
                half = real.shape[1] // 2
                real, imag = real[:, :half] + real[:, half:], imag[:, :half] + imag[:, half:]
            real = real + pltpu.roll(real, width, 1)
            imag = imag + pltpu.roll(imag, width, 1)
            put(kx, jnp.where(iota(real.shape, 1) < width, real, imag))


def x_inverse(take, out_ref, owners, lines, width):
    angles = line_angles()
    rows_here = RES // owners
    modes = [take(kx) for kx in range(MODES)]
    lane = iota(modes[0].shape, 1)
    turned = [
        jnp.where(lane < width, -pltpu.roll(mode, width, 1), pltpu.roll(mode, width, 1))
        for mode in modes
    ]

    def at(x):
        total = None
        for kx in range(MODES):
            for value, factor in ((modes[kx], np.cos(angles[kx, x])), (turned[kx], np.sin(angles[kx, x]))):
                factor = float(np.float32(factor)) if abs(factor) > 1e-9 else 0.0
                if factor == 0.0:
                    continue
                term = value if factor == 1.0 else value * factor
                total = term if total is None else total + term
        return total

    for owner in range(owners):
        if rows_here == 1:
            here = at(owner)
            out_ref[owner, :lines] = here[:, :width]
            out_ref[owner, lines:] = here[:, width:]
            continue
        for pair in range(rows_here // 2):
            one, two = at(owner * rows_here + 2 * pair), at(owner * rows_here + 2 * pair + 1)
            one_turned, two_turned = pltpu.roll(one, width, 1), pltpu.roll(two, width, 1)
            where = slice(2 * pair * width, (2 * pair + 2) * width)
            out_ref[owner, :lines, where] = jnp.where(lane < width, one, two_turned)
            out_ref[owner, lines:, where] = jnp.where(lane < width, one_turned, two)


def factor_column(place_ref, lines):
    line = place_ref[0] * lines + iota((lines, 1), 0)
    return jnp.where((line & (MODES - 1)) == 0, 1.0, 2.0) / float(RES**3)


def split_weights(spec_w, batch, width):
    block = spec_w[batch * 8 : (batch + 1) * 8].reshape(8 * width, 2 * width)
    return jnp.concatenate(halves(block), axis=1)


def mix_kernel(
    place_ref, lines_ref, cos_ref, sin_ref, spec_w, modes_out, out_ref, modes, mixed,
    *, owners, width,
):
    step = pl.program_id(0)
    lines = MODES * MODES // owners

    @pl.when(step == 0)
    def _():
        def put(kx, value):
            modes[pl.ds(kx, lines, MODES), :] = value

        x_forward(lines_ref, cos_ref, sin_ref, put, owners, lines, width)
        modes_out[...] = modes[...]

    base = step * STEP_MODES
    wide_lane = iota((8, 8 * width), 1) // width
    own = wide_lane == iota((8, 8 * width), 0)
    lane = iota((8, 2 * width), 1)
    for batch in range(STEP_MODES // 8):
        where = pl.ds(pl.multiple_of(base + batch * 8, 8), 8)
        u = modes[where, :]
        u_turned = pltpu.roll(u, width, 1)
        real = jnp.where(lane < width, u, u_turned)
        imag = jnp.where(lane < width, u_turned, u)
        rows = [jnp.where(own, jnp.concatenate([part] * 4, axis=1), 0.0) for part in (real, imag)]
        left = jnp.concatenate(halves(jnp.concatenate(rows, axis=0)), axis=0)
        product = dot(left, split_weights(spec_w, batch, width))
        product = product[:, : 2 * width] + product[:, 2 * width :]
        product = product[:16] + product[16:]
        turned = pltpu.roll(product[8:], width, 1)
        mixed[where, :] = product[:8] + jnp.where(lane < width, -turned, turned)

    @pl.when(step == pl.num_programs(0) - 1)
    def _():
        factor = factor_column(place_ref, lines)

        def take(kx):
            return mixed[pl.ds(kx, lines, MODES), :] * factor

        x_inverse(take, out_ref, owners, lines, width)


def mix_back_kernel(
    place_ref, lines_ref, cos_ref, sin_ref, spec_w, grads_out, out_ref, grads, back,
    *, owners, width,
):
    step = pl.program_id(0)
    lines = MODES * MODES // owners

    @pl.when(step == 0)
    def _():
        factor = factor_column(place_ref, lines)

        def put(kx, value):
            grads[pl.ds(kx, lines, MODES), :] = value * factor

        x_forward(lines_ref, cos_ref, sin_ref, put, owners, lines, width)
        grads_out[...] = grads[...]

    base = step * STEP_MODES
    wide_lane = iota((8, 8 * width), 1) // width
    own = wide_lane == iota((8, 8 * width), 0)
    lane = iota((8, 2 * width), 1)
    for batch in range(STEP_MODES // 8):
        where = pl.ds(pl.multiple_of(base + batch * 8, 8), 8)
        g = grads[where, :]
        g_turned = pltpu.roll(g, width, 1)
        rows = [g, jnp.where(lane < width, g_turned, -g_turned)]
        left = jnp.concatenate(halves(jnp.concatenate(rows, axis=0)), axis=0)
        left = jnp.concatenate([left, left], axis=1)
        product = dot(left, split_weights(spec_w, batch, width), NT)
        product = product[:16] + product[16:]
        parts = []
        for rows in (product[:8], product[8:]):
            rows = jnp.where(own, rows, 0.0)
            while rows.shape[1] > 2 * width:
                half = rows.shape[1] // 2
                rows = rows[:, :half] + rows[:, half:]
            parts.append(rows + pltpu.roll(rows, width, 1))
        back[where, :] = jnp.where(lane < width, parts[0], parts[1])

    @pl.when(step == pl.num_programs(0) - 1)
    def _():
        def take(kx):
            return back[pl.ds(kx, lines, MODES), :]

        x_inverse(take, out_ref, owners, lines, width)


def spec_grad_kernel(modes, grads, out, *, shapes, width):
    own = iota((8, 8 * width), 1) // width == iota((8, 8 * width), 0)
    lane = iota((8, 2 * width), 1)
    for batch in range(STEP_MODES // 8):
        where = slice(batch * 8, (batch + 1) * 8)
        left, right = [], []
        for shape in range(shapes):
            u, g = modes[shape, where], grads[shape, where]
            u_turned, g_turned = pltpu.roll(u, width, 1), pltpu.roll(g, width, 1)
            for part in (jnp.where(lane < width, u, u_turned), jnp.where(lane < width, u_turned, u)):
                left.append(jnp.where(own, jnp.concatenate([part] * 4, axis=1), 0.0))
            right += [g, jnp.where(lane < width, g_turned, -g_turned)]
        left_high, left_low = halves(jnp.concatenate(left, axis=0))
        right_high, right_low = halves(jnp.concatenate(right, axis=0))
        left = jnp.concatenate([left_high, left_low, left_high], axis=0)
        right = jnp.concatenate([right_high, right_high, right_low], axis=0)
        product = dot(left, right, TN)
        out[where] = product.reshape(8, width, 2 * width)


def grid_kernel(
    lines_ref, lat, sums, skip_w, skip_b, dec_w2, dec_b2, proj_w,
    inverse_high, inverse_low, plane_high, plane_low,
    plane_out, pre_bar_out, latent_out, reach_out, *, rows_here, width,
):
    high, low = halves(lines_ref[...])
    spectral = dot(inverse_high[...], high) + dot(inverse_low[...], high) + dot(inverse_high[...], low)
    skip = dot3(lat[...], spread(skip_w[...], rows_here))
    latent, slope = gelu_both(spectral + skip + tile_lanes(skip_b[...], rows_here))
    reach = dot3(sums[0], spread(dec_w2[...], rows_here))
    reach = reach + sums[1] * tile_lanes(dec_b2[...], rows_here)
    pre_bar = reach * tile_lanes(proj_w[...], rows_here) * slope
    high, low = halves(pre_bar)
    plane_out[...] = dot(plane_high[...], high) + dot(plane_low[...], high) + dot(plane_high[...], low)
    pre_bar_out[...] = pre_bar
    latent_out[...] = latent
    reach_out[...] = reach


def grid_grads_kernel(
    lat, pre_bar, latent, reach, sums, dec_w2, dec_b2, proj_w,
    skip_w_grad, dec_w2_grad, rows_out, table, *, rows_here, width,
):
    skip_w_grad[...] = gather_blocks(dot3(lat[...], pre_bar[...], TN), rows_here, width, width)
    scaled = latent[...] * tile_lanes(proj_w[...], rows_here)
    dec_w2_grad[...] = gather_blocks(dot3(sums[0], scaled, TN), rows_here, width, width)

    def column_sum(value):
        return fold_lanes(jnp.sum(value, axis=0, keepdims=True), rows_here, width)

    rows = [column_sum(pre_bar[...]), column_sum(sums[1] * scaled), column_sum(reach[...] * latent[...])]
    rows_out[...] = jnp.concatenate(rows + [jnp.zeros((5, width), F32)], axis=0)
    cell_kernel = dot3(scaled, spread(dec_w2[...], rows_here), NT)
    offset = scaled * tile_lanes(dec_b2[...], rows_here)
    cells = rows_here * PLANE
    table[cells:] = jnp.zeros((PAD, table.shape[1]), BF16)
    for row in range(rows_here):
        lanes = slice(row * width, (row + 1) * width)
        where = slice(row * PLANE, (row + 1) * PLANE)
        constant = jnp.sum(offset[:, lanes], axis=1, keepdims=True)
        high, low = halves(cell_kernel[:, lanes])
        c_high, c_low = halves(constant)
        lane = iota((PLANE, LANES), 1)
        tail = jnp.where(lane == 0, c_high.astype(F32), jnp.where(lane == 1, c_low.astype(F32), 0.0))
        table[where, : 2 * width] = jnp.concatenate([high.astype(F32), low.astype(F32)], axis=1).astype(BF16)
        table[where, 2 * width :] = tail.astype(BF16)


def dec_edges_kernel(
    place_ref, bounds, keys, saved, table, pred_out, w1_out, b1_out,
    found_scratch, pred_total, grad_total, *, owners, cells, width,
):
    step = pl.program_id(0)
    rows_here = cells // PLANE
    per = CHUNK // keys.shape[1]
    first_row = place_ref[0] * rows_here
    shift = log2(owners * LANES)

    @pl.when(step == 0)
    def _():
        pred_total[...] = jnp.zeros_like(pred_total)
        grad_total[...] = jnp.zeros_like(grad_total)

    low_cell, _ = cell_range(bounds, 2, step * GROUP, per)

    @pl.when(low_cell < cells)
    def _():
        windows = []
        for i in range(GROUP):
            chunk = step * GROUP + i
            key = key_row(keys, chunk)
            begin, end = cell_range(bounds, 2, chunk, per)
            begin = pl.multiple_of(begin & -16, 16)
            hot = one_hot(key >> shift, begin, DEC_WINDOW)
            part = dot(table[pl.ds(begin, DEC_WINDOW), : 2 * width + 16], hot, TN)
            found_scratch[:, i * CHUNK : (i + 1) * CHUNK] = part
            windows.append((key, begin, (end - begin) // DEC_WINDOW + 1))

        most = windows[0][2]
        for _, _, count in windows[1:]:
            most = jnp.maximum(most, count)

        @pl.when(most > 1)
        def _():
            for i, (key, begin, count) in enumerate(windows):

                def more(j, carry):
                    start = pl.multiple_of(begin + j * DEC_WINDOW, 16)
                    hot = one_hot(key >> shift, start, DEC_WINDOW)
                    part = dot(table[pl.ds(start, DEC_WINDOW), : 2 * width + 16], hot, TN)
                    found_scratch[:, i * CHUNK : (i + 1) * CHUNK] += part
                    return carry

                lax.fori_loop(1, count, more, 0)

        lefts, rights, values, hots = [], [], [], []
        for i, (key, _, _) in enumerate(windows):
            lanes = slice(i * CHUNK, (i + 1) * CHUNK)
            point = key & (owners * LANES - 1)
            found = found_scratch[:width, lanes] + found_scratch[width : 2 * width, lanes]
            constant = found_scratch[2 * width : 2 * width + 1, lanes] + found_scratch[2 * width + 1 : 2 * width + 2, lanes]
            edge = jnp.sum(saved[:width, lanes] * found, axis=0, keepdims=True) + constant
            owner = iota((max(owners, 8), CHUNK), 0)
            spread_edge = jnp.where(owner == (point >> 7), edge, 0.0)
            high, low = halves(spread_edge)
            values.append(jnp.concatenate([high.astype(F32), low.astype(F32)], axis=0).astype(BF16))
            hots.append(one_hot(point & (LANES - 1), 0, LANES))
            high, low = halves(saved[width : 2 * width, lanes] * found)
            lefts.append(jnp.concatenate([high, low], axis=0))
            feats = saved[2 * width :, lanes]
            f_high, f_low = halves(feats)
            place = place_rows(key >> shift, first_row)
            right = jnp.concatenate([f_high.astype(F32), f_low.astype(F32), place, place], axis=0)
            rights.append(right.astype(BF16))
        pred_total[...] += dot(jnp.concatenate(values, axis=1), jnp.concatenate(hots, axis=1), NT)
        grad_total[...] += dot(jnp.concatenate(lefts, axis=1), jnp.concatenate(rights, axis=1), NT)

    @pl.when(step == pl.num_programs(0) - 1)
    def _():
        count = max(owners, 8)
        pred_out[...] = pred_total[:owners] + pred_total[count : count + owners]
        grad = grad_total[:width] + grad_total[width:]
        feats = (grad[:, :8] + grad[:, 8:16]).T
        places = grad[:, 16:24].T / (RES - 1.0)
        w1_out[...] = jnp.concatenate([feats[:3], places[:3]], axis=0)
        b1_out[...] = feats[3:4]


def place_rows(cell, first_row):
    row = iota((8, cell.shape[1]), 0)
    shifts = jnp.where(row == 0, 2 * log2(RES), jnp.where(row == 1, log2(RES), 0))
    place = (cell >> shifts) & jnp.where(row < 3, RES - 1, 0)
    return (place + jnp.where(row == 0, first_row, 0)).astype(F32)


def enc_back_kernel(
    place_ref, bounds, keys, saved, lines_ref, pre_bar, scale, skip_w, w2, lift_w,
    inverse_high, inverse_low,
    feat_out, w1_out, b1_out, w2_out, b2_out, lift_w_out, lift_b_out,
    table, found_scratch, second, feat_total, grad_total, *, owners, cells, width,
):
    step = pl.program_id(0)
    rows_here = cells // PLANE
    per = CHUNK // keys.shape[1]
    first_row = place_ref[0] * rows_here
    shift = log2(owners * LANES)
    count8 = max(owners, 8)

    @pl.when(step == 0)
    def _():
        feat_total[...] = jnp.zeros_like(feat_total)
        grad_total[...] = jnp.zeros_like(grad_total)
        second[...] = weights3(w2[...])
        high, low = halves(lines_ref[...])
        spectral = (
            dot(inverse_high[...], high) + dot(inverse_low[...], high) + dot(inverse_high[...], low)
        )
        skip = dot3(pre_bar[...], spread(skip_w[...], rows_here), NT)
        field = (spectral + skip) * scale[...]
        table[cells:] = jnp.zeros((PAD, 2 * width), BF16)
        for row in range(rows_here):
            high, low = halves(field[:, row * width : (row + 1) * width])
            both = jnp.concatenate([high.astype(F32), low.astype(F32)], axis=1).astype(BF16)
            table[row * PLANE : (row + 1) * PLANE] = both

    low_cell, _ = cell_range(bounds, 0, step * GROUP, per)

    @pl.when(low_cell < cells)
    def _():
        lift_columns = jnp.concatenate([lift_w[...], jnp.zeros((4, width), F32)], axis=0).T
        windows = []
        for i in range(GROUP):
            chunk = step * GROUP + i
            key = key_row(keys, chunk)
            begin, end = cell_range(bounds, 0, chunk, per)
            begin = pl.multiple_of(begin & -16, 16)
            hot = one_hot(key >> shift, begin, ENC_WINDOW)
            part = dot(table[pl.ds(begin, ENC_WINDOW), :], hot, TN)
            found_scratch[:, i * CHUNK : (i + 1) * CHUNK] = part
            windows.append((key, begin, (end - begin) // ENC_WINDOW + 1))

        most = windows[0][2]
        for _, _, count in windows[1:]:
            most = jnp.maximum(most, count)

        @pl.when(most > 1)
        def _():
            for i, (key, begin, count) in enumerate(windows):

                def more(j, carry):
                    start = pl.multiple_of(begin + j * ENC_WINDOW, 16)
                    hot = one_hot(key >> shift, start, ENC_WINDOW)
                    part = dot(table[pl.ds(start, ENC_WINDOW), :], hot, TN)
                    found_scratch[:, i * CHUNK : (i + 1) * CHUNK] += part
                    return carry

                lax.fori_loop(1, count, more, 0)

        lefts, rights, values, hots = [], [], [], []
        for i, (key, _, _) in enumerate(windows):
            lanes = slice(i * CHUNK, (i + 1) * CHUNK)
            point = key & (owners * LANES - 1)
            found = found_scratch[:width, lanes] + found_scratch[width:, lanes]
            kernel_bar = found * saved[2 * width : 3 * width, lanes]
            source_bar = found * saved[3 * width : 4 * width, lanes]
            k_high, k_low = halves(kernel_bar)
            hidden_bar = dot(second[...], jnp.concatenate([k_high, k_low, k_high], axis=0))
            pre_edge = hidden_bar * saved[width : 2 * width, lanes]
            parts = [*halves(saved[:width, lanes]), *halves(pre_edge), *halves(source_bar)]
            lefts.append(jnp.concatenate(parts + [jnp.ones((16, CHUNK), BF16)], axis=0))
            feats = saved[4 * width :, lanes]
            f_high, f_low = halves(feats)
            place = place_rows(key >> shift, first_row)
            tail = jnp.concatenate([f_high.astype(F32), f_low.astype(F32), place, place], axis=0)
            rights.append(jnp.concatenate([k_high, k_low, tail.astype(BF16)], axis=0))
            owner_hot = iota((count8, CHUNK), 0) == (point >> 7)
            edges = []
            for feat in range(4):
                edge = jnp.sum(source_bar * lift_columns[:, feat : feat + 1], axis=0, keepdims=True)
                edges.append(jnp.where(owner_hot, edge, 0.0))
            values.append(jnp.concatenate(halves(jnp.concatenate(edges, axis=0)), axis=0))
            hots.append(one_hot(point & (LANES - 1), 0, LANES))
        feat_total[...] += dot(jnp.concatenate(values, axis=1), jnp.concatenate(hots, axis=1), NT)
        grad_total[...] += dot(jnp.concatenate(lefts, axis=1), jnp.concatenate(rights, axis=1), NT)

    @pl.when(step == pl.num_programs(0) - 1)
    def _():
        both = feat_total[: 4 * count8] + feat_total[4 * count8 :]
        for owner in range(owners):
            rows = [both[feat * count8 + owner : feat * count8 + owner + 1] for feat in range(4)]
            feat_out[owner] = jnp.concatenate(rows, axis=0)
        w2_part = grad_total[:width, : 2 * width] + grad_total[width : 2 * width, : 2 * width]
        w2_out[...] = w2_part[:, :width] + w2_part[:, width:]
        b2_part = grad_total[6 * width : 6 * width + 1, : 2 * width]
        b2_out[...] = b2_part[:, :width] + b2_part[:, width:]
        pre_part = grad_total[2 * width : 3 * width, 2 * width :] + grad_total[3 * width : 4 * width, 2 * width :]
        feats = (pre_part[:, :8] + pre_part[:, 8:16]).T
        places = pre_part[:, 16:24].T / (RES - 1.0)
        w1_out[...] = jnp.concatenate([places[:3], feats[:3]], axis=0)
        b1_out[...] = feats[3:4]
        lift_part = grad_total[4 * width : 5 * width, 2 * width :] + grad_total[5 * width : 6 * width, 2 * width :]
        lifts = (lift_part[:, :8] + lift_part[:, 8:16]).T
        lift_w_out[...] = lifts[4:8]
        lift_b_out[...] = lifts[3:4]


def params(mib):
    return pltpu.CompilerParams(vmem_limit_bytes=mib << 20)


def shape(*dims, dtype=F32):
    return jax.ShapeDtypeStruct(dims, dtype)


def on_device(
    mesh_feat,
    mesh_pos,
    query_pos,
    enc_cell,
    enc_point,
    enc_count,
    dec_cell,
    dec_query,
    dec_count,
    enc_w1,
    enc_b1,
    enc_w2,
    enc_b2,
    lift_w,
    lift_b,
    spec_w,
    skip_w,
    skip_b,
    dec_w1,
    dec_b1,
    dec_w2,
    dec_b2,
    proj_w,
    proj_b,
    pred_bar,
):
    width = lift_w.shape[1]
    owners = lax.axis_size("wide")
    shapes = lax.axis_size("grid")
    rows_here = RES // owners
    cells = rows_here * PLANE
    modes_here = spec_w.shape[0]
    lines = modes_here // MODES
    enc_blocks, dec_blocks = enc_cell.shape[1], dec_cell.shape[1]
    enc_edges, dec_edges = enc_blocks * LANES, dec_blocks * LANES
    span = GROUP * CHUNK
    lanes = rows_here * width
    place = lax.axis_index("wide").astype(jnp.int32).reshape(1)
    plane = plane_matrix(owners)
    plane_high, plane_low = (jnp.asarray(part) for part in halves_np(plane))
    inverse_high, inverse_low = (jnp.asarray(part) for part in halves_np(np.ascontiguousarray(plane.T)))
    cos_x, sin_x = (jnp.asarray(part) for part in x_tables(rows_here, width))
    rows = [value.reshape(1, -1) for value in (enc_b1, enc_b2, lift_b, skip_b, dec_b1, dec_b2, proj_w)]
    enc_b1, enc_b2, lift_b, skip_b, dec_b1, dec_b2, proj_w = rows

    enc_keys, dec_keys, bounds, payload = pl.pallas_call(
        partial(sort_kernel, owners=owners, cells=cells),
        in_specs=[VMEM] * 10,
        out_specs=[VMEM] * 4,
        out_shape=[
            shape(LANES, enc_blocks, dtype=jnp.int32),
            shape(LANES, dec_blocks, dtype=jnp.int32),
            shape(8, LANES, dtype=jnp.int32),
            shape(owners, 2 * FEAT_ROWS + owners, LANES),
        ],
        compiler_params=params(32),
        name="sort_edges",
    )(
        enc_cell[0], enc_point[0], enc_count, dec_cell[0], dec_query[0], dec_count,
        mesh_feat[0], mesh_pos[0], query_pos[0], pred_bar,
    )
    shared = lax.all_to_all(payload, "wide", 0, 0, tiled=True)

    fixed = owners * FEAT_ROWS
    depth = 3 * fixed + 16
    saved_rows = 4 * width + FEAT_ROWS
    saved, lat, scale, plane_lat = pl.pallas_call(
        partial(enc_forward_kernel, owners=owners, cells=cells, width=width),
        grid=(enc_edges // span,),
        in_specs=[SMEM, SMEM] + [VMEM] * 10,
        out_specs=[pl.BlockSpec((saved_rows, span), lambda i: (0, i)), VMEM, VMEM, VMEM],
        out_shape=[
            shape(saved_rows, enc_edges),
            shape(PLANE, lanes),
            shape(PLANE, lanes),
            shape(2 * MODES * MODES, lanes),
        ],
        scratch_shapes=[
            pltpu.VMEM((cells + PAD, 2 * LANES), F32),
            pltpu.VMEM((2 * fixed, LANES), BF16),
            pltpu.VMEM((2 * width, depth), BF16),
            pltpu.VMEM((width, 3 * width), BF16),
            pltpu.VMEM((2 * width + 16, span), BF16),
        ],
        compiler_params=params(48),
        name="encode",
    )(place, bounds, enc_keys, shared, enc_w1, enc_b1, enc_w2, enc_b2, lift_w, lift_b, plane_high, plane_low)

    def exchange(value):
        return lax.all_to_all(value.reshape(owners, 2 * lines, lanes), "wide", 0, 0, tiled=True)

    modes_lines = exchange(plane_lat)

    dec_rows = 2 * width + FEAT_ROWS
    dec_saved, sums = pl.pallas_call(
        partial(dec_sums_kernel, owners=owners, cells=cells, width=width),
        grid=(dec_edges // span,),
        in_specs=[SMEM, SMEM] + [VMEM] * 4,
        out_specs=[pl.BlockSpec((dec_rows, span), lambda i: (0, i)), VMEM],
        out_shape=[shape(dec_rows, dec_edges), shape(2, PLANE, lanes)],
        scratch_shapes=[
            pltpu.VMEM((cells + PAD, 2 * LANES), F32),
            pltpu.VMEM((2 * fixed, LANES), BF16),
            pltpu.VMEM((width, depth), BF16),
            pltpu.VMEM((2 * width + 16, span), BF16),
        ],
        compiler_params=params(48),
        name="decode_sums",
    )(place, bounds, dec_keys, shared, dec_w1, dec_b1)

    spec_block = pl.BlockSpec((STEP_MODES, width, 2 * width), lambda i: (i, 0, 0))

    def mode_pass(kernel, lines_in, name):
        return pl.pallas_call(
            partial(kernel, owners=owners, width=width),
            grid=(modes_here // STEP_MODES,),
            in_specs=[SMEM, VMEM, VMEM, VMEM, spec_block],
            out_specs=[VMEM, VMEM],
            out_shape=[shape(modes_here, 2 * width), shape(owners, 2 * lines, lanes)],
            scratch_shapes=[pltpu.VMEM((modes_here, 2 * width), F32)] * 2,
            compiler_params=params(48),
            name=name,
        )(place, lines_in, cos_x, sin_x, spec_w)

    modes, back_lines = mode_pass(mix_kernel, modes_lines, "mix_modes")

    def return_lines(value):
        swapped = lax.all_to_all(value, "wide", 0, 0, tiled=True)
        return swapped.reshape(2 * MODES * MODES, lanes)

    grid_lines = return_lines(back_lines)
    plane_bar, pre_bar, latent, reach = pl.pallas_call(
        partial(grid_kernel, rows_here=rows_here, width=width),
        in_specs=[VMEM] * 12,
        out_specs=[VMEM] * 4,
        out_shape=[shape(2 * MODES * MODES, lanes)] + [shape(PLANE, lanes)] * 3,
        compiler_params=params(48),
        name="grid_fields",
    )(
        grid_lines, lat, sums, skip_w, skip_b, dec_w2, dec_b2, proj_w,
        inverse_high, inverse_low, plane_high, plane_low,
    )
    bar_lines = exchange(plane_bar)

    skip_w_grad, dec_w2_grad, row_grads, dec_table = pl.pallas_call(
        partial(grid_grads_kernel, rows_here=rows_here, width=width),
        in_specs=[VMEM] * 8,
        out_specs=[VMEM] * 4,
        out_shape=[
            shape(width, width),
            shape(width, width),
            shape(8, width),
            shape(cells + PAD, 2 * LANES, dtype=BF16),
        ],
        compiler_params=params(48),
        name="grid_grads",
    )(lat, pre_bar, latent, reach, sums, dec_w2, dec_b2, proj_w)

    mixed_bar, bar_back = mode_pass(mix_back_kernel, bar_lines, "mix_back")
    bar_grid_lines = return_lines(bar_back)
    both_modes = lax.all_gather(jnp.stack([modes, mixed_bar]), "grid", axis=0)

    count8 = max(owners, 8)
    pred_part, dec_w1_grad, dec_b1_grad = pl.pallas_call(
        partial(dec_edges_kernel, owners=owners, cells=cells, width=width),
        grid=(dec_edges // span,),
        in_specs=[SMEM, SMEM, VMEM, pl.BlockSpec((dec_rows, span), lambda i: (0, i)), VMEM],
        out_specs=[VMEM] * 3,
        out_shape=[shape(owners, LANES), shape(6, width), shape(1, width)],
        scratch_shapes=[
            pltpu.VMEM((2 * width + 16, span), F32),
            pltpu.VMEM((2 * count8, LANES), F32),
            pltpu.VMEM((2 * width, 32), F32),
        ],
        compiler_params=params(48),
        name="decode_edges",
    )(place, bounds, dec_keys, dec_saved, dec_table)

    feat_part, enc_w1_grad, enc_b1_grad, enc_w2_grad, enc_b2_grad, lift_w_grad, lift_b_grad = pl.pallas_call(
        partial(enc_back_kernel, owners=owners, cells=cells, width=width),
        grid=(enc_edges // span,),
        in_specs=[SMEM, SMEM, VMEM, pl.BlockSpec((saved_rows, span), lambda i: (0, i))] + [VMEM] * 8,
        out_specs=[VMEM] * 7,
        out_shape=[
            shape(owners, 4, LANES),
            shape(6, width),
            shape(1, width),
            shape(width, width),
            shape(1, width),
            shape(4, width),
            shape(1, width),
        ],
        scratch_shapes=[
            pltpu.VMEM((cells + PAD, 2 * width), BF16),
            pltpu.VMEM((2 * width, span), F32),
            pltpu.VMEM((width, 3 * width), BF16),
            pltpu.VMEM((8 * count8, LANES), F32),
            pltpu.VMEM((6 * width + 16, 2 * width + 32), F32),
        ],
        compiler_params=params(48),
        name="encode_back",
    )(
        place, bounds, enc_keys, saved, bar_grid_lines, pre_bar, scale, skip_w, enc_w2, lift_w,
        inverse_high, inverse_low,
    )

    spec_grad = pl.pallas_call(
        partial(spec_grad_kernel, shapes=shapes, width=width),
        grid=(modes_here // STEP_MODES,),
        in_specs=[
            pl.BlockSpec((shapes, None, STEP_MODES, 2 * width), lambda i: (0, 0, i, 0)),
            pl.BlockSpec((shapes, None, STEP_MODES, 2 * width), lambda i: (0, 1, i, 0)),
        ],
        out_specs=spec_block,
        out_shape=shape(modes_here, width, 2 * width),
        compiler_params=params(48),
        name="spec_grad",
    )(both_modes, both_modes)

    summed = jnp.concatenate(
        [
            enc_w1_grad, enc_b1_grad, enc_w2_grad, enc_b2_grad, lift_w_grad, lift_b_grad,
            skip_w_grad, row_grads[0:1], dec_w1_grad, dec_b1_grad, dec_w2_grad,
            row_grads[1:2], row_grads[2:3],
            jnp.broadcast_to(jnp.sum(pred_bar), (1, width)),
        ],
        axis=0,
    )
    count = summed.shape[0]
    summed = jnp.concatenate([summed, jnp.zeros((count % 2, width), F32)], axis=0).reshape(-1, 2 * width)
    packed = jnp.concatenate(
        [
            jnp.broadcast_to(summed[None], (owners,) + summed.shape),
            feat_part,
            pred_part[:, None, :],
        ],
        axis=1,
    )
    arrived = lax.all_to_all(packed, "wide", 0, 0, tiled=True)
    arrived = jnp.sum(arrived, axis=0)
    sums_rows = summed.shape[0]
    grads = arrived[:sums_rows]
    step = 1
    while step < shapes:
        grads = grads + lax.ppermute(grads, "grid", [(i, i ^ step) for i in range(shapes)])
        step *= 2
    grads = grads.reshape(-1, width)
    mesh_feat_grad = arrived[sums_rows : sums_rows + 4][None]
    degree = jnp.sum(shared[:, 2 * FEAT_ROWS :, :], axis=0)
    degree_mine = lax.dynamic_slice_in_dim(degree, place[0], 1, axis=0)
    pred = arrived[sums_rows + 4 : sums_rows + 5] / jnp.maximum(degree_mine, 1.0) + proj_b[0]

    out, at = [], 0
    for size in (6, 1, width, 1, 4, 1, width, 1, 6, 1, width, 1, 1, 1):
        part = grads[at : at + size]
        out.append(part[0] if size == 1 else part)
        at += size
    out[-1] = out[-1][:1]
    return (pred, mesh_feat_grad, *out[:6], spec_grad, *out[6:])


def solution(mesh):
    placed = (
        P("grid", None, "wide"),
        P("grid", None, "wide"),
        P("grid", None, "wide"),
        P("grid", "wide", None),
        P("grid", "wide", None),
        P("grid", "wide"),
        P("grid", "wide", None),
        P("grid", "wide", None),
        P("grid", "wide"),
        P(),
        P(),
        P(),
        P(),
        P(),
        P(),
        P("wide", None, None),
        P(),
        P(),
        P(),
        P(),
        P(),
        P(),
        P(),
        P(),
        P("grid", "wide"),
    )
    return jax.shard_map(
        on_device,
        mesh=mesh,
        in_specs=placed,
        out_specs=(
            P("grid", "wide"),
            P("grid", None, "wide"),
            P(),
            P(),
            P(),
            P(),
            P(),
            P(),
            P("wide", None, None),
            P(),
            P(),
            P(),
            P(),
            P(),
            P(),
            P(),
            P(),
        ),
        check_vma=False,
    )
```

```python
from functools import partial
import math

import jax
import jax.numpy as jnp
import ml_dtypes
import numpy as np
from jax import lax
from jax.experimental import pallas as pl
from jax.experimental.pallas import tpu as pltpu
from jax.sharding import PartitionSpec as P

MODES = 16
RES = 32
PLANE = RES * RES
CHUNK = 256
LANES = 128
ENC_GROUP = 16
DEC_GROUP = 16
FEAT_ROWS = 8
ENC_WINDOW = 64
DEC_WINDOW = 128
PAD = 256
STEP_MODES = 32
F32 = jnp.float32
BF16 = jnp.bfloat16
GELU_A = 0.7978845608028654
GELU_B = 0.044715

NN = (((1,), (0,)), ((), ()))
NT = (((1,), (1,)), ((), ()))
TN = (((0,), (0,)), ((), ()))

VMEM = pl.BlockSpec(memory_space=pltpu.VMEM)
SMEM = pl.BlockSpec(memory_space=pltpu.SMEM)


def kept_freqs():
    half = MODES // 2
    return np.concatenate([np.arange(half), np.arange(RES - half, RES)])


def plane_matrix(owners):
    lines = MODES * MODES // owners
    line = np.arange(MODES * MODES)
    freq_y, freq_z = kept_freqs()[line // MODES], line % MODES
    cell = np.arange(PLANE)
    turns = (freq_y[:, None] * (cell // RES) + freq_z[:, None] * (cell % RES)) % RES
    angle = turns * (2.0 * math.pi / RES)
    both = np.stack([np.cos(angle), -np.sin(angle)]).reshape(2, owners, lines, PLANE)
    matrix = both.transpose(1, 0, 2, 3).reshape(2 * MODES * MODES, PLANE)
    return matrix.astype(np.float32)


def halves_np(matrix):
    high = matrix.astype(ml_dtypes.bfloat16)
    low = (matrix - high.astype(np.float32)).astype(ml_dtypes.bfloat16)
    return high, low


def line_angles():
    turns = (kept_freqs()[:, None] * np.arange(RES)[None, :]) % RES
    return turns * (2.0 * math.pi / RES)


def x_tables(rows_here, width):
    angle = line_angles().reshape(MODES, RES // rows_here, rows_here, 1)
    angle = np.broadcast_to(angle, (MODES, RES // rows_here, rows_here, width))
    angle = angle.reshape(MODES, RES // rows_here, rows_here * width)
    return np.cos(angle).astype(np.float32), np.sin(angle).astype(np.float32)


def log2(number):
    return number.bit_length() - 1


def iota(shape, axis):
    return lax.broadcasted_iota(jnp.int32, shape, axis)


def halves(value):
    high = value.astype(BF16)
    low = (value - high.astype(F32)).astype(BF16)
    return high, low


def dot(a, b, dims=NN):
    return lax.dot_general(a, b, dims, preferred_element_type=F32)


def dot3(a, b, dims=NN):
    a_high, a_low = halves(a)
    b_high, b_low = halves(b)
    return dot(a_high, b_high, dims) + dot(a_low, b_high, dims) + dot(a_high, b_low, dims)


def one_hot(index, first, rows):
    places = iota((rows, index.shape[1]), 0) + first
    return jnp.where(places == index, 1.0, 0.0).astype(BF16)


def gelu_both(value):
    square = value * value
    turn = jnp.tanh(value * (GELU_A + (GELU_A * GELU_B) * square))
    half = 0.5 * (1.0 + turn)
    slope = half + (0.5 * value) * (1.0 - turn * turn) * (
        GELU_A + (3.0 * GELU_A * GELU_B) * square
    )
    return value * half, slope


def sort_columns(values):
    rows = values.shape[0]
    regs = rows // 8
    low = log2(regs)
    total = low + 3 + 7
    sub = iota((8, LANES), 0)
    lane = iota((8, LANES), 1)
    x = values.reshape(regs, 8, LANES)

    def flip(x, bit):
        if bit >= total:
            return x
        if bit < low:
            y = x.reshape(regs >> (bit + 1), 2, 1 << bit, 8, LANES)
            return jnp.stack([y[:, 0], ~y[:, 1]], axis=1).reshape(regs, 8, LANES)
        if bit < low + 3:
            mask = -((sub >> (bit - low)) & 1)
        else:
            mask = -((lane >> (bit - low - 3)) & 1)
        return x ^ mask[None]

    def exchange(x, bit):
        if bit < low:
            y = x.reshape(regs >> (bit + 1), 2, 1 << bit, 8, LANES)
            one, two = y[:, 0], y[:, 1]
            pair = [jnp.minimum(one, two), jnp.maximum(one, two)]
            return jnp.stack(pair, axis=1).reshape(regs, 8, LANES)
        if bit < low + 3:
            axis, dist, size, place = 1, 1 << (bit - low), 8, sub
        else:
            axis, dist, size, place = 2, 1 << (bit - low - 3), LANES, lane
        after = pltpu.roll(x, size - dist, axis)
        before = after if 2 * dist == size else pltpu.roll(x, dist, axis)
        first = ((place & dist) == 0)[None]
        return jnp.where(first, jnp.minimum(x, after), jnp.maximum(x, before))

    for phase in range(1, total + 1):
        x = flip(x, phase)
        for bit in reversed(range(phase)):
            x = exchange(x, bit)
        x = flip(x, phase)
    return x.reshape(rows, LANES)


def layer_matrix(feat_rows, cell_rows, owners):
    feat_high, feat_low = halves(feat_rows)
    cell_high, cell_low = halves(cell_rows)
    parts = [feat_high] * owners + [feat_high] * owners + [feat_low] * owners
    parts += [cell_high, cell_low]
    stacked = jnp.concatenate([part.astype(F32) for part in parts], axis=0)
    depth = stacked.shape[0]
    more = -depth % LANES
    if more:
        stacked = jnp.concatenate([stacked, jnp.zeros((more, stacked.shape[1]), F32)], axis=0)
    return stacked.T[:, :depth].astype(BF16)


def edge_inputs(key, table, first_row, owners):
    shift = log2(owners * LANES)
    cell = key >> shift
    point = key & (owners * LANES - 1)
    low_hot = one_hot(point & (LANES - 1), 0, LANES)
    found = dot(table, low_hot)
    owner = (iota(found.shape, 0) >> 3) & (owners - 1)
    found = jnp.where(owner == (point >> 7), found, 0.0)
    row = iota((8, key.shape[1]), 0)
    shifts = jnp.where(row == 0, 2 * log2(RES), jnp.where(row == 1, log2(RES), 0))
    place = (cell >> shifts) & jnp.where(row < 3, RES - 1, 0)
    place = (place + jnp.where(row == 0, first_row, 0)).astype(F32)
    return cell, point, low_hot, found, place


def stack_inputs(found, place, owners):
    exact = found.astype(BF16)
    places = jnp.concatenate([place, place], axis=0).astype(BF16)
    return jnp.concatenate([exact, exact[: owners * FEAT_ROWS], places], axis=0)


def fold_feats(found, owners):
    return jnp.sum(found.reshape(2 * owners, FEAT_ROWS, found.shape[1]), axis=0)


def stack3(value):
    high, low = halves(value)
    return jnp.concatenate([high, low, high], axis=0)


def weights3(matrix):
    high, low = halves(matrix)
    return jnp.concatenate([high, high, low], axis=1)


def key_row(keys_ref, chunk):
    per = CHUNK // keys_ref.shape[1]
    rows = [keys_ref[pl.ds(chunk * per + i, 1), :] for i in range(per)]
    return rows[0] if per == 1 else jnp.concatenate(rows, axis=1)


def cell_range(bounds_ref, line, chunk, per):
    return bounds_ref[line, chunk * per], bounds_ref[line + 1, chunk * per + per - 1]


def spread(block, copies):
    rows, columns = block.shape
    tiled = jnp.concatenate([jnp.concatenate([block] * copies, axis=1)] * copies, axis=0)
    return jnp.where(
        iota(tiled.shape, 0) // rows == iota(tiled.shape, 1) // columns, tiled, 0.0
    )


def gather_blocks(product, copies, rows, columns):
    total = product[:rows, :columns]
    for i in range(1, copies):
        total = total + product[i * rows : (i + 1) * rows, i * columns : (i + 1) * columns]
    return total


def tile_lanes(row, copies):
    return row if copies == 1 else jnp.concatenate([row] * copies, axis=1)


def fold_lanes(row, copies, width):
    total = row[:, :width]
    for i in range(1, copies):
        total = total + row[:, i * width : (i + 1) * width]
    return total


def column(counts):
    return jnp.broadcast_to(counts, (8, counts.shape[1])).T[:, :1]


def share_kernel(feat, pos, query_pos, pred_bar, dec_query, dec_count, payload, *, owners):
    blocks = dec_query.shape[0]
    lane_valid = jnp.where(
        iota((blocks, LANES), 1) < column(dec_count[...]), dec_query[...], owners * LANES
    )
    ones = jnp.zeros((max(owners, 16), LANES), F32)
    degree = ones
    for block in range(0, blocks, 2):
        row = jnp.concatenate([lane_valid[block : block + 1], lane_valid[block + 1 : block + 2]], axis=1)
        high = one_hot(row >> 7, 0, ones.shape[0])
        low = one_hot(row & (LANES - 1), 0, LANES)
        degree = degree + dot(high, low, NT)
    filled = jnp.ones((1, LANES), F32)
    empty = jnp.zeros((3, LANES), F32)
    rows = [pos[...], filled, feat[...], query_pos[...], filled, pred_bar[...], empty, degree[:owners]]
    mine = jnp.concatenate(rows, axis=0)
    for owner in range(owners):
        payload[owner] = mine


def sort_kernel(
    enc_cell, enc_point, enc_count, dec_cell, dec_query, dec_count, after,
    enc_keys, dec_keys, bounds, *, owners, cells,
):
    shift = log2(owners * LANES)

    def keys(cell, point, count):
        lane = iota(cell.shape, 1)
        key = jnp.where(lane < column(count), (cell << shift) | point, cells << shift)
        return sort_columns(key)

    enc = keys(enc_cell[...], enc_point[...], enc_count[...])
    dec = keys(dec_cell[...], dec_query[...], dec_count[...])
    enc_keys[...] = enc.T
    dec_keys[...] = dec.T
    ends = [enc[:1], enc[-1:], dec[:1], dec[-1:]]
    bounds[...] = jnp.concatenate(ends + [jnp.zeros((4, LANES), jnp.int32)], axis=0) >> shift


def joined_keys(keys, chunk, group):
    rows = [key_row(keys, chunk + i) for i in range(group)]
    return rows, jnp.concatenate(rows, axis=1)


def later_windows(windows, size, visit):
    most = windows[0][1]
    for _, count in windows[1:]:
        most = jnp.maximum(most, count)

    @pl.when(most > 1)
    def _():
        for i, (begin, count) in enumerate(windows):

            def more(j, carry):
                visit(i, begin + j * size)
                return carry

            lax.fori_loop(1, count, more, 0)


def scatter_windows(total, keys, cell, message, bounds, line, chunk, group, size, shift, columns):
    per = CHUNK // keys.shape[1]
    windows, parts = [], []
    for i in range(group):
        begin, end = cell_range(bounds, line, chunk + i, per)
        begin = pl.multiple_of(begin & -8, 8)
        lanes = slice(i * CHUNK, (i + 1) * CHUNK)
        parts.append(dot(one_hot(cell[:, lanes], begin, size), message[:, lanes], NT))
        windows.append((begin, (end - begin) // size + 1))
    for (begin, _), part in zip(windows, parts):
        total[pl.ds(begin, size), :columns] += part

    def visit(i, start):
        start = pl.multiple_of(start, 8)
        hot = one_hot(key_row(keys, chunk + i) >> shift, start, size)
        part = dot(hot, message[:, i * CHUNK : (i + 1) * CHUNK], NT)
        total[pl.ds(start, size), :columns] += part

    later_windows(windows, size, visit)


def gather_windows(found, keys, rows, table, bounds, line, chunk, group, size, shift, columns):
    per = CHUNK // keys.shape[1]
    windows = []
    for i in range(group):
        begin, end = cell_range(bounds, line, chunk + i, per)
        begin = pl.multiple_of(begin & -16, 16)
        hot = one_hot(rows[i] >> shift, begin, size)
        found[:, i * CHUNK : (i + 1) * CHUNK] = dot(table[pl.ds(begin, size), :columns], hot, TN)
        windows.append((begin, (end - begin) // size + 1))

    def visit(i, start):
        start = pl.multiple_of(start, 16)
        hot = one_hot(key_row(keys, chunk + i) >> shift, start, size)
        part = dot(table[pl.ds(start, size), :columns], hot, TN)
        found[:, i * CHUNK : (i + 1) * CHUNK] += part

    later_windows(windows, size, visit)


def enc_forward_kernel(
    place_ref, bounds, keys, shared, w1, b1, w2, b2, lift_w, lift_b, plane_hbm,
    saved, lat, scale, plane_out,
    total, table, first, second, message, plane, copied, *, owners, cells, width,
):
    step = pl.program_id(0)
    rows_here = cells // PLANE
    group = message.shape[1] // CHUNK
    shift = log2(owners * LANES)
    first_row = place_ref[0] * rows_here
    copy = pltpu.make_async_copy(plane_hbm, plane, copied)

    @pl.when(step == 0)
    def _():
        copy.start()
        total[...] = jnp.zeros_like(total)
        feats = jnp.concatenate([shared[i, :FEAT_ROWS] for i in range(owners)], axis=0)
        table[...] = jnp.concatenate(halves(feats), axis=0)
        empty = jnp.zeros((3, width), F32)
        pre_rows = jnp.concatenate([w1[3:6], b1[...], jnp.zeros((4, width), F32)], axis=0)
        lift_rows = jnp.concatenate([empty, lift_b[...], lift_w[...]], axis=0)
        cell_rows = jnp.concatenate([w1[0:3] / (RES - 1.0), jnp.zeros((5, width), F32)], axis=0)
        first[...] = layer_matrix(
            jnp.concatenate([pre_rows, lift_rows], axis=1),
            jnp.concatenate([cell_rows, jnp.zeros((8, width), F32)], axis=1),
            owners,
        )
        second[...] = weights3(w2[...].T)

    chunk = step * group
    low_cell, _ = cell_range(bounds, 0, chunk, CHUNK // keys.shape[1])

    @pl.when(low_cell < cells)
    def _():
        bias = jnp.broadcast_to(b2[...], (8, width)).T[:, :1]
        _, key = joined_keys(keys, chunk, group)
        cell, _, _, found, place = edge_inputs(key, table[...], first_row, owners)
        both = dot(first[...], stack_inputs(found, place, owners))
        lifted = both[width:]
        hidden, slope = gelu_both(both[:width])
        kernel = dot(second[...], stack3(hidden)) + bias
        saved[0 * width : 1 * width] = hidden
        saved[1 * width : 2 * width] = slope
        saved[2 * width : 3 * width] = lifted
        saved[3 * width : 4 * width] = kernel
        saved[4 * width :] = fold_feats(found, owners)
        high, low = halves(kernel * lifted)
        message[...] = jnp.concatenate([high, low, jnp.ones((16, key.shape[1]), BF16)], axis=0)
        scatter_windows(
            total, keys, cell, message, bounds, 0, chunk, group, ENC_WINDOW, shift, 2 * width + 16
        )

    @pl.when(step == pl.num_programs(0) - 1)
    def _():
        fields, scales = [], []
        for row in range(rows_here):
            slab = total[row * PLANE : (row + 1) * PLANE]
            inverse = 1.0 / jnp.maximum(slab[:, 2 * width : 2 * width + 1], 1.0)
            fields.append((slab[:, :width] + slab[:, width : 2 * width]) * inverse)
            scales.append(jnp.broadcast_to(inverse, (PLANE, width)))
        field = jnp.concatenate(fields, axis=1)
        lat[...] = field
        scale[...] = jnp.concatenate(scales, axis=1)
        copy.wait()
        plane_out[...] = times_field(plane, field)


def times_field(matrix, field):
    high, low = halves(field)
    return dot(matrix[0], high) + dot(matrix[1], high) + dot(matrix[0], low)


def dec_sums_kernel(
    place_ref, bounds, keys, shared, w1, b1, before, saved_before, after,
    saved, total, inverse_out, table, first, message, *, owners, cells, width, first_step,
):
    step = pl.program_id(0)
    rows_here = cells // PLANE
    group = message.shape[1] // CHUNK
    shift = log2(owners * LANES)
    first_row = place_ref[0] * rows_here

    @pl.when(step == 0)
    def _():
        total[...] = jnp.zeros_like(total) if first_step == 0 else before[...]
        degree = shared[0, 2 * FEAT_ROWS :]
        for i in range(1, owners):
            degree = degree + shared[i, 2 * FEAT_ROWS :]
        inverse = 1.0 / jnp.maximum(degree, 1.0)
        inverse_out[...] = inverse
        feats = []
        for i in range(owners):
            rows = shared[i, FEAT_ROWS : 2 * FEAT_ROWS]
            weighted = rows * inverse[i : i + 1]
            feats.append(jnp.where(iota(rows.shape, 0) == 4, weighted, rows))
        table[...] = jnp.concatenate(halves(jnp.concatenate(feats, axis=0)), axis=0)
        feat_rows = jnp.concatenate([w1[0:3], b1[...], jnp.zeros((4, width), F32)], axis=0)
        cell_rows = jnp.concatenate([w1[3:6] / (RES - 1.0), jnp.zeros((5, width), F32)], axis=0)
        first[...] = layer_matrix(feat_rows, cell_rows, owners)

    chunk = (step + first_step) * group
    low_cell, _ = cell_range(bounds, 2, chunk, CHUNK // keys.shape[1])

    @pl.when(low_cell < cells)
    def _():
        _, key = joined_keys(keys, chunk, group)
        cell, _, _, found, place = edge_inputs(key, table[...], first_row, owners)
        hidden, slope = gelu_both(dot(first[...], stack_inputs(found, place, owners)))
        feats = fold_feats(found, owners)
        weight = feats[4:5]
        saved[0 * width : 1 * width] = hidden
        saved[1 * width : 2 * width] = slope * weight
        saved[2 * width :] = feats
        high, low = halves(hidden * weight)
        w_high, w_low = halves(feats)
        tail = jnp.concatenate([w_high.astype(F32), w_low.astype(F32)], axis=0).astype(BF16)
        message[...] = jnp.concatenate([high, low, tail], axis=0)
        scatter_windows(
            total, keys, cell, message, bounds, 2, chunk, group, DEC_WINDOW, shift, 2 * width + 16
        )


def x_forward(lines_ref, cos_ref, sin_ref, put, owners, lines, width):
    lanes = lines_ref.shape[2]
    for kx in range(MODES):
        real = jnp.zeros((lines, lanes), F32)
        imag = jnp.zeros((lines, lanes), F32)
        for owner in range(owners):
            cos, sin = cos_ref[kx, owner : owner + 1], sin_ref[kx, owner : owner + 1]
            line_real, line_imag = lines_ref[owner, :lines], lines_ref[owner, lines:]
            real = real + cos * line_real + sin * line_imag
            imag = imag + cos * line_imag - sin * line_real
        if lanes == width:
            put(kx, jnp.concatenate([real, imag], axis=1))
        else:
            pair = 2 * width
            while real.shape[1] > pair:
                half = real.shape[1] // 2
                real, imag = real[:, :half] + real[:, half:], imag[:, :half] + imag[:, half:]
            real = real + pltpu.roll(real, width, 1)
            imag = imag + pltpu.roll(imag, width, 1)
            put(kx, jnp.where(iota(real.shape, 1) < width, real, imag))


def x_inverse(take, out_ref, owners, lines, width):
    angles = line_angles()
    rows_here = RES // owners
    modes = [take(kx) for kx in range(MODES)]
    lane = iota(modes[0].shape, 1)
    turned = [
        jnp.where(lane < width, -pltpu.roll(mode, width, 1), pltpu.roll(mode, width, 1))
        for mode in modes
    ]

    def at(x):
        total = None
        for kx in range(MODES):
            for value, factor in ((modes[kx], np.cos(angles[kx, x])), (turned[kx], np.sin(angles[kx, x]))):
                factor = float(np.float32(factor)) if abs(factor) > 1e-9 else 0.0
                if factor == 0.0:
                    continue
                term = value if factor == 1.0 else value * factor
                total = term if total is None else total + term
        return total

    for owner in range(owners):
        if rows_here == 1:
            here = at(owner)
            out_ref[owner, :lines] = here[:, :width]
            out_ref[owner, lines:] = here[:, width:]
            continue
        for pair in range(rows_here // 2):
            one, two = at(owner * rows_here + 2 * pair), at(owner * rows_here + 2 * pair + 1)
            one_turned, two_turned = pltpu.roll(one, width, 1), pltpu.roll(two, width, 1)
            where = slice(2 * pair * width, (2 * pair + 2) * width)
            out_ref[owner, :lines, where] = jnp.where(lane < width, one, two_turned)
            out_ref[owner, lines:, where] = jnp.where(lane < width, one_turned, two)


def factor_column(place_ref, lines):
    line = place_ref[0] * lines + iota((lines, 1), 0)
    return jnp.where((line & (MODES - 1)) == 0, 1.0, 2.0) / float(RES**3)


def split_weights(spec_w, batch, width):
    block = spec_w[batch * 8 : (batch + 1) * 8].reshape(8 * width, 2 * width)
    return jnp.concatenate(halves(block), axis=1)


def mix_kernel(
    place_ref, lines_ref, cos_ref, sin_ref, spec_w, after, modes_out, out_ref, modes, mixed,
    *, owners, width,
):
    step = pl.program_id(0)
    lines = MODES * MODES // owners

    @pl.when(step == 0)
    def _():
        def put(kx, value):
            modes[pl.ds(kx, lines, MODES), :] = value

        x_forward(lines_ref, cos_ref, sin_ref, put, owners, lines, width)
        modes_out[...] = modes[...]

    base = step * STEP_MODES
    wide_lane = iota((8, 8 * width), 1) // width
    own = wide_lane == iota((8, 8 * width), 0)
    lane = iota((8, 2 * width), 1)
    for batch in range(STEP_MODES // 8):
        where = pl.ds(pl.multiple_of(base + batch * 8, 8), 8)
        u = modes[where, :]
        u_turned = pltpu.roll(u, width, 1)
        real = jnp.where(lane < width, u, u_turned)
        imag = jnp.where(lane < width, u_turned, u)
        rows = [jnp.where(own, jnp.concatenate([part] * 4, axis=1), 0.0) for part in (real, imag)]
        left = jnp.concatenate(halves(jnp.concatenate(rows, axis=0)), axis=0)
        product = dot(left, split_weights(spec_w, batch, width))
        product = product[:, : 2 * width] + product[:, 2 * width :]
        product = product[:16] + product[16:]
        turned = pltpu.roll(product[8:], width, 1)
        mixed[where, :] = product[:8] + jnp.where(lane < width, -turned, turned)

    @pl.when(step == pl.num_programs(0) - 1)
    def _():
        factor = factor_column(place_ref, lines)

        def take(kx):
            return mixed[pl.ds(kx, lines, MODES), :] * factor

        x_inverse(take, out_ref, owners, lines, width)


def mix_back_kernel(
    place_ref, lines_ref, cos_ref, sin_ref, spec_w, after, grads_out, out_ref, grads, back,
    *, owners, width,
):
    step = pl.program_id(0)
    lines = MODES * MODES // owners

    @pl.when(step == 0)
    def _():
        factor = factor_column(place_ref, lines)

        def put(kx, value):
            grads[pl.ds(kx, lines, MODES), :] = value * factor

        x_forward(lines_ref, cos_ref, sin_ref, put, owners, lines, width)
        grads_out[...] = grads[...]

    base = step * STEP_MODES
    wide_lane = iota((8, 8 * width), 1) // width
    own = wide_lane == iota((8, 8 * width), 0)
    lane = iota((8, 2 * width), 1)
    for batch in range(STEP_MODES // 8):
        where = pl.ds(pl.multiple_of(base + batch * 8, 8), 8)
        g = grads[where, :]
        g_turned = pltpu.roll(g, width, 1)
        rows = [g, jnp.where(lane < width, g_turned, -g_turned)]
        left = jnp.concatenate(halves(jnp.concatenate(rows, axis=0)), axis=0)
        left = jnp.concatenate([left, left], axis=1)
        product = dot(left, split_weights(spec_w, batch, width), NT)
        product = product[:16] + product[16:]
        parts = []
        for rows in (product[:8], product[8:]):
            rows = jnp.where(own, rows, 0.0)
            while rows.shape[1] > 2 * width:
                half = rows.shape[1] // 2
                rows = rows[:, :half] + rows[:, half:]
            parts.append(rows + pltpu.roll(rows, width, 1))
        back[where, :] = jnp.where(lane < width, parts[0], parts[1])

    @pl.when(step == pl.num_programs(0) - 1)
    def _():
        def take(kx):
            return back[pl.ds(kx, lines, MODES), :]

        x_inverse(take, out_ref, owners, lines, width)


def spec_grad_kernel(modes, grads, after, out, *, shapes, width):
    own = iota((8, 8 * width), 1) // width == iota((8, 8 * width), 0)
    lane = iota((8, 2 * width), 1)
    for batch in range(STEP_MODES // 8):
        where = slice(batch * 8, (batch + 1) * 8)
        left, right = [], []
        for shape in range(shapes):
            u, g = modes[shape, where], grads[shape, where]
            u_turned, g_turned = pltpu.roll(u, width, 1), pltpu.roll(g, width, 1)
            for part in (jnp.where(lane < width, u, u_turned), jnp.where(lane < width, u_turned, u)):
                left.append(jnp.where(own, jnp.concatenate([part] * 4, axis=1), 0.0))
            right += [g, jnp.where(lane < width, g_turned, -g_turned)]
        left_high, left_low = halves(jnp.concatenate(left, axis=0))
        right_high, right_low = halves(jnp.concatenate(right, axis=0))
        left = jnp.concatenate([left_high, left_low, left_high], axis=0)
        right = jnp.concatenate([right_high, right_high, right_low], axis=0)
        product = dot(left, right, TN)
        out[where] = product.reshape(8, width, 2 * width)


def cell_sums(total, rows_here, width):
    hidden_sums, weight_sums = [], []
    for row in range(rows_here):
        slab = total[row * PLANE : (row + 1) * PLANE]
        hidden_sums.append(slab[:, :width] + slab[:, width : 2 * width])
        weight = slab[:, 2 * width + 4 : 2 * width + 5] + slab[:, 2 * width + 12 : 2 * width + 13]
        weight_sums.append(jnp.broadcast_to(weight, (PLANE, width)))
    return jnp.concatenate(hidden_sums, axis=1), jnp.concatenate(weight_sums, axis=1)


def grid_kernel(
    lines_ref, lat, total, skip_w, skip_b, dec_w2, dec_b2, proj_w, inverse_hbm, plane_hbm,
    plane_out, pre_bar_out, latent_out, reach_out, sums, inverse, plane, copied, *, rows_here, width,
):
    copies = [
        pltpu.make_async_copy(inverse_hbm, inverse, copied.at[0]),
        pltpu.make_async_copy(plane_hbm, plane, copied.at[1]),
    ]
    for copy in copies:
        copy.start()
    sums[0], sums[1] = cell_sums(total, rows_here, width)
    reach = dot3(sums[0], spread(dec_w2[...], rows_here))
    reach = reach + sums[1] * tile_lanes(dec_b2[...], rows_here)
    reach_out[...] = reach
    skip = dot3(lat[...], spread(skip_w[...], rows_here)) + tile_lanes(skip_b[...], rows_here)
    copies[0].wait()
    latent, slope = gelu_both(times_field(inverse, lines_ref[...]) + skip)
    pre_bar = reach * tile_lanes(proj_w[...], rows_here) * slope
    copies[1].wait()
    plane_out[...] = times_field(plane, pre_bar)
    pre_bar_out[...] = pre_bar
    latent_out[...] = latent


def grid_grads_kernel(
    lat, pre_bar, latent, reach, sums, dec_w2, dec_b2, proj_w,
    skip_w_grad, dec_w2_grad, rows_out, table, *, rows_here, width,
):
    skip_w_grad[...] = gather_blocks(dot3(lat[...], pre_bar[...], TN), rows_here, width, width)
    scaled = latent[...] * tile_lanes(proj_w[...], rows_here)
    dec_w2_grad[...] = gather_blocks(dot3(sums[0], scaled, TN), rows_here, width, width)

    def column_sum(value):
        return fold_lanes(jnp.sum(value, axis=0, keepdims=True), rows_here, width)

    rows = [column_sum(pre_bar[...]), column_sum(sums[1] * scaled), column_sum(reach[...] * latent[...])]
    rows_out[...] = jnp.concatenate(rows + [jnp.zeros((5, width), F32)], axis=0)
    cell_kernel = dot3(scaled, spread(dec_w2[...], rows_here), NT)
    offset = scaled * tile_lanes(dec_b2[...], rows_here)
    cells = rows_here * PLANE
    table[cells:] = jnp.zeros((PAD, table.shape[1]), BF16)
    for row in range(rows_here):
        lanes = slice(row * width, (row + 1) * width)
        where = slice(row * PLANE, (row + 1) * PLANE)
        constant = jnp.sum(offset[:, lanes], axis=1, keepdims=True)
        high, low = halves(cell_kernel[:, lanes])
        c_high, c_low = halves(constant)
        lane = iota((PLANE, LANES), 1)
        tail = jnp.where(lane == 0, c_high.astype(F32), jnp.where(lane == 1, c_low.astype(F32), 0.0))
        table[where, : 2 * width] = jnp.concatenate([high.astype(F32), low.astype(F32)], axis=1).astype(BF16)
        table[where, 2 * width :] = tail.astype(BF16)


def place_rows(cell, first_row):
    row = iota((8, cell.shape[1]), 0)
    shifts = jnp.where(row == 0, 2 * log2(RES), jnp.where(row == 1, log2(RES), 0))
    place = (cell >> shifts) & jnp.where(row < 3, RES - 1, 0)
    return (place + jnp.where(row == 0, first_row, 0)).astype(F32)


def input_columns(feats, cell, first_row):
    high, low = halves(feats)
    place = place_rows(cell, first_row)
    return jnp.concatenate([high.astype(F32), low.astype(F32), place, place], axis=0).astype(BF16)


def dec_edges_kernel(
    place_ref, bounds, keys, inverse_degree, saved, table, pred_out, w1_out, b1_out,
    found_scratch, pred_total, grad_total, *, owners, cells, width,
):
    step = pl.program_id(0)
    rows_here = cells // PLANE
    group = found_scratch.shape[1] // CHUNK
    first_row = place_ref[0] * rows_here
    shift = log2(owners * LANES)
    count8 = max(owners, 8)

    @pl.when(step == 0)
    def _():
        pred_total[...] = jnp.zeros_like(pred_total)
        grad_total[...] = jnp.zeros_like(grad_total)

    chunk = step * group
    low_cell, _ = cell_range(bounds, 2, chunk, CHUNK // keys.shape[1])

    @pl.when(low_cell < cells)
    def _():
        rows, key = joined_keys(keys, chunk, group)
        gather_windows(
            found_scratch, keys, rows, table, bounds, 2, chunk, group, DEC_WINDOW, shift, 2 * width + 16
        )
        point = key & (owners * LANES - 1)
        found = found_scratch[:width] + found_scratch[width : 2 * width]
        constant = found_scratch[2 * width : 2 * width + 1] + found_scratch[2 * width + 1 : 2 * width + 2]
        edge = jnp.sum(saved[:width] * found, axis=0, keepdims=True) + constant
        owner = iota((count8, key.shape[1]), 0)
        high, low = halves(jnp.where(owner == (point >> 7), edge, 0.0))
        values = jnp.concatenate([high.astype(F32), low.astype(F32)], axis=0).astype(BF16)
        pred_total[...] += dot(values, one_hot(point & (LANES - 1), 0, LANES), NT)
        left = jnp.concatenate(halves(saved[width : 2 * width] * found), axis=0)
        right = input_columns(saved[2 * width :], key >> shift, first_row)
        grad_total[...] += dot(left, right, NT)

    @pl.when(step == pl.num_programs(0) - 1)
    def _():
        pred_out[...] = (pred_total[:owners] + pred_total[count8 : count8 + owners]) * inverse_degree[...]
        grad = grad_total[:width] + grad_total[width:]
        feats = (grad[:, :8] + grad[:, 8:16]).T
        places = grad[:, 16:24].T / (RES - 1.0)
        w1_out[...] = jnp.concatenate([feats[:3], places[:3]], axis=0)
        b1_out[...] = feats[3:4]


GRAD_ROWS = 108
PACKED_ROWS = 120


def enc_back_kernel(
    place_ref, bounds, keys, saved, lines_ref, pre_bar, scale, skip_w, w2, lift_w, pred_bar,
    skip_w_grad, dec_w2_grad, row_grads, pred_part, dec_w1_grad, dec_b1_grad, inverse_hbm,
    packed,
    table, found_scratch, second, feat_total, grad_total, inverse, copied, *, owners, cells, width,
):
    step = pl.program_id(0)
    rows_here = cells // PLANE
    group = found_scratch.shape[1] // CHUNK
    first_row = place_ref[0] * rows_here
    shift = log2(owners * LANES)
    count8 = max(owners, 8)

    @pl.when(step == 0)
    def _():
        copy = pltpu.make_async_copy(inverse_hbm, inverse, copied)
        copy.start()
        feat_total[...] = jnp.zeros_like(feat_total)
        grad_total[...] = jnp.zeros_like(grad_total)
        second[...] = weights3(w2[...])
        skip = dot3(pre_bar[...], spread(skip_w[...], rows_here), NT)
        copy.wait()
        field = (times_field(inverse, lines_ref[...]) + skip) * scale[...]
        table[cells:] = jnp.zeros((PAD, 2 * width), BF16)
        for row in range(rows_here):
            high, low = halves(field[:, row * width : (row + 1) * width])
            both = jnp.concatenate([high.astype(F32), low.astype(F32)], axis=1).astype(BF16)
            table[row * PLANE : (row + 1) * PLANE] = both

    chunk = step * group
    low_cell, _ = cell_range(bounds, 0, chunk, CHUNK // keys.shape[1])

    @pl.when(low_cell < cells)
    def _():
        lift_columns = jnp.concatenate([lift_w[...], jnp.zeros((4, width), F32)], axis=0).T
        rows, key = joined_keys(keys, chunk, group)
        gather_windows(
            found_scratch, keys, rows, table, bounds, 0, chunk, group, ENC_WINDOW, shift, 2 * width
        )
        point = key & (owners * LANES - 1)
        found = found_scratch[:width] + found_scratch[width:]
        source_bar = found * saved[3 * width : 4 * width]
        k_high, k_low = halves(found * saved[2 * width : 3 * width])
        hidden_bar = dot(second[...], jnp.concatenate([k_high, k_low, k_high], axis=0))
        pre_edge = hidden_bar * saved[width : 2 * width]
        parts = [*halves(saved[:width]), *halves(pre_edge), *halves(source_bar)]
        left = jnp.concatenate(parts + [jnp.ones((16, key.shape[1]), BF16)], axis=0)
        tail = input_columns(saved[4 * width :], key >> shift, first_row)
        grad_total[...] += dot(left, jnp.concatenate([k_high, k_low, tail], axis=0), NT)
        owner_hot = iota((count8, key.shape[1]), 0) == (point >> 7)
        edges = []
        for feat in range(4):
            edge = jnp.sum(source_bar * lift_columns[:, feat : feat + 1], axis=0, keepdims=True)
            edges.append(jnp.where(owner_hot, edge, 0.0))
        values = jnp.concatenate(halves(jnp.concatenate(edges, axis=0)), axis=0)
        feat_total[...] += dot(values, one_hot(point & (LANES - 1), 0, LANES), NT)

    @pl.when(step == pl.num_programs(0) - 1)
    def _():
        w2_part = grad_total[:width, : 2 * width] + grad_total[width : 2 * width, : 2 * width]
        w2_grad = w2_part[:, :width] + w2_part[:, width:]
        b2_part = grad_total[6 * width : 6 * width + 1, : 2 * width]
        b2_grad = b2_part[:, :width] + b2_part[:, width:]
        pre_part = grad_total[2 * width : 3 * width, 2 * width :] + grad_total[3 * width : 4 * width, 2 * width :]
        feats = (pre_part[:, :8] + pre_part[:, 8:16]).T
        places = pre_part[:, 16:24].T / (RES - 1.0)
        lift_part = grad_total[4 * width : 5 * width, 2 * width :] + grad_total[5 * width : 6 * width, 2 * width :]
        lifts = (lift_part[:, :8] + lift_part[:, 8:16]).T
        pair = partial(jnp.concatenate, axis=1)
        stack = partial(jnp.concatenate, axis=0)
        half = width // 2
        bar_sum = jnp.broadcast_to(jnp.sum(pred_bar[...], axis=1, keepdims=True), (1, width))
        fixed = stack(
            [
                pair([w2_grad, dec_w2_grad[...]]),
                pair([skip_w_grad[:half], skip_w_grad[half:]]),
                pair([stack([places[:3], feats[:3]]), dec_w1_grad[...]]),
                pair([feats[3:4], dec_b1_grad[...]]),
                pair([b2_grad, row_grads[1:2]]),
                pair([lifts[4:8], stack([lifts[3:4], row_grads[0:1], row_grads[2:3], bar_sum])]),
            ]
        )
        both = feat_total[: 4 * count8] + feat_total[4 * count8 :]
        empty = jnp.zeros((PACKED_ROWS - GRAD_ROWS - 5, LANES), F32)
        for owner in range(owners):
            rows = [both[feat * count8 + owner : feat * count8 + owner + 1] for feat in range(4)]
            packed[owner] = stack([fixed] + rows + [pred_part[owner : owner + 1], empty])


def arrive_kernel(arrived, proj_b, after, grads, feat_grad, pred, *, owners):
    total = arrived[0]
    for owner in range(1, owners):
        total = total + arrived[owner]
    grads[...] = total[:GRAD_ROWS]
    feat_grad[...] = total[GRAD_ROWS : GRAD_ROWS + 4]
    pred[...] = total[GRAD_ROWS + 4 : GRAD_ROWS + 5] + proj_b[...]


def leave_kernel(mine, other, *outs, width):
    half = width // 2
    left = mine[:, :width] + other[:, :width]
    right = mine[:, width:] + other[:, width:]
    at = width + half
    enc_w1, enc_b1, enc_w2, enc_b2, lift_w, lift_b, skip_w, skip_b, dec_w1, dec_b1, dec_w2, dec_b2, proj_w, proj_b = outs
    enc_w2[...] = left[:width]
    dec_w2[...] = right[:width]
    skip_w[:half] = left[width:at]
    skip_w[half:] = right[width:at]
    enc_w1[...] = left[at : at + 6]
    dec_w1[...] = right[at : at + 6]
    enc_b1[...] = left[at + 6 : at + 7]
    dec_b1[...] = right[at + 6 : at + 7]
    enc_b2[...] = left[at + 7 : at + 8]
    dec_b2[...] = right[at + 7 : at + 8]
    lift_w[...] = left[at + 8 : at + 12]
    lift_b[...] = right[at + 8 : at + 9]
    skip_b[...] = right[at + 9 : at + 10]
    proj_w[...] = right[at + 10 : at + 11]
    proj_b[...] = right[at + 11 : at + 12, :1]


def shape(*dims, dtype=F32):
    return jax.ShapeDtypeStruct(dims, dtype)


def whole(array):
    zeros = (0,) * array.ndim
    return pl.BlockSpec(array.shape, lambda i: zeros, pipeline_mode=pl.Buffered(1))


HELD = VMEM
FAR = pl.BlockSpec(memory_space=pl.ANY)


def kernel_call(kernel, name, steps, operands, out_shape, out_specs, scratch=(), mib=62, micros=10, **more):
    arrays = [array for array, _ in operands]
    specs = [whole(array) if spec is None else spec for array, spec in operands]
    return pl.pallas_call(
        kernel,
        grid=(steps,),
        in_specs=specs,
        out_specs=out_specs,
        out_shape=out_shape,
        scratch_shapes=list(scratch),
        compiler_params=pltpu.CompilerParams(vmem_limit_bytes=mib << 20),
        cost_estimate=pl.CostEstimate(flops=0, bytes_accessed=micros * 2_000_000, transcendentals=0),
        name=name,
        **more,
    )(*arrays)


def on_device(
    mesh_feat,
    mesh_pos,
    query_pos,
    enc_cell,
    enc_point,
    enc_count,
    dec_cell,
    dec_query,
    dec_count,
    enc_w1,
    enc_b1,
    enc_w2,
    enc_b2,
    lift_w,
    lift_b,
    spec_w,
    skip_w,
    skip_b,
    dec_w1,
    dec_b1,
    dec_w2,
    dec_b2,
    proj_w,
    proj_b,
    pred_bar,
):
    width = lift_w.shape[1]
    owners = lax.axis_size("wide")
    shapes = lax.axis_size("grid")
    rows_here = RES // owners
    cells = rows_here * PLANE
    modes_here = spec_w.shape[0]
    lines = modes_here // MODES
    enc_blocks, dec_blocks = enc_cell.shape[1], dec_cell.shape[1]
    enc_edges, dec_edges = enc_blocks * LANES, dec_blocks * LANES
    enc_span, dec_span = ENC_GROUP * CHUNK, DEC_GROUP * CHUNK
    lanes = rows_here * width
    place = lax.axis_index("wide").astype(jnp.int32).reshape(1)
    plane_np = plane_matrix(owners)
    plane = jnp.asarray(np.stack(halves_np(plane_np)))
    inverse = jnp.asarray(np.stack(halves_np(np.ascontiguousarray(plane_np.T))))
    cos_x, sin_x = (jnp.asarray(part) for part in x_tables(rows_here, width))
    rows = [value.reshape(1, -1) for value in (enc_b1, enc_b2, lift_b, skip_b, dec_b1, dec_b2, proj_w, proj_b)]
    enc_b1, enc_b2, lift_b, skip_b, dec_b1, dec_b2, proj_w, proj_b = rows
    sizes = dict(owners=owners, cells=cells, width=width)
    dma = pltpu.SemaphoreType.DMA

    def exchange(value):
        return lax.all_to_all(value, "wide", 0, 0, tiled=True)

    payload = kernel_call(
        partial(share_kernel, owners=owners),
        "share_points",
        1,
        [(value, None) for value in (mesh_feat[0], mesh_pos[0], query_pos[0], pred_bar, dec_query[0], dec_count)],
        shape(owners, 2 * FEAT_ROWS + owners, LANES),
        HELD,
    )
    shared = exchange(payload)
    local = [enc_cell[0], enc_point[0], enc_count, dec_cell[0], dec_query[0], dec_count]
    enc_keys, dec_keys, bounds = kernel_call(
        partial(sort_kernel, owners=owners, cells=cells),
        "sort_edges",
        1,
        [(value, None) for value in local] + [(payload, FAR)],
        [
            shape(LANES, enc_blocks, dtype=jnp.int32),
            shape(LANES, dec_blocks, dtype=jnp.int32),
            shape(8, LANES, dtype=jnp.int32),
        ],
        [HELD] * 3,
    )

    fixed = owners * FEAT_ROWS
    depth = 3 * fixed + 16
    saved_rows = 4 * width + FEAT_ROWS
    plane_scratch = pltpu.VMEM((2, 2 * MODES * MODES, PLANE), BF16)
    inverse_scratch = pltpu.VMEM((2, PLANE, 2 * MODES * MODES), BF16)
    saved_spec = pl.BlockSpec((saved_rows, enc_span), lambda i: (0, i))
    saved, lat, scale, plane_lat = kernel_call(
        partial(enc_forward_kernel, **sizes),
        "encode",
        enc_edges // enc_span,
        [(place, SMEM), (bounds, SMEM), (enc_keys, HELD), (shared, HELD)]
        + [(value, None) for value in (enc_w1, enc_b1, enc_w2, enc_b2, lift_w, lift_b)]
        + [(plane, FAR)],
        [
            shape(saved_rows, enc_edges),
            shape(PLANE, lanes),
            shape(PLANE, lanes),
            shape(2 * MODES * MODES, lanes),
        ],
        [saved_spec, HELD, HELD, HELD],
        [
            pltpu.VMEM((cells + PAD, 2 * LANES), F32),
            pltpu.VMEM((2 * fixed, LANES), BF16),
            pltpu.VMEM((2 * width, depth), BF16),
            pltpu.VMEM((width, 3 * width), BF16),
            pltpu.VMEM((2 * width + 16, enc_span), BF16),
            plane_scratch,
            dma,
        ],
    )
    modes_lines = exchange(plane_lat.reshape(owners, 2 * lines, lanes))

    dec_rows = 2 * width + FEAT_ROWS
    dec_steps = dec_edges // dec_span
    half_steps = dec_steps // 2

    def dec_sums(first_step, steps, before, saved_before, after, name):
        return kernel_call(
            partial(dec_sums_kernel, first_step=first_step, **sizes),
            name,
            steps,
            [
                (place, SMEM), (bounds, SMEM), (dec_keys, HELD), (shared, HELD), (dec_w1, None), (dec_b1, None),
                (before, HELD if first_step else FAR), (saved_before, FAR), (after, FAR),
            ],
            [
                shape(dec_rows, dec_edges),
                shape(cells + PAD, 2 * LANES),
                shape(owners, LANES),
            ],
            [pl.BlockSpec((dec_rows, dec_span), lambda i: (0, i + first_step)), HELD, HELD],
            [
                pltpu.VMEM((2 * fixed, LANES), BF16),
                pltpu.VMEM((width, depth), BF16),
                pltpu.VMEM((2 * width + 16, dec_span), BF16),
            ],
            input_output_aliases={7: 0} if first_step else {},
        )

    dec_saved, dec_total, inverse_degree = dec_sums(0, half_steps, plane_lat, plane_lat, plane_lat, "decode_sums_a")

    spec_block = pl.BlockSpec((STEP_MODES, width, 2 * width), lambda i: (i, 0, 0))

    def mode_pass(kernel, lines_in, after, name):
        return kernel_call(
            partial(kernel, owners=owners, width=width),
            name,
            modes_here // STEP_MODES,
            [(place, SMEM), (lines_in, HELD), (cos_x, None), (sin_x, None), (spec_w, spec_block), (after, FAR)],
            [shape(modes_here, 2 * width), shape(owners, 2 * lines, lanes)],
            [HELD, HELD],
            [pltpu.VMEM((modes_here, 2 * width), F32)] * 2,
        )

    modes, back_lines = mode_pass(mix_kernel, modes_lines, inverse_degree, "mix_modes")
    grid_lines = exchange(back_lines).reshape(2 * MODES * MODES, lanes)
    dec_saved, dec_total, inverse_degree = dec_sums(
        half_steps, dec_steps - half_steps, dec_total, dec_saved, back_lines, "decode_sums_b"
    )

    plane_bar, pre_bar, latent, reach, sums = kernel_call(
        partial(grid_kernel, rows_here=rows_here, width=width),
        "grid_fields",
        1,
        [(grid_lines, HELD), (lat, HELD), (dec_total, HELD)]
        + [(value, None) for value in (skip_w, skip_b, dec_w2, dec_b2, proj_w)]
        + [(inverse, FAR), (plane, FAR)],
        [shape(2 * MODES * MODES, lanes)] + [shape(PLANE, lanes)] * 3 + [shape(2, PLANE, lanes)],
        [HELD] * 5,
        [inverse_scratch, plane_scratch, dma((2,))],
    )
    bar_lines = exchange(plane_bar.reshape(owners, 2 * lines, lanes))

    skip_w_grad, dec_w2_grad, row_grads, dec_table = kernel_call(
        partial(grid_grads_kernel, rows_here=rows_here, width=width),
        "grid_grads",
        1,
        [(value, HELD) for value in (lat, pre_bar, latent, reach, sums)]
        + [(value, None) for value in (dec_w2, dec_b2, proj_w)],
        [
            shape(width, width),
            shape(width, width),
            shape(8, width),
            shape(cells + PAD, 2 * LANES, dtype=BF16),
        ],
        [HELD] * 4,
    )

    mixed_bar, bar_back = mode_pass(mix_back_kernel, bar_lines, row_grads, "mix_back")
    bar_grid_lines = exchange(bar_back).reshape(2 * MODES * MODES, lanes)
    all_modes = lax.all_gather(modes, "grid", axis=0)
    all_grads = lax.all_gather(mixed_bar, "grid", axis=0)

    count8 = max(owners, 8)
    pred_part, dec_w1_grad, dec_b1_grad = kernel_call(
        partial(dec_edges_kernel, **sizes),
        "decode_edges",
        dec_steps,
        [
            (place, SMEM), (bounds, SMEM), (dec_keys, HELD), (inverse_degree, HELD),
            (dec_saved, pl.BlockSpec((dec_rows, dec_span), lambda i: (0, i))), (dec_table, HELD),
        ],
        [shape(owners, LANES), shape(6, width), shape(1, width)],
        [HELD] * 3,
        [
            pltpu.VMEM((2 * width + 16, dec_span), F32),
            pltpu.VMEM((2 * count8, LANES), F32),
            pltpu.VMEM((2 * width, 32), F32),
        ],
    )

    packed = kernel_call(
        partial(enc_back_kernel, **sizes),
        "encode_back",
        enc_edges // enc_span,
        [(place, SMEM), (bounds, SMEM), (enc_keys, HELD), (saved, saved_spec)]
        + [(value, HELD) for value in (bar_grid_lines, pre_bar, scale)]
        + [(value, None) for value in (skip_w, enc_w2, lift_w, pred_bar)]
        + [(value, HELD) for value in (skip_w_grad, dec_w2_grad, row_grads, pred_part, dec_w1_grad, dec_b1_grad)]
        + [(inverse, FAR)],
        shape(owners, PACKED_ROWS, LANES),
        HELD,
        [
            pltpu.VMEM((cells + PAD, 2 * width), BF16),
            pltpu.VMEM((2 * width, enc_span), F32),
            pltpu.VMEM((width, 3 * width), BF16),
            pltpu.VMEM((8 * count8, LANES), F32),
            pltpu.VMEM((6 * width + 16, 2 * width + 32), F32),
            inverse_scratch,
            dma,
        ],
    )
    arrived = exchange(packed)

    spec_grad = kernel_call(
        partial(spec_grad_kernel, shapes=shapes, width=width),
        "spec_grad",
        modes_here // STEP_MODES,
        [
            (value, pl.BlockSpec((shapes, STEP_MODES, 2 * width), lambda i: (0, i, 0)))
            for value in (all_modes, all_grads)
        ]
        + [(packed, FAR)],
        shape(modes_here, width, 2 * width),
        spec_block,
    )

    grads, feat_grad, pred = kernel_call(
        partial(arrive_kernel, owners=owners),
        "arrive",
        1,
        [(arrived, HELD), (proj_b, None), (spec_grad, FAR)],
        [shape(GRAD_ROWS, LANES), shape(4, LANES), shape(1, LANES)],
        [HELD] * 3,
    )
    other, step = jnp.zeros_like(grads), 1
    while step < shapes:
        grads = grads if step == 1 else grads + other
        other = lax.ppermute(grads, "grid", [(i, i ^ step) for i in range(shapes)])
        step *= 2
    vector = shape(1, width)
    square = shape(width, width)
    first = shape(6, width)
    outs = kernel_call(
        partial(leave_kernel, width=width),
        "leave",
        1,
        [(grads, HELD), (other, HELD)],
        [
            first, vector, square, vector, shape(4, width), vector,
            square, vector, first, vector, square, vector, vector, shape(1, 1),
        ],
        [HELD] * 14,
    )
    outs = [out.reshape(-1) if out.shape[0] == 1 else out for out in outs]
    return (pred, feat_grad[None], *outs[:6], spec_grad, *outs[6:])


def solution(mesh):
    placed = (
        P("grid", None, "wide"),
        P("grid", None, "wide"),
        P("grid", None, "wide"),
        P("grid", "wide", None),
        P("grid", "wide", None),
        P("grid", "wide"),
        P("grid", "wide", None),
        P("grid", "wide", None),
        P("grid", "wide"),
        P(),
        P(),
        P(),
        P(),
        P(),
        P(),
        P("wide", None, None),
        P(),
        P(),
        P(),
        P(),
        P(),
        P(),
        P(),
        P(),
        P("grid", "wide"),
    )
    return jax.shard_map(
        on_device,
        mesh=mesh,
        in_specs=placed,
        out_specs=(
            P("grid", "wide"),
            P("grid", None, "wide"),
            P(),
            P(),
            P(),
            P(),
            P(),
            P(),
            P("wide", None, None),
            P(),
            P(),
            P(),
            P(),
            P(),
            P(),
            P(),
            P(),
        ),
        check_vma=False,
    )
```

```python
from functools import partial
import math

import jax
import jax.numpy as jnp
import ml_dtypes
import numpy as np
from jax import lax
from jax.experimental import pallas as pl
from jax.experimental.pallas import tpu as pltpu
from jax.sharding import PartitionSpec as P

MODES = 16
RES = 32
PLANE = RES * RES
CHUNK = 256
LANES = 128
ENC_GROUP = 16
DEC_GROUP = 16
FEAT_ROWS = 8
ENC_WINDOW = 64
DEC_WINDOW = 128
PAD = 256
MIX_STEP = 64
GRAD_STEP = 128
F32 = jnp.float32
BF16 = jnp.bfloat16
GELU_A = 0.7978845608028654
GELU_B = 0.044715

NN = (((1,), (0,)), ((), ()))
NT = (((1,), (1,)), ((), ()))
TN = (((0,), (0,)), ((), ()))

VMEM = pl.BlockSpec(memory_space=pltpu.VMEM)
SMEM = pl.BlockSpec(memory_space=pltpu.SMEM)


def kept_freqs():
    half = MODES // 2
    return np.concatenate([np.arange(half), np.arange(RES - half, RES)])


def plane_matrix(owners):
    lines = MODES * MODES // owners
    line = np.arange(MODES * MODES)
    freq_y, freq_z = kept_freqs()[line // MODES], line % MODES
    cell = np.arange(PLANE)
    turns = (freq_y[:, None] * (cell // RES) + freq_z[:, None] * (cell % RES)) % RES
    angle = turns * (2.0 * math.pi / RES)
    both = np.stack([np.cos(angle), -np.sin(angle)]).reshape(2, owners, lines, PLANE)
    matrix = both.transpose(1, 0, 2, 3).reshape(2 * MODES * MODES, PLANE)
    return matrix.astype(np.float32)


def halves_np(matrix):
    high = matrix.astype(ml_dtypes.bfloat16)
    low = (matrix - high.astype(np.float32)).astype(ml_dtypes.bfloat16)
    return high, low


def line_angles():
    turns = (kept_freqs()[:, None] * np.arange(RES)[None, :]) % RES
    return turns * (2.0 * math.pi / RES)


def x_tables(rows_here, width):
    angle = line_angles().reshape(MODES, RES // rows_here, rows_here, 1)
    angle = np.broadcast_to(angle, (MODES, RES // rows_here, rows_here, width))
    angle = angle.reshape(MODES, RES // rows_here, rows_here * width)
    return np.cos(angle).astype(np.float32), np.sin(angle).astype(np.float32)


def log2(number):
    return number.bit_length() - 1


def iota(shape, axis):
    return lax.broadcasted_iota(jnp.int32, shape, axis)


def halves(value):
    high = value.astype(BF16)
    low = (value - high.astype(F32)).astype(BF16)
    return high, low


def dot(a, b, dims=NN):
    return lax.dot_general(a, b, dims, preferred_element_type=F32)


def dot3(a, b, dims=NN):
    a_high, a_low = halves(a)
    b_high, b_low = halves(b)
    return dot(a_high, b_high, dims) + dot(a_low, b_high, dims) + dot(a_high, b_low, dims)


def one_hot(index, first, rows):
    places = iota((rows, index.shape[1]), 0) + first
    return jnp.where(places == index, 1.0, 0.0).astype(BF16)


def gelu_both(value):
    square = value * value
    turn = jnp.tanh(value * (GELU_A + (GELU_A * GELU_B) * square))
    half = 0.5 * (1.0 + turn)
    slope = half + (0.5 * value) * (1.0 - turn * turn) * (
        GELU_A + (3.0 * GELU_A * GELU_B) * square
    )
    return value * half, slope


def sort_columns(values):
    rows = values.shape[0]
    regs = rows // 8
    low = log2(regs)
    total = low + 3 + 7
    sub = iota((8, LANES), 0)
    lane = iota((8, LANES), 1)
    x = values.reshape(regs, 8, LANES)

    def flip(x, bit):
        if bit >= total:
            return x
        if bit < low:
            y = x.reshape(regs >> (bit + 1), 2, 1 << bit, 8, LANES)
            return jnp.stack([y[:, 0], ~y[:, 1]], axis=1).reshape(regs, 8, LANES)
        if bit < low + 3:
            mask = -((sub >> (bit - low)) & 1)
        else:
            mask = -((lane >> (bit - low - 3)) & 1)
        return x ^ mask[None]

    def exchange(x, bit):
        if bit < low:
            y = x.reshape(regs >> (bit + 1), 2, 1 << bit, 8, LANES)
            one, two = y[:, 0], y[:, 1]
            pair = [jnp.minimum(one, two), jnp.maximum(one, two)]
            return jnp.stack(pair, axis=1).reshape(regs, 8, LANES)
        if bit < low + 3:
            axis, dist, size, place = 1, 1 << (bit - low), 8, sub
        else:
            axis, dist, size, place = 2, 1 << (bit - low - 3), LANES, lane
        after = pltpu.roll(x, size - dist, axis)
        before = after if 2 * dist == size else pltpu.roll(x, dist, axis)
        first = ((place & dist) == 0)[None]
        return jnp.where(first, jnp.minimum(x, after), jnp.maximum(x, before))

    for phase in range(1, total + 1):
        x = flip(x, phase)
        for bit in reversed(range(phase)):
            x = exchange(x, bit)
        x = flip(x, phase)
    return x.reshape(rows, LANES)


def layer_matrix(feat_rows, cell_rows, owners):
    feat_high, feat_low = halves(feat_rows)
    cell_high, cell_low = halves(cell_rows)
    parts = [feat_high] * owners + [feat_high] * owners + [feat_low] * owners
    parts += [cell_high, cell_low]
    stacked = jnp.concatenate([part.astype(F32) for part in parts], axis=0)
    depth = stacked.shape[0]
    more = -depth % LANES
    if more:
        stacked = jnp.concatenate([stacked, jnp.zeros((more, stacked.shape[1]), F32)], axis=0)
    return stacked.T[:, :depth].astype(BF16)


def edge_inputs(key, table, first_row, owners):
    shift = log2(owners * LANES)
    cell = key >> shift
    point = key & (owners * LANES - 1)
    low_hot = one_hot(point & (LANES - 1), 0, LANES)
    found = dot(table, low_hot)
    owner = (iota(found.shape, 0) >> 3) & (owners - 1)
    found = jnp.where(owner == (point >> 7), found, 0.0)
    row = iota((8, key.shape[1]), 0)
    shifts = jnp.where(row == 0, 2 * log2(RES), jnp.where(row == 1, log2(RES), 0))
    place = (cell >> shifts) & jnp.where(row < 3, RES - 1, 0)
    place = (place + jnp.where(row == 0, first_row, 0)).astype(F32)
    return cell, point, low_hot, found, place


def stack_inputs(found, place, owners):
    exact = found.astype(BF16)
    places = jnp.concatenate([place, place], axis=0).astype(BF16)
    return jnp.concatenate([exact, exact[: owners * FEAT_ROWS], places], axis=0)


def fold_feats(found, owners):
    return jnp.sum(found.reshape(2 * owners, FEAT_ROWS, found.shape[1]), axis=0)


def stack3(value):
    high, low = halves(value)
    return jnp.concatenate([high, low, high], axis=0)


def weights3(matrix):
    high, low = halves(matrix)
    return jnp.concatenate([high, high, low], axis=1)


def key_row(keys_ref, chunk):
    per = CHUNK // keys_ref.shape[1]
    rows = [keys_ref[pl.ds(chunk * per + i, 1), :] for i in range(per)]
    return rows[0] if per == 1 else jnp.concatenate(rows, axis=1)


def cell_range(bounds_ref, line, chunk, per):
    return bounds_ref[line, chunk * per], bounds_ref[line + 1, chunk * per + per - 1]


def spread(block, copies):
    rows, columns = block.shape
    tiled = jnp.concatenate([jnp.concatenate([block] * copies, axis=1)] * copies, axis=0)
    return jnp.where(
        iota(tiled.shape, 0) // rows == iota(tiled.shape, 1) // columns, tiled, 0.0
    )


def gather_blocks(product, copies, rows, columns):
    total = product[:rows, :columns]
    for i in range(1, copies):
        total = total + product[i * rows : (i + 1) * rows, i * columns : (i + 1) * columns]
    return total


def tile_lanes(row, copies):
    return row if copies == 1 else jnp.concatenate([row] * copies, axis=1)


def fold_lanes(row, copies, width):
    total = row[:, :width]
    for i in range(1, copies):
        total = total + row[:, i * width : (i + 1) * width]
    return total


def column(counts):
    return jnp.broadcast_to(counts, (8, counts.shape[1])).T[:, :1]


def share_kernel(feat, pos, query_pos, pred_bar, dec_query, dec_count, payload, *, owners):
    blocks = dec_query.shape[0]
    lane_valid = jnp.where(
        iota((blocks, LANES), 1) < column(dec_count[...]), dec_query[...], owners * LANES
    )
    ones = jnp.zeros((max(owners, 16), LANES), F32)
    degree = ones
    for block in range(0, blocks, 2):
        row = jnp.concatenate([lane_valid[block : block + 1], lane_valid[block + 1 : block + 2]], axis=1)
        high = one_hot(row >> 7, 0, ones.shape[0])
        low = one_hot(row & (LANES - 1), 0, LANES)
        degree = degree + dot(high, low, NT)
    filled = jnp.ones((1, LANES), F32)
    empty = jnp.zeros((3, LANES), F32)
    rows = [pos[...], filled, feat[...], query_pos[...], filled, pred_bar[...], empty, degree[:owners]]
    mine = jnp.concatenate(rows, axis=0)
    for owner in range(owners):
        payload[owner] = mine


def sort_kernel(
    enc_cell, enc_point, enc_count, dec_cell, dec_query, dec_count, after,
    enc_keys, dec_keys, bounds, *, owners, cells,
):
    shift = log2(owners * LANES)

    def keys(cell, point, count):
        lane = iota(cell.shape, 1)
        key = jnp.where(lane < column(count), (cell << shift) | point, cells << shift)
        return sort_columns(key)

    enc = keys(enc_cell[...], enc_point[...], enc_count[...])
    dec = keys(dec_cell[...], dec_query[...], dec_count[...])
    enc_keys[...] = enc.T
    dec_keys[...] = dec.T
    ends = [enc[:1], enc[-1:], dec[:1], dec[-1:]]
    bounds[...] = jnp.concatenate(ends + [jnp.zeros((4, LANES), jnp.int32)], axis=0) >> shift


def joined_keys(keys, chunk, group):
    rows = [key_row(keys, chunk + i) for i in range(group)]
    return rows, jnp.concatenate(rows, axis=1)


def later_windows(windows, size, visit):
    most = windows[0][1]
    for _, count in windows[1:]:
        most = jnp.maximum(most, count)

    @pl.when(most > 1)
    def _():
        for i, (begin, count) in enumerate(windows):

            def more(j, carry):
                visit(i, begin + j * size)
                return carry

            lax.fori_loop(1, count, more, 0)


def scatter_windows(total, keys, cell, message, bounds, line, chunk, group, size, shift, columns):
    per = CHUNK // keys.shape[1]
    windows, parts = [], []
    for i in range(group):
        begin, end = cell_range(bounds, line, chunk + i, per)
        begin = pl.multiple_of(begin & -8, 8)
        lanes = slice(i * CHUNK, (i + 1) * CHUNK)
        parts.append(dot(one_hot(cell[:, lanes], begin, size), message[:, lanes], NT))
        windows.append((begin, (end - begin) // size + 1))
    for (begin, _), part in zip(windows, parts):
        total[pl.ds(begin, size), :columns] += part

    def visit(i, start):
        start = pl.multiple_of(start, 8)
        hot = one_hot(key_row(keys, chunk + i) >> shift, start, size)
        part = dot(hot, message[:, i * CHUNK : (i + 1) * CHUNK], NT)
        total[pl.ds(start, size), :columns] += part

    later_windows(windows, size, visit)


def gather_windows(found, keys, rows, table, bounds, line, chunk, group, size, shift, columns):
    per = CHUNK // keys.shape[1]
    windows = []
    for i in range(group):
        begin, end = cell_range(bounds, line, chunk + i, per)
        begin = pl.multiple_of(begin & -16, 16)
        hot = one_hot(rows[i] >> shift, begin, size)
        found[:, i * CHUNK : (i + 1) * CHUNK] = dot(table[pl.ds(begin, size), :columns], hot, TN)
        windows.append((begin, (end - begin) // size + 1))

    def visit(i, start):
        start = pl.multiple_of(start, 16)
        hot = one_hot(key_row(keys, chunk + i) >> shift, start, size)
        part = dot(table[pl.ds(start, size), :columns], hot, TN)
        found[:, i * CHUNK : (i + 1) * CHUNK] += part

    later_windows(windows, size, visit)


def enc_forward_kernel(
    place_ref, bounds, keys, shared, w1, b1, w2, b2, lift_w, lift_b, plane_hbm,
    saved, lat, scale, plane_out,
    total, table, first, second, message, plane, copied, *, owners, cells, width,
):
    step = pl.program_id(0)
    rows_here = cells // PLANE
    group = message.shape[1] // CHUNK
    shift = log2(owners * LANES)
    first_row = place_ref[0] * rows_here
    copy = pltpu.make_async_copy(plane_hbm, plane, copied)

    @pl.when(step == 0)
    def _():
        copy.start()
        total[...] = jnp.zeros_like(total)
        feats = jnp.concatenate([shared[i, :FEAT_ROWS] for i in range(owners)], axis=0)
        table[...] = jnp.concatenate(halves(feats), axis=0)
        empty = jnp.zeros((3, width), F32)
        pre_rows = jnp.concatenate([w1[3:6], b1[...], jnp.zeros((4, width), F32)], axis=0)
        lift_rows = jnp.concatenate([empty, lift_b[...], lift_w[...]], axis=0)
        cell_rows = jnp.concatenate([w1[0:3] / (RES - 1.0), jnp.zeros((5, width), F32)], axis=0)
        first[...] = layer_matrix(
            jnp.concatenate([pre_rows, lift_rows], axis=1),
            jnp.concatenate([cell_rows, jnp.zeros((8, width), F32)], axis=1),
            owners,
        )
        second[...] = weights3(w2[...].T)

    chunk = step * group
    low_cell, _ = cell_range(bounds, 0, chunk, CHUNK // keys.shape[1])

    @pl.when(low_cell < cells)
    def _():
        bias = jnp.broadcast_to(b2[...], (8, width)).T[:, :1]
        _, key = joined_keys(keys, chunk, group)
        cell, _, _, found, place = edge_inputs(key, table[...], first_row, owners)
        both = dot(first[...], stack_inputs(found, place, owners))
        lifted = both[width:]
        hidden, slope = gelu_both(both[:width])
        kernel = dot(second[...], stack3(hidden)) + bias
        saved[0 * width : 1 * width] = hidden
        saved[1 * width : 2 * width] = slope
        saved[2 * width : 3 * width] = lifted
        saved[3 * width : 4 * width] = kernel
        saved[4 * width :] = fold_feats(found, owners)
        high, low = halves(kernel * lifted)
        message[...] = jnp.concatenate([high, low, jnp.ones((16, key.shape[1]), BF16)], axis=0)
        scatter_windows(
            total, keys, cell, message, bounds, 0, chunk, group, ENC_WINDOW, shift, 2 * width + 16
        )

    @pl.when(step == pl.num_programs(0) - 1)
    def _():
        fields, scales = [], []
        for row in range(rows_here):
            slab = total[row * PLANE : (row + 1) * PLANE]
            inverse = 1.0 / jnp.maximum(slab[:, 2 * width : 2 * width + 1], 1.0)
            fields.append((slab[:, :width] + slab[:, width : 2 * width]) * inverse)
            scales.append(jnp.broadcast_to(inverse, (PLANE, width)))
        field = jnp.concatenate(fields, axis=1)
        lat[...] = field
        scale[...] = jnp.concatenate(scales, axis=1)
        copy.wait()
        plane_out[...] = times_field(plane, field)


def times_field(matrix, field):
    high, low = halves(field)
    return dot(matrix[0], high) + dot(matrix[1], high) + dot(matrix[0], low)


def dec_sums_kernel(
    place_ref, bounds, keys, shared, w1, b1, before, saved_before, after,
    saved, total, inverse_out, table, first, message, *, owners, cells, width, first_step,
):
    step = pl.program_id(0)
    rows_here = cells // PLANE
    group = message.shape[1] // CHUNK
    shift = log2(owners * LANES)
    first_row = place_ref[0] * rows_here

    @pl.when(step == 0)
    def _():
        total[...] = jnp.zeros_like(total) if first_step == 0 else before[...]
        degree = shared[0, 2 * FEAT_ROWS :]
        for i in range(1, owners):
            degree = degree + shared[i, 2 * FEAT_ROWS :]
        inverse = 1.0 / jnp.maximum(degree, 1.0)
        inverse_out[...] = inverse
        feats = []
        for i in range(owners):
            rows = shared[i, FEAT_ROWS : 2 * FEAT_ROWS]
            weighted = rows * inverse[i : i + 1]
            feats.append(jnp.where(iota(rows.shape, 0) == 4, weighted, rows))
        table[...] = jnp.concatenate(halves(jnp.concatenate(feats, axis=0)), axis=0)
        feat_rows = jnp.concatenate([w1[0:3], b1[...], jnp.zeros((4, width), F32)], axis=0)
        cell_rows = jnp.concatenate([w1[3:6] / (RES - 1.0), jnp.zeros((5, width), F32)], axis=0)
        first[...] = layer_matrix(feat_rows, cell_rows, owners)

    chunk = (step + first_step) * group
    low_cell, _ = cell_range(bounds, 2, chunk, CHUNK // keys.shape[1])

    @pl.when(low_cell < cells)
    def _():
        _, key = joined_keys(keys, chunk, group)
        cell, _, _, found, place = edge_inputs(key, table[...], first_row, owners)
        hidden, slope = gelu_both(dot(first[...], stack_inputs(found, place, owners)))
        feats = fold_feats(found, owners)
        weight = feats[4:5]
        saved[0 * width : 1 * width] = hidden
        saved[1 * width : 2 * width] = slope * weight
        saved[2 * width :] = feats
        high, low = halves(hidden * weight)
        w_high, w_low = halves(feats)
        tail = jnp.concatenate([w_high.astype(F32), w_low.astype(F32)], axis=0).astype(BF16)
        message[...] = jnp.concatenate([high, low, tail], axis=0)
        scatter_windows(
            total, keys, cell, message, bounds, 2, chunk, group, DEC_WINDOW, shift, 2 * width + 16
        )


def x_forward(lines_ref, cos_ref, sin_ref, put, owners, lines, width):
    lanes = lines_ref.shape[2]
    for kx in range(MODES):
        real = jnp.zeros((lines, lanes), F32)
        imag = jnp.zeros((lines, lanes), F32)
        for owner in range(owners):
            cos, sin = cos_ref[kx, owner : owner + 1], sin_ref[kx, owner : owner + 1]
            line_real, line_imag = lines_ref[owner, :lines], lines_ref[owner, lines:]
            real = real + cos * line_real + sin * line_imag
            imag = imag + cos * line_imag - sin * line_real
        if lanes == width:
            put(kx, jnp.concatenate([real, imag], axis=1))
        else:
            pair = 2 * width
            while real.shape[1] > pair:
                half = real.shape[1] // 2
                real, imag = real[:, :half] + real[:, half:], imag[:, :half] + imag[:, half:]
            real = real + pltpu.roll(real, width, 1)
            imag = imag + pltpu.roll(imag, width, 1)
            put(kx, jnp.where(iota(real.shape, 1) < width, real, imag))


def x_inverse(take, out_ref, owners, lines, width):
    angles = line_angles()
    rows_here = RES // owners
    modes = [take(kx) for kx in range(MODES)]
    lane = iota(modes[0].shape, 1)
    turned = [
        jnp.where(lane < width, -pltpu.roll(mode, width, 1), pltpu.roll(mode, width, 1))
        for mode in modes
    ]

    def at(x):
        total = None
        for kx in range(MODES):
            for value, factor in ((modes[kx], np.cos(angles[kx, x])), (turned[kx], np.sin(angles[kx, x]))):
                factor = float(np.float32(factor)) if abs(factor) > 1e-9 else 0.0
                if factor == 0.0:
                    continue
                term = value if factor == 1.0 else value * factor
                total = term if total is None else total + term
        return total

    for owner in range(owners):
        if rows_here == 1:
            here = at(owner)
            out_ref[owner, :lines] = here[:, :width]
            out_ref[owner, lines:] = here[:, width:]
            continue
        for pair in range(rows_here // 2):
            one, two = at(owner * rows_here + 2 * pair), at(owner * rows_here + 2 * pair + 1)
            one_turned, two_turned = pltpu.roll(one, width, 1), pltpu.roll(two, width, 1)
            where = slice(2 * pair * width, (2 * pair + 2) * width)
            out_ref[owner, :lines, where] = jnp.where(lane < width, one, two_turned)
            out_ref[owner, lines:, where] = jnp.where(lane < width, one_turned, two)


def factor_column(place_ref, lines):
    line = place_ref[0] * lines + iota((lines, 1), 0)
    return jnp.where((line & (MODES - 1)) == 0, 1.0, 2.0) / float(RES**3)


def split_weights(spec_w, base, width):
    block = spec_w[pl.ds(base, 8)].reshape(8 * width, 2 * width)
    return jnp.concatenate(halves(block), axis=1)


def interleave(one, two):
    parts = []
    for at in range(0, one.shape[0], 8):
        parts += [one[at : at + 8], two[at : at + 8]]
    return jnp.concatenate(parts, axis=0)


def fetch_weights(spec_hbm, spec_w, copied):
    count = spec_w.shape[0] // copied.shape[0]

    def copy(i):
        where = pl.ds(i * count, count)
        return pltpu.make_async_copy(spec_hbm.at[where], spec_w.at[where], copied.at[i])

    return count, copy


def mix_kernel(
    place_ref, lines_ref, cos_ref, sin_ref, spec_hbm, after, modes, out_ref, mixed, spec_w, copied,
    *, owners, width,
):
    lines = MODES * MODES // owners
    count, copy = fetch_weights(spec_hbm, spec_w, copied)
    for i in range(copied.shape[0]):
        copy(i).start()

    def put(kx, value):
        modes[pl.ds(kx, lines, MODES), :] = value

    x_forward(lines_ref, cos_ref, sin_ref, put, owners, lines, width)
    lane = iota((count, 2 * width), 1)

    def mix(i, carry):
        copy(i).wait()
        base = pl.multiple_of(i * count, count)
        u = modes[pl.ds(base, count), :]
        u_turned = pltpu.roll(u, width, 1)
        both = interleave(jnp.where(lane < width, u, u_turned), jnp.where(lane < width, u_turned, u))
        both = jnp.concatenate([both] * 4, axis=1)
        own = iota(both.shape, 1) // width == iota(both.shape, 0) % 8
        high, low = halves(jnp.where(own, both, 0.0))
        products = []
        for batch in range(count // 8):
            rows = slice(batch * 16, (batch + 1) * 16)
            left = jnp.concatenate([high[rows], low[rows]], axis=0)
            products.append(dot(left, split_weights(spec_w, base + batch * 8, width)))
        outs = []
        for product in products:
            product = product[:, : 2 * width] + product[:, 2 * width :]
            product = product[:16] + product[16:]
            turned = pltpu.roll(product[8:], width, 1)
            outs.append(product[:8] + jnp.where(lane[:8] < width, -turned, turned))
        mixed[pl.ds(base, count), :] = jnp.concatenate(outs, axis=0)
        return carry

    lax.fori_loop(0, copied.shape[0], mix, 0)
    factor = factor_column(place_ref, lines)

    def take(kx):
        return mixed[pl.ds(kx, lines, MODES), :] * factor

    x_inverse(take, out_ref, owners, lines, width)


def mix_back_kernel(
    place_ref, lines_ref, cos_ref, sin_ref, spec_hbm, after, grads, out_ref, back, spec_w, copied,
    *, owners, width,
):
    lines = MODES * MODES // owners
    count, copy = fetch_weights(spec_hbm, spec_w, copied)
    for i in range(copied.shape[0]):
        copy(i).start()
    factor = factor_column(place_ref, lines)

    def put(kx, value):
        grads[pl.ds(kx, lines, MODES), :] = value * factor

    x_forward(lines_ref, cos_ref, sin_ref, put, owners, lines, width)
    lane = iota((count, 2 * width), 1)
    own = iota((16, 8 * width), 1) // width == iota((16, 8 * width), 0) % 8

    def mix(i, carry):
        copy(i).wait()
        base = pl.multiple_of(i * count, count)
        g = grads[pl.ds(base, count), :]
        g_turned = pltpu.roll(g, width, 1)
        high, low = halves(interleave(g, jnp.where(lane < width, g_turned, -g_turned)))
        products = []
        for batch in range(count // 8):
            rows = slice(batch * 16, (batch + 1) * 16)
            left = jnp.concatenate([high[rows], low[rows]], axis=0)
            left = jnp.concatenate([left, left], axis=1)
            products.append(dot(left, split_weights(spec_w, base + batch * 8, width), NT))
        outs = []
        for product in products:
            rows = jnp.where(own, product[:16] + product[16:], 0.0)
            while rows.shape[1] > 2 * width:
                half = rows.shape[1] // 2
                rows = rows[:, :half] + rows[:, half:]
            rows = rows + pltpu.roll(rows, width, 1)
            outs.append(jnp.where(lane[:8] < width, rows[:8], rows[8:]))
        back[pl.ds(base, count), :] = jnp.concatenate(outs, axis=0)
        return carry

    lax.fori_loop(0, copied.shape[0], mix, 0)

    def take(kx):
        return back[pl.ds(kx, lines, MODES), :]

    x_inverse(take, out_ref, owners, lines, width)


def spec_grad_kernel(rank_ref, *refs, shapes, width):
    count = shapes
    mode_refs, grad_refs, out, modes, grads = refs[:count], refs[count : 2 * count], refs[-3], refs[-2], refs[-1]
    for parts, held in ((mode_refs, modes), (grad_refs, grads)):
        distance = 0
        for part in parts:
            for i in range(part.shape[0]):
                held[rank_ref[0] ^ distance] = part[i]
                distance += 1
    row = iota((8, 2 * width), 0)
    lane = iota((8, 2 * width), 1)
    own = iota((8, 4 * width), 1) // width == iota((8, 4 * width), 0) % 4
    lefts, rights = [], []
    for batch in range(out.shape[0] // 8):
        where = slice(batch * 8, (batch + 1) * 8)
        left, right = [], []
        for shape in range(shapes):
            u, g = modes[shape, where], grads[shape, where]
            u_turned, g_turned = pltpu.roll(u, width, 1), pltpu.roll(g, width, 1)
            for part in (jnp.where(lane < width, u, u_turned), jnp.where(lane < width, u_turned, u)):
                left.append(jnp.where(own, jnp.concatenate([part] * 2, axis=1), 0.0))
            for part in (g, jnp.where(lane < width, g_turned, -g_turned)):
                pair = [jnp.where(row < 4, part, 0.0), jnp.where(row < 4, 0.0, part)]
                right.append(jnp.concatenate(pair, axis=1))
        left_high, left_low = halves(jnp.concatenate(left, axis=0))
        right_high, right_low = halves(jnp.concatenate(right, axis=0))
        lefts.append(jnp.concatenate([left_high, left_low, left_high], axis=0))
        rights.append(jnp.concatenate([right_high, right_high, right_low], axis=0))
    products = [dot(left, right, TN) for left, right in zip(lefts, rights)]
    for batch, product in enumerate(products):
        out[batch * 8 : batch * 8 + 4] = product[:, : 2 * width].reshape(4, width, 2 * width)
        out[batch * 8 + 4 : batch * 8 + 8] = product[:, 2 * width :].reshape(4, width, 2 * width)


def cell_sums(total, rows_here, width):
    hidden_sums, weight_sums = [], []
    for row in range(rows_here):
        slab = total[row * PLANE : (row + 1) * PLANE]
        hidden_sums.append(slab[:, :width] + slab[:, width : 2 * width])
        weight = slab[:, 2 * width + 4 : 2 * width + 5] + slab[:, 2 * width + 12 : 2 * width + 13]
        weight_sums.append(jnp.broadcast_to(weight, (PLANE, width)))
    return jnp.concatenate(hidden_sums, axis=1), jnp.concatenate(weight_sums, axis=1)


def grid_kernel(
    lines_ref, lat, total, skip_w, skip_b, dec_w2, dec_b2, proj_w, inverse_hbm, plane_hbm,
    *refs, rows_here, width,
):
    plane_out, pre_bar_out, latent_out, reach_out, sums, inverse, plane, copied = refs[-8:]
    copies = [
        pltpu.make_async_copy(inverse_hbm, inverse, copied.at[0]),
        pltpu.make_async_copy(plane_hbm, plane, copied.at[1]),
    ]
    for copy in copies:
        copy.start()
    sums[0], sums[1] = cell_sums(total, rows_here, width)
    reach = dot3(sums[0], spread(dec_w2[...], rows_here))
    reach = reach + sums[1] * tile_lanes(dec_b2[...], rows_here)
    reach_out[...] = reach
    skip = dot3(lat[...], spread(skip_w[...], rows_here)) + tile_lanes(skip_b[...], rows_here)
    copies[0].wait()
    latent, slope = gelu_both(times_field(inverse, lines_ref[...]) + skip)
    pre_bar = reach * tile_lanes(proj_w[...], rows_here) * slope
    copies[1].wait()
    plane_out[...] = times_field(plane, pre_bar)
    pre_bar_out[...] = pre_bar
    latent_out[...] = latent


def grid_grads_kernel(
    lat, pre_bar, latent, reach, sums, dec_w2, dec_b2, proj_w,
    skip_w_grad, dec_w2_grad, rows_out, table, *, rows_here, width,
):
    skip_w_grad[...] = gather_blocks(dot3(lat[...], pre_bar[...], TN), rows_here, width, width)
    scaled = latent[...] * tile_lanes(proj_w[...], rows_here)
    dec_w2_grad[...] = gather_blocks(dot3(sums[0], scaled, TN), rows_here, width, width)

    def column_sum(value):
        return fold_lanes(jnp.sum(value, axis=0, keepdims=True), rows_here, width)

    rows = [column_sum(pre_bar[...]), column_sum(sums[1] * scaled), column_sum(reach[...] * latent[...])]
    rows_out[...] = jnp.concatenate(rows + [jnp.zeros((5, width), F32)], axis=0)
    cell_kernel = dot3(scaled, spread(dec_w2[...], rows_here), NT)
    offset = scaled * tile_lanes(dec_b2[...], rows_here)
    cells = rows_here * PLANE
    table[cells:] = jnp.zeros((PAD, table.shape[1]), BF16)
    for row in range(rows_here):
        lanes = slice(row * width, (row + 1) * width)
        where = slice(row * PLANE, (row + 1) * PLANE)
        constant = jnp.sum(offset[:, lanes], axis=1, keepdims=True)
        high, low = halves(cell_kernel[:, lanes])
        c_high, c_low = halves(constant)
        lane = iota((PLANE, LANES), 1)
        tail = jnp.where(lane == 0, c_high.astype(F32), jnp.where(lane == 1, c_low.astype(F32), 0.0))
        table[where, : 2 * width] = jnp.concatenate([high.astype(F32), low.astype(F32)], axis=1).astype(BF16)
        table[where, 2 * width :] = tail.astype(BF16)


def place_rows(cell, first_row):
    row = iota((8, cell.shape[1]), 0)
    shifts = jnp.where(row == 0, 2 * log2(RES), jnp.where(row == 1, log2(RES), 0))
    place = (cell >> shifts) & jnp.where(row < 3, RES - 1, 0)
    return (place + jnp.where(row == 0, first_row, 0)).astype(F32)


def input_columns(feats, cell, first_row):
    high, low = halves(feats)
    place = place_rows(cell, first_row)
    return jnp.concatenate([high.astype(F32), low.astype(F32), place, place], axis=0).astype(BF16)


def dec_edges_kernel(
    place_ref, bounds, keys, inverse_degree, saved, table, pred_out, w1_out, b1_out,
    found_scratch, pred_total, grad_total, *, owners, cells, width,
):
    step = pl.program_id(0)
    rows_here = cells // PLANE
    group = found_scratch.shape[1] // CHUNK
    first_row = place_ref[0] * rows_here
    shift = log2(owners * LANES)
    count8 = max(owners, 8)

    @pl.when(step == 0)
    def _():
        pred_total[...] = jnp.zeros_like(pred_total)
        grad_total[...] = jnp.zeros_like(grad_total)

    chunk = step * group
    low_cell, _ = cell_range(bounds, 2, chunk, CHUNK // keys.shape[1])

    @pl.when(low_cell < cells)
    def _():
        rows, key = joined_keys(keys, chunk, group)
        gather_windows(
            found_scratch, keys, rows, table, bounds, 2, chunk, group, DEC_WINDOW, shift, 2 * width + 16
        )
        point = key & (owners * LANES - 1)
        found = found_scratch[:width] + found_scratch[width : 2 * width]
        constant = found_scratch[2 * width : 2 * width + 1] + found_scratch[2 * width + 1 : 2 * width + 2]
        edge = jnp.sum(saved[:width] * found, axis=0, keepdims=True) + constant
        owner = iota((count8, key.shape[1]), 0)
        high, low = halves(jnp.where(owner == (point >> 7), edge, 0.0))
        values = jnp.concatenate([high.astype(F32), low.astype(F32)], axis=0).astype(BF16)
        pred_total[...] += dot(values, one_hot(point & (LANES - 1), 0, LANES), NT)
        left = jnp.concatenate(halves(saved[width : 2 * width] * found), axis=0)
        right = input_columns(saved[2 * width :], key >> shift, first_row)
        grad_total[...] += dot(left, right, NT)

    @pl.when(step == pl.num_programs(0) - 1)
    def _():
        pred_out[...] = (pred_total[:owners] + pred_total[count8 : count8 + owners]) * inverse_degree[...]
        grad = grad_total[:width] + grad_total[width:]
        feats = (grad[:, :8] + grad[:, 8:16]).T
        places = grad[:, 16:24].T / (RES - 1.0)
        w1_out[...] = jnp.concatenate([feats[:3], places[:3]], axis=0)
        b1_out[...] = feats[3:4]


GRAD_ROWS = 108
PACKED_ROWS = 120


def enc_back_kernel(
    place_ref, bounds, keys, saved, lines_ref, pre_bar, scale, skip_w, w2, lift_w, pred_bar,
    skip_w_grad, dec_w2_grad, row_grads, pred_part, dec_w1_grad, dec_b1_grad, inverse_hbm,
    *refs, owners, cells, width,
):
    packed, table, found_scratch, second, feat_total, grad_total, inverse, copied = refs[-8:]
    step = pl.program_id(0)
    rows_here = cells // PLANE
    group = found_scratch.shape[1] // CHUNK
    first_row = place_ref[0] * rows_here
    shift = log2(owners * LANES)
    count8 = max(owners, 8)

    @pl.when(step == 0)
    def _():
        copy = pltpu.make_async_copy(inverse_hbm, inverse, copied)
        copy.start()
        feat_total[...] = jnp.zeros_like(feat_total)
        grad_total[...] = jnp.zeros_like(grad_total)
        second[...] = weights3(w2[...])
        skip = dot3(pre_bar[...], spread(skip_w[...], rows_here), NT)
        copy.wait()
        field = (times_field(inverse, lines_ref[...]) + skip) * scale[...]
        table[cells:] = jnp.zeros((PAD, 2 * width), BF16)
        for row in range(rows_here):
            high, low = halves(field[:, row * width : (row + 1) * width])
            both = jnp.concatenate([high.astype(F32), low.astype(F32)], axis=1).astype(BF16)
            table[row * PLANE : (row + 1) * PLANE] = both

    chunk = step * group
    low_cell, _ = cell_range(bounds, 0, chunk, CHUNK // keys.shape[1])

    @pl.when(low_cell < cells)
    def _():
        lift_columns = jnp.concatenate([lift_w[...], jnp.zeros((4, width), F32)], axis=0).T
        rows, key = joined_keys(keys, chunk, group)
        gather_windows(
            found_scratch, keys, rows, table, bounds, 0, chunk, group, ENC_WINDOW, shift, 2 * width
        )
        point = key & (owners * LANES - 1)
        found = found_scratch[:width] + found_scratch[width:]
        source_bar = found * saved[3 * width : 4 * width]
        k_high, k_low = halves(found * saved[2 * width : 3 * width])
        hidden_bar = dot(second[...], jnp.concatenate([k_high, k_low, k_high], axis=0))
        pre_edge = hidden_bar * saved[width : 2 * width]
        parts = [*halves(saved[:width]), *halves(pre_edge), *halves(source_bar)]
        left = jnp.concatenate(parts + [jnp.ones((16, key.shape[1]), BF16)], axis=0)
        tail = input_columns(saved[4 * width :], key >> shift, first_row)
        grad_total[...] += dot(left, jnp.concatenate([k_high, k_low, tail], axis=0), NT)
        owner_hot = iota((count8, key.shape[1]), 0) == (point >> 7)
        edges = []
        for feat in range(4):
            edge = jnp.sum(source_bar * lift_columns[:, feat : feat + 1], axis=0, keepdims=True)
            edges.append(jnp.where(owner_hot, edge, 0.0))
        values = jnp.concatenate(halves(jnp.concatenate(edges, axis=0)), axis=0)
        feat_total[...] += dot(values, one_hot(point & (LANES - 1), 0, LANES), NT)

    @pl.when(step == pl.num_programs(0) - 1)
    def _():
        w2_part = grad_total[:width, : 2 * width] + grad_total[width : 2 * width, : 2 * width]
        w2_grad = w2_part[:, :width] + w2_part[:, width:]
        b2_part = grad_total[6 * width : 6 * width + 1, : 2 * width]
        b2_grad = b2_part[:, :width] + b2_part[:, width:]
        pre_part = grad_total[2 * width : 3 * width, 2 * width :] + grad_total[3 * width : 4 * width, 2 * width :]
        feats = (pre_part[:, :8] + pre_part[:, 8:16]).T
        places = pre_part[:, 16:24].T / (RES - 1.0)
        lift_part = grad_total[4 * width : 5 * width, 2 * width :] + grad_total[5 * width : 6 * width, 2 * width :]
        lifts = (lift_part[:, :8] + lift_part[:, 8:16]).T
        pair = partial(jnp.concatenate, axis=1)
        stack = partial(jnp.concatenate, axis=0)
        half = width // 2
        bar_sum = jnp.broadcast_to(jnp.sum(pred_bar[...], axis=1, keepdims=True), (1, width))
        fixed = stack(
            [
                pair([w2_grad, dec_w2_grad[...]]),
                pair([skip_w_grad[:half], skip_w_grad[half:]]),
                pair([stack([places[:3], feats[:3]]), dec_w1_grad[...]]),
                pair([feats[3:4], dec_b1_grad[...]]),
                pair([b2_grad, row_grads[1:2]]),
                pair([lifts[4:8], stack([lifts[3:4], row_grads[0:1], row_grads[2:3], bar_sum])]),
            ]
        )
        both = feat_total[: 4 * count8] + feat_total[4 * count8 :]
        empty = jnp.zeros((PACKED_ROWS - GRAD_ROWS - 5, LANES), F32)
        for owner in range(owners):
            rows = [both[feat * count8 + owner : feat * count8 + owner + 1] for feat in range(4)]
            packed[owner] = stack([fixed] + rows + [pred_part[owner : owner + 1], empty])


def arrive_kernel(arrived, proj_b, after, grads, feat_grad, pred, *, owners):
    total = arrived[0]
    for owner in range(1, owners):
        total = total + arrived[owner]
    grads[...] = total[:GRAD_ROWS]
    feat_grad[...] = total[GRAD_ROWS : GRAD_ROWS + 4]
    pred[...] = total[GRAD_ROWS + 4 : GRAD_ROWS + 5] + proj_b[...]


def leave_kernel(mine, other, *outs, width):
    half = width // 2
    left = mine[:, :width] + other[:, :width]
    right = mine[:, width:] + other[:, width:]
    at = width + half
    enc_w1, enc_b1, enc_w2, enc_b2, lift_w, lift_b, skip_w, skip_b, dec_w1, dec_b1, dec_w2, dec_b2, proj_w, proj_b = outs
    enc_w2[...] = left[:width]
    dec_w2[...] = right[:width]
    skip_w[:half] = left[width:at]
    skip_w[half:] = right[width:at]
    enc_w1[...] = left[at : at + 6]
    dec_w1[...] = right[at : at + 6]
    enc_b1[...] = left[at + 6 : at + 7]
    dec_b1[...] = right[at + 6 : at + 7]
    enc_b2[...] = left[at + 7 : at + 8]
    dec_b2[...] = right[at + 7 : at + 8]
    lift_w[...] = left[at + 8 : at + 12]
    lift_b[...] = right[at + 8 : at + 9]
    skip_b[...] = right[at + 9 : at + 10]
    proj_w[...] = right[at + 10 : at + 11]
    proj_b[...] = right[at + 11 : at + 12, :1]


def shape(*dims, dtype=F32):
    return jax.ShapeDtypeStruct(dims, dtype)


def whole(array):
    zeros = (0,) * array.ndim
    return pl.BlockSpec(array.shape, lambda i: zeros, pipeline_mode=pl.Buffered(1))


HELD = VMEM
FAR = pl.BlockSpec(memory_space=pl.ANY)


def kernel_call(kernel, name, steps, operands, out_shape, out_specs, scratch=(), mib=62, micros=10, **more):
    arrays = [array for array, _ in operands]
    specs = [whole(array) if spec is None else spec for array, spec in operands]
    return pl.pallas_call(
        kernel,
        grid=(steps,),
        in_specs=specs,
        out_specs=out_specs,
        out_shape=out_shape,
        scratch_shapes=list(scratch),
        compiler_params=pltpu.CompilerParams(vmem_limit_bytes=mib << 20),
        cost_estimate=pl.CostEstimate(flops=0, bytes_accessed=micros * 2_000_000, transcendentals=0),
        name=name,
        **more,
    )(*arrays)


def on_device(
    mesh_feat,
    mesh_pos,
    query_pos,
    enc_cell,
    enc_point,
    enc_count,
    dec_cell,
    dec_query,
    dec_count,
    enc_w1,
    enc_b1,
    enc_w2,
    enc_b2,
    lift_w,
    lift_b,
    spec_w,
    skip_w,
    skip_b,
    dec_w1,
    dec_b1,
    dec_w2,
    dec_b2,
    proj_w,
    proj_b,
    pred_bar,
):
    width = lift_w.shape[1]
    owners = lax.axis_size("wide")
    shapes = lax.axis_size("grid")
    rows_here = RES // owners
    cells = rows_here * PLANE
    modes_here = spec_w.shape[0]
    lines = modes_here // MODES
    enc_blocks, dec_blocks = enc_cell.shape[1], dec_cell.shape[1]
    enc_edges, dec_edges = enc_blocks * LANES, dec_blocks * LANES
    enc_span, dec_span = ENC_GROUP * CHUNK, DEC_GROUP * CHUNK
    lanes = rows_here * width
    place = lax.axis_index("wide").astype(jnp.int32).reshape(1)
    plane_np = plane_matrix(owners)
    plane = jnp.asarray(np.stack(halves_np(plane_np)))
    inverse = jnp.asarray(np.stack(halves_np(np.ascontiguousarray(plane_np.T))))
    cos_x, sin_x = (jnp.asarray(part) for part in x_tables(rows_here, width))
    rows = [value.reshape(1, -1) for value in (enc_b1, enc_b2, lift_b, skip_b, dec_b1, dec_b2, proj_w, proj_b)]
    enc_b1, enc_b2, lift_b, skip_b, dec_b1, dec_b2, proj_w, proj_b = rows
    sizes = dict(owners=owners, cells=cells, width=width)
    dma = pltpu.SemaphoreType.DMA

    def exchange(value):
        return lax.all_to_all(value, "wide", 0, 0, tiled=True)

    payload = kernel_call(
        partial(share_kernel, owners=owners),
        "share_points",
        1,
        [(value, None) for value in (mesh_feat[0], mesh_pos[0], query_pos[0], pred_bar, dec_query[0], dec_count)],
        shape(owners, 2 * FEAT_ROWS + owners, LANES),
        HELD,
    )
    shared = exchange(payload)
    local = [enc_cell[0], enc_point[0], enc_count, dec_cell[0], dec_query[0], dec_count]
    enc_keys, dec_keys, bounds = kernel_call(
        partial(sort_kernel, owners=owners, cells=cells),
        "sort_edges",
        1,
        [(value, None) for value in local] + [(payload, FAR)],
        [
            shape(LANES, enc_blocks, dtype=jnp.int32),
            shape(LANES, dec_blocks, dtype=jnp.int32),
            shape(8, LANES, dtype=jnp.int32),
        ],
        [HELD] * 3,
    )

    fixed = owners * FEAT_ROWS
    depth = 3 * fixed + 16
    saved_rows = 4 * width + FEAT_ROWS
    plane_scratch = pltpu.VMEM((2, 2 * MODES * MODES, PLANE), BF16)
    inverse_scratch = pltpu.VMEM((2, PLANE, 2 * MODES * MODES), BF16)
    saved_spec = pl.BlockSpec((saved_rows, enc_span), lambda i: (0, i))
    saved, lat, scale, plane_lat = kernel_call(
        partial(enc_forward_kernel, **sizes),
        "encode",
        enc_edges // enc_span,
        [(place, SMEM), (bounds, SMEM), (enc_keys, HELD), (shared, HELD)]
        + [(value, None) for value in (enc_w1, enc_b1, enc_w2, enc_b2, lift_w, lift_b)]
        + [(plane, FAR)],
        [
            shape(saved_rows, enc_edges),
            shape(PLANE, lanes),
            shape(PLANE, lanes),
            shape(2 * MODES * MODES, lanes),
        ],
        [saved_spec, HELD, HELD, HELD],
        [
            pltpu.VMEM((cells + PAD, 2 * LANES), F32),
            pltpu.VMEM((2 * fixed, LANES), BF16),
            pltpu.VMEM((2 * width, depth), BF16),
            pltpu.VMEM((width, 3 * width), BF16),
            pltpu.VMEM((2 * width + 16, enc_span), BF16),
            plane_scratch,
            dma,
        ],
    )
    modes_lines = exchange(plane_lat.reshape(owners, 2 * lines, lanes))

    dec_rows = 2 * width + FEAT_ROWS
    dec_steps = dec_edges // dec_span
    half_steps = dec_steps // 2

    def dec_sums(first_step, steps, before, saved_before, after, name):
        return kernel_call(
            partial(dec_sums_kernel, first_step=first_step, **sizes),
            name,
            steps,
            [
                (place, SMEM), (bounds, SMEM), (dec_keys, HELD), (shared, HELD), (dec_w1, None), (dec_b1, None),
                (before, HELD if first_step else FAR), (saved_before, FAR), (after, FAR),
            ],
            [
                shape(dec_rows, dec_edges),
                shape(cells + PAD, 2 * LANES),
                shape(owners, LANES),
            ],
            [pl.BlockSpec((dec_rows, dec_span), lambda i: (0, i + first_step)), HELD, HELD],
            [
                pltpu.VMEM((2 * fixed, LANES), BF16),
                pltpu.VMEM((width, depth), BF16),
                pltpu.VMEM((2 * width + 16, dec_span), BF16),
            ],
            input_output_aliases={7: 0} if first_step else {},
        )

    dec_saved, dec_total, inverse_degree = dec_sums(0, half_steps, plane_lat, plane_lat, plane_lat, "decode_sums_a")

    mix_step, grad_step = min(MIX_STEP, modes_here), min(GRAD_STEP, modes_here)

    def spec_block(step):
        return pl.BlockSpec((step, width, 2 * width), lambda i: (i, 0, 0))

    def mode_pass(kernel, lines_in, after, name):
        return kernel_call(
            partial(kernel, owners=owners, width=width),
            name,
            1,
            [(place, SMEM), (lines_in, HELD), (cos_x, None), (sin_x, None), (spec_w, FAR), (after, FAR)],
            [shape(modes_here, 2 * width), shape(owners, 2 * lines, lanes)],
            [HELD, HELD],
            [
                pltpu.VMEM((modes_here, 2 * width), F32),
                pltpu.VMEM((modes_here, width, 2 * width), F32),
                dma((modes_here // mix_step,)),
            ],
        )

    modes, back_lines = mode_pass(mix_kernel, modes_lines, inverse_degree, "mix_modes")
    def from_shapes(value):
        parts = [value]
        for step in range(1, shapes):
            parts.append(lax.ppermute(value, "grid", [(i, i ^ step) for i in range(shapes)]))
        return [part[None] for part in parts]

    all_modes = from_shapes(modes)
    grid_lines = exchange(back_lines).reshape(2 * MODES * MODES, lanes)
    dec_saved, dec_total, inverse_degree = dec_sums(
        half_steps, dec_steps - half_steps, dec_total, dec_saved, back_lines, "decode_sums_b"
    )

    plane_bar, pre_bar, latent, reach, sums = kernel_call(
        partial(grid_kernel, rows_here=rows_here, width=width),
        "grid_fields",
        1,
        [(grid_lines, HELD), (lat, HELD), (dec_total, HELD)]
        + [(value, None) for value in (skip_w, skip_b, dec_w2, dec_b2, proj_w)]
        + [(inverse, FAR), (plane, FAR)]
        + [(value, FAR) for value in all_modes[1:]],
        [shape(2 * MODES * MODES, lanes)] + [shape(PLANE, lanes)] * 3 + [shape(2, PLANE, lanes)],
        [HELD] * 5,
        [inverse_scratch, plane_scratch, dma((2,))],
    )
    bar_lines = exchange(plane_bar.reshape(owners, 2 * lines, lanes))

    skip_w_grad, dec_w2_grad, row_grads, dec_table = kernel_call(
        partial(grid_grads_kernel, rows_here=rows_here, width=width),
        "grid_grads",
        1,
        [(value, HELD) for value in (lat, pre_bar, latent, reach, sums)]
        + [(value, None) for value in (dec_w2, dec_b2, proj_w)],
        [
            shape(width, width),
            shape(width, width),
            shape(8, width),
            shape(cells + PAD, 2 * LANES, dtype=BF16),
        ],
        [HELD] * 4,
    )

    mixed_bar, bar_back = mode_pass(mix_back_kernel, bar_lines, row_grads, "mix_back")
    bar_grid_lines = exchange(bar_back).reshape(2 * MODES * MODES, lanes)

    all_grads = from_shapes(mixed_bar)

    count8 = max(owners, 8)
    pred_part, dec_w1_grad, dec_b1_grad = kernel_call(
        partial(dec_edges_kernel, **sizes),
        "decode_edges",
        dec_steps,
        [
            (place, SMEM), (bounds, SMEM), (dec_keys, HELD), (inverse_degree, HELD),
            (dec_saved, pl.BlockSpec((dec_rows, dec_span), lambda i: (0, i))), (dec_table, HELD),
        ],
        [shape(owners, LANES), shape(6, width), shape(1, width)],
        [HELD] * 3,
        [
            pltpu.VMEM((2 * width + 16, dec_span), F32),
            pltpu.VMEM((2 * count8, LANES), F32),
            pltpu.VMEM((2 * width, 32), F32),
        ],
    )

    packed = kernel_call(
        partial(enc_back_kernel, **sizes),
        "encode_back",
        enc_edges // enc_span,
        [(place, SMEM), (bounds, SMEM), (enc_keys, HELD), (saved, saved_spec)]
        + [(value, HELD) for value in (bar_grid_lines, pre_bar, scale)]
        + [(value, None) for value in (skip_w, enc_w2, lift_w, pred_bar)]
        + [(value, HELD) for value in (skip_w_grad, dec_w2_grad, row_grads, pred_part, dec_w1_grad, dec_b1_grad)]
        + [(inverse, FAR)]
        + [(value, FAR) for value in all_grads[1:]],
        shape(owners, PACKED_ROWS, LANES),
        HELD,
        [
            pltpu.VMEM((cells + PAD, 2 * width), BF16),
            pltpu.VMEM((2 * width, enc_span), F32),
            pltpu.VMEM((width, 3 * width), BF16),
            pltpu.VMEM((8 * count8, LANES), F32),
            pltpu.VMEM((6 * width + 16, 2 * width + 32), F32),
            inverse_scratch,
            dma,
        ],
    )
    arrived = exchange(packed)

    rank = lax.axis_index("grid").astype(jnp.int32).reshape(1)
    spec_grad = kernel_call(
        partial(spec_grad_kernel, shapes=shapes, width=width),
        "spec_grad",
        modes_here // grad_step,
        [(rank, SMEM)]
        + [
            (value, pl.BlockSpec((value.shape[0], grad_step, 2 * width), lambda i: (0, i, 0)))
            for value in all_modes + all_grads
        ]
        + [(packed, FAR)],
        shape(modes_here, width, 2 * width),
        spec_block(grad_step),
        [pltpu.VMEM((shapes, grad_step, 2 * width), F32)] * 2,
    )

    grads, feat_grad, pred = kernel_call(
        partial(arrive_kernel, owners=owners),
        "arrive",
        1,
        [(arrived, HELD), (proj_b, None), (spec_grad, FAR)],
        [shape(GRAD_ROWS, LANES), shape(4, LANES), shape(1, LANES)],
        [HELD] * 3,
    )
    other, step = jnp.zeros_like(grads), 1
    while step < shapes:
        grads = grads if step == 1 else grads + other
        other = lax.ppermute(grads, "grid", [(i, i ^ step) for i in range(shapes)])
        step *= 2
    vector = shape(1, width)
    square = shape(width, width)
    first = shape(6, width)
    outs = kernel_call(
        partial(leave_kernel, width=width),
        "leave",
        1,
        [(grads, HELD), (other, HELD)],
        [
            first, vector, square, vector, shape(4, width), vector,
            square, vector, first, vector, square, vector, vector, shape(1, 1),
        ],
        [HELD] * 14,
    )
    outs = [out.reshape(-1) if out.shape[0] == 1 else out for out in outs]
    return (pred, feat_grad[None], *outs[:6], spec_grad, *outs[6:])


def solution(mesh):
    placed = (
        P("grid", None, "wide"),
        P("grid", None, "wide"),
        P("grid", None, "wide"),
        P("grid", "wide", None),
        P("grid", "wide", None),
        P("grid", "wide"),
        P("grid", "wide", None),
        P("grid", "wide", None),
        P("grid", "wide"),
        P(),
        P(),
        P(),
        P(),
        P(),
        P(),
        P("wide", None, None),
        P(),
        P(),
        P(),
        P(),
        P(),
        P(),
        P(),
        P(),
        P("grid", "wide"),
    )
    return jax.shard_map(
        on_device,
        mesh=mesh,
        in_specs=placed,
        out_specs=(
            P("grid", "wide"),
            P("grid", None, "wide"),
            P(),
            P(),
            P(),
            P(),
            P(),
            P(),
            P("wide", None, None),
            P(),
            P(),
            P(),
            P(),
            P(),
            P(),
            P(),
            P(),
        ),
        check_vma=False,
    )
```

```python
from functools import partial
import math

import jax
import jax.numpy as jnp
import ml_dtypes
import numpy as np
from jax import lax
from jax.experimental import pallas as pl
from jax.experimental.pallas import tpu as pltpu
from jax.sharding import PartitionSpec as P

MODES = 16
RES = 32
PLANE = RES * RES
CHUNK = 256
LANES = 128
ENC_GROUP = 16
DEC_GROUP = 16
FEAT_ROWS = 8
INPUT_ROWS = 48
ENC_WINDOW = 64
DEC_WINDOW = 128
PAD = 256
MIX_STEP = 64
GRAD_STEP = 128
F32 = jnp.float32
BF16 = jnp.bfloat16
GELU_A = 0.7978845608028654
GELU_B = 0.044715

NN = (((1,), (0,)), ((), ()))
NT = (((1,), (1,)), ((), ()))
TN = (((0,), (0,)), ((), ()))

VMEM = pl.BlockSpec(memory_space=pltpu.VMEM)
SMEM = pl.BlockSpec(memory_space=pltpu.SMEM)


def kept_freqs():
    half = MODES // 2
    return np.concatenate([np.arange(half), np.arange(RES - half, RES)])


def plane_matrix(owners):
    lines = MODES * MODES // owners
    line = np.arange(MODES * MODES)
    freq_y, freq_z = kept_freqs()[line // MODES], line % MODES
    cell = np.arange(PLANE)
    turns = (freq_y[:, None] * (cell // RES) + freq_z[:, None] * (cell % RES)) % RES
    angle = turns * (2.0 * math.pi / RES)
    both = np.stack([np.cos(angle), -np.sin(angle)]).reshape(2, owners, lines, PLANE)
    matrix = both.transpose(1, 0, 2, 3).reshape(2 * MODES * MODES, PLANE)
    return matrix.astype(np.float32)


def halves_np(matrix):
    high = matrix.astype(ml_dtypes.bfloat16)
    low = (matrix - high.astype(np.float32)).astype(ml_dtypes.bfloat16)
    return high, low


def line_angles():
    turns = (kept_freqs()[:, None] * np.arange(RES)[None, :]) % RES
    return turns * (2.0 * math.pi / RES)


def x_tables(rows_here, width):
    angle = line_angles().reshape(MODES, RES // rows_here, rows_here, 1)
    angle = np.broadcast_to(angle, (MODES, RES // rows_here, rows_here, width))
    angle = angle.reshape(MODES, RES // rows_here, rows_here * width)
    return np.cos(angle).astype(np.float32), np.sin(angle).astype(np.float32)


def log2(number):
    return number.bit_length() - 1


def iota(shape, axis):
    return lax.broadcasted_iota(jnp.int32, shape, axis)


def halves(value):
    high = value.astype(BF16)
    low = (value - high.astype(F32)).astype(BF16)
    return high, low


def dot(a, b, dims=NN):
    return lax.dot_general(a, b, dims, preferred_element_type=F32)


def dot3(a, b, dims=NN):
    a_high, a_low = halves(a)
    b_high, b_low = halves(b)
    return dot(a_high, b_high, dims) + dot(a_low, b_high, dims) + dot(a_high, b_low, dims)


def one_hot(index, first, rows):
    places = iota((rows, index.shape[1]), 0) + first
    return jnp.where(places == index, 1.0, 0.0).astype(BF16)


def gelu_both(value):
    square = value * value
    turn = jnp.tanh(value * (GELU_A + (GELU_A * GELU_B) * square))
    half = 0.5 * (1.0 + turn)
    slope = half + (0.5 * value) * (1.0 - turn * turn) * (
        GELU_A + (3.0 * GELU_A * GELU_B) * square
    )
    return value * half, slope


def sort_columns(values):
    rows = values.shape[0]
    regs = rows // 8
    low = log2(regs)
    total = low + 3 + 7
    sub = iota((8, LANES), 0)
    lane = iota((8, LANES), 1)
    x = values.reshape(regs, 8, LANES)

    def flip(x, bit):
        if bit >= total:
            return x
        if bit < low:
            y = x.reshape(regs >> (bit + 1), 2, 1 << bit, 8, LANES)
            return jnp.stack([y[:, 0], ~y[:, 1]], axis=1).reshape(regs, 8, LANES)
        if bit < low + 3:
            mask = -((sub >> (bit - low)) & 1)
        else:
            mask = -((lane >> (bit - low - 3)) & 1)
        return x ^ mask[None]

    def exchange(x, bit):
        if bit < low:
            y = x.reshape(regs >> (bit + 1), 2, 1 << bit, 8, LANES)
            one, two = y[:, 0], y[:, 1]
            pair = [jnp.minimum(one, two), jnp.maximum(one, two)]
            return jnp.stack(pair, axis=1).reshape(regs, 8, LANES)
        if bit < low + 3:
            axis, dist, size, place = 1, 1 << (bit - low), 8, sub
        else:
            axis, dist, size, place = 2, 1 << (bit - low - 3), LANES, lane
        after = pltpu.roll(x, size - dist, axis)
        before = after if 2 * dist == size else pltpu.roll(x, dist, axis)
        first = ((place & dist) == 0)[None]
        return jnp.where(first, jnp.minimum(x, after), jnp.maximum(x, before))

    for phase in range(1, total + 1):
        x = flip(x, phase)
        for bit in reversed(range(phase)):
            x = exchange(x, bit)
        x = flip(x, phase)
    return x.reshape(rows, LANES)


def layer_matrix(feat_rows, cell_rows):
    feat_high, feat_low = halves(feat_rows)
    cell_high, cell_low = halves(cell_rows)
    parts = [feat_high, feat_high, feat_low, cell_high, cell_low]
    parts = [part.astype(F32) for part in parts] + [jnp.zeros((LANES - 40, feat_rows.shape[1]), F32)]
    return jnp.concatenate(parts, axis=0).T[:, :INPUT_ROWS].astype(BF16)


def place_rows(cell, first_row):
    row = iota((8, cell.shape[1]), 0)
    shifts = jnp.where(row == 0, 2 * log2(RES), jnp.where(row == 1, log2(RES), 0))
    place = (cell >> shifts) & jnp.where(row < 3, RES - 1, 0)
    return (place + jnp.where(row == 0, first_row, 0)).astype(F32)


def edge_feats(key, table, owners):
    point = key & (owners * LANES - 1)
    found = dot(table, one_hot(point & (LANES - 1), 0, LANES))
    owner = (iota(found.shape, 0) >> 3) & (owners - 1)
    found = jnp.where(owner == (point >> 7), found, 0.0)
    return jnp.sum(found.reshape(2 * owners, FEAT_ROWS, key.shape[1]), axis=0)


def stack_inputs(feats, place):
    high, low = halves(feats)
    parts = [high.astype(F32), low.astype(F32), high.astype(F32), place, place, jnp.zeros_like(place)]
    return jnp.concatenate(parts, axis=0).astype(BF16)


def stack3(value):
    high, low = halves(value)
    return jnp.concatenate([high, low, high], axis=0)


def weights3(matrix):
    high, low = halves(matrix)
    return jnp.concatenate([high, high, low], axis=1)


def key_row(keys_ref, chunk):
    per = CHUNK // keys_ref.shape[1]
    rows = [keys_ref[pl.ds(chunk * per + i, 1), :] for i in range(per)]
    return rows[0] if per == 1 else jnp.concatenate(rows, axis=1)


def cell_range(bounds_ref, line, chunk, per):
    return bounds_ref[line, chunk * per], bounds_ref[line + 1, chunk * per + per - 1]


def spread(block, copies):
    rows, columns = block.shape
    tiled = jnp.concatenate([jnp.concatenate([block] * copies, axis=1)] * copies, axis=0)
    return jnp.where(
        iota(tiled.shape, 0) // rows == iota(tiled.shape, 1) // columns, tiled, 0.0
    )


def gather_blocks(product, copies, rows, columns):
    total = product[:rows, :columns]
    for i in range(1, copies):
        total = total + product[i * rows : (i + 1) * rows, i * columns : (i + 1) * columns]
    return total


def tile_lanes(row, copies):
    return row if copies == 1 else jnp.concatenate([row] * copies, axis=1)


def fold_lanes(row, copies, width):
    total = row[:, :width]
    for i in range(1, copies):
        total = total + row[:, i * width : (i + 1) * width]
    return total


def column(counts):
    return jnp.broadcast_to(counts, (8, counts.shape[1])).T[:, :1]


def share_kernel(feat, pos, query_pos, pred_bar, dec_query, dec_count, payload, *, owners):
    blocks = dec_query.shape[0]
    lane_valid = jnp.where(
        iota((blocks, LANES), 1) < column(dec_count[...]), dec_query[...], owners * LANES
    )
    ones = jnp.zeros((max(owners, 16), LANES), F32)
    degree = ones
    for block in range(0, blocks, 2):
        row = jnp.concatenate([lane_valid[block : block + 1], lane_valid[block + 1 : block + 2]], axis=1)
        high = one_hot(row >> 7, 0, ones.shape[0])
        low = one_hot(row & (LANES - 1), 0, LANES)
        degree = degree + dot(high, low, NT)
    filled = jnp.ones((1, LANES), F32)
    empty = jnp.zeros((3, LANES), F32)
    places = [pos[i] for i in range(3)]
    queries = [query_pos[i] for i in range(3)]
    rows = places + [filled, feat[0]] + queries + [filled, pred_bar[...], empty, degree[:owners]]
    mine = jnp.concatenate(rows, axis=0)
    for owner in range(owners):
        payload[owner] = mine


def sort_kernel(
    enc_cell, enc_point, enc_count, dec_cell, dec_query, dec_count, after,
    enc_keys, dec_keys, bounds, *, owners, cells,
):
    shift = log2(owners * LANES)

    def keys(cell, point, count):
        lane = iota(cell.shape, 1)
        key = jnp.where(lane < column(count), (cell << shift) | point, cells << shift)
        return sort_columns(key)

    enc = keys(enc_cell[...], enc_point[...], enc_count[...])
    dec = keys(dec_cell[...], dec_query[...], dec_count[...])
    enc_keys[...] = enc.T
    dec_keys[...] = dec.T
    ends = [enc[:1], enc[-1:], dec[:1], dec[-1:]]
    bounds[...] = jnp.concatenate(ends + [jnp.zeros((4, LANES), jnp.int32)], axis=0) >> shift


def joined_keys(keys, chunk, group):
    rows = [key_row(keys, chunk + i) for i in range(group)]
    return rows, jnp.concatenate(rows, axis=1)


def later_windows(windows, size, visit):
    most = windows[0][1]
    for _, count in windows[1:]:
        most = jnp.maximum(most, count)

    @pl.when(most > 1)
    def _():
        for i, (begin, count) in enumerate(windows):

            def more(j, carry):
                visit(i, begin + j * size)
                return carry

            lax.fori_loop(1, count, more, 0)


def scatter_windows(total, keys, cell, message, bounds, line, chunk, group, size, shift, columns):
    per = CHUNK // keys.shape[1]
    windows, parts = [], []
    for i in range(group):
        begin, end = cell_range(bounds, line, chunk + i, per)
        begin = pl.multiple_of(begin & -8, 8)
        lanes = slice(i * CHUNK, (i + 1) * CHUNK)
        parts.append(dot(one_hot(cell[:, lanes], begin, size), message[:, lanes], NT))
        windows.append((begin, (end - begin) // size + 1))
    for (begin, _), part in zip(windows, parts):
        total[pl.ds(begin, size), :columns] += part

    def visit(i, start):
        start = pl.multiple_of(start, 8)
        hot = one_hot(key_row(keys, chunk + i) >> shift, start, size)
        part = dot(hot, message[:, i * CHUNK : (i + 1) * CHUNK], NT)
        total[pl.ds(start, size), :columns] += part

    later_windows(windows, size, visit)


def gather_windows(found, keys, rows, table, bounds, line, chunk, group, size, shift, columns):
    per = CHUNK // keys.shape[1]
    windows = []
    for i in range(group):
        begin, end = cell_range(bounds, line, chunk + i, per)
        begin = pl.multiple_of(begin & -16, 16)
        hot = one_hot(rows[i] >> shift, begin, size)
        found[:, i * CHUNK : (i + 1) * CHUNK] = dot(table[pl.ds(begin, size), :columns], hot, TN)
        windows.append((begin, (end - begin) // size + 1))

    def visit(i, start):
        start = pl.multiple_of(start, 16)
        hot = one_hot(key_row(keys, chunk + i) >> shift, start, size)
        part = dot(table[pl.ds(start, size), :columns], hot, TN)
        found[:, i * CHUNK : (i + 1) * CHUNK] += part

    later_windows(windows, size, visit)


def slot_copies(far, slots, semaphores, out):
    span = slots.shape[2]

    def copy(step):
        slot = step % 2
        columns = far.at[:, pl.ds(pl.multiple_of(step * span, span), span)]
        ends = (slots.at[slot], columns) if out else (columns, slots.at[slot])
        return pltpu.make_async_copy(*ends, semaphores.at[slot])

    return copy


def used_steps(bounds, line, group, per, cells, steps):
    used = 0
    for step in range(steps):
        used = used + jnp.where(bounds[line, step * group * per] < cells, 1, 0)
    return used


def enc_forward_kernel(
    place_ref, bounds, keys, shared, w1, b1, w2, b2, lift_w, lift_b, plane_hbm,
    saved_hbm, lat, scale, plane_out,
    total, table, first, second, message, plane, copied, slots, stored, *, owners, cells, width,
):
    step = pl.program_id(0)
    rows_here = cells // PLANE
    group = message.shape[1] // CHUNK
    shift = log2(owners * LANES)
    first_row = place_ref[0] * rows_here
    copy = pltpu.make_async_copy(plane_hbm, plane, copied)
    save = slot_copies(saved_hbm, slots, stored, out=True)

    @pl.when(step == 0)
    def _():
        copy.start()
        total[...] = jnp.zeros_like(total)
        feats = jnp.concatenate([shared[i, :FEAT_ROWS] for i in range(owners)], axis=0)
        table[...] = jnp.concatenate(halves(feats), axis=0)
        empty = jnp.zeros((3, width), F32)
        pre_rows = jnp.concatenate([w1[3:6], b1[...], jnp.zeros((4, width), F32)], axis=0)
        lift_rows = jnp.concatenate([empty, lift_b[...], lift_w[...]], axis=0)
        cell_rows = jnp.concatenate([w1[0:3] / (RES - 1.0), jnp.zeros((5, width), F32)], axis=0)
        first[...] = layer_matrix(
            jnp.concatenate([pre_rows, lift_rows], axis=1),
            jnp.concatenate([cell_rows, jnp.zeros((8, width), F32)], axis=1),
        )
        second[...] = weights3(w2[...].T)

    chunk = step * group
    low_cell, _ = cell_range(bounds, 0, chunk, CHUNK // keys.shape[1])

    @pl.when(low_cell < cells)
    def _():
        bias = jnp.broadcast_to(b2[...], (8, width)).T[:, :1]
        _, key = joined_keys(keys, chunk, group)
        cell = key >> shift
        feats = edge_feats(key, table[...], owners)
        both = dot(first[...], stack_inputs(feats, place_rows(cell, first_row)))
        lifted = both[width:]
        hidden, slope = gelu_both(both[:width])
        kernel = dot(second[...], stack3(hidden)) + bias

        @pl.when(step >= 2)
        def _():
            save(step - 2).wait()

        saved = slots.at[step % 2]
        saved[0 * width : 1 * width] = hidden
        saved[1 * width : 2 * width] = slope
        saved[2 * width : 3 * width] = lifted
        saved[3 * width : 4 * width] = kernel
        saved[4 * width :] = feats
        save(step).start()
        high, low = halves(kernel * lifted)
        message[...] = jnp.concatenate([high, low, jnp.ones((16, key.shape[1]), BF16)], axis=0)
        scatter_windows(
            total, keys, cell, message, bounds, 0, chunk, group, ENC_WINDOW, shift, 2 * width + 16
        )

    @pl.when(step == pl.num_programs(0) - 1)
    def _():
        fields, scales = [], []
        for row in range(rows_here):
            slab = total[row * PLANE : (row + 1) * PLANE]
            inverse = 1.0 / jnp.maximum(slab[:, 2 * width : 2 * width + 1], 1.0)
            fields.append((slab[:, :width] + slab[:, width : 2 * width]) * inverse)
            scales.append(jnp.broadcast_to(inverse, (PLANE, width)))
        field = jnp.concatenate(fields, axis=1)
        lat[...] = field
        scale[...] = jnp.concatenate(scales, axis=1)
        copy.wait()
        plane_out[...] = times_field(plane, field)
        steps = keys.shape[0] * keys.shape[1] // slots.shape[2]
        used = used_steps(bounds, 0, group, CHUNK // keys.shape[1], cells, steps)

        @pl.when(used >= 2)
        def _():
            save(used - 2).wait()

        @pl.when(used >= 1)
        def _():
            save(used - 1).wait()


def times_field(matrix, field):
    high, low = halves(field)
    return dot(matrix[0], high) + dot(matrix[1], high) + dot(matrix[0], low)


def dec_sums_kernel(
    place_ref, bounds, keys, shared, w1, b1, before, saved_before, after, *refs,
    owners, cells, width, first_step,
):
    if first_step == 0:
        saved, total, inverse_out, table, first, message = refs
    else:
        lat, skip_w, skip_b, dec_w2, dec_b2, saved, sums, reach, skip, total, table, first, message = refs
    step = pl.program_id(0)
    rows_here = cells // PLANE
    group = message.shape[1] // CHUNK
    shift = log2(owners * LANES)
    first_row = place_ref[0] * rows_here

    @pl.when(step == 0)
    def _():
        total[...] = jnp.zeros_like(total) if first_step == 0 else before[...]
        degree = shared[0, 2 * FEAT_ROWS :]
        for i in range(1, owners):
            degree = degree + shared[i, 2 * FEAT_ROWS :]
        inverse = 1.0 / jnp.maximum(degree, 1.0)
        if first_step == 0:
            inverse_out[...] = inverse
        feats = []
        for i in range(owners):
            rows = shared[i, FEAT_ROWS : 2 * FEAT_ROWS]
            weighted = rows * inverse[i : i + 1]
            feats.append(jnp.where(iota(rows.shape, 0) == 4, weighted, rows))
        table[...] = jnp.concatenate(halves(jnp.concatenate(feats, axis=0)), axis=0)
        feat_rows = jnp.concatenate([w1[0:3], b1[...], jnp.zeros((4, width), F32)], axis=0)
        cell_rows = jnp.concatenate([w1[3:6] / (RES - 1.0), jnp.zeros((5, width), F32)], axis=0)
        first[...] = layer_matrix(feat_rows, cell_rows)

    chunk = (step + first_step) * group
    low_cell, _ = cell_range(bounds, 2, chunk, CHUNK // keys.shape[1])

    @pl.when(low_cell < cells)
    def _():
        _, key = joined_keys(keys, chunk, group)
        cell = key >> shift
        feats = edge_feats(key, table[...], owners)
        hidden, slope = gelu_both(dot(first[...], stack_inputs(feats, place_rows(cell, first_row))))
        weight = feats[4:5]
        saved[0 * width : 1 * width] = hidden
        saved[1 * width : 2 * width] = slope * weight
        saved[2 * width :] = feats
        high, low = halves(hidden * weight)
        w_high, w_low = halves(feats)
        tail = jnp.concatenate([w_high.astype(F32), w_low.astype(F32)], axis=0).astype(BF16)
        message[...] = jnp.concatenate([high, low, tail], axis=0)
        scatter_windows(
            total, keys, cell, message, bounds, 2, chunk, group, DEC_WINDOW, shift, 2 * width + 16
        )

    if first_step == 0:
        return

    @pl.when(step == pl.num_programs(0) - 1)
    def _():
        sums[0], sums[1] = cell_sums(total, rows_here, width)
        reached = dot3(sums[0], spread(dec_w2[...], rows_here))
        reach[...] = reached + sums[1] * tile_lanes(dec_b2[...], rows_here)
        skipped = dot3(lat[...], spread(skip_w[...], rows_here))
        skip[...] = skipped + tile_lanes(skip_b[...], rows_here)


def x_forward(lines_ref, cos_ref, sin_ref, put, owners, lines, width):
    lanes = lines_ref.shape[2]
    for kx in range(MODES):
        real = jnp.zeros((lines, lanes), F32)
        imag = jnp.zeros((lines, lanes), F32)
        for owner in range(owners):
            cos, sin = cos_ref[kx, owner : owner + 1], sin_ref[kx, owner : owner + 1]
            line_real, line_imag = lines_ref[owner, :lines], lines_ref[owner, lines:]
            real = real + cos * line_real + sin * line_imag
            imag = imag + cos * line_imag - sin * line_real
        if lanes == width:
            put(kx, jnp.concatenate([real, imag], axis=1))
        else:
            pair = 2 * width
            while real.shape[1] > pair:
                half = real.shape[1] // 2
                real, imag = real[:, :half] + real[:, half:], imag[:, :half] + imag[:, half:]
            real = real + pltpu.roll(real, width, 1)
            imag = imag + pltpu.roll(imag, width, 1)
            put(kx, jnp.where(iota(real.shape, 1) < width, real, imag))


def x_inverse(take, out_ref, owners, lines, width):
    angles = line_angles()
    rows_here = RES // owners
    modes = [take(kx) for kx in range(MODES)]
    lane = iota(modes[0].shape, 1)
    turned = [
        jnp.where(lane < width, -pltpu.roll(mode, width, 1), pltpu.roll(mode, width, 1))
        for mode in modes
    ]

    def at(x):
        total = None
        for kx in range(MODES):
            for value, factor in ((modes[kx], np.cos(angles[kx, x])), (turned[kx], np.sin(angles[kx, x]))):
                factor = float(np.float32(factor)) if abs(factor) > 1e-9 else 0.0
                if factor == 0.0:
                    continue
                term = value if factor == 1.0 else value * factor
                total = term if total is None else total + term
        return total

    for owner in range(owners):
        if rows_here == 1:
            here = at(owner)
            out_ref[owner, :lines] = here[:, :width]
            out_ref[owner, lines:] = here[:, width:]
            continue
        for pair in range(rows_here // 2):
            one, two = at(owner * rows_here + 2 * pair), at(owner * rows_here + 2 * pair + 1)
            one_turned, two_turned = pltpu.roll(one, width, 1), pltpu.roll(two, width, 1)
            where = slice(2 * pair * width, (2 * pair + 2) * width)
            out_ref[owner, :lines, where] = jnp.where(lane < width, one, two_turned)
            out_ref[owner, lines:, where] = jnp.where(lane < width, one_turned, two)


def factor_column(place_ref, lines):
    line = place_ref[0] * lines + iota((lines, 1), 0)
    return jnp.where((line & (MODES - 1)) == 0, 1.0, 2.0) / float(RES**3)


def split_weights(spec_w, base, width):
    block = spec_w[pl.ds(base, 8)].reshape(8 * width, 2 * width)
    return jnp.concatenate(halves(block), axis=1)


def interleave(one, two):
    parts = []
    for at in range(0, one.shape[0], 8):
        parts += [one[at : at + 8], two[at : at + 8]]
    return jnp.concatenate(parts, axis=0)


def fetch_weights(spec_hbm, spec_w, copied):
    count = spec_w.shape[0] // copied.shape[0]

    def copy(i):
        where = pl.ds(i * count, count)
        return pltpu.make_async_copy(spec_hbm.at[where], spec_w.at[where], copied.at[i])

    return count, copy


def mix_kernel(
    place_ref, lines_ref, cos_ref, sin_ref, spec_hbm, after, modes, out_ref, mixed, spec_w, copied,
    *, owners, width,
):
    lines = MODES * MODES // owners
    count, copy = fetch_weights(spec_hbm, spec_w, copied)
    for i in range(copied.shape[0]):
        copy(i).start()

    def put(kx, value):
        modes[pl.ds(kx, lines, MODES), :] = value

    x_forward(lines_ref, cos_ref, sin_ref, put, owners, lines, width)
    lane = iota((count, 2 * width), 1)

    def mix(i, carry):
        copy(i).wait()
        base = pl.multiple_of(i * count, count)
        u = modes[pl.ds(base, count), :]
        u_turned = pltpu.roll(u, width, 1)
        both = interleave(jnp.where(lane < width, u, u_turned), jnp.where(lane < width, u_turned, u))
        both = jnp.concatenate([both] * 4, axis=1)
        own = iota(both.shape, 1) // width == iota(both.shape, 0) % 8
        high, low = halves(jnp.where(own, both, 0.0))
        products = []
        for batch in range(count // 8):
            rows = slice(batch * 16, (batch + 1) * 16)
            left = jnp.concatenate([high[rows], low[rows]], axis=0)
            products.append(dot(left, split_weights(spec_w, base + batch * 8, width)))
        outs = []
        for product in products:
            product = product[:, : 2 * width] + product[:, 2 * width :]
            product = product[:16] + product[16:]
            turned = pltpu.roll(product[8:], width, 1)
            outs.append(product[:8] + jnp.where(lane[:8] < width, -turned, turned))
        mixed[pl.ds(base, count), :] = jnp.concatenate(outs, axis=0)
        return carry

    lax.fori_loop(0, copied.shape[0], mix, 0)
    factor = factor_column(place_ref, lines)

    def take(kx):
        return mixed[pl.ds(kx, lines, MODES), :] * factor

    x_inverse(take, out_ref, owners, lines, width)


def mix_back_kernel(
    place_ref, lines_ref, cos_ref, sin_ref, spec_hbm, after, grads, out_ref, back, spec_w, copied,
    *, owners, width,
):
    lines = MODES * MODES // owners
    count, copy = fetch_weights(spec_hbm, spec_w, copied)
    for i in range(copied.shape[0]):
        copy(i).start()
    factor = factor_column(place_ref, lines)

    def put(kx, value):
        grads[pl.ds(kx, lines, MODES), :] = value * factor

    x_forward(lines_ref, cos_ref, sin_ref, put, owners, lines, width)
    lane = iota((count, 2 * width), 1)
    own = iota((16, 8 * width), 1) // width == iota((16, 8 * width), 0) % 8

    def mix(i, carry):
        copy(i).wait()
        base = pl.multiple_of(i * count, count)
        g = grads[pl.ds(base, count), :]
        g_turned = pltpu.roll(g, width, 1)
        high, low = halves(interleave(g, jnp.where(lane < width, g_turned, -g_turned)))
        products = []
        for batch in range(count // 8):
            rows = slice(batch * 16, (batch + 1) * 16)
            left = jnp.concatenate([high[rows], low[rows]], axis=0)
            left = jnp.concatenate([left, left], axis=1)
            products.append(dot(left, split_weights(spec_w, base + batch * 8, width), NT))
        outs = []
        for product in products:
            rows = jnp.where(own, product[:16] + product[16:], 0.0)
            while rows.shape[1] > 2 * width:
                half = rows.shape[1] // 2
                rows = rows[:, :half] + rows[:, half:]
            rows = rows + pltpu.roll(rows, width, 1)
            outs.append(jnp.where(lane[:8] < width, rows[:8], rows[8:]))
        back[pl.ds(base, count), :] = jnp.concatenate(outs, axis=0)
        return carry

    lax.fori_loop(0, copied.shape[0], mix, 0)

    def take(kx):
        return back[pl.ds(kx, lines, MODES), :]

    x_inverse(take, out_ref, owners, lines, width)


def spec_grad_kernel(rank_ref, *refs, shapes, width):
    mode_refs, grad_refs, (out, modes, grads) = refs[:shapes], refs[shapes : 2 * shapes], refs[-3:]
    for parts, held in ((mode_refs, modes), (grad_refs, grads)):
        for distance, part in enumerate(parts):
            held[rank_ref[0] ^ distance] = part[...]
    row = iota((8, 2 * width), 0)
    lane = iota((8, 2 * width), 1)
    own = iota((8, 4 * width), 1) // width == iota((8, 4 * width), 0) % 4
    lefts, rights = [], []
    for batch in range(out.shape[0] // 8):
        where = slice(batch * 8, (batch + 1) * 8)
        left, right = [], []
        for shape in range(shapes):
            u, g = modes[shape, where], grads[shape, where]
            u_turned, g_turned = pltpu.roll(u, width, 1), pltpu.roll(g, width, 1)
            for part in (jnp.where(lane < width, u, u_turned), jnp.where(lane < width, u_turned, u)):
                left.append(jnp.where(own, jnp.concatenate([part] * 2, axis=1), 0.0))
            for part in (g, jnp.where(lane < width, g_turned, -g_turned)):
                pair = [jnp.where(row < 4, part, 0.0), jnp.where(row < 4, 0.0, part)]
                right.append(jnp.concatenate(pair, axis=1))
        left_high, left_low = halves(jnp.concatenate(left, axis=0))
        right_high, right_low = halves(jnp.concatenate(right, axis=0))
        lefts.append(jnp.concatenate([left_high, left_low, left_high], axis=0))
        rights.append(jnp.concatenate([right_high, right_high, right_low], axis=0))
    products = [dot(left, right, TN) for left, right in zip(lefts, rights)]
    for batch, product in enumerate(products):
        out[batch * 8 : batch * 8 + 4] = product[:, : 2 * width].reshape(4, width, 2 * width)
        out[batch * 8 + 4 : batch * 8 + 8] = product[:, 2 * width :].reshape(4, width, 2 * width)


def cell_sums(total, rows_here, width):
    hidden_sums, weight_sums = [], []
    for row in range(rows_here):
        slab = total[row * PLANE : (row + 1) * PLANE]
        hidden_sums.append(slab[:, :width] + slab[:, width : 2 * width])
        weight = slab[:, 2 * width + 4 : 2 * width + 5] + slab[:, 2 * width + 12 : 2 * width + 13]
        weight_sums.append(jnp.broadcast_to(weight, (PLANE, width)))
    return jnp.concatenate(hidden_sums, axis=1), jnp.concatenate(weight_sums, axis=1)


def grid_kernel(lines_ref, reach, skip, proj_w, inverse_hbm, plane_hbm, *refs, rows_here):
    plane_out, pre_bar_out, latent_out, inverse, plane, copied = refs[-6:]
    copies = [
        pltpu.make_async_copy(inverse_hbm, inverse, copied.at[0]),
        pltpu.make_async_copy(plane_hbm, plane, copied.at[1]),
    ]
    for copy in copies:
        copy.start()
    copies[0].wait()
    latent, slope = gelu_both(times_field(inverse, lines_ref[...]) + skip[...])
    pre_bar = reach[...] * tile_lanes(proj_w[...], rows_here) * slope
    copies[1].wait()
    plane_out[...] = times_field(plane, pre_bar)
    pre_bar_out[...] = pre_bar
    latent_out[...] = latent


def grid_grads_kernel(
    lat, pre_bar, latent, reach, sums, skip_w, dec_w2, dec_b2, proj_w,
    skip_w_grad, dec_w2_grad, rows_out, table, skip_back, *, rows_here, width,
):
    skip_back[...] = dot3(pre_bar[...], spread(skip_w[...], rows_here), NT)
    skip_w_grad[...] = gather_blocks(dot3(lat[...], pre_bar[...], TN), rows_here, width, width)
    scaled = latent[...] * tile_lanes(proj_w[...], rows_here)
    dec_w2_grad[...] = gather_blocks(dot3(sums[0], scaled, TN), rows_here, width, width)

    def column_sum(value):
        return fold_lanes(jnp.sum(value, axis=0, keepdims=True), rows_here, width)

    rows = [column_sum(pre_bar[...]), column_sum(sums[1] * scaled), column_sum(reach[...] * latent[...])]
    rows_out[...] = jnp.concatenate(rows + [jnp.zeros((5, width), F32)], axis=0)
    cell_kernel = dot3(scaled, spread(dec_w2[...], rows_here), NT)
    offset = scaled * tile_lanes(dec_b2[...], rows_here)
    cells = rows_here * PLANE
    table[cells:] = jnp.zeros((PAD, table.shape[1]), BF16)
    for row in range(rows_here):
        lanes = slice(row * width, (row + 1) * width)
        where = slice(row * PLANE, (row + 1) * PLANE)
        constant = jnp.sum(offset[:, lanes], axis=1, keepdims=True)
        high, low = halves(cell_kernel[:, lanes])
        c_high, c_low = halves(constant)
        lane = iota((PLANE, LANES), 1)
        tail = jnp.where(lane == 0, c_high.astype(F32), jnp.where(lane == 1, c_low.astype(F32), 0.0))
        table[where, : 2 * width] = jnp.concatenate([high.astype(F32), low.astype(F32)], axis=1).astype(BF16)
        table[where, 2 * width :] = tail.astype(BF16)


def input_columns(feats, cell, first_row):
    high, low = halves(feats)
    place = place_rows(cell, first_row)
    return jnp.concatenate([high.astype(F32), low.astype(F32), place, place], axis=0).astype(BF16)


def dec_edges_kernel(
    place_ref, bounds, keys, inverse_degree, saved, table, pred_out, w1_out, b1_out,
    found_scratch, pred_total, grad_total, *, owners, cells, width,
):
    step = pl.program_id(0)
    rows_here = cells // PLANE
    group = found_scratch.shape[1] // CHUNK
    first_row = place_ref[0] * rows_here
    shift = log2(owners * LANES)
    count8 = max(owners, 8)

    @pl.when(step == 0)
    def _():
        pred_total[...] = jnp.zeros_like(pred_total)
        grad_total[...] = jnp.zeros_like(grad_total)

    chunk = step * group
    low_cell, _ = cell_range(bounds, 2, chunk, CHUNK // keys.shape[1])

    @pl.when(low_cell < cells)
    def _():
        rows, key = joined_keys(keys, chunk, group)
        gather_windows(
            found_scratch, keys, rows, table, bounds, 2, chunk, group, DEC_WINDOW, shift, 2 * width + 16
        )
        point = key & (owners * LANES - 1)
        found = found_scratch[:width] + found_scratch[width : 2 * width]
        constant = found_scratch[2 * width : 2 * width + 1] + found_scratch[2 * width + 1 : 2 * width + 2]
        edge = jnp.sum(saved[:width] * found, axis=0, keepdims=True) + constant
        owner = iota((count8, key.shape[1]), 0)
        high, low = halves(jnp.where(owner == (point >> 7), edge, 0.0))
        values = jnp.concatenate([high.astype(F32), low.astype(F32)], axis=0).astype(BF16)
        pred_total[...] += dot(values, one_hot(point & (LANES - 1), 0, LANES), NT)
        left = jnp.concatenate(halves(saved[width : 2 * width] * found), axis=0)
        right = input_columns(saved[2 * width :], key >> shift, first_row)
        grad_total[...] += dot(left, right, NT)

    @pl.when(step == pl.num_programs(0) - 1)
    def _():
        pred_out[...] = (pred_total[:owners] + pred_total[count8 : count8 + owners]) * inverse_degree[...]
        grad = grad_total[:width] + grad_total[width:]
        feats = (grad[:, :8] + grad[:, 8:16]).T
        places = grad[:, 16:24].T / (RES - 1.0)
        w1_out[...] = jnp.concatenate([feats[:3], places[:3]], axis=0)
        b1_out[...] = feats[3:4]


GRAD_ROWS = 108
PACKED_ROWS = 120


def enc_back_kernel(
    place_ref, bounds, keys, saved_hbm, lines_ref, skip_back, scale, w2, lift_w, pred_bar,
    skip_w_grad, dec_w2_grad, row_grads, pred_part, dec_w1_grad, dec_b1_grad, inverse_hbm,
    *refs, owners, cells, width,
):
    packed, table, found_scratch, second, feat_total, grad_total, inverse, copied, slots, loaded = refs[-10:]
    step = pl.program_id(0)
    rows_here = cells // PLANE
    group = found_scratch.shape[1] // CHUNK
    first_row = place_ref[0] * rows_here
    shift = log2(owners * LANES)
    count8 = max(owners, 8)
    per = CHUNK // keys.shape[1]
    load = slot_copies(saved_hbm, slots, loaded, out=False)
    steps = keys.shape[0] * keys.shape[1] // slots.shape[2]

    def load_used(at):
        @pl.when(at < steps)
        def _():
            first_cell, _ = cell_range(bounds, 0, jnp.minimum(at, steps - 1) * group, per)

            @pl.when(first_cell < cells)
            def _():
                load(at).start()

    @pl.when(step == 0)
    def _():
        copy = pltpu.make_async_copy(inverse_hbm, inverse, copied)
        copy.start()
        load_used(0)
        load_used(1)
        feat_total[...] = jnp.zeros_like(feat_total)
        grad_total[...] = jnp.zeros_like(grad_total)
        second[...] = weights3(w2[...])
        copy.wait()
        field = (times_field(inverse, lines_ref[...]) + skip_back[...]) * scale[...]
        table[cells:] = jnp.zeros((PAD, 2 * width), BF16)
        for row in range(rows_here):
            high, low = halves(field[:, row * width : (row + 1) * width])
            both = jnp.concatenate([high.astype(F32), low.astype(F32)], axis=1).astype(BF16)
            table[row * PLANE : (row + 1) * PLANE] = both

    chunk = step * group
    low_cell, _ = cell_range(bounds, 0, chunk, CHUNK // keys.shape[1])

    @pl.when(low_cell < cells)
    def _():
        lift_columns = jnp.concatenate([lift_w[...], jnp.zeros((4, width), F32)], axis=0).T
        rows, key = joined_keys(keys, chunk, group)
        gather_windows(
            found_scratch, keys, rows, table, bounds, 0, chunk, group, ENC_WINDOW, shift, 2 * width
        )
        load(step).wait()
        saved = slots.at[step % 2]
        point = key & (owners * LANES - 1)
        found = found_scratch[:width] + found_scratch[width:]
        source_bar = found * saved[3 * width : 4 * width]
        k_high, k_low = halves(found * saved[2 * width : 3 * width])
        hidden_bar = dot(second[...], jnp.concatenate([k_high, k_low, k_high], axis=0))
        pre_edge = hidden_bar * saved[width : 2 * width]
        parts = [*halves(saved[:width]), *halves(pre_edge), *halves(source_bar)]
        left = jnp.concatenate(parts + [jnp.ones((16, key.shape[1]), BF16)], axis=0)
        tail = input_columns(saved[4 * width :], key >> shift, first_row)
        grad_total[...] += dot(left, jnp.concatenate([k_high, k_low, tail], axis=0), NT)
        owner_hot = iota((count8, key.shape[1]), 0) == (point >> 7)
        edges = []
        for feat in range(4):
            edge = jnp.sum(source_bar * lift_columns[:, feat : feat + 1], axis=0, keepdims=True)
            edges.append(jnp.where(owner_hot, edge, 0.0))
        values = jnp.concatenate(halves(jnp.concatenate(edges, axis=0)), axis=0)
        feat_total[...] += dot(values, one_hot(point & (LANES - 1), 0, LANES), NT)
        load_used(step + 2)

    @pl.when(step == pl.num_programs(0) - 1)
    def _():
        w2_part = grad_total[:width, : 2 * width] + grad_total[width : 2 * width, : 2 * width]
        w2_grad = w2_part[:, :width] + w2_part[:, width:]
        b2_part = grad_total[6 * width : 6 * width + 1, : 2 * width]
        b2_grad = b2_part[:, :width] + b2_part[:, width:]
        pre_part = grad_total[2 * width : 3 * width, 2 * width :] + grad_total[3 * width : 4 * width, 2 * width :]
        feats = (pre_part[:, :8] + pre_part[:, 8:16]).T
        places = pre_part[:, 16:24].T / (RES - 1.0)
        lift_part = grad_total[4 * width : 5 * width, 2 * width :] + grad_total[5 * width : 6 * width, 2 * width :]
        lifts = (lift_part[:, :8] + lift_part[:, 8:16]).T
        pair = partial(jnp.concatenate, axis=1)
        stack = partial(jnp.concatenate, axis=0)
        half = width // 2
        bar_sum = jnp.broadcast_to(jnp.sum(pred_bar[...], axis=1, keepdims=True), (1, width))
        fixed = stack(
            [
                pair([w2_grad, dec_w2_grad[...]]),
                pair([skip_w_grad[:half], skip_w_grad[half:]]),
                pair([stack([places[:3], feats[:3]]), dec_w1_grad[...]]),
                pair([feats[3:4], dec_b1_grad[...]]),
                pair([b2_grad, row_grads[1:2]]),
                pair([lifts[4:8], stack([lifts[3:4], row_grads[0:1], row_grads[2:3], bar_sum])]),
            ]
        )
        both = feat_total[: 4 * count8] + feat_total[4 * count8 :]
        empty = jnp.zeros((PACKED_ROWS - GRAD_ROWS - 5, LANES), F32)
        for owner in range(owners):
            rows = [both[feat * count8 + owner : feat * count8 + owner + 1] for feat in range(4)]
            packed[owner] = stack([fixed] + rows + [pred_part[owner : owner + 1], empty])


def arrive_kernel(arrived, proj_b, after, grads, feat_grad, pred, *, owners):
    total = arrived[0]
    for owner in range(1, owners):
        total = total + arrived[owner]
    grads[...] = total[:GRAD_ROWS]
    feat_grad[...] = total[GRAD_ROWS : GRAD_ROWS + 4]
    pred[...] = total[GRAD_ROWS + 4 : GRAD_ROWS + 5] + proj_b[...]


def leave_kernel(*refs, shapes, width):
    half = width // 2
    terms = [ref[...] for ref in refs[:shapes]]
    while len(terms) > 1:
        terms = [terms[i] + terms[i + 1] for i in range(0, len(terms), 2)]
    left, right = terms[0][:, :width], terms[0][:, width:]
    outs = refs[shapes:]
    at = width + half
    enc_w1, enc_b1, enc_w2, enc_b2, lift_w, lift_b, skip_w, skip_b, dec_w1, dec_b1, dec_w2, dec_b2, proj_w, proj_b = outs
    enc_w2[...] = left[:width]
    dec_w2[...] = right[:width]
    skip_w[:half] = left[width:at]
    skip_w[half:] = right[width:at]
    enc_w1[...] = left[at : at + 6]
    dec_w1[...] = right[at : at + 6]
    enc_b1[...] = left[at + 6 : at + 7]
    dec_b1[...] = right[at + 6 : at + 7]
    enc_b2[...] = left[at + 7 : at + 8]
    dec_b2[...] = right[at + 7 : at + 8]
    lift_w[...] = left[at + 8 : at + 12]
    lift_b[...] = right[at + 8 : at + 9]
    skip_b[...] = right[at + 9 : at + 10]
    proj_w[...] = right[at + 10 : at + 11]
    proj_b[...] = right[at + 11 : at + 12, :1]


def shape(*dims, dtype=F32):
    return jax.ShapeDtypeStruct(dims, dtype)


def whole(array):
    zeros = (0,) * array.ndim
    return pl.BlockSpec(array.shape, lambda i: zeros, pipeline_mode=pl.Buffered(1))


HELD = VMEM
VMEM_BYTES = 65280 << 10
FAR = pl.BlockSpec(memory_space=pl.ANY)


def kernel_call(kernel, name, steps, operands, out_shape, out_specs, scratch=(), micros=10, **more):
    arrays = [array for array, _ in operands]
    specs = [whole(array) if spec is None else spec for array, spec in operands]
    return pl.pallas_call(
        kernel,
        grid=(steps,),
        in_specs=specs,
        out_specs=out_specs,
        out_shape=out_shape,
        scratch_shapes=list(scratch),
        compiler_params=pltpu.CompilerParams(vmem_limit_bytes=VMEM_BYTES),
        cost_estimate=pl.CostEstimate(flops=0, bytes_accessed=micros * 2_000_000, transcendentals=0),
        name=name,
        **more,
    )(*arrays)


def on_device(
    mesh_feat,
    mesh_pos,
    query_pos,
    enc_cell,
    enc_point,
    enc_count,
    dec_cell,
    dec_query,
    dec_count,
    enc_w1,
    enc_b1,
    enc_w2,
    enc_b2,
    lift_w,
    lift_b,
    spec_w,
    skip_w,
    skip_b,
    dec_w1,
    dec_b1,
    dec_w2,
    dec_b2,
    proj_w,
    proj_b,
    pred_bar,
):
    width = lift_w.shape[1]
    owners = lax.axis_size("wide")
    shapes = lax.axis_size("grid")
    rows_here = RES // owners
    cells = rows_here * PLANE
    modes_here = spec_w.shape[0]
    lines = modes_here // MODES
    enc_blocks, dec_blocks = enc_cell.shape[1], dec_cell.shape[1]
    enc_edges, dec_edges = enc_blocks * LANES, dec_blocks * LANES
    enc_span, dec_span = ENC_GROUP * CHUNK, DEC_GROUP * CHUNK
    lanes = rows_here * width
    place = lax.axis_index("wide").astype(jnp.int32).reshape(1)
    plane_np = plane_matrix(owners)
    plane = jnp.asarray(np.stack(halves_np(plane_np)))
    inverse = jnp.asarray(np.stack(halves_np(np.ascontiguousarray(plane_np.T))))
    cos_x, sin_x = (jnp.asarray(part) for part in x_tables(rows_here, width))
    rows = [value.reshape(1, -1) for value in (enc_b1, enc_b2, lift_b, skip_b, dec_b1, dec_b2, proj_w, proj_b)]
    enc_b1, enc_b2, lift_b, skip_b, dec_b1, dec_b2, proj_w, proj_b = rows
    sizes = dict(owners=owners, cells=cells, width=width)
    dma = pltpu.SemaphoreType.DMA

    def exchange(value):
        return lax.all_to_all(value, "wide", 0, 0, tiled=True)

    payload = kernel_call(
        partial(share_kernel, owners=owners),
        "share_points",
        1,
        [
            (value, None)
            for value in (
                mesh_feat, mesh_pos.transpose(1, 0, 2), query_pos.transpose(1, 0, 2), pred_bar, dec_query[0], dec_count
            )
        ],
        shape(owners, 2 * FEAT_ROWS + owners, LANES),
        HELD,
    )
    shared = exchange(payload)
    local = [enc_cell[0], enc_point[0], enc_count, dec_cell[0], dec_query[0], dec_count]
    enc_keys, dec_keys, bounds = kernel_call(
        partial(sort_kernel, owners=owners, cells=cells),
        "sort_edges",
        1,
        [(value, None) for value in local] + [(payload, FAR)],
        [
            shape(LANES, enc_blocks, dtype=jnp.int32),
            shape(LANES, dec_blocks, dtype=jnp.int32),
            shape(8, LANES, dtype=jnp.int32),
        ],
        [HELD] * 3,
    )

    fixed = owners * FEAT_ROWS
    saved_rows = 4 * width + FEAT_ROWS
    plane_scratch = pltpu.VMEM((2, 2 * MODES * MODES, PLANE), BF16)
    inverse_scratch = pltpu.VMEM((2, PLANE, 2 * MODES * MODES), BF16)
    saved, lat, scale, plane_lat = kernel_call(
        partial(enc_forward_kernel, **sizes),
        "encode",
        enc_edges // enc_span,
        [(place, SMEM), (bounds, SMEM), (enc_keys, HELD), (shared, HELD)]
        + [(value, None) for value in (enc_w1, enc_b1, enc_w2, enc_b2, lift_w, lift_b)]
        + [(plane, FAR)],
        [
            shape(saved_rows, enc_edges),
            shape(PLANE, lanes),
            shape(PLANE, lanes),
            shape(2 * MODES * MODES, lanes),
        ],
        [FAR, HELD, HELD, HELD],
        [
            pltpu.VMEM((cells + PAD, 2 * LANES), F32),
            pltpu.VMEM((2 * fixed, LANES), BF16),
            pltpu.VMEM((2 * width, INPUT_ROWS), BF16),
            pltpu.VMEM((width, 3 * width), BF16),
            pltpu.VMEM((2 * width + 16, enc_span), BF16),
            plane_scratch,
            dma,
            pltpu.VMEM((2, saved_rows, enc_span), F32),
            dma((2,)),
        ],
    )
    modes_lines = exchange(plane_lat.reshape(owners, 2 * lines, lanes))

    dec_rows = 2 * width + FEAT_ROWS
    dec_steps = dec_edges // dec_span
    half_steps = dec_steps // 2

    def dec_sums(first_step, steps, before, saved_before, after, more, out_shape, scratch, name):
        return kernel_call(
            partial(dec_sums_kernel, first_step=first_step, **sizes),
            name,
            steps,
            [
                (place, SMEM), (bounds, SMEM), (dec_keys, HELD), (shared, HELD), (dec_w1, None), (dec_b1, None),
                (before, HELD if first_step else FAR), (saved_before, FAR), (after, FAR),
            ]
            + more,
            [shape(dec_rows, dec_edges)] + out_shape,
            [pl.BlockSpec((dec_rows, dec_span), lambda i: (0, i + first_step))] + [HELD] * len(out_shape),
            scratch
            + [
                pltpu.VMEM((2 * fixed, LANES), BF16),
                pltpu.VMEM((width, INPUT_ROWS), BF16),
                pltpu.VMEM((2 * width + 16, dec_span), BF16),
            ],
            input_output_aliases={7: 0} if first_step else {},
        )

    dec_saved, dec_total, inverse_degree = dec_sums(
        0, half_steps, plane_lat, plane_lat, plane_lat, [],
        [shape(cells + PAD, 2 * LANES), shape(owners, LANES)], [], "decode_sums_a",
    )

    mix_step, grad_step = min(MIX_STEP, modes_here), min(GRAD_STEP, modes_here)

    def spec_block(step):
        return pl.BlockSpec((step, width, 2 * width), lambda i: (i, 0, 0))

    def mode_pass(kernel, lines_in, after, name):
        return kernel_call(
            partial(kernel, owners=owners, width=width),
            name,
            1,
            [(place, SMEM), (lines_in, HELD), (cos_x, None), (sin_x, None), (spec_w, FAR), (after, FAR)],
            [shape(modes_here, 2 * width), shape(owners, 2 * lines, lanes)],
            [HELD, HELD],
            [
                pltpu.VMEM((modes_here, 2 * width), F32),
                pltpu.VMEM((modes_here, width, 2 * width), F32),
                dma((modes_here // mix_step,)),
            ],
        )

    modes, back_lines = mode_pass(mix_kernel, modes_lines, inverse_degree, "mix_modes")
    def from_shapes(value):
        parts = [value]
        for step in range(1, shapes):
            parts.append(lax.ppermute(value, "grid", [(i, i ^ step) for i in range(shapes)]))
        return parts

    all_modes = from_shapes(modes)
    grid_lines = exchange(back_lines).reshape(2 * MODES * MODES, lanes)
    dec_saved, sums, reach, skip = dec_sums(
        half_steps, dec_steps - half_steps, dec_total, dec_saved, back_lines,
        [(lat, HELD)] + [(value, None) for value in (skip_w, skip_b, dec_w2, dec_b2)],
        [shape(2, PLANE, lanes), shape(PLANE, lanes), shape(PLANE, lanes)],
        [pltpu.VMEM((cells + PAD, 2 * LANES), F32)],
        "decode_sums_b",
    )

    plane_bar, pre_bar, latent = kernel_call(
        partial(grid_kernel, rows_here=rows_here),
        "grid_fields",
        1,
        [(grid_lines, HELD), (reach, HELD), (skip, HELD), (proj_w, None), (inverse, FAR), (plane, FAR)]
        + [(value, FAR) for value in all_modes[1:]],
        [shape(2 * MODES * MODES, lanes)] + [shape(PLANE, lanes)] * 2,
        [HELD] * 3,
        [inverse_scratch, plane_scratch, dma((2,))],
    )
    bar_lines = exchange(plane_bar.reshape(owners, 2 * lines, lanes))

    skip_w_grad, dec_w2_grad, row_grads, dec_table, skip_back = kernel_call(
        partial(grid_grads_kernel, rows_here=rows_here, width=width),
        "grid_grads",
        1,
        [(value, HELD) for value in (lat, pre_bar, latent, reach, sums)]
        + [(value, None) for value in (skip_w, dec_w2, dec_b2, proj_w)],
        [
            shape(width, width),
            shape(width, width),
            shape(8, width),
            shape(cells + PAD, 2 * LANES, dtype=BF16),
            shape(PLANE, lanes),
        ],
        [HELD] * 5,
    )

    mixed_bar, bar_back = mode_pass(mix_back_kernel, bar_lines, row_grads, "mix_back")
    bar_grid_lines = exchange(bar_back).reshape(2 * MODES * MODES, lanes)

    all_grads = from_shapes(mixed_bar)

    count8 = max(owners, 8)
    pred_part, dec_w1_grad, dec_b1_grad = kernel_call(
        partial(dec_edges_kernel, **sizes),
        "decode_edges",
        dec_steps,
        [
            (place, SMEM), (bounds, SMEM), (dec_keys, HELD), (inverse_degree, HELD),
            (dec_saved, pl.BlockSpec((dec_rows, dec_span), lambda i: (0, i))), (dec_table, HELD),
        ],
        [shape(owners, LANES), shape(6, width), shape(1, width)],
        [HELD] * 3,
        [
            pltpu.VMEM((2 * width + 16, dec_span), F32),
            pltpu.VMEM((2 * count8, LANES), F32),
            pltpu.VMEM((2 * width, 32), F32),
        ],
    )

    packed = kernel_call(
        partial(enc_back_kernel, **sizes),
        "encode_back",
        enc_edges // enc_span,
        [(place, SMEM), (bounds, SMEM), (enc_keys, HELD), (saved, FAR)]
        + [(value, HELD) for value in (bar_grid_lines, skip_back, scale)]
        + [(value, None) for value in (enc_w2, lift_w, pred_bar)]
        + [(value, HELD) for value in (skip_w_grad, dec_w2_grad, row_grads, pred_part, dec_w1_grad, dec_b1_grad)]
        + [(inverse, FAR)]
        + [(value, FAR) for value in all_grads[1:]],
        shape(owners, PACKED_ROWS, LANES),
        HELD,
        [
            pltpu.VMEM((cells + PAD, 2 * width), BF16),
            pltpu.VMEM((2 * width, enc_span), F32),
            pltpu.VMEM((width, 3 * width), BF16),
            pltpu.VMEM((8 * count8, LANES), F32),
            pltpu.VMEM((6 * width + 16, 2 * width + 32), F32),
            inverse_scratch,
            dma,
            pltpu.VMEM((2, saved_rows, enc_span), F32),
            dma((2,)),
        ],
    )
    arrived = exchange(packed)

    rank = lax.axis_index("grid").astype(jnp.int32).reshape(1)
    spec_grad = kernel_call(
        partial(spec_grad_kernel, shapes=shapes, width=width),
        "spec_grad",
        modes_here // grad_step,
        [(rank, SMEM)]
        + [
            (value, pl.BlockSpec((grad_step, 2 * width), lambda i: (i, 0)))
            for value in all_modes + all_grads
        ]
        + [(packed, FAR)],
        shape(modes_here, width, 2 * width),
        spec_block(grad_step),
        [pltpu.VMEM((shapes, grad_step, 2 * width), F32)] * 2,
    )

    grads, feat_grad, pred = kernel_call(
        partial(arrive_kernel, owners=owners),
        "arrive",
        1,
        [(arrived, HELD), (proj_b, None), (spec_grad, FAR)],
        [shape(GRAD_ROWS, LANES), shape(4, LANES), shape(1, LANES)],
        [HELD] * 3,
    )
    terms = from_shapes(grads)
    vector = shape(1, width)
    square = shape(width, width)
    first = shape(6, width)
    outs = kernel_call(
        partial(leave_kernel, shapes=shapes, width=width),
        "leave",
        1,
        [(term, HELD) for term in terms],
        [
            first, vector, square, vector, shape(4, width), vector,
            square, vector, first, vector, square, vector, vector, shape(1, 1),
        ],
        [HELD] * 14,
    )
    outs = [out.reshape(-1) if out.shape[0] == 1 else out for out in outs]
    return (pred, feat_grad[None], *outs[:6], spec_grad, *outs[6:])


def solution(mesh):
    placed = (
        P("grid", None, "wide"),
        P("grid", None, "wide"),
        P("grid", None, "wide"),
        P("grid", "wide", None),
        P("grid", "wide", None),
        P("grid", "wide"),
        P("grid", "wide", None),
        P("grid", "wide", None),
        P("grid", "wide"),
        P(),
        P(),
        P(),
        P(),
        P(),
        P(),
        P("wide", None, None),
        P(),
        P(),
        P(),
        P(),
        P(),
        P(),
        P(),
        P(),
        P("grid", "wide"),
    )
    return jax.shard_map(
        on_device,
        mesh=mesh,
        in_specs=placed,
        out_specs=(
            P("grid", "wide"),
            P("grid", None, "wide"),
            P(),
            P(),
            P(),
            P(),
            P(),
            P(),
            P("wide", None, None),
            P(),
            P(),
            P(),
            P(),
            P(),
            P(),
            P(),
            P(),
        ),
        check_vma=False,
    )
```

```python
from functools import partial
import math

import jax
import jax.numpy as jnp
import ml_dtypes
import numpy as np
from jax import lax
from jax.experimental import pallas as pl
from jax.experimental.pallas import tpu as pltpu
from jax.sharding import PartitionSpec as P

MODES = 16
RES = 32
PLANE = RES * RES
CHUNK = 256
LANES = 128
ENC_GROUP = 16
DEC_GROUP = 16
FORWARD_PARTS = 1
BACK_PARTS = 1
FEAT_ROWS = 8
INPUT_ROWS = 48
ENC_WINDOW = 64
DEC_WINDOW = 128
PAD = 256
MIX_STEP = 64
GRAD_STEP = 128
F32 = jnp.float32
BF16 = jnp.bfloat16
GELU_A = 0.7978845608028654
GELU_B = 0.044715

NN = (((1,), (0,)), ((), ()))
NT = (((1,), (1,)), ((), ()))
TN = (((0,), (0,)), ((), ()))

VMEM = pl.BlockSpec(memory_space=pltpu.VMEM)
SMEM = pl.BlockSpec(memory_space=pltpu.SMEM)


def kept_freqs():
    half = MODES // 2
    return np.concatenate([np.arange(half), np.arange(RES - half, RES)])


def plane_matrix(owners):
    lines = MODES * MODES // owners
    line = np.arange(MODES * MODES)
    freq_y, freq_z = kept_freqs()[line // MODES], line % MODES
    cell = np.arange(PLANE)
    turns = (freq_y[:, None] * (cell // RES) + freq_z[:, None] * (cell % RES)) % RES
    angle = turns * (2.0 * math.pi / RES)
    both = np.stack([np.cos(angle), -np.sin(angle)]).reshape(2, owners, lines, PLANE)
    matrix = both.transpose(1, 0, 2, 3).reshape(2 * MODES * MODES, PLANE)
    return matrix.astype(np.float32)


def halves_np(matrix):
    high = matrix.astype(ml_dtypes.bfloat16)
    low = (matrix - high.astype(np.float32)).astype(ml_dtypes.bfloat16)
    return high, low


def line_angles():
    turns = (kept_freqs()[:, None] * np.arange(RES)[None, :]) % RES
    return turns * (2.0 * math.pi / RES)


def x_tables(rows_here, width):
    angle = line_angles().reshape(MODES, RES // rows_here, rows_here, 1)
    angle = np.broadcast_to(angle, (MODES, RES // rows_here, rows_here, width))
    angle = angle.reshape(MODES, RES // rows_here, rows_here * width)
    return np.cos(angle).astype(np.float32), np.sin(angle).astype(np.float32)


def log2(number):
    return number.bit_length() - 1


def iota(shape, axis):
    return lax.broadcasted_iota(jnp.int32, shape, axis)


def halves(value):
    high = value.astype(BF16)
    low = (value - high.astype(F32)).astype(BF16)
    return high, low


def dot(a, b, dims=NN):
    return lax.dot_general(a, b, dims, preferred_element_type=F32)


def dot3(a, b, dims=NN):
    a_high, a_low = halves(a)
    b_high, b_low = halves(b)
    return dot(a_high, b_high, dims) + dot(a_low, b_high, dims) + dot(a_high, b_low, dims)


def one_hot(index, first, rows):
    places = iota((rows, index.shape[1]), 0)
    return jnp.where(places == index - first, 1.0, 0.0).astype(BF16)


def gelu_both(value):
    square = value * value
    half = 0.5 + 0.5 * jnp.tanh(value * (GELU_A + (GELU_A * GELU_B) * square))
    out = value * half
    return out, half + (out - out * half) * (2.0 * GELU_A + (6.0 * GELU_A * GELU_B) * square)


def sort_columns(values):
    rows = values.shape[0]
    regs = rows // 8
    low = log2(regs)
    total = low + 3 + 7
    sub = iota((8, LANES), 0)
    lane = iota((8, LANES), 1)
    x = values.reshape(regs, 8, LANES)

    def flip(x, bit):
        if bit >= total:
            return x
        if bit < low:
            y = x.reshape(regs >> (bit + 1), 2, 1 << bit, 8, LANES)
            return jnp.stack([y[:, 0], -y[:, 1]], axis=1).reshape(regs, 8, LANES)
        if bit < low + 3:
            sign = 1 - 2 * ((sub >> (bit - low)) & 1)
        else:
            sign = 1 - 2 * ((lane >> (bit - low - 3)) & 1)
        return x * sign.astype(F32)[None]

    def exchange(x, bit):
        if bit < low:
            y = x.reshape(regs >> (bit + 1), 2, 1 << bit, 8, LANES)
            one, two = y[:, 0], y[:, 1]
            pair = [jnp.minimum(one, two), jnp.maximum(one, two)]
            return jnp.stack(pair, axis=1).reshape(regs, 8, LANES)
        if bit < low + 3:
            axis, dist, size, place = 1, 1 << (bit - low), 8, sub
        else:
            axis, dist, size, place = 2, 1 << (bit - low - 3), LANES, lane
        after = pltpu.roll(x, size - dist, axis)
        before = after if 2 * dist == size else pltpu.roll(x, dist, axis)
        first = ((place & dist) == 0)[None]
        return jnp.where(first, jnp.minimum(x, after), jnp.maximum(x, before))

    for phase in range(1, total + 1):
        x = flip(x, phase)
        for bit in reversed(range(phase)):
            x = exchange(x, bit)
        x = flip(x, phase)
    return x.reshape(rows, LANES)


def layer_matrix(feat_rows, cell_rows):
    feat_high, feat_low = halves(feat_rows)
    cell_high, cell_low = halves(cell_rows)
    parts = [feat_high, feat_high, feat_low, cell_high, cell_low]
    parts = [part.astype(F32) for part in parts] + [jnp.zeros((LANES - 40, feat_rows.shape[1]), F32)]
    return jnp.concatenate(parts, axis=0).T[:, :INPUT_ROWS].astype(BF16)


def place_rows(cell, first_row):
    row = iota((8, cell.shape[1]), 0)
    shifts = jnp.where(row == 0, 2 * log2(RES), jnp.where(row == 1, log2(RES), 0))
    place = (cell >> shifts) & jnp.where(row < 3, RES - 1, 0)
    return (place + jnp.where(row == 0, first_row, 0)).astype(F32)


def edge_feats(key, table, owners):
    point = key & (owners * LANES - 1)
    found = dot(table, one_hot(point & (LANES - 1), 0, LANES))
    owner = (iota(found.shape, 0) >> 3) & (owners - 1)
    found = jnp.where(owner == (point >> 7), found, 0.0)
    return jnp.sum(found.reshape(2 * owners, FEAT_ROWS, key.shape[1]), axis=0)


def stack_inputs(feats, place):
    high, low = halves(feats)
    parts = [high.astype(F32), low.astype(F32), high.astype(F32), place, place, jnp.zeros_like(place)]
    return jnp.concatenate(parts, axis=0).astype(BF16)


def stack3(value):
    high, low = halves(value)
    return jnp.concatenate([high, low, high], axis=0)


def weights3(matrix):
    high, low = halves(matrix)
    return jnp.concatenate([high, high, low], axis=1)


def key_row(keys_ref, chunk):
    per = CHUNK // keys_ref.shape[1]
    rows = [keys_ref[pl.ds(chunk * per + i, 1), :] for i in range(per)]
    return rows[0] if per == 1 else jnp.concatenate(rows, axis=1)


def cell_range(bounds_ref, line, chunk, per):
    return bounds_ref[line, chunk * per], bounds_ref[line + 1, chunk * per + per - 1]


def spread(block, copies):
    rows, columns = block.shape
    tiled = jnp.concatenate([jnp.concatenate([block] * copies, axis=1)] * copies, axis=0)
    return jnp.where(
        iota(tiled.shape, 0) // rows == iota(tiled.shape, 1) // columns, tiled, 0.0
    )


def gather_blocks(product, copies, rows, columns):
    total = product[:rows, :columns]
    for i in range(1, copies):
        total = total + product[i * rows : (i + 1) * rows, i * columns : (i + 1) * columns]
    return total


def tile_lanes(row, copies):
    return row if copies == 1 else jnp.concatenate([row] * copies, axis=1)


def fold_lanes(row, copies, width):
    total = row[:, :width]
    for i in range(1, copies):
        total = total + row[:, i * width : (i + 1) * width]
    return total


def column(counts):
    return jnp.broadcast_to(counts, (8, counts.shape[1])).T[:, :1]


def share_kernel(feat, pos, query_pos, pred_bar, dec_query, dec_count, payload, *, owners):
    blocks = dec_query.shape[0]
    lane_valid = jnp.where(
        iota((blocks, LANES), 1) < column(dec_count[...]), dec_query[...], owners * LANES
    )
    ones = jnp.zeros((max(owners, 16), LANES), F32)
    degree = ones
    for block in range(0, blocks, 2):
        row = jnp.concatenate([lane_valid[block : block + 1], lane_valid[block + 1 : block + 2]], axis=1)
        high = one_hot(row >> 7, 0, ones.shape[0])
        low = one_hot(row & (LANES - 1), 0, LANES)
        degree = degree + dot(high, low, NT)
    filled = jnp.ones((1, LANES), F32)
    empty = jnp.zeros((3, LANES), F32)
    places = [pos[i] for i in range(3)]
    queries = [query_pos[i] for i in range(3)]
    rows = places + [filled, feat[0]] + queries + [filled, pred_bar[...], empty, degree[:owners]]
    mine = jnp.concatenate(rows, axis=0)
    for owner in range(owners):
        payload[owner] = mine


def sort_kernel(
    enc_cell, enc_point, enc_count, dec_cell, dec_query, dec_count, after,
    enc_keys, dec_keys, bounds, *, owners, cells,
):
    shift = log2(owners * LANES)

    def keys(cell, point, count):
        lane = iota(cell.shape, 1)
        key = jnp.where(lane < column(count), (cell << shift) | point, cells << shift)
        return sort_columns(key.astype(F32)).astype(jnp.int32)

    enc = keys(enc_cell[...], enc_point[...], enc_count[...])
    dec = keys(dec_cell[...], dec_query[...], dec_count[...])
    enc_keys[...] = enc.T
    dec_keys[...] = dec.T
    ends = [enc[:1], enc[-1:], dec[:1], dec[-1:]]
    bounds[...] = jnp.concatenate(ends + [jnp.zeros((4, LANES), jnp.int32)], axis=0) >> shift


def joined_keys(keys, chunk, group):
    rows = [key_row(keys, chunk + i) for i in range(group)]
    return rows, jnp.concatenate(rows, axis=1)


def later_windows(windows, size, visit):
    most = windows[0][1]
    for _, count in windows[1:]:
        most = jnp.maximum(most, count)

    @pl.when(most > 1)
    def _():
        for i, (begin, count) in enumerate(windows):

            def more(j, carry):
                visit(i, begin + j * size)
                return carry

            lax.fori_loop(1, count, more, 0)


def scatter_windows(total, keys, cell, message, bounds, line, chunk, group, size, shift, columns):
    per = CHUNK // keys.shape[1]
    windows, parts = [], []
    for i in range(group):
        begin, end = cell_range(bounds, line, chunk + i, per)
        begin = pl.multiple_of(begin & -8, 8)
        lanes = slice(i * CHUNK, (i + 1) * CHUNK)
        parts.append(dot(one_hot(cell[:, lanes], begin, size), message[:, lanes], NT))
        windows.append((begin, (end - begin) // size + 1))
    for (begin, _), part in zip(windows, parts):
        total[pl.ds(begin, size), :columns] += part

    def visit(i, start):
        start = pl.multiple_of(start, 8)
        hot = one_hot(key_row(keys, chunk + i) >> shift, start, size)
        part = dot(hot, message[:, i * CHUNK : (i + 1) * CHUNK], NT)
        total[pl.ds(start, size), :columns] += part

    later_windows(windows, size, visit)


def gather_windows(found, keys, rows, table, bounds, line, chunk, group, size, shift, columns):
    per = CHUNK // keys.shape[1]
    windows = []
    for i in range(group):
        begin, end = cell_range(bounds, line, chunk + i, per)
        begin = pl.multiple_of(begin & -16, 16)
        hot = one_hot(rows[i] >> shift, begin, size)
        found[:, i * CHUNK : (i + 1) * CHUNK] = dot(table[pl.ds(begin, size), :columns], hot, TN)
        windows.append((begin, (end - begin) // size + 1))

    def visit(i, start):
        start = pl.multiple_of(start, 16)
        hot = one_hot(key_row(keys, chunk + i) >> shift, start, size)
        part = dot(table[pl.ds(start, size), :columns], hot, TN)
        found[:, i * CHUNK : (i + 1) * CHUNK] += part

    later_windows(windows, size, visit)


def slot_copies(far, slots, semaphores, out):
    span = slots.shape[2]

    def copy(step):
        slot = step % 2
        columns = far.at[:, pl.ds(pl.multiple_of(step * span, span), span)]
        ends = (slots.at[slot], columns) if out else (columns, slots.at[slot])
        return pltpu.make_async_copy(*ends, semaphores.at[slot])

    return copy


def used_steps(bounds, line, group, per, cells, steps):
    used = 0
    for step in range(steps):
        used = used + jnp.where(bounds[line, step * group * per] < cells, 1, 0)
    return used


def enc_forward_kernel(
    place_ref, bounds, keys, shared, w1, b1, w2, b2, lift_w, lift_b, plane_hbm,
    saved_hbm, lat_far, scale_far, plane_out,
    total, table, first, second, message, plane, lat, scale, copied, slots, stored,
    *, owners, cells, width,
):
    step = pl.program_id(0)
    rows_here = cells // PLANE
    group = message.shape[1] // CHUNK
    shift = log2(owners * LANES)
    first_row = place_ref[0] * rows_here
    copy = pltpu.make_async_copy(plane_hbm, plane, copied.at[0])
    save = slot_copies(saved_hbm, slots, stored, out=True)

    @pl.when(step == 0)
    def _():
        copy.start()
        total[...] = jnp.zeros_like(total)
        feats = jnp.concatenate([shared[i, :FEAT_ROWS] for i in range(owners)], axis=0)
        table[...] = jnp.concatenate(halves(feats), axis=0)
        empty = jnp.zeros((3, width), F32)
        pre_rows = jnp.concatenate([w1[3:6], b1[...], jnp.zeros((4, width), F32)], axis=0)
        lift_rows = jnp.concatenate([empty, lift_b[...], lift_w[...]], axis=0)
        cell_rows = jnp.concatenate([w1[0:3] / (RES - 1.0), jnp.zeros((5, width), F32)], axis=0)
        first[...] = layer_matrix(
            jnp.concatenate([pre_rows, lift_rows], axis=1),
            jnp.concatenate([cell_rows, jnp.zeros((8, width), F32)], axis=1),
        )
        second[...] = weights3(w2[...].T)

    chunk = step * group
    low_cell, _ = cell_range(bounds, 0, chunk, CHUNK // keys.shape[1])

    @pl.when(low_cell < cells)
    def _():
        bias = jnp.broadcast_to(b2[...], (8, width)).T[:, :1]
        _, key = joined_keys(keys, chunk, group)
        cell = key >> shift

        @pl.when(step >= 2)
        def _():
            save(step - 2).wait()

        saved = slots.at[step % 2]
        part = key.shape[1] // FORWARD_PARTS
        for at in range(0, key.shape[1], part):
            run = slice(at, at + part)
            feats = edge_feats(key[:, run], table[...], owners)
            both = dot(first[...], stack_inputs(feats, place_rows(cell[:, run], first_row)))
            lifted = both[width:]
            hidden, slope = gelu_both(both[:width])
            kernel = dot(second[...], stack3(hidden)) + bias
            saved[0 * width : 1 * width, run] = hidden
            saved[1 * width : 2 * width, run] = slope
            saved[2 * width : 3 * width, run] = lifted
            saved[3 * width : 4 * width, run] = kernel
            saved[4 * width :, run] = feats
            high, low = halves(kernel * lifted)
            message[:, run] = jnp.concatenate([high, low, jnp.ones((16, part), BF16)], axis=0)
        save(step).start()
        scatter_windows(
            total, keys, cell, message, bounds, 0, chunk, group, ENC_WINDOW, shift, 2 * width + 16
        )

    @pl.when(step == pl.num_programs(0) - 1)
    def _():
        fields, scales = [], []
        for row in range(rows_here):
            slab = total[row * PLANE : (row + 1) * PLANE]
            inverse = 1.0 / jnp.maximum(slab[:, 2 * width : 2 * width + 1], 1.0)
            fields.append((slab[:, :width] + slab[:, width : 2 * width]) * inverse)
            scales.append(jnp.broadcast_to(inverse, (PLANE, width)))
        field = jnp.concatenate(fields, axis=1)
        lat[...] = field
        scale[...] = jnp.concatenate(scales, axis=1)
        leaving = [
            pltpu.make_async_copy(lat, lat_far, copied.at[1]),
            pltpu.make_async_copy(scale, scale_far, copied.at[2]),
        ]
        for out in leaving:
            out.start()
        copy.wait()
        plane_out[...] = times_field(plane, field)
        for out in leaving:
            out.wait()
        steps = keys.shape[0] * keys.shape[1] // slots.shape[2]
        used = used_steps(bounds, 0, group, CHUNK // keys.shape[1], cells, steps)

        @pl.when(used >= 2)
        def _():
            save(used - 2).wait()

        @pl.when(used >= 1)
        def _():
            save(used - 1).wait()


def times_field(matrix, field):
    high, low = halves(field)
    return dot(matrix[0], high) + dot(matrix[1], high) + dot(matrix[0], low)


def dec_sums_kernel(
    place_ref, bounds, keys, shared, w1, b1, before, saved_before, after, *refs,
    owners, cells, width, first_step,
):
    if first_step == 0:
        lat, skip_w, skip_b, saved, total, inverse_out, skip, table, first, message = refs
    else:
        dec_w2, dec_b2, saved, sums, reach, total, table, first, message = refs
    step = pl.program_id(0)
    rows_here = cells // PLANE
    group = message.shape[1] // CHUNK
    shift = log2(owners * LANES)
    first_row = place_ref[0] * rows_here

    @pl.when(step == 0)
    def _():
        total[...] = jnp.zeros_like(total) if first_step == 0 else before[...]
        degree = shared[0, 2 * FEAT_ROWS :]
        for i in range(1, owners):
            degree = degree + shared[i, 2 * FEAT_ROWS :]
        inverse = 1.0 / jnp.maximum(degree, 1.0)
        if first_step == 0:
            inverse_out[...] = inverse
        feats = []
        for i in range(owners):
            rows = shared[i, FEAT_ROWS : 2 * FEAT_ROWS]
            weighted = rows * inverse[i : i + 1]
            feats.append(jnp.where(iota(rows.shape, 0) == 4, weighted, rows))
        table[...] = jnp.concatenate(halves(jnp.concatenate(feats, axis=0)), axis=0)
        feat_rows = jnp.concatenate([w1[0:3], b1[...], jnp.zeros((4, width), F32)], axis=0)
        cell_rows = jnp.concatenate([w1[3:6] / (RES - 1.0), jnp.zeros((5, width), F32)], axis=0)
        first[...] = layer_matrix(feat_rows, cell_rows)

    chunk = (step + first_step) * group
    low_cell, _ = cell_range(bounds, 2, chunk, CHUNK // keys.shape[1])

    @pl.when(low_cell < cells)
    def _():
        _, key = joined_keys(keys, chunk, group)
        cell = key >> shift
        feats = edge_feats(key, table[...], owners)
        hidden, slope = gelu_both(dot(first[...], stack_inputs(feats, place_rows(cell, first_row))))
        weight = feats[4:5]
        saved[0 * width : 1 * width] = hidden
        saved[1 * width : 2 * width] = slope * weight
        saved[2 * width :] = feats
        high, low = halves(hidden * weight)
        w_high, w_low = halves(feats)
        tail = jnp.concatenate([w_high.astype(F32), w_low.astype(F32)], axis=0).astype(BF16)
        message[...] = jnp.concatenate([high, low, tail], axis=0)
        scatter_windows(
            total, keys, cell, message, bounds, 2, chunk, group, DEC_WINDOW, shift, 2 * width + 16
        )

    @pl.when(step == pl.num_programs(0) - 1)
    def _():
        if first_step == 0:
            skipped = dot3(lat[...], spread(skip_w[...], rows_here))
            skip[...] = skipped + tile_lanes(skip_b[...], rows_here)
            return
        sums[0], sums[1] = cell_sums(total, rows_here, width)
        reached = dot3(sums[0], spread(dec_w2[...], rows_here))
        reach[...] = reached + sums[1] * tile_lanes(dec_b2[...], rows_here)


def x_forward(lines_ref, cos_ref, sin_ref, put, owners, lines, width):
    lanes = lines_ref.shape[2]
    for kx in range(MODES):
        real = jnp.zeros((lines, lanes), F32)
        imag = jnp.zeros((lines, lanes), F32)
        for owner in range(owners):
            cos, sin = cos_ref[kx, owner : owner + 1], sin_ref[kx, owner : owner + 1]
            line_real, line_imag = lines_ref[owner, :lines], lines_ref[owner, lines:]
            real = real + cos * line_real + sin * line_imag
            imag = imag + cos * line_imag - sin * line_real
        if lanes == width:
            put(kx, jnp.concatenate([real, imag], axis=1))
        else:
            pair = 2 * width
            while real.shape[1] > pair:
                half = real.shape[1] // 2
                real, imag = real[:, :half] + real[:, half:], imag[:, :half] + imag[:, half:]
            real = real + pltpu.roll(real, width, 1)
            imag = imag + pltpu.roll(imag, width, 1)
            put(kx, jnp.where(iota(real.shape, 1) < width, real, imag))


def x_inverse(take, out_ref, owners, lines, width):
    angles = line_angles()
    rows_here = RES // owners
    modes = [take(kx) for kx in range(MODES)]
    lane = iota(modes[0].shape, 1)
    turned = [
        jnp.where(lane < width, -pltpu.roll(mode, width, 1), pltpu.roll(mode, width, 1))
        for mode in modes
    ]

    def at(x):
        total = None
        for kx in range(MODES):
            for value, factor in ((modes[kx], np.cos(angles[kx, x])), (turned[kx], np.sin(angles[kx, x]))):
                factor = float(np.float32(factor)) if abs(factor) > 1e-9 else 0.0
                if factor == 0.0:
                    continue
                term = value if factor == 1.0 else value * factor
                total = term if total is None else total + term
        return total

    for owner in range(owners):
        if rows_here == 1:
            here = at(owner)
            out_ref[owner, :lines] = here[:, :width]
            out_ref[owner, lines:] = here[:, width:]
            continue
        for pair in range(rows_here // 2):
            one, two = at(owner * rows_here + 2 * pair), at(owner * rows_here + 2 * pair + 1)
            one_turned, two_turned = pltpu.roll(one, width, 1), pltpu.roll(two, width, 1)
            where = slice(2 * pair * width, (2 * pair + 2) * width)
            out_ref[owner, :lines, where] = jnp.where(lane < width, one, two_turned)
            out_ref[owner, lines:, where] = jnp.where(lane < width, one_turned, two)


def factor_column(place_ref, lines):
    line = place_ref[0] * lines + iota((lines, 1), 0)
    return jnp.where((line & (MODES - 1)) == 0, 1.0, 2.0) / float(RES**3)


def split_weights(spec_w, base, width):
    block = spec_w[pl.ds(base, 8)].reshape(8 * width, 2 * width)
    return jnp.concatenate(halves(block), axis=1)


def interleave(one, two):
    parts = []
    for at in range(0, one.shape[0], 8):
        parts += [one[at : at + 8], two[at : at + 8]]
    return jnp.concatenate(parts, axis=0)


def fetch_weights(spec_hbm, spec_w, copied):
    count = spec_w.shape[0] // copied.shape[0]

    def copy(i):
        where = pl.ds(i * count, count)
        return pltpu.make_async_copy(spec_hbm.at[where], spec_w.at[where], copied.at[i])

    return count, copy


def mix_kernel(
    place_ref, lines_ref, cos_ref, sin_ref, spec_hbm, *refs, owners, width,
):
    modes, out_ref, mixed, spec_w, copied = refs[-5:]
    lines = MODES * MODES // owners
    count, copy = fetch_weights(spec_hbm, spec_w, copied)
    for i in range(copied.shape[0]):
        copy(i).start()

    def put(kx, value):
        modes[pl.ds(kx, lines, MODES), :] = value

    x_forward(lines_ref, cos_ref, sin_ref, put, owners, lines, width)
    lane = iota((count, 2 * width), 1)

    def mix(i, carry):
        copy(i).wait()
        base = pl.multiple_of(i * count, count)
        u = modes[pl.ds(base, count), :]
        u_turned = pltpu.roll(u, width, 1)
        both = interleave(jnp.where(lane < width, u, u_turned), jnp.where(lane < width, u_turned, u))
        both = jnp.concatenate([both] * 4, axis=1)
        own = iota(both.shape, 1) // width == iota(both.shape, 0) % 8
        high, low = halves(jnp.where(own, both, 0.0))
        products = []
        for batch in range(count // 8):
            rows = slice(batch * 16, (batch + 1) * 16)
            left = jnp.concatenate([high[rows], low[rows]], axis=0)
            products.append(dot(left, split_weights(spec_w, base + batch * 8, width)))
        outs = []
        for product in products:
            product = product[:, : 2 * width] + product[:, 2 * width :]
            product = product[:16] + product[16:]
            turned = pltpu.roll(product[8:], width, 1)
            outs.append(product[:8] + jnp.where(lane[:8] < width, -turned, turned))
        mixed[pl.ds(base, count), :] = jnp.concatenate(outs, axis=0)
        return carry

    lax.fori_loop(0, copied.shape[0], mix, 0)
    factor = factor_column(place_ref, lines)

    def take(kx):
        return mixed[pl.ds(kx, lines, MODES), :] * factor

    x_inverse(take, out_ref, owners, lines, width)


def mix_back_kernel(
    place_ref, lines_ref, cos_ref, sin_ref, spec_hbm, *refs, owners, width,
):
    grads, out_ref, back, spec_w, copied = refs[-5:]
    lines = MODES * MODES // owners
    count, copy = fetch_weights(spec_hbm, spec_w, copied)
    for i in range(copied.shape[0]):
        copy(i).start()
    factor = factor_column(place_ref, lines)

    def put(kx, value):
        grads[pl.ds(kx, lines, MODES), :] = value * factor

    x_forward(lines_ref, cos_ref, sin_ref, put, owners, lines, width)
    lane = iota((count, 2 * width), 1)
    own = iota((16, 8 * width), 1) // width == iota((16, 8 * width), 0) % 8

    def mix(i, carry):
        copy(i).wait()
        base = pl.multiple_of(i * count, count)
        g = grads[pl.ds(base, count), :]
        g_turned = pltpu.roll(g, width, 1)
        high, low = halves(interleave(g, jnp.where(lane < width, g_turned, -g_turned)))
        products = []
        for batch in range(count // 8):
            rows = slice(batch * 16, (batch + 1) * 16)
            left = jnp.concatenate([high[rows], low[rows]], axis=0)
            left = jnp.concatenate([left, left], axis=1)
            products.append(dot(left, split_weights(spec_w, base + batch * 8, width), NT))
        outs = []
        for product in products:
            rows = jnp.where(own, product[:16] + product[16:], 0.0)
            while rows.shape[1] > 2 * width:
                half = rows.shape[1] // 2
                rows = rows[:, :half] + rows[:, half:]
            rows = rows + pltpu.roll(rows, width, 1)
            outs.append(jnp.where(lane[:8] < width, rows[:8], rows[8:]))
        back[pl.ds(base, count), :] = jnp.concatenate(outs, axis=0)
        return carry

    lax.fori_loop(0, copied.shape[0], mix, 0)

    def take(kx):
        return back[pl.ds(kx, lines, MODES), :]

    x_inverse(take, out_ref, owners, lines, width)


def spec_grad_kernel(rank_ref, *refs, shapes, width):
    mode_refs, grad_refs, (out, modes, grads) = refs[:shapes], refs[shapes : 2 * shapes], refs[-3:]
    for parts, held in ((mode_refs, modes), (grad_refs, grads)):
        for distance, part in enumerate(parts):
            held[rank_ref[0] ^ distance] = part[...]
    row = iota((8, 2 * width), 0)
    lane = iota((8, 2 * width), 1)
    own = iota((8, 4 * width), 1) // width == iota((8, 4 * width), 0) % 4
    lefts, rights = [], []
    for batch in range(out.shape[0] // 8):
        where = slice(batch * 8, (batch + 1) * 8)
        left, right = [], []
        for shape in range(shapes):
            u, g = modes[shape, where], grads[shape, where]
            u_turned, g_turned = pltpu.roll(u, width, 1), pltpu.roll(g, width, 1)
            for part in (jnp.where(lane < width, u, u_turned), jnp.where(lane < width, u_turned, u)):
                left.append(jnp.where(own, jnp.concatenate([part] * 2, axis=1), 0.0))
            for part in (g, jnp.where(lane < width, g_turned, -g_turned)):
                pair = [jnp.where(row < 4, part, 0.0), jnp.where(row < 4, 0.0, part)]
                right.append(jnp.concatenate(pair, axis=1))
        left_high, left_low = halves(jnp.concatenate(left, axis=0))
        right_high, right_low = halves(jnp.concatenate(right, axis=0))
        lefts.append(jnp.concatenate([left_high, left_low, left_high], axis=0))
        rights.append(jnp.concatenate([right_high, right_high, right_low], axis=0))
    products = [dot(left, right, TN) for left, right in zip(lefts, rights)]
    for batch, product in enumerate(products):
        out[batch * 8 : batch * 8 + 4] = product[:, : 2 * width].reshape(4, width, 2 * width)
        out[batch * 8 + 4 : batch * 8 + 8] = product[:, 2 * width :].reshape(4, width, 2 * width)


def cell_sums(total, rows_here, width):
    hidden_sums, weight_sums = [], []
    for row in range(rows_here):
        slab = total[row * PLANE : (row + 1) * PLANE]
        hidden_sums.append(slab[:, :width] + slab[:, width : 2 * width])
        weight = slab[:, 2 * width + 4 : 2 * width + 5] + slab[:, 2 * width + 12 : 2 * width + 13]
        weight_sums.append(jnp.broadcast_to(weight, (PLANE, width)))
    return jnp.concatenate(hidden_sums, axis=1), jnp.concatenate(weight_sums, axis=1)


def grid_kernel(
    lines_far, reach_far, skip_far, proj_w, inverse_far, plane_far, after, plane_out, pre_bar_far, latent_far,
    lines, inverse, skip, reach, plane, latent, pre_bar, copied, *, rows_here,
):
    ends = [
        (lines_far, lines),
        (inverse_far, inverse),
        (skip_far, skip),
        (reach_far, reach),
        (plane_far, plane),
        (latent, latent_far),
        (pre_bar, pre_bar_far),
    ]
    copies = [pltpu.make_async_copy(*pair, copied.at[i]) for i, pair in enumerate(ends)]
    for copy in copies[:5]:
        copy.start()
    copies[0].wait()
    copies[1].wait()
    spectral = times_field(inverse, lines[...])
    copies[2].wait()
    value, slope = gelu_both(spectral + skip[...])
    latent[...] = value
    copies[5].start()
    copies[3].wait()
    bar = reach[...] * tile_lanes(proj_w[...], rows_here) * slope
    pre_bar[...] = bar
    copies[6].start()
    copies[4].wait()
    plane_out[...] = times_field(plane, bar)
    copies[5].wait()
    copies[6].wait()


def grid_grads_kernel(
    lat, pre_bar, latent, reach, sums, skip_w, dec_w2, dec_b2, proj_w,
    skip_w_grad, dec_w2_grad, rows_out, table, skip_back, *, rows_here, width,
):
    skip_back[...] = dot3(pre_bar[...], spread(skip_w[...], rows_here), NT)
    skip_w_grad[...] = gather_blocks(dot3(lat[...], pre_bar[...], TN), rows_here, width, width)
    scaled = latent[...] * tile_lanes(proj_w[...], rows_here)
    dec_w2_grad[...] = gather_blocks(dot3(sums[0], scaled, TN), rows_here, width, width)

    def column_sum(value):
        return fold_lanes(jnp.sum(value, axis=0, keepdims=True), rows_here, width)

    rows = [column_sum(pre_bar[...]), column_sum(sums[1] * scaled), column_sum(reach[...] * latent[...])]
    rows_out[...] = jnp.concatenate(rows + [jnp.zeros((5, width), F32)], axis=0)
    cell_kernel = dot3(scaled, spread(dec_w2[...], rows_here), NT)
    offset = scaled * tile_lanes(dec_b2[...], rows_here)
    cells = rows_here * PLANE
    table[cells:] = jnp.zeros((PAD, table.shape[1]), BF16)
    for row in range(rows_here):
        lanes = slice(row * width, (row + 1) * width)
        where = slice(row * PLANE, (row + 1) * PLANE)
        constant = jnp.sum(offset[:, lanes], axis=1, keepdims=True)
        high, low = halves(cell_kernel[:, lanes])
        c_high, c_low = halves(constant)
        lane = iota((PLANE, LANES), 1)
        tail = jnp.where(lane == 0, c_high.astype(F32), jnp.where(lane == 1, c_low.astype(F32), 0.0))
        table[where, : 2 * width] = jnp.concatenate([high.astype(F32), low.astype(F32)], axis=1).astype(BF16)
        table[where, 2 * width :] = tail.astype(BF16)


def input_columns(feats, cell, first_row):
    high, low = halves(feats)
    place = place_rows(cell, first_row)
    return jnp.concatenate([high.astype(F32), low.astype(F32), place, place], axis=0).astype(BF16)


def dec_edges_kernel(
    place_ref, bounds, keys, inverse_degree, saved, table, pred_out, w1_out, b1_out,
    found_scratch, pred_total, grad_total, *, owners, cells, width,
):
    step = pl.program_id(0)
    rows_here = cells // PLANE
    group = found_scratch.shape[1] // CHUNK
    first_row = place_ref[0] * rows_here
    shift = log2(owners * LANES)
    count8 = max(owners, 8)

    @pl.when(step == 0)
    def _():
        pred_total[...] = jnp.zeros_like(pred_total)
        grad_total[...] = jnp.zeros_like(grad_total)

    chunk = step * group
    low_cell, _ = cell_range(bounds, 2, chunk, CHUNK // keys.shape[1])

    @pl.when(low_cell < cells)
    def _():
        rows, key = joined_keys(keys, chunk, group)
        gather_windows(
            found_scratch, keys, rows, table, bounds, 2, chunk, group, DEC_WINDOW, shift, 2 * width + 16
        )
        point = key & (owners * LANES - 1)
        found = found_scratch[:width] + found_scratch[width : 2 * width]
        constant = found_scratch[2 * width : 2 * width + 1] + found_scratch[2 * width + 1 : 2 * width + 2]
        edge = jnp.sum(saved[:width] * found, axis=0, keepdims=True) + constant
        owner = iota((count8, key.shape[1]), 0)
        high, low = halves(jnp.where(owner == (point >> 7), edge, 0.0))
        values = jnp.concatenate([high.astype(F32), low.astype(F32)], axis=0).astype(BF16)
        pred_total[...] += dot(values, one_hot(point & (LANES - 1), 0, LANES), NT)
        left = jnp.concatenate(halves(saved[width : 2 * width] * found), axis=0)
        right = input_columns(saved[2 * width :], key >> shift, first_row)
        grad_total[...] += dot(left, right, NT)

    @pl.when(step == pl.num_programs(0) - 1)
    def _():
        pred_out[...] = (pred_total[:owners] + pred_total[count8 : count8 + owners]) * inverse_degree[...]
        grad = grad_total[:width] + grad_total[width:]
        feats = (grad[:, :8] + grad[:, 8:16]).T
        places = grad[:, 16:24].T / (RES - 1.0)
        w1_out[...] = jnp.concatenate([feats[:3], places[:3]], axis=0)
        b1_out[...] = feats[3:4]


GRAD_ROWS = 108
PACKED_ROWS = 120


def enc_back_kernel(
    place_ref, bounds, keys, saved_hbm, lines_far, skip_far, scale_far, w2, lift_w, pred_bar,
    skip_w_grad, dec_w2_grad, row_grads, pred_part, dec_w1_grad, dec_b1_grad, inverse_hbm,
    *refs, owners, cells, width,
):
    packed, table, found_scratch, second, lifts, feat_total, grad_total, inverse, lines, skip, scale, copied, slots, loaded = refs[-14:]
    step = pl.program_id(0)
    rows_here = cells // PLANE
    group = found_scratch.shape[1] // CHUNK
    first_row = place_ref[0] * rows_here
    shift = log2(owners * LANES)
    count8 = max(owners, 8)
    per = CHUNK // keys.shape[1]
    load = slot_copies(saved_hbm, slots, loaded, out=False)
    steps = keys.shape[0] * keys.shape[1] // slots.shape[2]

    def load_used(at):
        @pl.when(at < steps)
        def _():
            first_cell, _ = cell_range(bounds, 0, jnp.minimum(at, steps - 1) * group, per)

            @pl.when(first_cell < cells)
            def _():
                load(at).start()

    @pl.when(step == 0)
    def _():
        ends = [(lines_far, lines), (inverse_hbm, inverse), (skip_far, skip), (scale_far, scale)]
        copies = [pltpu.make_async_copy(*pair, copied.at[i]) for i, pair in enumerate(ends)]
        for copy in copies:
            copy.start()
        feat_total[...] = jnp.zeros_like(feat_total)
        grad_total[...] = jnp.zeros_like(grad_total)
        second[...] = weights3(w2[...])
        high, low = halves(jnp.concatenate([lift_w[...], jnp.zeros((4, width), F32)], axis=0))
        rows = jnp.concatenate([high.astype(F32), low.astype(F32)], axis=0)
        lifts[...] = jnp.concatenate([rows, rows], axis=1).astype(BF16)
        copies[0].wait()
        copies[1].wait()
        load_used(0)
        field = times_field(inverse, lines[...])
        copies[2].wait()
        copies[3].wait()
        field = (field + skip[...]) * scale[...]
        table[cells:] = jnp.zeros((PAD, 2 * width), BF16)
        for row in range(rows_here):
            high, low = halves(field[:, row * width : (row + 1) * width])
            both = jnp.concatenate([high.astype(F32), low.astype(F32)], axis=1).astype(BF16)
            table[row * PLANE : (row + 1) * PLANE] = both
        load_used(1)

    chunk = step * group
    low_cell, _ = cell_range(bounds, 0, chunk, CHUNK // keys.shape[1])

    @pl.when(low_cell < cells)
    def _():
        rows, key = joined_keys(keys, chunk, group)
        gather_windows(
            found_scratch, keys, rows, table, bounds, 0, chunk, group, ENC_WINDOW, shift, 2 * width
        )
        load(step).wait()
        saved = slots.at[step % 2]
        part = key.shape[1] // BACK_PARTS
        for at in range(0, key.shape[1], part):
            run = slice(at, at + part)
            key_run = key[:, run]
            point = key_run & (owners * LANES - 1)
            found = found_scratch[:width, run] + found_scratch[width:, run]
            source_bar = found * saved[3 * width : 4 * width, run]
            k_high, k_low = halves(found * saved[2 * width : 3 * width, run])
            hidden_bar = dot(second[...], jnp.concatenate([k_high, k_low, k_high], axis=0))
            pre_edge = hidden_bar * saved[width : 2 * width, run]
            source_parts = halves(source_bar)
            parts = [*halves(saved[:width, run]), *halves(pre_edge), *source_parts]
            left = jnp.concatenate(parts + [jnp.ones((16, part), BF16)], axis=0)
            tail = input_columns(saved[4 * width :, run], key_run >> shift, first_row)
            grad_total[...] += dot(left, jnp.concatenate([k_high, k_low, tail], axis=0), NT)
            owner_hot = iota((count8, part), 0) == (point >> 7)
            both = dot(lifts[...], jnp.concatenate(source_parts, axis=0))
            both = both[:8] + both[8:]
            edges = [jnp.where(owner_hot, both[feat : feat + 1], 0.0) for feat in range(4)]
            values = jnp.concatenate(halves(jnp.concatenate(edges, axis=0)), axis=0)
            feat_total[...] += dot(values, one_hot(point & (LANES - 1), 0, LANES), NT)
        load_used(step + 2)

    @pl.when(step == pl.num_programs(0) - 1)
    def _():
        w2_part = grad_total[:width, : 2 * width] + grad_total[width : 2 * width, : 2 * width]
        w2_grad = w2_part[:, :width] + w2_part[:, width:]
        b2_part = grad_total[6 * width : 6 * width + 1, : 2 * width]
        b2_grad = b2_part[:, :width] + b2_part[:, width:]
        pre_part = grad_total[2 * width : 3 * width, 2 * width :] + grad_total[3 * width : 4 * width, 2 * width :]
        feats = (pre_part[:, :8] + pre_part[:, 8:16]).T
        places = pre_part[:, 16:24].T / (RES - 1.0)
        lift_part = grad_total[4 * width : 5 * width, 2 * width :] + grad_total[5 * width : 6 * width, 2 * width :]
        lifts = (lift_part[:, :8] + lift_part[:, 8:16]).T
        pair = partial(jnp.concatenate, axis=1)
        stack = partial(jnp.concatenate, axis=0)
        half = width // 2
        bar_sum = jnp.broadcast_to(jnp.sum(pred_bar[...], axis=1, keepdims=True), (1, width))
        fixed = stack(
            [
                pair([w2_grad, dec_w2_grad[...]]),
                pair([skip_w_grad[:half], skip_w_grad[half:]]),
                pair([stack([places[:3], feats[:3]]), dec_w1_grad[...]]),
                pair([feats[3:4], dec_b1_grad[...]]),
                pair([b2_grad, row_grads[1:2]]),
                pair([lifts[4:8], stack([lifts[3:4], row_grads[0:1], row_grads[2:3], bar_sum])]),
            ]
        )
        both = feat_total[: 4 * count8] + feat_total[4 * count8 :]
        empty = jnp.zeros((PACKED_ROWS - GRAD_ROWS - 5, LANES), F32)
        for owner in range(owners):
            rows = [both[feat * count8 + owner : feat * count8 + owner + 1] for feat in range(4)]
            packed[owner] = stack([fixed] + rows + [pred_part[owner : owner + 1], empty])


def arrive_kernel(arrived, proj_b, after, grads, feat_grad, pred, *, owners):
    total = arrived[0]
    for owner in range(1, owners):
        total = total + arrived[owner]
    grads[...] = total[:GRAD_ROWS]
    feat_grad[...] = total[GRAD_ROWS : GRAD_ROWS + 4]
    pred[...] = total[GRAD_ROWS + 4 : GRAD_ROWS + 5] + proj_b[...]


def leave_kernel(*refs, shapes, width):
    half = width // 2
    terms = [ref[...] for ref in refs[:shapes]]
    while len(terms) > 1:
        terms = [terms[i] + terms[i + 1] for i in range(0, len(terms), 2)]
    left, right = terms[0][:, :width], terms[0][:, width:]
    outs = refs[shapes:]
    at = width + half
    enc_w1, enc_b1, enc_w2, enc_b2, lift_w, lift_b, skip_w, skip_b, dec_w1, dec_b1, dec_w2, dec_b2, proj_w, proj_b = outs
    enc_w2[...] = left[:width]
    dec_w2[...] = right[:width]
    skip_w[:half] = left[width:at]
    skip_w[half:] = right[width:at]
    enc_w1[...] = left[at : at + 6]
    dec_w1[...] = right[at : at + 6]
    enc_b1[...] = left[at + 6 : at + 7]
    dec_b1[...] = right[at + 6 : at + 7]
    enc_b2[...] = left[at + 7 : at + 8]
    dec_b2[...] = right[at + 7 : at + 8]
    lift_w[...] = left[at + 8 : at + 12]
    lift_b[...] = right[at + 8 : at + 9]
    skip_b[...] = right[at + 9 : at + 10]
    proj_w[...] = right[at + 10 : at + 11]
    proj_b[...] = right[at + 11 : at + 12, :1]


def shape(*dims, dtype=F32):
    return jax.ShapeDtypeStruct(dims, dtype)


def whole(array):
    zeros = (0,) * array.ndim
    return pl.BlockSpec(array.shape, lambda i: zeros, pipeline_mode=pl.Buffered(1))


HELD = VMEM
VMEM_BYTES = 65280 << 10
FAR = pl.BlockSpec(memory_space=pl.ANY)


def kernel_call(kernel, name, steps, operands, out_shape, out_specs, scratch=(), micros=10, **more):
    arrays = [array for array, _ in operands]
    specs = [whole(array) if spec is None else spec for array, spec in operands]
    return pl.pallas_call(
        kernel,
        grid=(steps,),
        in_specs=specs,
        out_specs=out_specs,
        out_shape=out_shape,
        scratch_shapes=list(scratch),
        compiler_params=pltpu.CompilerParams(vmem_limit_bytes=VMEM_BYTES),
        cost_estimate=pl.CostEstimate(flops=0, bytes_accessed=micros * 2_000_000, transcendentals=0),
        name=name,
        **more,
    )(*arrays)


def on_device(
    mesh_feat,
    mesh_pos,
    query_pos,
    enc_cell,
    enc_point,
    enc_count,
    dec_cell,
    dec_query,
    dec_count,
    enc_w1,
    enc_b1,
    enc_w2,
    enc_b2,
    lift_w,
    lift_b,
    spec_w,
    skip_w,
    skip_b,
    dec_w1,
    dec_b1,
    dec_w2,
    dec_b2,
    proj_w,
    proj_b,
    pred_bar,
):
    width = lift_w.shape[1]
    owners = lax.axis_size("wide")
    shapes = lax.axis_size("grid")
    rows_here = RES // owners
    cells = rows_here * PLANE
    modes_here = spec_w.shape[0]
    lines = modes_here // MODES
    enc_blocks, dec_blocks = enc_cell.shape[1], dec_cell.shape[1]
    enc_edges, dec_edges = enc_blocks * LANES, dec_blocks * LANES
    enc_span, dec_span = ENC_GROUP * CHUNK, DEC_GROUP * CHUNK
    lanes = rows_here * width
    place = lax.axis_index("wide").astype(jnp.int32).reshape(1)
    plane_np = plane_matrix(owners)
    plane = jnp.asarray(np.stack(halves_np(plane_np)))
    inverse = jnp.asarray(np.stack(halves_np(np.ascontiguousarray(plane_np.T))))
    cos_x, sin_x = (jnp.asarray(part) for part in x_tables(rows_here, width))
    rows = [value.reshape(1, -1) for value in (enc_b1, enc_b2, lift_b, skip_b, dec_b1, dec_b2, proj_w, proj_b)]
    enc_b1, enc_b2, lift_b, skip_b, dec_b1, dec_b2, proj_w, proj_b = rows
    sizes = dict(owners=owners, cells=cells, width=width)
    dma = pltpu.SemaphoreType.DMA

    def exchange(value):
        return lax.all_to_all(value, "wide", 0, 0, tiled=True)

    payload = kernel_call(
        partial(share_kernel, owners=owners),
        "share_points",
        1,
        [
            (value, None)
            for value in (
                mesh_feat, mesh_pos.transpose(1, 0, 2), query_pos.transpose(1, 0, 2), pred_bar, dec_query[0], dec_count
            )
        ],
        shape(owners, 2 * FEAT_ROWS + owners, LANES),
        HELD,
    )
    shared = exchange(payload)
    local = [enc_cell[0], enc_point[0], enc_count, dec_cell[0], dec_query[0], dec_count]
    enc_keys, dec_keys, bounds = kernel_call(
        partial(sort_kernel, owners=owners, cells=cells),
        "sort_edges",
        1,
        [(value, None) for value in local] + [(payload, FAR)],
        [
            shape(LANES, enc_blocks, dtype=jnp.int32),
            shape(LANES, dec_blocks, dtype=jnp.int32),
            shape(8, LANES, dtype=jnp.int32),
        ],
        [HELD] * 3,
    )

    fixed = owners * FEAT_ROWS
    saved_rows = 4 * width + FEAT_ROWS
    plane_scratch = pltpu.VMEM((2, 2 * MODES * MODES, PLANE), BF16)
    inverse_scratch = pltpu.VMEM((2, PLANE, 2 * MODES * MODES), BF16)
    saved, lat, scale, plane_lat = kernel_call(
        partial(enc_forward_kernel, **sizes),
        "encode",
        enc_edges // enc_span,
        [(place, SMEM), (bounds, SMEM), (enc_keys, HELD), (shared, HELD)]
        + [(value, None) for value in (enc_w1, enc_b1, enc_w2, enc_b2, lift_w, lift_b)]
        + [(plane, FAR)],
        [
            shape(saved_rows, enc_edges),
            shape(PLANE, lanes),
            shape(PLANE, lanes),
            shape(2 * MODES * MODES, lanes),
        ],
        [FAR, FAR, FAR, HELD],
        [
            pltpu.VMEM((cells + PAD, 2 * LANES), F32),
            pltpu.VMEM((2 * fixed, LANES), BF16),
            pltpu.VMEM((2 * width, INPUT_ROWS), BF16),
            pltpu.VMEM((width, 3 * width), BF16),
            pltpu.VMEM((2 * width + 16, enc_span), BF16),
            plane_scratch,
            pltpu.VMEM((PLANE, lanes), F32),
            pltpu.VMEM((PLANE, lanes), F32),
            dma((3,)),
            pltpu.VMEM((2, saved_rows, enc_span), F32),
            dma((2,)),
        ],
    )
    modes_lines = exchange(plane_lat.reshape(owners, 2 * lines, lanes))

    dec_rows = 2 * width + FEAT_ROWS
    dec_steps = dec_edges // dec_span
    half_steps = dec_steps // 2

    def dec_sums(first_step, steps, before, saved_before, after, more, out_shape, scratch, name):
        return kernel_call(
            partial(dec_sums_kernel, first_step=first_step, **sizes),
            name,
            steps,
            [
                (place, SMEM), (bounds, SMEM), (dec_keys, HELD), (shared, HELD), (dec_w1, None), (dec_b1, None),
                (before, HELD if first_step else FAR), (saved_before, FAR), (after, FAR),
            ]
            + more,
            [shape(dec_rows, dec_edges)] + out_shape,
            [pl.BlockSpec((dec_rows, dec_span), lambda i: (0, i + first_step))] + [HELD] * len(out_shape),
            scratch
            + [
                pltpu.VMEM((2 * fixed, LANES), BF16),
                pltpu.VMEM((width, INPUT_ROWS), BF16),
                pltpu.VMEM((2 * width + 16, dec_span), BF16),
            ],
            input_output_aliases={7: 0} if first_step else {},
        )

    dec_saved, dec_total, inverse_degree, skip = dec_sums(
        0, half_steps, plane_lat, plane_lat, plane_lat, [(lat, HELD), (skip_w, None), (skip_b, None)],
        [shape(cells + PAD, 2 * LANES), shape(owners, LANES), shape(PLANE, lanes)], [], "decode_sums_a",
    )

    mix_step, grad_step = min(MIX_STEP, modes_here), min(GRAD_STEP, modes_here)

    def spec_block(step):
        return pl.BlockSpec((step, width, 2 * width), lambda i: (i, 0, 0))

    def mode_pass(kernel, lines_in, after, name):
        return kernel_call(
            partial(kernel, owners=owners, width=width),
            name,
            1,
            [(place, SMEM), (lines_in, HELD), (cos_x, None), (sin_x, None), (spec_w, FAR)]
            + [(value, FAR) for value in after],
            [shape(modes_here, 2 * width), shape(owners, 2 * lines, lanes)],
            [HELD, HELD],
            [
                pltpu.VMEM((modes_here, 2 * width), F32),
                pltpu.VMEM((modes_here, width, 2 * width), F32),
                dma((modes_here // mix_step,)),
            ],
        )

    modes, back_lines = mode_pass(mix_kernel, modes_lines, [inverse_degree], "mix_modes")
    def from_shapes(value, staged=True):
        parts, step = {0: value}, shapes // 2
        if staged:
            while step:
                pairs = [(i, i ^ step) for i in range(shapes)]
                parts.update({d ^ step: lax.ppermute(part, "grid", pairs) for d, part in parts.items()})
                step //= 2
        else:
            for step in range(1, shapes):
                parts[step] = lax.ppermute(value, "grid", [(i, i ^ step) for i in range(shapes)])
        return [parts[d] for d in range(shapes)]

    all_modes = from_shapes(modes)
    grid_lines = exchange(back_lines).reshape(2 * MODES * MODES, lanes)
    dec_saved, sums, reach = dec_sums(
        half_steps, dec_steps - half_steps, dec_total, dec_saved, back_lines,
        [(dec_w2, None), (dec_b2, None)],
        [shape(2, PLANE, lanes), shape(PLANE, lanes)],
        [pltpu.VMEM((cells + PAD, 2 * LANES), F32)],
        "decode_sums_b",
    )

    plane_bar, pre_bar, latent = kernel_call(
        partial(grid_kernel, rows_here=rows_here),
        "grid_fields",
        1,
        [(grid_lines, FAR), (reach, FAR), (skip, FAR), (proj_w, None), (inverse, FAR), (plane, FAR)]
        + [(value, FAR) for value in all_modes[shapes // 2 :][:1]],
        [shape(2 * MODES * MODES, lanes)] + [shape(PLANE, lanes)] * 2,
        [HELD, FAR, FAR],
        [
            pltpu.VMEM((2 * MODES * MODES, lanes), F32),
            inverse_scratch,
            pltpu.VMEM((PLANE, lanes), F32),
            pltpu.VMEM((PLANE, lanes), F32),
            plane_scratch,
            pltpu.VMEM((PLANE, lanes), F32),
            pltpu.VMEM((PLANE, lanes), F32),
            dma((7,)),
        ],
    )
    bar_lines = exchange(plane_bar.reshape(owners, 2 * lines, lanes))

    skip_w_grad, dec_w2_grad, row_grads, dec_table, skip_back = kernel_call(
        partial(grid_grads_kernel, rows_here=rows_here, width=width),
        "grid_grads",
        1,
        [(value, HELD) for value in (lat, pre_bar, latent, reach, sums)]
        + [(value, None) for value in (skip_w, dec_w2, dec_b2, proj_w)],
        [
            shape(width, width),
            shape(width, width),
            shape(8, width),
            shape(cells + PAD, 2 * LANES, dtype=BF16),
            shape(PLANE, lanes),
        ],
        [HELD] * 5,
    )

    mixed_bar, bar_back = mode_pass(mix_back_kernel, bar_lines, [row_grads] + all_modes[1:], "mix_back")
    bar_grid_lines = exchange(bar_back).reshape(2 * MODES * MODES, lanes)

    all_grads = from_shapes(mixed_bar)

    count8 = max(owners, 8)
    pred_part, dec_w1_grad, dec_b1_grad = kernel_call(
        partial(dec_edges_kernel, **sizes),
        "decode_edges",
        dec_steps,
        [
            (place, SMEM), (bounds, SMEM), (dec_keys, HELD), (inverse_degree, HELD),
            (dec_saved, pl.BlockSpec((dec_rows, dec_span), lambda i: (0, i))), (dec_table, HELD),
        ],
        [shape(owners, LANES), shape(6, width), shape(1, width)],
        [HELD] * 3,
        [
            pltpu.VMEM((2 * width + 16, dec_span), F32),
            pltpu.VMEM((2 * count8, LANES), F32),
            pltpu.VMEM((2 * width, 32), F32),
        ],
    )

    packed = kernel_call(
        partial(enc_back_kernel, **sizes),
        "encode_back",
        enc_edges // enc_span,
        [(place, SMEM), (bounds, SMEM), (enc_keys, HELD), (saved, FAR)]
        + [(value, FAR) for value in (bar_grid_lines, skip_back, scale)]
        + [(value, None) for value in (enc_w2, lift_w, pred_bar)]
        + [(value, HELD) for value in (skip_w_grad, dec_w2_grad, row_grads, pred_part, dec_w1_grad, dec_b1_grad)]
        + [(inverse, FAR)]
        + [(value, FAR) for value in all_grads[shapes // 2 :][:1]],
        shape(owners, PACKED_ROWS, LANES),
        HELD,
        [
            pltpu.VMEM((cells + PAD, 2 * width), BF16),
            pltpu.VMEM((2 * width, enc_span), F32),
            pltpu.VMEM((width, 3 * width), BF16),
            pltpu.VMEM((16, 2 * width), BF16),
            pltpu.VMEM((8 * count8, LANES), F32),
            pltpu.VMEM((6 * width + 16, 2 * width + 32), F32),
            inverse_scratch,
            pltpu.VMEM((2 * MODES * MODES, lanes), F32),
            pltpu.VMEM((PLANE, lanes), F32),
            pltpu.VMEM((PLANE, lanes), F32),
            dma((4,)),
            pltpu.VMEM((2, saved_rows, enc_span), F32),
            dma((2,)),
        ],
    )
    arrived = exchange(packed)

    rank = lax.axis_index("grid").astype(jnp.int32).reshape(1)
    spec_grad = kernel_call(
        partial(spec_grad_kernel, shapes=shapes, width=width),
        "spec_grad",
        modes_here // grad_step,
        [(rank, SMEM)]
        + [
            (value, pl.BlockSpec((grad_step, 2 * width), lambda i: (i, 0)))
            for value in all_modes + all_grads
        ]
        + [(packed, FAR)],
        shape(modes_here, width, 2 * width),
        spec_block(grad_step),
        [pltpu.VMEM((shapes, grad_step, 2 * width), F32)] * 2,
    )

    grads, feat_grad, pred = kernel_call(
        partial(arrive_kernel, owners=owners),
        "arrive",
        1,
        [(arrived, HELD), (proj_b, None), (spec_grad, FAR)],
        [shape(GRAD_ROWS, LANES), shape(4, LANES), shape(1, LANES)],
        [HELD] * 3,
    )
    terms = from_shapes(grads, staged=False)
    vector = shape(1, width)
    square = shape(width, width)
    first = shape(6, width)
    outs = kernel_call(
        partial(leave_kernel, shapes=shapes, width=width),
        "leave",
        1,
        [(term, HELD) for term in terms],
        [
            first, vector, square, vector, shape(4, width), vector,
            square, vector, first, vector, square, vector, vector, shape(1, 1),
        ],
        [HELD] * 14,
    )
    outs = [out.reshape(-1) if out.shape[0] == 1 else out for out in outs]
    return (pred, feat_grad[None], *outs[:6], spec_grad, *outs[6:])


def solution(mesh):
    placed = (
        P("grid", None, "wide"),
        P("grid", None, "wide"),
        P("grid", None, "wide"),
        P("grid", "wide", None),
        P("grid", "wide", None),
        P("grid", "wide"),
        P("grid", "wide", None),
        P("grid", "wide", None),
        P("grid", "wide"),
        P(),
        P(),
        P(),
        P(),
        P(),
        P(),
        P("wide", None, None),
        P(),
        P(),
        P(),
        P(),
        P(),
        P(),
        P(),
        P(),
        P("grid", "wide"),
    )
    return jax.shard_map(
        on_device,
        mesh=mesh,
        in_specs=placed,
        out_specs=(
            P("grid", "wide"),
            P("grid", None, "wide"),
            P(),
            P(),
            P(),
            P(),
            P(),
            P(),
            P("wide", None, None),
            P(),
            P(),
            P(),
            P(),
            P(),
            P(),
            P(),
            P(),
        ),
        check_vma=False,
    )
```

```python
from functools import partial
import math

import jax
import jax.numpy as jnp
import ml_dtypes
import numpy as np
from jax import lax
from jax.experimental import pallas as pl
from jax.experimental.pallas import tpu as pltpu
from jax.sharding import PartitionSpec as P

MODES = 16
RES = 32
PLANE = RES * RES
CHUNK = 256
LANES = 128
ENC_GROUP = 16
DEC_GROUP = 16
FEW = 4
FEAT_ROWS = 8
INPUT_ROWS = 48
ENC_WINDOW = 64
DEC_WINDOW = 128
PAD = 256
MIX_STEP = 64
GRAD_STEP = 128
F32 = jnp.float32
BF16 = jnp.bfloat16
GELU_A = 0.7978845608028654
GELU_B = 0.044715

NN = (((1,), (0,)), ((), ()))
NT = (((1,), (1,)), ((), ()))
TN = (((0,), (0,)), ((), ()))

VMEM = pl.BlockSpec(memory_space=pltpu.VMEM)
SMEM = pl.BlockSpec(memory_space=pltpu.SMEM)


def kept_freqs():
    half = MODES // 2
    return np.concatenate([np.arange(half), np.arange(RES - half, RES)])


def plane_matrix(owners):
    lines = MODES * MODES // owners
    line = np.arange(MODES * MODES)
    freq_y, freq_z = kept_freqs()[line // MODES], line % MODES
    cell = np.arange(PLANE)
    turns = (freq_y[:, None] * (cell // RES) + freq_z[:, None] * (cell % RES)) % RES
    angle = turns * (2.0 * math.pi / RES)
    both = np.stack([np.cos(angle), -np.sin(angle)]).reshape(2, owners, lines, PLANE)
    matrix = both.transpose(1, 0, 2, 3).reshape(2 * MODES * MODES, PLANE)
    return matrix.astype(np.float32)


def halves_np(matrix):
    high = matrix.astype(ml_dtypes.bfloat16)
    low = (matrix - high.astype(np.float32)).astype(ml_dtypes.bfloat16)
    return high, low


def line_angles():
    turns = (kept_freqs()[:, None] * np.arange(RES)[None, :]) % RES
    return turns * (2.0 * math.pi / RES)


def x_tables(rows_here, width):
    angle = line_angles().reshape(MODES, RES // rows_here, rows_here, 1)
    angle = np.broadcast_to(angle, (MODES, RES // rows_here, rows_here, width))
    angle = angle.reshape(MODES, RES // rows_here, rows_here * width)
    return np.cos(angle).astype(np.float32), np.sin(angle).astype(np.float32)


def log2(number):
    return number.bit_length() - 1


def iota(shape, axis):
    return lax.broadcasted_iota(jnp.int32, shape, axis)


def halves(value):
    high = value.astype(BF16)
    low = (value - high.astype(F32)).astype(BF16)
    return high, low


def dot(a, b, dims=NN):
    return lax.dot_general(a, b, dims, preferred_element_type=F32)


def dot3(a, b, dims=NN):
    a_high, a_low = halves(a)
    b_high, b_low = halves(b)
    return dot(a_high, b_high, dims) + dot(a_low, b_high, dims) + dot(a_high, b_low, dims)


def one_hot(index, first, rows):
    places = iota((rows, index.shape[1]), 0)
    return jnp.where(places == index - first, 1.0, 0.0).astype(BF16)


def gelu_both(value):
    square = value * value
    half = 0.5 + 0.5 * jnp.tanh(value * (GELU_A + (GELU_A * GELU_B) * square))
    out = value * half
    return out, half + (out - out * half) * (2.0 * GELU_A + (6.0 * GELU_A * GELU_B) * square)


def sort_columns(values):
    rows = values.shape[0]
    regs = rows // 8
    low = log2(regs)
    total = low + 3 + 7
    sub = iota((8, LANES), 0)
    lane = iota((8, LANES), 1)
    x = values.reshape(regs, 8, LANES)

    def flip(x, bit):
        if bit >= total:
            return x
        if bit < low:
            y = x.reshape(regs >> (bit + 1), 2, 1 << bit, 8, LANES)
            return jnp.stack([y[:, 0], -y[:, 1]], axis=1).reshape(regs, 8, LANES)
        if bit < low + 3:
            sign = 1 - 2 * ((sub >> (bit - low)) & 1)
        else:
            sign = 1 - 2 * ((lane >> (bit - low - 3)) & 1)
        return x * sign.astype(F32)[None]

    def exchange(x, bit):
        if bit < low:
            y = x.reshape(regs >> (bit + 1), 2, 1 << bit, 8, LANES)
            one, two = y[:, 0], y[:, 1]
            pair = [jnp.minimum(one, two), jnp.maximum(one, two)]
            return jnp.stack(pair, axis=1).reshape(regs, 8, LANES)
        if bit < low + 3:
            axis, dist, size, place = 1, 1 << (bit - low), 8, sub
        else:
            axis, dist, size, place = 2, 1 << (bit - low - 3), LANES, lane
        after = pltpu.roll(x, size - dist, axis)
        before = after if 2 * dist == size else pltpu.roll(x, dist, axis)
        first = ((place & dist) == 0)[None]
        return jnp.where(first, jnp.minimum(x, after), jnp.maximum(x, before))

    for phase in range(1, total + 1):
        x = flip(x, phase)
        for bit in reversed(range(phase)):
            x = exchange(x, bit)
        x = flip(x, phase)
    return x.reshape(rows, LANES)


def layer_matrix(feat_rows, cell_rows):
    feat_high, feat_low = halves(feat_rows)
    cell_high, cell_low = halves(cell_rows)
    parts = [feat_high, feat_high, feat_low, cell_high, cell_low]
    parts = [part.astype(F32) for part in parts] + [jnp.zeros((LANES - 40, feat_rows.shape[1]), F32)]
    return jnp.concatenate(parts, axis=0).T[:, :INPUT_ROWS].astype(BF16)


def place_rows(cell, first_row):
    row = iota((8, cell.shape[1]), 0)
    shifts = jnp.where(row == 0, 2 * log2(RES), jnp.where(row == 1, log2(RES), 0))
    place = (cell >> shifts) & jnp.where(row < 3, RES - 1, 0)
    return (place + jnp.where(row == 0, first_row, 0)).astype(F32)


def edge_feats(key, table, owners):
    point = key & (owners * LANES - 1)
    found = dot(table, one_hot(point & (LANES - 1), 0, LANES))
    owner = (iota(found.shape, 0) >> 3) & (owners - 1)
    found = jnp.where(owner == (point >> 7), found, 0.0)
    return jnp.sum(found.reshape(2 * owners, FEAT_ROWS, key.shape[1]), axis=0)


def stack_inputs(feats, place):
    high, low = halves(feats)
    parts = [high.astype(F32), low.astype(F32), high.astype(F32), place, place, jnp.zeros_like(place)]
    return jnp.concatenate(parts, axis=0).astype(BF16)


def stack3(value):
    high, low = halves(value)
    return jnp.concatenate([high, low, high], axis=0)


def weights3(matrix):
    high, low = halves(matrix)
    return jnp.concatenate([high, high, low], axis=1)


def key_row(keys_ref, chunk):
    per = CHUNK // keys_ref.shape[1]
    rows = [keys_ref[pl.ds(chunk * per + i, 1), :] for i in range(per)]
    return rows[0] if per == 1 else jnp.concatenate(rows, axis=1)


def cell_range(bounds_ref, line, chunk, per):
    return bounds_ref[line, chunk * per], bounds_ref[line + 1, chunk * per + per - 1]


def spread(block, copies):
    rows, columns = block.shape
    tiled = jnp.concatenate([jnp.concatenate([block] * copies, axis=1)] * copies, axis=0)
    return jnp.where(
        iota(tiled.shape, 0) // rows == iota(tiled.shape, 1) // columns, tiled, 0.0
    )


def gather_blocks(product, copies, rows, columns):
    total = product[:rows, :columns]
    for i in range(1, copies):
        total = total + product[i * rows : (i + 1) * rows, i * columns : (i + 1) * columns]
    return total


def tile_lanes(row, copies):
    return row if copies == 1 else jnp.concatenate([row] * copies, axis=1)


def fold_lanes(row, copies, width):
    total = row[:, :width]
    for i in range(1, copies):
        total = total + row[:, i * width : (i + 1) * width]
    return total


def column(counts):
    return jnp.broadcast_to(counts, (8, counts.shape[1])).T[:, :1]


def share_kernel(feat, pos, query_pos, pred_bar, dec_query, dec_count, payload, *, owners):
    blocks = dec_query.shape[0]
    lane_valid = jnp.where(
        iota((blocks, LANES), 1) < column(dec_count[...]), dec_query[...], owners * LANES
    )
    ones = jnp.zeros((max(owners, 16), LANES), F32)
    degree = ones
    for block in range(0, blocks, 2):
        row = jnp.concatenate([lane_valid[block : block + 1], lane_valid[block + 1 : block + 2]], axis=1)
        high = one_hot(row >> 7, 0, ones.shape[0])
        low = one_hot(row & (LANES - 1), 0, LANES)
        degree = degree + dot(high, low, NT)
    filled = jnp.ones((1, LANES), F32)
    empty = jnp.zeros((3, LANES), F32)
    places = [pos[i] for i in range(3)]
    queries = [query_pos[i] for i in range(3)]
    rows = places + [filled, feat[0]] + queries + [filled, pred_bar[...], empty, degree[:owners]]
    mine = jnp.concatenate(rows, axis=0)
    for owner in range(owners):
        payload[owner] = mine


def sort_kernel(
    enc_cell, enc_point, enc_count, dec_cell, dec_query, dec_count, after,
    enc_keys, dec_keys, bounds, *, owners, cells,
):
    shift = log2(owners * LANES)

    def keys(cell, point, count):
        lane = iota(cell.shape, 1)
        key = jnp.where(lane < column(count), (cell << shift) | point, cells << shift)
        return sort_columns(key.astype(F32)).astype(jnp.int32)

    enc = keys(enc_cell[...], enc_point[...], enc_count[...])
    dec = keys(dec_cell[...], dec_query[...], dec_count[...])
    enc_keys[...] = enc.T
    dec_keys[...] = dec.T
    ends = [enc[:1], enc[-1:], dec[:1], dec[-1:]]
    bounds[...] = jnp.concatenate(ends + [jnp.zeros((4, LANES), jnp.int32)], axis=0) >> shift


def joined_keys(keys, chunk, group):
    rows = [key_row(keys, chunk + i) for i in range(group)]
    return rows, jnp.concatenate(rows, axis=1)


def later_windows(windows, size, visit):
    most = windows[0][1]
    for _, count in windows[1:]:
        most = jnp.maximum(most, count)

    @pl.when(most > 1)
    def _():
        for i, (begin, count) in enumerate(windows):

            def more(j, carry):
                visit(i, begin + j * size)
                return carry

            lax.fori_loop(1, count, more, 0)


def scatter_windows(total, keys, cell, message, bounds, line, chunk, group, size, shift, columns):
    per = CHUNK // keys.shape[1]
    windows, parts = [], []
    for i in range(group):
        begin, end = cell_range(bounds, line, chunk + i, per)
        begin = pl.multiple_of(begin & -8, 8)
        lanes = slice(i * CHUNK, (i + 1) * CHUNK)
        parts.append(dot(one_hot(cell[:, lanes], begin, size), message[:, lanes], NT))
        windows.append((begin, (end - begin) // size + 1))
    for (begin, _), part in zip(windows, parts):
        total[pl.ds(begin, size), :columns] += part

    def visit(i, start):
        start = pl.multiple_of(start, 8)
        hot = one_hot(key_row(keys, chunk + i) >> shift, start, size)
        part = dot(hot, message[:, i * CHUNK : (i + 1) * CHUNK], NT)
        total[pl.ds(start, size), :columns] += part

    later_windows(windows, size, visit)


def gather_windows(found, keys, rows, table, bounds, line, chunk, group, size, shift, columns):
    per = CHUNK // keys.shape[1]
    windows = []
    for i in range(group):
        begin, end = cell_range(bounds, line, chunk + i, per)
        begin = pl.multiple_of(begin & -16, 16)
        hot = one_hot(rows[i] >> shift, begin, size)
        found[:, i * CHUNK : (i + 1) * CHUNK] = dot(table[pl.ds(begin, size), :columns], hot, TN)
        windows.append((begin, (end - begin) // size + 1))

    def visit(i, start):
        start = pl.multiple_of(start, 16)
        hot = one_hot(key_row(keys, chunk + i) >> shift, start, size)
        part = dot(table[pl.ds(start, size), :columns], hot, TN)
        found[:, i * CHUNK : (i + 1) * CHUNK] += part

    later_windows(windows, size, visit)


def slot_copies(far, slots, semaphores, out):
    span = slots.shape[2]

    def copy(step):
        slot = step % 2
        columns = far.at[:, pl.ds(pl.multiple_of(step * span, span), span)]
        ends = (slots.at[slot], columns) if out else (columns, slots.at[slot])
        return pltpu.make_async_copy(*ends, semaphores.at[slot])

    return copy


def used_steps(bounds, line, group, per, cells, steps):
    used = 0
    for step in range(steps):
        used = used + jnp.where(bounds[line, step * group * per] < cells, 1, 0)
    return used


def each_size(bounds, line, chunk, group, per, cells, body):
    few = min(FEW, group)
    some = bounds[line, chunk * per] < cells
    if few == group:
        pl.when(some)(lambda: body(group))
        return
    many = bounds[line, (chunk + few) * per] < cells
    pl.when(many)(lambda: body(group))
    pl.when(some & jnp.logical_not(many))(lambda: body(few))


def enc_forward_kernel(
    place_ref, bounds, keys, shared, w1, b1, w2, b2, lift_w, lift_b, plane_hbm,
    saved_hbm, lat_far, scale_far, plane_out,
    total, table, first, second, message, plane, lat, scale, copied, slots, stored,
    *, owners, cells, width,
):
    rows_here = cells // PLANE
    group = message.shape[1] // CHUNK
    shift = log2(owners * LANES)
    first_row = place_ref[0] * rows_here
    copy = pltpu.make_async_copy(plane_hbm, plane, copied.at[0])
    save = slot_copies(saved_hbm, slots, stored, out=True)

    def begin():
        copy.start()
        total[...] = jnp.zeros_like(total)
        feats = jnp.concatenate([shared[i, :FEAT_ROWS] for i in range(owners)], axis=0)
        table[...] = jnp.concatenate(halves(feats), axis=0)
        empty = jnp.zeros((3, width), F32)
        pre_rows = jnp.concatenate([w1[3:6], b1[...], jnp.zeros((4, width), F32)], axis=0)
        lift_rows = jnp.concatenate([empty, lift_b[...], lift_w[...]], axis=0)
        cell_rows = jnp.concatenate([w1[0:3] / (RES - 1.0), jnp.zeros((5, width), F32)], axis=0)
        first[...] = layer_matrix(
            jnp.concatenate([pre_rows, lift_rows], axis=1),
            jnp.concatenate([cell_rows, jnp.zeros((8, width), F32)], axis=1),
        )
        second[...] = weights3(w2[...].T)

    def run_step(step, carry):
        chunk = step * group
        per = CHUNK // keys.shape[1]

        def body(count):
            bias = jnp.broadcast_to(b2[...], (8, width)).T[:, :1]
            _, key = joined_keys(keys, chunk, count)
            cell = key >> shift

            @pl.when(step >= 2)
            def _():
                save(step - 2).wait()

            saved = slots.at[step % 2]
            run = slice(0, count * CHUNK)
            feats = edge_feats(key, table[...], owners)
            both = dot(first[...], stack_inputs(feats, place_rows(cell, first_row)))
            lifted = both[width:]
            hidden, slope = gelu_both(both[:width])
            kernel = dot(second[...], stack3(hidden)) + bias
            saved[0 * width : 1 * width, run] = hidden
            saved[1 * width : 2 * width, run] = slope
            saved[2 * width : 3 * width, run] = lifted
            saved[3 * width : 4 * width, run] = kernel
            saved[4 * width :, run] = feats
            high, low = halves(kernel * lifted)
            message[:, run] = jnp.concatenate([high, low, jnp.ones((16, count * CHUNK), BF16)], axis=0)
            save(step).start()
            scatter_windows(
                total, keys, cell, message, bounds, 0, chunk, count, ENC_WINDOW, shift, 2 * width + 16
            )

        each_size(bounds, 0, chunk, group, per, cells, body)
        return carry

    begin()
    steps = keys.shape[0] * keys.shape[1] // slots.shape[2]
    used = used_steps(bounds, 0, group, CHUNK // keys.shape[1], cells, steps)
    lax.fori_loop(0, used, run_step, 0)
    def end():
        fields, scales = [], []
        for row in range(rows_here):
            slab = total[row * PLANE : (row + 1) * PLANE]
            inverse = 1.0 / jnp.maximum(slab[:, 2 * width : 2 * width + 1], 1.0)
            fields.append((slab[:, :width] + slab[:, width : 2 * width]) * inverse)
            scales.append(jnp.broadcast_to(inverse, (PLANE, width)))
        field = jnp.concatenate(fields, axis=1)
        lat[...] = field
        scale[...] = jnp.concatenate(scales, axis=1)
        leaving = [
            pltpu.make_async_copy(lat, lat_far, copied.at[1]),
            pltpu.make_async_copy(scale, scale_far, copied.at[2]),
        ]
        for out in leaving:
            out.start()
        copy.wait()
        plane_out[...] = times_field(plane, field)
        for out in leaving:
            out.wait()

        @pl.when(used >= 2)
        def _():
            save(used - 2).wait()

        @pl.when(used >= 1)
        def _():
            save(used - 1).wait()

    end()


def times_field(matrix, field):
    high, low = halves(field)
    return dot(matrix[0], high) + dot(matrix[1], high) + dot(matrix[0], low)


def dec_sums_kernel(
    place_ref, bounds, keys, shared, w1, b1, before, saved_before, after, *refs,
    owners, cells, width, first_step,
):
    if first_step == 0:
        lat, skip_w, skip_b, saved, total, inverse_out, skip, table, first, message = refs
    else:
        dec_w2, dec_b2, saved, sums, reach, total, table, first, message = refs
    step = pl.program_id(0)
    rows_here = cells // PLANE
    group = message.shape[1] // CHUNK
    shift = log2(owners * LANES)
    first_row = place_ref[0] * rows_here

    @pl.when(step == 0)
    def _():
        total[...] = jnp.zeros_like(total) if first_step == 0 else before[...]
        degree = shared[0, 2 * FEAT_ROWS :]
        for i in range(1, owners):
            degree = degree + shared[i, 2 * FEAT_ROWS :]
        inverse = 1.0 / jnp.maximum(degree, 1.0)
        if first_step == 0:
            inverse_out[...] = inverse
        feats = []
        for i in range(owners):
            rows = shared[i, FEAT_ROWS : 2 * FEAT_ROWS]
            weighted = rows * inverse[i : i + 1]
            feats.append(jnp.where(iota(rows.shape, 0) == 4, weighted, rows))
        table[...] = jnp.concatenate(halves(jnp.concatenate(feats, axis=0)), axis=0)
        feat_rows = jnp.concatenate([w1[0:3], b1[...], jnp.zeros((4, width), F32)], axis=0)
        cell_rows = jnp.concatenate([w1[3:6] / (RES - 1.0), jnp.zeros((5, width), F32)], axis=0)
        first[...] = layer_matrix(feat_rows, cell_rows)

    chunk = (step + first_step) * group
    per = CHUNK // keys.shape[1]

    def body(count):
        _, key = joined_keys(keys, chunk, count)
        run = slice(0, count * CHUNK)
        cell = key >> shift
        feats = edge_feats(key, table[...], owners)
        hidden, slope = gelu_both(dot(first[...], stack_inputs(feats, place_rows(cell, first_row))))
        weight = feats[4:5]
        saved[0 * width : 1 * width, run] = hidden
        saved[1 * width : 2 * width, run] = slope * weight
        saved[2 * width :, run] = feats
        high, low = halves(hidden * weight)
        w_high, w_low = halves(feats)
        tail = jnp.concatenate([w_high.astype(F32), w_low.astype(F32)], axis=0).astype(BF16)
        message[:, run] = jnp.concatenate([high, low, tail], axis=0)
        scatter_windows(
            total, keys, cell, message, bounds, 2, chunk, count, DEC_WINDOW, shift, 2 * width + 16
        )

    each_size(bounds, 2, chunk, group, per, cells, body)

    @pl.when(step == pl.num_programs(0) - 1)
    def _():
        if first_step == 0:
            skipped = dot3(lat[...], spread(skip_w[...], rows_here))
            skip[...] = skipped + tile_lanes(skip_b[...], rows_here)
            return
        sums[0], sums[1] = cell_sums(total, rows_here, width)
        reached = dot3(sums[0], spread(dec_w2[...], rows_here))
        reach[...] = reached + sums[1] * tile_lanes(dec_b2[...], rows_here)


def x_forward(lines_ref, cos_ref, sin_ref, put, owners, lines, width):
    lanes = lines_ref.shape[2]
    for kx in range(MODES):
        real = jnp.zeros((lines, lanes), F32)
        imag = jnp.zeros((lines, lanes), F32)
        for owner in range(owners):
            cos, sin = cos_ref[kx, owner : owner + 1], sin_ref[kx, owner : owner + 1]
            line_real, line_imag = lines_ref[owner, :lines], lines_ref[owner, lines:]
            real = real + cos * line_real + sin * line_imag
            imag = imag + cos * line_imag - sin * line_real
        if lanes == width:
            put(kx, jnp.concatenate([real, imag], axis=1))
        else:
            pair = 2 * width
            while real.shape[1] > pair:
                half = real.shape[1] // 2
                real, imag = real[:, :half] + real[:, half:], imag[:, :half] + imag[:, half:]
            real = real + pltpu.roll(real, width, 1)
            imag = imag + pltpu.roll(imag, width, 1)
            put(kx, jnp.where(iota(real.shape, 1) < width, real, imag))


def x_inverse(take, out_ref, owners, lines, width):
    angles = line_angles()
    rows_here = RES // owners
    modes = [take(kx) for kx in range(MODES)]
    lane = iota(modes[0].shape, 1)
    turned = [
        jnp.where(lane < width, -pltpu.roll(mode, width, 1), pltpu.roll(mode, width, 1))
        for mode in modes
    ]

    def at(x):
        total = None
        for kx in range(MODES):
            for value, factor in ((modes[kx], np.cos(angles[kx, x])), (turned[kx], np.sin(angles[kx, x]))):
                factor = float(np.float32(factor)) if abs(factor) > 1e-9 else 0.0
                if factor == 0.0:
                    continue
                term = value if factor == 1.0 else value * factor
                total = term if total is None else total + term
        return total

    for owner in range(owners):
        if rows_here == 1:
            here = at(owner)
            out_ref[owner, :lines] = here[:, :width]
            out_ref[owner, lines:] = here[:, width:]
            continue
        for pair in range(rows_here // 2):
            one, two = at(owner * rows_here + 2 * pair), at(owner * rows_here + 2 * pair + 1)
            one_turned, two_turned = pltpu.roll(one, width, 1), pltpu.roll(two, width, 1)
            where = slice(2 * pair * width, (2 * pair + 2) * width)
            out_ref[owner, :lines, where] = jnp.where(lane < width, one, two_turned)
            out_ref[owner, lines:, where] = jnp.where(lane < width, one_turned, two)


def factor_column(place_ref, lines):
    line = place_ref[0] * lines + iota((lines, 1), 0)
    return jnp.where((line & (MODES - 1)) == 0, 1.0, 2.0) / float(RES**3)


def split_weights(spec_w, base, width):
    block = spec_w[pl.ds(base, 8)].reshape(8 * width, 2 * width)
    return jnp.concatenate(halves(block), axis=1)


def interleave(one, two):
    parts = []
    for at in range(0, one.shape[0], 8):
        parts += [one[at : at + 8], two[at : at + 8]]
    return jnp.concatenate(parts, axis=0)


def fetch_weights(spec_hbm, spec_w, copied):
    count = spec_w.shape[0] // copied.shape[0]

    def copy(i):
        where = pl.ds(i * count, count)
        return pltpu.make_async_copy(spec_hbm.at[where], spec_w.at[where], copied.at[i])

    return count, copy


def mix_kernel(
    place_ref, lines_ref, cos_ref, sin_ref, spec_hbm, *refs, owners, width,
):
    modes, out_ref, mixed, spec_w, copied = refs[-5:]
    lines = MODES * MODES // owners
    count, copy = fetch_weights(spec_hbm, spec_w, copied)
    for i in range(copied.shape[0]):
        copy(i).start()

    def put(kx, value):
        modes[pl.ds(kx, lines, MODES), :] = value

    x_forward(lines_ref, cos_ref, sin_ref, put, owners, lines, width)
    lane = iota((count, 2 * width), 1)

    def mix(i, carry):
        copy(i).wait()
        base = pl.multiple_of(i * count, count)
        u = modes[pl.ds(base, count), :]
        u_turned = pltpu.roll(u, width, 1)
        both = interleave(jnp.where(lane < width, u, u_turned), jnp.where(lane < width, u_turned, u))
        both = jnp.concatenate([both] * 4, axis=1)
        own = iota(both.shape, 1) // width == iota(both.shape, 0) % 8
        high, low = halves(jnp.where(own, both, 0.0))
        products = []
        for batch in range(count // 8):
            rows = slice(batch * 16, (batch + 1) * 16)
            left = jnp.concatenate([high[rows], low[rows]], axis=0)
            products.append(dot(left, split_weights(spec_w, base + batch * 8, width)))
        outs = []
        for product in products:
            product = product[:, : 2 * width] + product[:, 2 * width :]
            product = product[:16] + product[16:]
            turned = pltpu.roll(product[8:], width, 1)
            outs.append(product[:8] + jnp.where(lane[:8] < width, -turned, turned))
        mixed[pl.ds(base, count), :] = jnp.concatenate(outs, axis=0)
        return carry

    lax.fori_loop(0, copied.shape[0], mix, 0)
    factor = factor_column(place_ref, lines)

    def take(kx):
        return mixed[pl.ds(kx, lines, MODES), :] * factor

    x_inverse(take, out_ref, owners, lines, width)


def mix_back_kernel(
    place_ref, lines_ref, cos_ref, sin_ref, spec_hbm, *refs, owners, width,
):
    grads, out_ref, back, spec_w, copied = refs[-5:]
    lines = MODES * MODES // owners
    count, copy = fetch_weights(spec_hbm, spec_w, copied)
    for i in range(copied.shape[0]):
        copy(i).start()
    factor = factor_column(place_ref, lines)

    def put(kx, value):
        grads[pl.ds(kx, lines, MODES), :] = value * factor

    x_forward(lines_ref, cos_ref, sin_ref, put, owners, lines, width)
    lane = iota((count, 2 * width), 1)
    own = iota((16, 8 * width), 1) // width == iota((16, 8 * width), 0) % 8

    def mix(i, carry):
        copy(i).wait()
        base = pl.multiple_of(i * count, count)
        g = grads[pl.ds(base, count), :]
        g_turned = pltpu.roll(g, width, 1)
        high, low = halves(interleave(g, jnp.where(lane < width, g_turned, -g_turned)))
        products = []
        for batch in range(count // 8):
            rows = slice(batch * 16, (batch + 1) * 16)
            left = jnp.concatenate([high[rows], low[rows]], axis=0)
            left = jnp.concatenate([left, left], axis=1)
            products.append(dot(left, split_weights(spec_w, base + batch * 8, width), NT))
        outs = []
        for product in products:
            rows = jnp.where(own, product[:16] + product[16:], 0.0)
            while rows.shape[1] > 2 * width:
                half = rows.shape[1] // 2
                rows = rows[:, :half] + rows[:, half:]
            rows = rows + pltpu.roll(rows, width, 1)
            outs.append(jnp.where(lane[:8] < width, rows[:8], rows[8:]))
        back[pl.ds(base, count), :] = jnp.concatenate(outs, axis=0)
        return carry

    lax.fori_loop(0, copied.shape[0], mix, 0)

    def take(kx):
        return back[pl.ds(kx, lines, MODES), :]

    x_inverse(take, out_ref, owners, lines, width)


def spec_grad_kernel(rank_ref, *refs, shapes, width):
    mode_refs, grad_refs, (out, modes, grads) = refs[:shapes], refs[shapes : 2 * shapes], refs[-3:]
    for parts, held in ((mode_refs, modes), (grad_refs, grads)):
        for distance, part in enumerate(parts):
            held[rank_ref[0] ^ distance] = part[...]
    row = iota((8, 2 * width), 0)
    lane = iota((8, 2 * width), 1)
    own = iota((8, 4 * width), 1) // width == iota((8, 4 * width), 0) % 4
    lefts, rights = [], []
    for batch in range(out.shape[0] // 8):
        where = slice(batch * 8, (batch + 1) * 8)
        left, right = [], []
        for shape in range(shapes):
            u, g = modes[shape, where], grads[shape, where]
            u_turned, g_turned = pltpu.roll(u, width, 1), pltpu.roll(g, width, 1)
            for part in (jnp.where(lane < width, u, u_turned), jnp.where(lane < width, u_turned, u)):
                left.append(jnp.where(own, jnp.concatenate([part] * 2, axis=1), 0.0))
            for part in (g, jnp.where(lane < width, g_turned, -g_turned)):
                pair = [jnp.where(row < 4, part, 0.0), jnp.where(row < 4, 0.0, part)]
                right.append(jnp.concatenate(pair, axis=1))
        left_high, left_low = halves(jnp.concatenate(left, axis=0))
        right_high, right_low = halves(jnp.concatenate(right, axis=0))
        lefts.append(jnp.concatenate([left_high, left_low, left_high], axis=0))
        rights.append(jnp.concatenate([right_high, right_high, right_low], axis=0))
    products = [dot(left, right, TN) for left, right in zip(lefts, rights)]
    for batch, product in enumerate(products):
        out[batch * 8 : batch * 8 + 4] = product[:, : 2 * width].reshape(4, width, 2 * width)
        out[batch * 8 + 4 : batch * 8 + 8] = product[:, 2 * width :].reshape(4, width, 2 * width)


def cell_sums(total, rows_here, width):
    hidden_sums, weight_sums = [], []
    for row in range(rows_here):
        slab = total[row * PLANE : (row + 1) * PLANE]
        hidden_sums.append(slab[:, :width] + slab[:, width : 2 * width])
        weight = slab[:, 2 * width + 4 : 2 * width + 5] + slab[:, 2 * width + 12 : 2 * width + 13]
        weight_sums.append(jnp.broadcast_to(weight, (PLANE, width)))
    return jnp.concatenate(hidden_sums, axis=1), jnp.concatenate(weight_sums, axis=1)


def grid_kernel(
    lines_far, reach_far, skip_far, proj_w, inverse_far, plane_far, after, plane_out, pre_bar_far, latent_far,
    lines, inverse, skip, reach, plane, latent, pre_bar, copied, *, rows_here,
):
    ends = [
        (lines_far, lines),
        (inverse_far, inverse),
        (skip_far, skip),
        (reach_far, reach),
        (plane_far, plane),
        (latent, latent_far),
        (pre_bar, pre_bar_far),
    ]
    copies = [pltpu.make_async_copy(*pair, copied.at[i]) for i, pair in enumerate(ends)]
    for copy in copies[:5]:
        copy.start()
    copies[0].wait()
    copies[1].wait()
    spectral = times_field(inverse, lines[...])
    copies[2].wait()
    value, slope = gelu_both(spectral + skip[...])
    latent[...] = value
    copies[5].start()
    copies[3].wait()
    bar = reach[...] * tile_lanes(proj_w[...], rows_here) * slope
    pre_bar[...] = bar
    copies[6].start()
    copies[4].wait()
    plane_out[...] = times_field(plane, bar)
    copies[5].wait()
    copies[6].wait()


def grid_grads_kernel(
    lat, pre_bar, latent, reach, sums, skip_w, dec_w2, dec_b2, proj_w,
    skip_w_grad, dec_w2_grad, rows_out, table, skip_back, *, rows_here, width,
):
    skip_back[...] = dot3(pre_bar[...], spread(skip_w[...], rows_here), NT)
    skip_w_grad[...] = gather_blocks(dot3(lat[...], pre_bar[...], TN), rows_here, width, width)
    scaled = latent[...] * tile_lanes(proj_w[...], rows_here)
    dec_w2_grad[...] = gather_blocks(dot3(sums[0], scaled, TN), rows_here, width, width)

    def column_sum(value):
        return fold_lanes(jnp.sum(value, axis=0, keepdims=True), rows_here, width)

    rows = [column_sum(pre_bar[...]), column_sum(sums[1] * scaled), column_sum(reach[...] * latent[...])]
    rows_out[...] = jnp.concatenate(rows + [jnp.zeros((5, width), F32)], axis=0)
    cell_kernel = dot3(scaled, spread(dec_w2[...], rows_here), NT)
    offset = scaled * tile_lanes(dec_b2[...], rows_here)
    cells = rows_here * PLANE
    table[cells:] = jnp.zeros((PAD, table.shape[1]), BF16)
    for row in range(rows_here):
        lanes = slice(row * width, (row + 1) * width)
        where = slice(row * PLANE, (row + 1) * PLANE)
        constant = jnp.sum(offset[:, lanes], axis=1, keepdims=True)
        high, low = halves(cell_kernel[:, lanes])
        c_high, c_low = halves(constant)
        lane = iota((PLANE, LANES), 1)
        tail = jnp.where(lane == 0, c_high.astype(F32), jnp.where(lane == 1, c_low.astype(F32), 0.0))
        table[where, : 2 * width] = jnp.concatenate([high.astype(F32), low.astype(F32)], axis=1).astype(BF16)
        table[where, 2 * width :] = tail.astype(BF16)


def input_columns(feats, cell, first_row):
    high, low = halves(feats)
    place = place_rows(cell, first_row)
    return jnp.concatenate([high.astype(F32), low.astype(F32), place, place], axis=0).astype(BF16)


def dec_edges_kernel(
    place_ref, bounds, keys, inverse_degree, saved, table, pred_out, w1_out, b1_out,
    found_scratch, pred_total, grad_total, *, owners, cells, width,
):
    step = pl.program_id(0)
    rows_here = cells // PLANE
    group = found_scratch.shape[1] // CHUNK
    first_row = place_ref[0] * rows_here
    shift = log2(owners * LANES)
    count8 = max(owners, 8)

    @pl.when(step == 0)
    def _():
        pred_total[...] = jnp.zeros_like(pred_total)
        grad_total[...] = jnp.zeros_like(grad_total)

    chunk = step * group
    per = CHUNK // keys.shape[1]

    def body(count):
        rows, key = joined_keys(keys, chunk, count)
        run = slice(0, count * CHUNK)
        gather_windows(
            found_scratch, keys, rows, table, bounds, 2, chunk, count, DEC_WINDOW, shift, 2 * width + 16
        )
        point = key & (owners * LANES - 1)
        found = found_scratch[:width, run] + found_scratch[width : 2 * width, run]
        constant = found_scratch[2 * width : 2 * width + 1, run] + found_scratch[2 * width + 1 : 2 * width + 2, run]
        edge = jnp.sum(saved[:width, run] * found, axis=0, keepdims=True) + constant
        owner = iota((count8, key.shape[1]), 0)
        high, low = halves(jnp.where(owner == (point >> 7), edge, 0.0))
        values = jnp.concatenate([high.astype(F32), low.astype(F32)], axis=0).astype(BF16)
        pred_total[...] += dot(values, one_hot(point & (LANES - 1), 0, LANES), NT)
        left = jnp.concatenate(halves(saved[width : 2 * width, run] * found), axis=0)
        right = input_columns(saved[2 * width :, run], key >> shift, first_row)
        grad_total[...] += dot(left, right, NT)

    each_size(bounds, 2, chunk, group, per, cells, body)

    @pl.when(step == pl.num_programs(0) - 1)
    def _():
        pred_out[...] = (pred_total[:owners] + pred_total[count8 : count8 + owners]) * inverse_degree[...]
        grad = grad_total[:width] + grad_total[width:]
        feats = (grad[:, :8] + grad[:, 8:16]).T
        places = grad[:, 16:24].T / (RES - 1.0)
        w1_out[...] = jnp.concatenate([feats[:3], places[:3]], axis=0)
        b1_out[...] = feats[3:4]


GRAD_ROWS = 108
PACKED_ROWS = 120


def enc_back_kernel(
    place_ref, bounds, keys, saved_hbm, lines_far, skip_far, scale_far, w2, lift_w, pred_bar,
    skip_w_grad, dec_w2_grad, row_grads, pred_part, dec_w1_grad, dec_b1_grad, inverse_hbm,
    *refs, owners, cells, width,
):
    packed, table, found_scratch, second, lifts, feat_total, grad_total, inverse, lines, skip, scale, copied, slots, loaded = refs[-14:]
    rows_here = cells // PLANE
    group = found_scratch.shape[1] // CHUNK
    first_row = place_ref[0] * rows_here
    shift = log2(owners * LANES)
    count8 = max(owners, 8)
    per = CHUNK // keys.shape[1]
    load = slot_copies(saved_hbm, slots, loaded, out=False)
    steps = keys.shape[0] * keys.shape[1] // slots.shape[2]

    def load_used(at):
        @pl.when(at < steps)
        def _():
            first_cell, _ = cell_range(bounds, 0, jnp.minimum(at, steps - 1) * group, per)

            @pl.when(first_cell < cells)
            def _():
                load(at).start()

    def begin():
        ends = [(lines_far, lines), (inverse_hbm, inverse), (skip_far, skip), (scale_far, scale)]
        copies = [pltpu.make_async_copy(*pair, copied.at[i]) for i, pair in enumerate(ends)]
        for copy in copies:
            copy.start()
        feat_total[...] = jnp.zeros_like(feat_total)
        grad_total[...] = jnp.zeros_like(grad_total)
        second[...] = weights3(w2[...])
        high, low = halves(jnp.concatenate([lift_w[...], jnp.zeros((4, width), F32)], axis=0))
        rows = jnp.concatenate([high.astype(F32), low.astype(F32)], axis=0)
        lifts[...] = jnp.concatenate([rows, rows], axis=1).astype(BF16)
        copies[0].wait()
        copies[1].wait()
        load_used(0)
        field = times_field(inverse, lines[...])
        copies[2].wait()
        copies[3].wait()
        field = (field + skip[...]) * scale[...]
        table[cells:] = jnp.zeros((PAD, 2 * width), BF16)
        for row in range(rows_here):
            high, low = halves(field[:, row * width : (row + 1) * width])
            both = jnp.concatenate([high.astype(F32), low.astype(F32)], axis=1).astype(BF16)
            table[row * PLANE : (row + 1) * PLANE] = both
        load_used(1)

    def run_step(step, carry):
        chunk = step * group

        def body(count):
            rows, key = joined_keys(keys, chunk, count)
            run = slice(0, count * CHUNK)
            gather_windows(
                found_scratch, keys, rows, table, bounds, 0, chunk, count, ENC_WINDOW, shift, 2 * width
            )
            load(step).wait()
            saved = slots.at[step % 2]
            point = key & (owners * LANES - 1)
            found = found_scratch[:width, run] + found_scratch[width:, run]
            source_bar = found * saved[3 * width : 4 * width, run]
            k_high, k_low = halves(found * saved[2 * width : 3 * width, run])
            hidden_bar = dot(second[...], jnp.concatenate([k_high, k_low, k_high], axis=0))
            pre_edge = hidden_bar * saved[width : 2 * width, run]
            source_parts = halves(source_bar)
            parts = [*halves(saved[:width, run]), *halves(pre_edge), *source_parts]
            left = jnp.concatenate(parts + [jnp.ones((16, count * CHUNK), BF16)], axis=0)
            tail = input_columns(saved[4 * width :, run], key >> shift, first_row)
            grad_total[...] += dot(left, jnp.concatenate([k_high, k_low, tail], axis=0), NT)
            owner_hot = iota((count8, count * CHUNK), 0) == (point >> 7)
            both = dot(lifts[...], jnp.concatenate(source_parts, axis=0))
            both = both[:8] + both[8:]
            edges = [jnp.where(owner_hot, both[feat : feat + 1], 0.0) for feat in range(4)]
            values = jnp.concatenate(halves(jnp.concatenate(edges, axis=0)), axis=0)
            feat_total[...] += dot(values, one_hot(point & (LANES - 1), 0, LANES), NT)
            load_used(step + 2)

        each_size(bounds, 0, chunk, group, per, cells, body)
        return carry

    begin()
    lax.fori_loop(0, used_steps(bounds, 0, group, per, cells, steps), run_step, 0)
    def end():
        w2_part = grad_total[:width, : 2 * width] + grad_total[width : 2 * width, : 2 * width]
        w2_grad = w2_part[:, :width] + w2_part[:, width:]
        b2_part = grad_total[6 * width : 6 * width + 1, : 2 * width]
        b2_grad = b2_part[:, :width] + b2_part[:, width:]
        pre_part = grad_total[2 * width : 3 * width, 2 * width :] + grad_total[3 * width : 4 * width, 2 * width :]
        feats = (pre_part[:, :8] + pre_part[:, 8:16]).T
        places = pre_part[:, 16:24].T / (RES - 1.0)
        lift_part = grad_total[4 * width : 5 * width, 2 * width :] + grad_total[5 * width : 6 * width, 2 * width :]
        lifts = (lift_part[:, :8] + lift_part[:, 8:16]).T
        pair = partial(jnp.concatenate, axis=1)
        stack = partial(jnp.concatenate, axis=0)
        half = width // 2
        bar_sum = jnp.broadcast_to(jnp.sum(pred_bar[...], axis=1, keepdims=True), (1, width))
        fixed = stack(
            [
                pair([w2_grad, dec_w2_grad[...]]),
                pair([skip_w_grad[:half], skip_w_grad[half:]]),
                pair([stack([places[:3], feats[:3]]), dec_w1_grad[...]]),
                pair([feats[3:4], dec_b1_grad[...]]),
                pair([b2_grad, row_grads[1:2]]),
                pair([lifts[4:8], stack([lifts[3:4], row_grads[0:1], row_grads[2:3], bar_sum])]),
            ]
        )
        both = feat_total[: 4 * count8] + feat_total[4 * count8 :]
        empty = jnp.zeros((PACKED_ROWS - GRAD_ROWS - 5, LANES), F32)
        for owner in range(owners):
            rows = [both[feat * count8 + owner : feat * count8 + owner + 1] for feat in range(4)]
            packed[owner] = stack([fixed] + rows + [pred_part[owner : owner + 1], empty])

    end()


def arrive_kernel(arrived, proj_b, after, grads, feat_grad, pred, *, owners):
    total = arrived[0]
    for owner in range(1, owners):
        total = total + arrived[owner]
    grads[...] = total[:GRAD_ROWS]
    feat_grad[...] = total[GRAD_ROWS : GRAD_ROWS + 4]
    pred[...] = total[GRAD_ROWS + 4 : GRAD_ROWS + 5] + proj_b[...]


def leave_kernel(*refs, shapes, width):
    half = width // 2
    terms = [ref[...] for ref in refs[:shapes]]
    while len(terms) > 1:
        terms = [terms[i] + terms[i + 1] for i in range(0, len(terms), 2)]
    left, right = terms[0][:, :width], terms[0][:, width:]
    outs = refs[shapes:]
    at = width + half
    enc_w1, enc_b1, enc_w2, enc_b2, lift_w, lift_b, skip_w, skip_b, dec_w1, dec_b1, dec_w2, dec_b2, proj_w, proj_b = outs
    enc_w2[...] = left[:width]
    dec_w2[...] = right[:width]
    skip_w[:half] = left[width:at]
    skip_w[half:] = right[width:at]
    enc_w1[...] = left[at : at + 6]
    dec_w1[...] = right[at : at + 6]
    enc_b1[...] = left[at + 6 : at + 7]
    dec_b1[...] = right[at + 6 : at + 7]
    enc_b2[...] = left[at + 7 : at + 8]
    dec_b2[...] = right[at + 7 : at + 8]
    lift_w[...] = left[at + 8 : at + 12]
    lift_b[...] = right[at + 8 : at + 9]
    skip_b[...] = right[at + 9 : at + 10]
    proj_w[...] = right[at + 10 : at + 11]
    proj_b[...] = right[at + 11 : at + 12, :1]


def shape(*dims, dtype=F32):
    return jax.ShapeDtypeStruct(dims, dtype)


def whole(array):
    zeros = (0,) * array.ndim
    return pl.BlockSpec(array.shape, lambda i: zeros, pipeline_mode=pl.Buffered(1))


HELD = VMEM
VMEM_BYTES = 65280 << 10
FAR = pl.BlockSpec(memory_space=pl.ANY)


def kernel_call(kernel, name, steps, operands, out_shape, out_specs, scratch=(), micros=10, **more):
    arrays = [array for array, _ in operands]
    specs = [whole(array) if spec is None else spec for array, spec in operands]
    return pl.pallas_call(
        kernel,
        grid=(steps,),
        in_specs=specs,
        out_specs=out_specs,
        out_shape=out_shape,
        scratch_shapes=list(scratch),
        compiler_params=pltpu.CompilerParams(vmem_limit_bytes=VMEM_BYTES),
        cost_estimate=pl.CostEstimate(flops=0, bytes_accessed=micros * 2_000_000, transcendentals=0),
        name=name,
        **more,
    )(*arrays)


def on_device(
    mesh_feat,
    mesh_pos,
    query_pos,
    enc_cell,
    enc_point,
    enc_count,
    dec_cell,
    dec_query,
    dec_count,
    enc_w1,
    enc_b1,
    enc_w2,
    enc_b2,
    lift_w,
    lift_b,
    spec_w,
    skip_w,
    skip_b,
    dec_w1,
    dec_b1,
    dec_w2,
    dec_b2,
    proj_w,
    proj_b,
    pred_bar,
):
    width = lift_w.shape[1]
    owners = lax.axis_size("wide")
    shapes = lax.axis_size("grid")
    rows_here = RES // owners
    cells = rows_here * PLANE
    modes_here = spec_w.shape[0]
    lines = modes_here // MODES
    enc_blocks, dec_blocks = enc_cell.shape[1], dec_cell.shape[1]
    enc_edges, dec_edges = enc_blocks * LANES, dec_blocks * LANES
    enc_span, dec_span = ENC_GROUP * CHUNK, DEC_GROUP * CHUNK
    lanes = rows_here * width
    place = lax.axis_index("wide").astype(jnp.int32).reshape(1)
    plane_np = plane_matrix(owners)
    plane = jnp.asarray(np.stack(halves_np(plane_np)))
    inverse = jnp.asarray(np.stack(halves_np(np.ascontiguousarray(plane_np.T))))
    cos_x, sin_x = (jnp.asarray(part) for part in x_tables(rows_here, width))
    rows = [value.reshape(1, -1) for value in (enc_b1, enc_b2, lift_b, skip_b, dec_b1, dec_b2, proj_w, proj_b)]
    enc_b1, enc_b2, lift_b, skip_b, dec_b1, dec_b2, proj_w, proj_b = rows
    sizes = dict(owners=owners, cells=cells, width=width)
    dma = pltpu.SemaphoreType.DMA

    def exchange(value):
        return lax.all_to_all(value, "wide", 0, 0, tiled=True)

    payload = kernel_call(
        partial(share_kernel, owners=owners),
        "share_points",
        1,
        [
            (value, None)
            for value in (
                mesh_feat, mesh_pos.transpose(1, 0, 2), query_pos.transpose(1, 0, 2), pred_bar, dec_query[0], dec_count
            )
        ],
        shape(owners, 2 * FEAT_ROWS + owners, LANES),
        HELD,
    )
    shared = exchange(payload)
    local = [enc_cell[0], enc_point[0], enc_count, dec_cell[0], dec_query[0], dec_count]
    enc_keys, dec_keys, bounds = kernel_call(
        partial(sort_kernel, owners=owners, cells=cells),
        "sort_edges",
        1,
        [(value, None) for value in local] + [(payload, FAR)],
        [
            shape(LANES, enc_blocks, dtype=jnp.int32),
            shape(LANES, dec_blocks, dtype=jnp.int32),
            shape(8, LANES, dtype=jnp.int32),
        ],
        [HELD] * 3,
    )

    fixed = owners * FEAT_ROWS
    saved_rows = 4 * width + FEAT_ROWS
    plane_scratch = pltpu.VMEM((2, 2 * MODES * MODES, PLANE), BF16)
    inverse_scratch = pltpu.VMEM((2, PLANE, 2 * MODES * MODES), BF16)
    saved, lat, scale, plane_lat = kernel_call(
        partial(enc_forward_kernel, **sizes),
        "encode",
        1,
        [(place, SMEM), (bounds, SMEM), (enc_keys, HELD), (shared, HELD)]
        + [(value, None) for value in (enc_w1, enc_b1, enc_w2, enc_b2, lift_w, lift_b)]
        + [(plane, FAR)],
        [
            shape(saved_rows, enc_edges),
            shape(PLANE, lanes),
            shape(PLANE, lanes),
            shape(2 * MODES * MODES, lanes),
        ],
        [FAR, FAR, FAR, HELD],
        [
            pltpu.VMEM((cells + PAD, 2 * LANES), F32),
            pltpu.VMEM((2 * fixed, LANES), BF16),
            pltpu.VMEM((2 * width, INPUT_ROWS), BF16),
            pltpu.VMEM((width, 3 * width), BF16),
            pltpu.VMEM((2 * width + 16, enc_span), BF16),
            plane_scratch,
            pltpu.VMEM((PLANE, lanes), F32),
            pltpu.VMEM((PLANE, lanes), F32),
            dma((3,)),
            pltpu.VMEM((2, saved_rows, enc_span), F32),
            dma((2,)),
        ],
    )
    modes_lines = exchange(plane_lat.reshape(owners, 2 * lines, lanes))

    dec_rows = 2 * width + FEAT_ROWS
    dec_steps = dec_edges // dec_span
    half_steps = dec_steps // 2

    def dec_sums(first_step, steps, before, saved_before, after, more, out_shape, scratch, name):
        return kernel_call(
            partial(dec_sums_kernel, first_step=first_step, **sizes),
            name,
            steps,
            [
                (place, SMEM), (bounds, SMEM), (dec_keys, HELD), (shared, HELD), (dec_w1, None), (dec_b1, None),
                (before, HELD if first_step else FAR), (saved_before, FAR), (after, FAR),
            ]
            + more,
            [shape(dec_rows, dec_edges)] + out_shape,
            [pl.BlockSpec((dec_rows, dec_span), lambda i: (0, i + first_step))] + [HELD] * len(out_shape),
            scratch
            + [
                pltpu.VMEM((2 * fixed, LANES), BF16),
                pltpu.VMEM((width, INPUT_ROWS), BF16),
                pltpu.VMEM((2 * width + 16, dec_span), BF16),
            ],
            input_output_aliases={7: 0} if first_step else {},
        )

    dec_saved, dec_total, inverse_degree, skip = dec_sums(
        0, half_steps, plane_lat, plane_lat, plane_lat, [(lat, HELD), (skip_w, None), (skip_b, None)],
        [shape(cells + PAD, 2 * LANES), shape(owners, LANES), shape(PLANE, lanes)], [], "decode_sums_a",
    )

    mix_step, grad_step = min(MIX_STEP, modes_here), min(GRAD_STEP, modes_here)

    def spec_block(step):
        return pl.BlockSpec((step, width, 2 * width), lambda i: (i, 0, 0))

    def mode_pass(kernel, lines_in, after, name):
        return kernel_call(
            partial(kernel, owners=owners, width=width),
            name,
            1,
            [(place, SMEM), (lines_in, HELD), (cos_x, None), (sin_x, None), (spec_w, FAR)]
            + [(value, FAR) for value in after],
            [shape(modes_here, 2 * width), shape(owners, 2 * lines, lanes)],
            [HELD, HELD],
            [
                pltpu.VMEM((modes_here, 2 * width), F32),
                pltpu.VMEM((modes_here, width, 2 * width), F32),
                dma((modes_here // mix_step,)),
            ],
        )

    modes, back_lines = mode_pass(mix_kernel, modes_lines, [inverse_degree], "mix_modes")
    def from_shapes(value, staged=True):
        parts, step = {0: value}, shapes // 2
        if staged:
            while step:
                pairs = [(i, i ^ step) for i in range(shapes)]
                parts.update({d ^ step: lax.ppermute(part, "grid", pairs) for d, part in parts.items()})
                step //= 2
        else:
            for step in range(1, shapes):
                parts[step] = lax.ppermute(value, "grid", [(i, i ^ step) for i in range(shapes)])
        return [parts[d] for d in range(shapes)]

    all_modes = from_shapes(modes)
    grid_lines = exchange(back_lines).reshape(2 * MODES * MODES, lanes)
    dec_saved, sums, reach = dec_sums(
        half_steps, dec_steps - half_steps, dec_total, dec_saved, back_lines,
        [(dec_w2, None), (dec_b2, None)],
        [shape(2, PLANE, lanes), shape(PLANE, lanes)],
        [pltpu.VMEM((cells + PAD, 2 * LANES), F32)],
        "decode_sums_b",
    )

    plane_bar, pre_bar, latent = kernel_call(
        partial(grid_kernel, rows_here=rows_here),
        "grid_fields",
        1,
        [(grid_lines, FAR), (reach, FAR), (skip, FAR), (proj_w, None), (inverse, FAR), (plane, FAR)]
        + [(value, FAR) for value in all_modes[shapes // 2 :][:1]],
        [shape(2 * MODES * MODES, lanes)] + [shape(PLANE, lanes)] * 2,
        [HELD, FAR, FAR],
        [
            pltpu.VMEM((2 * MODES * MODES, lanes), F32),
            inverse_scratch,
            pltpu.VMEM((PLANE, lanes), F32),
            pltpu.VMEM((PLANE, lanes), F32),
            plane_scratch,
            pltpu.VMEM((PLANE, lanes), F32),
            pltpu.VMEM((PLANE, lanes), F32),
            dma((7,)),
        ],
    )
    bar_lines = exchange(plane_bar.reshape(owners, 2 * lines, lanes))

    skip_w_grad, dec_w2_grad, row_grads, dec_table, skip_back = kernel_call(
        partial(grid_grads_kernel, rows_here=rows_here, width=width),
        "grid_grads",
        1,
        [(value, HELD) for value in (lat, pre_bar, latent, reach, sums)]
        + [(value, None) for value in (skip_w, dec_w2, dec_b2, proj_w)],
        [
            shape(width, width),
            shape(width, width),
            shape(8, width),
            shape(cells + PAD, 2 * LANES, dtype=BF16),
            shape(PLANE, lanes),
        ],
        [HELD] * 5,
    )

    mixed_bar, bar_back = mode_pass(mix_back_kernel, bar_lines, [row_grads] + all_modes[1:], "mix_back")
    bar_grid_lines = exchange(bar_back).reshape(2 * MODES * MODES, lanes)

    all_grads = from_shapes(mixed_bar)

    count8 = max(owners, 8)
    pred_part, dec_w1_grad, dec_b1_grad = kernel_call(
        partial(dec_edges_kernel, **sizes),
        "decode_edges",
        dec_steps,
        [
            (place, SMEM), (bounds, SMEM), (dec_keys, HELD), (inverse_degree, HELD),
            (dec_saved, pl.BlockSpec((dec_rows, dec_span), lambda i: (0, i))), (dec_table, HELD),
        ],
        [shape(owners, LANES), shape(6, width), shape(1, width)],
        [HELD] * 3,
        [
            pltpu.VMEM((2 * width + 16, dec_span), F32),
            pltpu.VMEM((2 * count8, LANES), F32),
            pltpu.VMEM((2 * width, 32), F32),
        ],
    )

    packed = kernel_call(
        partial(enc_back_kernel, **sizes),
        "encode_back",
        1,
        [(place, SMEM), (bounds, SMEM), (enc_keys, HELD), (saved, FAR)]
        + [(value, FAR) for value in (bar_grid_lines, skip_back, scale)]
        + [(value, None) for value in (enc_w2, lift_w, pred_bar)]
        + [(value, HELD) for value in (skip_w_grad, dec_w2_grad, row_grads, pred_part, dec_w1_grad, dec_b1_grad)]
        + [(inverse, FAR)]
        + [(value, FAR) for value in all_grads[shapes // 2 :][:1]],
        shape(owners, PACKED_ROWS, LANES),
        HELD,
        [
            pltpu.VMEM((cells + PAD, 2 * width), BF16),
            pltpu.VMEM((2 * width, enc_span), F32),
            pltpu.VMEM((width, 3 * width), BF16),
            pltpu.VMEM((16, 2 * width), BF16),
            pltpu.VMEM((8 * count8, LANES), F32),
            pltpu.VMEM((6 * width + 16, 2 * width + 32), F32),
            inverse_scratch,
            pltpu.VMEM((2 * MODES * MODES, lanes), F32),
            pltpu.VMEM((PLANE, lanes), F32),
            pltpu.VMEM((PLANE, lanes), F32),
            dma((4,)),
            pltpu.VMEM((2, saved_rows, enc_span), F32),
            dma((2,)),
        ],
    )
    arrived = exchange(packed)

    rank = lax.axis_index("grid").astype(jnp.int32).reshape(1)
    spec_grad = kernel_call(
        partial(spec_grad_kernel, shapes=shapes, width=width),
        "spec_grad",
        modes_here // grad_step,
        [(rank, SMEM)]
        + [
            (value, pl.BlockSpec((grad_step, 2 * width), lambda i: (i, 0)))
            for value in all_modes + all_grads
        ]
        + [(packed, FAR)],
        shape(modes_here, width, 2 * width),
        spec_block(grad_step),
        [pltpu.VMEM((shapes, grad_step, 2 * width), F32)] * 2,
    )

    grads, feat_grad, pred = kernel_call(
        partial(arrive_kernel, owners=owners),
        "arrive",
        1,
        [(arrived, HELD), (proj_b, None), (spec_grad, FAR)],
        [shape(GRAD_ROWS, LANES), shape(4, LANES), shape(1, LANES)],
        [HELD] * 3,
    )
    terms = from_shapes(grads, staged=False)
    vector = shape(1, width)
    square = shape(width, width)
    first = shape(6, width)
    outs = kernel_call(
        partial(leave_kernel, shapes=shapes, width=width),
        "leave",
        1,
        [(term, HELD) for term in terms],
        [
            first, vector, square, vector, shape(4, width), vector,
            square, vector, first, vector, square, vector, vector, shape(1, 1),
        ],
        [HELD] * 14,
    )
    outs = [out.reshape(-1) if out.shape[0] == 1 else out for out in outs]
    return (pred, feat_grad[None], *outs[:6], spec_grad, *outs[6:])


def solution(mesh):
    placed = (
        P("grid", None, "wide"),
        P("grid", None, "wide"),
        P("grid", None, "wide"),
        P("grid", "wide", None),
        P("grid", "wide", None),
        P("grid", "wide"),
        P("grid", "wide", None),
        P("grid", "wide", None),
        P("grid", "wide"),
        P(),
        P(),
        P(),
        P(),
        P(),
        P(),
        P("wide", None, None),
        P(),
        P(),
        P(),
        P(),
        P(),
        P(),
        P(),
        P(),
        P("grid", "wide"),
    )
    return jax.shard_map(
        on_device,
        mesh=mesh,
        in_specs=placed,
        out_specs=(
            P("grid", "wide"),
            P("grid", None, "wide"),
            P(),
            P(),
            P(),
            P(),
            P(),
            P(),
            P("wide", None, None),
            P(),
            P(),
            P(),
            P(),
            P(),
            P(),
            P(),
            P(),
        ),
        check_vma=False,
    )
```

```python
from functools import partial
import math

import jax
import jax.numpy as jnp
import ml_dtypes
import numpy as np
from jax import lax
from jax.experimental import pallas as pl
from jax.experimental.pallas import tpu as pltpu
from jax.sharding import PartitionSpec as P

MODES = 16
RES = 32
PLANE = RES * RES
ENC_CELLS = RES * (RES - RES // 4)
CHUNK = 256
LANES = 128
ENC_GROUP = 16
DEC_GROUP = 16
FEW = 4
FEAT_ROWS = 8
INPUT_ROWS = 48
ENC_WINDOW = 64
DEC_WINDOW = 128
PAD = 256
MIX_STEP = 64
GRAD_STEP = 128
F32 = jnp.float32
BF16 = jnp.bfloat16
GELU_A = 0.7978845608028654
GELU_B = 0.044715

NN = (((1,), (0,)), ((), ()))
NT = (((1,), (1,)), ((), ()))
TN = (((0,), (0,)), ((), ()))

VMEM = pl.BlockSpec(memory_space=pltpu.VMEM)
SMEM = pl.BlockSpec(memory_space=pltpu.SMEM)


def kept_freqs():
    half = MODES // 2
    return np.concatenate([np.arange(half), np.arange(RES - half, RES)])


def plane_matrix(owners):
    lines = MODES * MODES // owners
    line = np.arange(MODES * MODES)
    freq_y, freq_z = kept_freqs()[line // MODES], line % MODES
    cell = np.arange(PLANE)
    turns = (freq_y[:, None] * (cell // RES) + freq_z[:, None] * (cell % RES)) % RES
    angle = turns * (2.0 * math.pi / RES)
    both = np.stack([np.cos(angle), -np.sin(angle)]).reshape(2, owners, lines, PLANE)
    matrix = both.transpose(1, 0, 2, 3).reshape(2 * MODES * MODES, PLANE)
    return matrix.astype(np.float32)


def halves_np(matrix):
    high = matrix.astype(ml_dtypes.bfloat16)
    low = (matrix - high.astype(np.float32)).astype(ml_dtypes.bfloat16)
    return high, low


def line_angles():
    turns = (kept_freqs()[:, None] * np.arange(RES)[None, :]) % RES
    return turns * (2.0 * math.pi / RES)


def x_tables(rows_here, width):
    angle = line_angles().reshape(MODES, RES // rows_here, rows_here, 1)
    angle = np.broadcast_to(angle, (MODES, RES // rows_here, rows_here, width))
    angle = angle.reshape(MODES, RES // rows_here, rows_here * width)
    return np.cos(angle).astype(np.float32), np.sin(angle).astype(np.float32)


def log2(number):
    return number.bit_length() - 1


def iota(shape, axis):
    return lax.broadcasted_iota(jnp.int32, shape, axis)


def halves(value):
    high = value.astype(BF16)
    low = (value - high.astype(F32)).astype(BF16)
    return high, low


def dot(a, b, dims=NN):
    return lax.dot_general(a, b, dims, preferred_element_type=F32)


def dot3(a, b, dims=NN):
    a_high, a_low = halves(a)
    b_high, b_low = halves(b)
    return dot(a_high, b_high, dims) + dot(a_low, b_high, dims) + dot(a_high, b_low, dims)


def one_hot(index, first, rows):
    places = iota((rows, index.shape[1]), 0)
    return jnp.where(places == index - first, 1.0, 0.0).astype(BF16)


def gelu_both(value):
    square = value * value
    half = 0.5 + 0.5 * jnp.tanh(value * (GELU_A + (GELU_A * GELU_B) * square))
    out = value * half
    return out, half + (out - out * half) * (2.0 * GELU_A + (6.0 * GELU_A * GELU_B) * square)


def sort_columns(values):
    rows = values.shape[0]
    regs = rows // 8
    low = log2(regs)
    total = low + 3 + 7
    sub = iota((8, LANES), 0)
    lane = iota((8, LANES), 1)
    x = values.reshape(regs, 8, LANES)

    def flip(x, bit):
        if bit >= total:
            return x
        if bit < low:
            y = x.reshape(regs >> (bit + 1), 2, 1 << bit, 8, LANES)
            return jnp.stack([y[:, 0], -y[:, 1]], axis=1).reshape(regs, 8, LANES)
        if bit < low + 3:
            sign = 1 - 2 * ((sub >> (bit - low)) & 1)
        else:
            sign = 1 - 2 * ((lane >> (bit - low - 3)) & 1)
        return x * sign.astype(F32)[None]

    def exchange(x, bit):
        if bit < low:
            y = x.reshape(regs >> (bit + 1), 2, 1 << bit, 8, LANES)
            one, two = y[:, 0], y[:, 1]
            pair = [jnp.minimum(one, two), jnp.maximum(one, two)]
            return jnp.stack(pair, axis=1).reshape(regs, 8, LANES)
        if bit < low + 3:
            axis, dist, size, place = 1, 1 << (bit - low), 8, sub
        else:
            axis, dist, size, place = 2, 1 << (bit - low - 3), LANES, lane
        after = pltpu.roll(x, size - dist, axis)
        before = after if 2 * dist == size else pltpu.roll(x, dist, axis)
        first = ((place & dist) == 0)[None]
        return jnp.where(first, jnp.minimum(x, after), jnp.maximum(x, before))

    for phase in range(1, total + 1):
        x = flip(x, phase)
        for bit in reversed(range(phase)):
            x = exchange(x, bit)
        x = flip(x, phase)
    return x.reshape(rows, LANES)


def layer_matrix(feat_rows, cell_rows):
    feat_high, feat_low = halves(feat_rows)
    cell_high, cell_low = halves(cell_rows)
    parts = [feat_high, feat_high, feat_low, cell_high, cell_low]
    parts = [part.astype(F32) for part in parts] + [jnp.zeros((LANES - 40, feat_rows.shape[1]), F32)]
    return jnp.concatenate(parts, axis=0).T[:, :INPUT_ROWS].astype(BF16)


def place_rows(cell, first_row):
    row = iota((8, cell.shape[1]), 0)
    shifts = jnp.where(row == 0, 2 * log2(RES), jnp.where(row == 1, log2(RES), 0))
    place = (cell >> shifts) & jnp.where(row < 3, RES - 1, 0)
    return (place + jnp.where(row == 0, first_row, 0)).astype(F32)


def edge_feats(key, table, owners):
    point = key & (owners * LANES - 1)
    found = dot(table, one_hot(point & (LANES - 1), 0, LANES))
    owner = (iota(found.shape, 0) >> 3) & (owners - 1)
    found = jnp.where(owner == (point >> 7), found, 0.0)
    return jnp.sum(found.reshape(2 * owners, FEAT_ROWS, key.shape[1]), axis=0)


def stack_inputs(feats, place):
    high, low = halves(feats)
    parts = [high.astype(F32), low.astype(F32), high.astype(F32), place, place, jnp.zeros_like(place)]
    return jnp.concatenate(parts, axis=0).astype(BF16)


def stack3(value):
    high, low = halves(value)
    return jnp.concatenate([high, low, high], axis=0)


def weights3(matrix):
    high, low = halves(matrix)
    return jnp.concatenate([high, high, low], axis=1)


def key_row(keys_ref, chunk):
    per = CHUNK // keys_ref.shape[1]
    rows = [keys_ref[pl.ds(chunk * per + i, 1), :] for i in range(per)]
    return rows[0] if per == 1 else jnp.concatenate(rows, axis=1)


def cell_range(bounds_ref, line, chunk, per):
    return bounds_ref[line, chunk * per], bounds_ref[line + 1, chunk * per + per - 1]


def spread(block, copies):
    rows, columns = block.shape
    tiled = jnp.concatenate([jnp.concatenate([block] * copies, axis=1)] * copies, axis=0)
    return jnp.where(
        iota(tiled.shape, 0) // rows == iota(tiled.shape, 1) // columns, tiled, 0.0
    )


def gather_blocks(product, copies, rows, columns):
    total = product[:rows, :columns]
    for i in range(1, copies):
        total = total + product[i * rows : (i + 1) * rows, i * columns : (i + 1) * columns]
    return total


def tile_lanes(row, copies):
    return row if copies == 1 else jnp.concatenate([row] * copies, axis=1)


def fold_lanes(row, copies, width):
    total = row[:, :width]
    for i in range(1, copies):
        total = total + row[:, i * width : (i + 1) * width]
    return total


def column(counts):
    return jnp.broadcast_to(counts, (8, counts.shape[1])).T[:, :1]


def share_kernel(feat, pos, query_pos, pred_bar, dec_query, dec_count, payload, *, owners):
    blocks = dec_query.shape[0]
    lane_valid = jnp.where(
        iota((blocks, LANES), 1) < column(dec_count[...]), dec_query[...], owners * LANES
    )
    ones = jnp.zeros((max(owners, 16), LANES), F32)
    degree = ones
    for block in range(0, blocks, 2):
        row = jnp.concatenate([lane_valid[block : block + 1], lane_valid[block + 1 : block + 2]], axis=1)
        high = one_hot(row >> 7, 0, ones.shape[0])
        low = one_hot(row & (LANES - 1), 0, LANES)
        degree = degree + dot(high, low, NT)
    filled = jnp.ones((1, LANES), F32)
    empty = jnp.zeros((3, LANES), F32)
    places = [pos[i] for i in range(3)]
    queries = [query_pos[i] for i in range(3)]
    rows = places + [filled, feat[0]] + queries + [filled, pred_bar[...], empty, degree[:owners]]
    mine = jnp.concatenate(rows, axis=0)
    for owner in range(owners):
        payload[owner] = mine


def sort_kernel(
    enc_cell, enc_point, enc_count, dec_cell, dec_query, dec_count, after,
    enc_keys, dec_keys, bounds, *, owners, cells,
):
    shift = log2(owners * LANES)

    def keys(cell, point, count):
        lane = iota(cell.shape, 1)
        key = jnp.where(lane < column(count), (cell << shift) | point, cells << shift)
        return sort_columns(key.astype(F32)).astype(jnp.int32)

    enc = keys(enc_cell[...], enc_point[...], enc_count[...])
    dec = keys(dec_cell[...], dec_query[...], dec_count[...])
    enc_keys[...] = enc.T
    dec_keys[...] = dec.T
    ends = [enc[:1], enc[-1:], dec[:1], dec[-1:]]
    bounds[...] = jnp.concatenate(ends + [jnp.zeros((4, LANES), jnp.int32)], axis=0) >> shift


def joined_keys(keys, chunk, group):
    rows = [key_row(keys, chunk + i) for i in range(group)]
    return rows, jnp.concatenate(rows, axis=1)


def later_windows(windows, size, visit):
    most = windows[0][1]
    for _, count in windows[1:]:
        most = jnp.maximum(most, count)

    @pl.when(most > 1)
    def _():
        for i, (begin, count) in enumerate(windows):

            def more(j, carry):
                visit(i, begin + j * size)
                return carry

            lax.fori_loop(1, count, more, 0)


def scatter_windows(total, keys, cell, message, bounds, line, chunk, group, size, shift, columns):
    per = CHUNK // keys.shape[1]
    windows, parts = [], []
    for i in range(group):
        begin, end = cell_range(bounds, line, chunk + i, per)
        begin = pl.multiple_of(begin & -8, 8)
        lanes = slice(i * CHUNK, (i + 1) * CHUNK)
        parts.append(dot(one_hot(cell[:, lanes], begin, size), message[:, lanes], NT))
        windows.append((begin, (end - begin) // size + 1))
    for (begin, _), part in zip(windows, parts):
        total[pl.ds(begin, size), :columns] += part

    def visit(i, start):
        start = pl.multiple_of(start, 8)
        hot = one_hot(key_row(keys, chunk + i) >> shift, start, size)
        part = dot(hot, message[:, i * CHUNK : (i + 1) * CHUNK], NT)
        total[pl.ds(start, size), :columns] += part

    later_windows(windows, size, visit)


def gather_windows(found, keys, rows, table, bounds, line, chunk, group, size, shift, columns):
    per = CHUNK // keys.shape[1]
    windows = []
    for i in range(group):
        begin, end = cell_range(bounds, line, chunk + i, per)
        begin = pl.multiple_of(begin & -16, 16)
        hot = one_hot(rows[i] >> shift, begin, size)
        found[:, i * CHUNK : (i + 1) * CHUNK] = dot(table[pl.ds(begin, size), :columns], hot, TN)
        windows.append((begin, (end - begin) // size + 1))

    def visit(i, start):
        start = pl.multiple_of(start, 16)
        hot = one_hot(key_row(keys, chunk + i) >> shift, start, size)
        part = dot(table[pl.ds(start, size), :columns], hot, TN)
        found[:, i * CHUNK : (i + 1) * CHUNK] += part

    later_windows(windows, size, visit)


def slot_copies(far, slots, semaphores, out):
    span = slots.shape[2]

    def copy(step):
        slot = step % 2
        columns = far.at[:, pl.ds(pl.multiple_of(step * span, span), span)]
        ends = (slots.at[slot], columns) if out else (columns, slots.at[slot])
        return pltpu.make_async_copy(*ends, semaphores.at[slot])

    return copy


def used_steps(bounds, line, group, per, cells, steps):
    used = 0
    for step in range(steps):
        used = used + jnp.where(bounds[line, step * group * per] < cells, 1, 0)
    return used


def each_size(bounds, line, chunk, group, per, cells, body):
    few = min(FEW, group)
    some = bounds[line, chunk * per] < cells
    if few == group:
        pl.when(some)(lambda: body(group))
        return
    many = bounds[line, (chunk + few) * per] < cells
    pl.when(many)(lambda: body(group))
    pl.when(some & jnp.logical_not(many))(lambda: body(few))


def enc_forward_kernel(
    place_ref, bounds, keys, shared, w1, b1, w2, b2, lift_w, lift_b, plane_hbm,
    saved_hbm, lat_far, scale_far, plane_out,
    total, table, first, second, message, plane, lat, scale, copied, slots, stored,
    *, owners, cells, width,
):
    rows_here = cells // PLANE
    group = message.shape[1] // CHUNK
    shift = log2(owners * LANES)
    first_row = place_ref[0] * rows_here
    copy = pltpu.make_async_copy(plane_hbm, plane, copied.at[0])
    save = slot_copies(saved_hbm, slots, stored, out=True)

    def begin():
        copy.start()
        total[...] = jnp.zeros_like(total)
        feats = jnp.concatenate([shared[i, :FEAT_ROWS] for i in range(owners)], axis=0)
        table[...] = jnp.concatenate(halves(feats), axis=0)
        empty = jnp.zeros((3, width), F32)
        pre_rows = jnp.concatenate([w1[3:6], b1[...], jnp.zeros((4, width), F32)], axis=0)
        lift_rows = jnp.concatenate([empty, lift_b[...], lift_w[...]], axis=0)
        cell_rows = jnp.concatenate([w1[0:3] / (RES - 1.0), jnp.zeros((5, width), F32)], axis=0)
        first[...] = layer_matrix(
            jnp.concatenate([pre_rows, lift_rows], axis=1),
            jnp.concatenate([cell_rows, jnp.zeros((8, width), F32)], axis=1),
        )
        second[...] = weights3(w2[...].T)

    def run_step(step, carry):
        chunk = step * group
        per = CHUNK // keys.shape[1]

        def body(count):
            bias = jnp.broadcast_to(b2[...], (8, width)).T[:, :1]
            _, key = joined_keys(keys, chunk, count)
            cell = key >> shift

            @pl.when(step >= 2)
            def _():
                save(step - 2).wait()

            saved = slots.at[step % 2]
            run = slice(0, count * CHUNK)
            feats = edge_feats(key, table[...], owners)
            both = dot(first[...], stack_inputs(feats, place_rows(cell, first_row)))
            lifted = both[width:]
            hidden, slope = gelu_both(both[:width])
            kernel = dot(second[...], stack3(hidden)) + bias
            saved[0 * width : 1 * width, run] = hidden
            saved[1 * width : 2 * width, run] = slope
            saved[2 * width : 3 * width, run] = lifted
            saved[3 * width : 4 * width, run] = kernel
            saved[4 * width :, run] = feats
            high, low = halves(kernel * lifted)
            message[:, run] = jnp.concatenate([high, low, jnp.ones((16, count * CHUNK), BF16)], axis=0)
            save(step).start()
            scatter_windows(
                total, keys, cell, message, bounds, 0, chunk, count, ENC_WINDOW, shift, 2 * width + 16
            )

        each_size(bounds, 0, chunk, group, per, cells, body)
        return carry

    begin()
    steps = keys.shape[0] * keys.shape[1] // slots.shape[2]
    used = used_steps(bounds, 0, group, CHUNK // keys.shape[1], cells, steps)
    lax.fori_loop(0, used, run_step, 0)
    def end():
        fields, scales = [], []
        for row in range(rows_here):
            slab = total[row * PLANE : row * PLANE + ENC_CELLS]
            inverse = 1.0 / jnp.maximum(slab[:, 2 * width : 2 * width + 1], 1.0)
            fields.append((slab[:, :width] + slab[:, width : 2 * width]) * inverse)
            scales.append(jnp.broadcast_to(inverse, (ENC_CELLS, width)))
        field = jnp.concatenate(fields, axis=1)
        lat[:ENC_CELLS] = field
        lat[ENC_CELLS:] = jnp.zeros((PLANE - ENC_CELLS, field.shape[1]), F32)
        scale[...] = jnp.concatenate(scales, axis=1)
        leaving = [
            pltpu.make_async_copy(lat, lat_far, copied.at[1]),
            pltpu.make_async_copy(scale, scale_far, copied.at[2]),
        ]
        for out in leaving:
            out.start()
        copy.wait()
        plane_out[...] = times_field(plane.at[:, :, pl.ds(0, ENC_CELLS)], field)
        for out in leaving:
            out.wait()

        @pl.when(used >= 2)
        def _():
            save(used - 2).wait()

        @pl.when(used >= 1)
        def _():
            save(used - 1).wait()

    end()


def times_field(matrix, field):
    high, low = halves(field)
    first, second = matrix[0], matrix[1]
    return dot(first, high) + dot(second, high) + dot(first, low)


def dec_sums_kernel(
    place_ref, bounds, keys, shared, w1, b1, before, saved_before, after, *refs,
    owners, cells, width, first_step,
):
    if first_step == 0:
        lat, skip_w, skip_b, saved, total, inverse_out, skip, table, first, message = refs
    else:
        dec_w2, dec_b2, saved, sums, reach, total, table, first, message = refs
    step = pl.program_id(0)
    rows_here = cells // PLANE
    group = message.shape[1] // CHUNK
    shift = log2(owners * LANES)
    first_row = place_ref[0] * rows_here

    @pl.when(step == 0)
    def _():
        total[...] = jnp.zeros_like(total) if first_step == 0 else before[...]
        degree = shared[0, 2 * FEAT_ROWS :]
        for i in range(1, owners):
            degree = degree + shared[i, 2 * FEAT_ROWS :]
        inverse = 1.0 / jnp.maximum(degree, 1.0)
        if first_step == 0:
            inverse_out[...] = inverse
        feats = []
        for i in range(owners):
            rows = shared[i, FEAT_ROWS : 2 * FEAT_ROWS]
            weighted = rows * inverse[i : i + 1]
            feats.append(jnp.where(iota(rows.shape, 0) == 4, weighted, rows))
        table[...] = jnp.concatenate(halves(jnp.concatenate(feats, axis=0)), axis=0)
        feat_rows = jnp.concatenate([w1[0:3], b1[...], jnp.zeros((4, width), F32)], axis=0)
        cell_rows = jnp.concatenate([w1[3:6] / (RES - 1.0), jnp.zeros((5, width), F32)], axis=0)
        first[...] = layer_matrix(feat_rows, cell_rows)

    chunk = (step + first_step) * group
    per = CHUNK // keys.shape[1]

    def body(count):
        _, key = joined_keys(keys, chunk, count)
        run = slice(0, count * CHUNK)
        cell = key >> shift
        feats = edge_feats(key, table[...], owners)
        hidden, slope = gelu_both(dot(first[...], stack_inputs(feats, place_rows(cell, first_row))))
        weight = feats[4:5]
        saved[0 * width : 1 * width, run] = hidden
        saved[1 * width : 2 * width, run] = slope * weight
        saved[2 * width :, run] = feats
        high, low = halves(hidden * weight)
        w_high, w_low = halves(feats)
        tail = jnp.concatenate([w_high.astype(F32), w_low.astype(F32)], axis=0).astype(BF16)
        message[:, run] = jnp.concatenate([high, low, tail], axis=0)
        scatter_windows(
            total, keys, cell, message, bounds, 2, chunk, count, DEC_WINDOW, shift, 2 * width + 16
        )

    each_size(bounds, 2, chunk, group, per, cells, body)

    @pl.when(step == pl.num_programs(0) - 1)
    def _():
        if first_step == 0:
            skipped = dot3(lat[...], spread(skip_w[...], rows_here))
            skip[...] = skipped + tile_lanes(skip_b[...], rows_here)
            return
        sums[0], sums[1] = cell_sums(total, rows_here, width)
        reached = dot3(sums[0], spread(dec_w2[...], rows_here))
        reach[...] = reached + sums[1] * tile_lanes(dec_b2[...], rows_here)


def x_forward(lines_ref, cos_ref, sin_ref, put, owners, lines, width):
    lanes = lines_ref.shape[2]

    def fold(value):
        if lanes == width:
            return value
        while value.shape[1] > 2 * width:
            half = value.shape[1] // 2
            value = value[:, :half] + value[:, half:]
        return value + pltpu.roll(value, width, 1)

    def join(real, imag):
        if lanes == width:
            return jnp.concatenate([real, imag], axis=1)
        return jnp.where(iota(real.shape, 1) < width, real, imag)

    for kx in range(MODES // 2 + 1):
        cos_real = cos_imag = sin_real = sin_imag = jnp.zeros((lines, lanes), F32)
        for owner in range(owners):
            cos, sin = cos_ref[kx, owner : owner + 1], sin_ref[kx, owner : owner + 1]
            line_real, line_imag = lines_ref[owner, :lines], lines_ref[owner, lines:]
            cos_real, cos_imag = cos_real + cos * line_real, cos_imag + cos * line_imag
            if kx > 0:
                sin_real, sin_imag = sin_real + sin * line_real, sin_imag + sin * line_imag
        put(kx, join(fold(cos_real + sin_imag), fold(cos_imag - sin_real)))
        if 0 < kx < MODES // 2:
            put(MODES - kx, join(fold(cos_real - sin_imag), fold(cos_imag + sin_real)))


def x_inverse(take, out_ref, owners, lines, width):
    rows_here = RES // owners
    half = MODES // 2
    modes = [take(kx) for kx in range(MODES)]
    lane = iota(modes[0].shape, 1)

    def turn(mode):
        turned = pltpu.roll(mode, width, 1)
        return jnp.where(lane < width, -turned, turned)

    even = [modes[0]] + [modes[k] + modes[MODES - k] for k in range(1, half)] + [modes[half]]
    odd = [None] + [turn(modes[k] - modes[MODES - k]) for k in range(1, half)] + [-turn(modes[half])]

    def weighted(values, factors):
        total = None
        for value, factor in zip(values, factors):
            if value is None or abs(factor) < 1e-9:
                continue
            factor = float(np.float32(factor))
            term = value if factor == 1.0 else value * factor
            total = term if total is None else total + term
        return total

    rows = {}
    for x in range(RES // 2 + 1):
        angles = np.arange(half + 1) * x % RES * (2.0 * math.pi / RES)
        cos_part, sin_part = weighted(even, np.cos(angles)), weighted(odd, np.sin(angles))
        rows[x] = cos_part if sin_part is None else cos_part + sin_part
        if 0 < x < RES // 2:
            rows[RES - x] = cos_part - sin_part
        for owner in {x // rows_here, (RES - x) % RES // rows_here}:
            here = [rows.get(owner * rows_here + i) for i in range(rows_here)]
            if any(value is None for value in here):
                continue
            if rows_here == 1:
                out_ref[owner, :lines] = here[0][:, :width]
                out_ref[owner, lines:] = here[0][:, width:]
                continue
            for pair in range(rows_here // 2):
                one, two = here[2 * pair], here[2 * pair + 1]
                one_turned, two_turned = pltpu.roll(one, width, 1), pltpu.roll(two, width, 1)
                where = slice(2 * pair * width, (2 * pair + 2) * width)
                out_ref[owner, :lines, where] = jnp.where(lane < width, one, two_turned)
                out_ref[owner, lines:, where] = jnp.where(lane < width, one_turned, two)


def factor_column(place_ref, lines):
    line = place_ref[0] * lines + iota((lines, 1), 0)
    return jnp.where((line & (MODES - 1)) == 0, 1.0, 2.0) / float(RES**3)


def split_weights(spec_w, base, width):
    block = spec_w[pl.ds(base, 8)].reshape(8 * width, 2 * width)
    return jnp.concatenate(halves(block), axis=1)


def interleave(one, two):
    parts = []
    for at in range(0, one.shape[0], 8):
        parts += [one[at : at + 8], two[at : at + 8]]
    return jnp.concatenate(parts, axis=0)


def fetch_weights(spec_hbm, spec_w, copied):
    count = spec_w.shape[0] // copied.shape[0]

    def copy(i):
        where = pl.ds(i * count, count)
        return pltpu.make_async_copy(spec_hbm.at[where], spec_w.at[where], copied.at[i])

    return count, copy


def mix_kernel(
    place_ref, lines_ref, cos_ref, sin_ref, spec_hbm, *refs, owners, width,
):
    modes, out_ref, mixed, spec_w, copied = refs[-5:]
    lines = MODES * MODES // owners
    count, copy = fetch_weights(spec_hbm, spec_w, copied)
    for i in range(copied.shape[0]):
        copy(i).start()

    def put(kx, value):
        modes[pl.ds(kx, lines, MODES), :] = value

    x_forward(lines_ref, cos_ref, sin_ref, put, owners, lines, width)
    lane = iota((count, 2 * width), 1)

    def mix(i, carry):
        copy(i).wait()
        base = pl.multiple_of(i * count, count)
        u = modes[pl.ds(base, count), :]
        u_turned = pltpu.roll(u, width, 1)
        both = interleave(jnp.where(lane < width, u, u_turned), jnp.where(lane < width, u_turned, u))
        both = jnp.concatenate([both] * 4, axis=1)
        own = iota(both.shape, 1) // width == iota(both.shape, 0) % 8
        high, low = halves(jnp.where(own, both, 0.0))
        products = []
        for batch in range(count // 8):
            rows = slice(batch * 16, (batch + 1) * 16)
            left = jnp.concatenate([high[rows], low[rows]], axis=0)
            products.append(dot(left, split_weights(spec_w, base + batch * 8, width)))
        outs = []
        for product in products:
            product = product[:, : 2 * width] + product[:, 2 * width :]
            product = product[:16] + product[16:]
            turned = pltpu.roll(product[8:], width, 1)
            outs.append(product[:8] + jnp.where(lane[:8] < width, -turned, turned))
        mixed[pl.ds(base, count), :] = jnp.concatenate(outs, axis=0)
        return carry

    lax.fori_loop(0, copied.shape[0], mix, 0)
    factor = factor_column(place_ref, lines)

    def take(kx):
        return mixed[pl.ds(kx, lines, MODES), :] * factor

    x_inverse(take, out_ref, owners, lines, width)


def mix_back_kernel(
    place_ref, lines_ref, cos_ref, sin_ref, spec_hbm, *refs, owners, width,
):
    grads, out_ref, back, spec_w, copied = refs[-5:]
    lines = MODES * MODES // owners
    count, copy = fetch_weights(spec_hbm, spec_w, copied)
    for i in range(copied.shape[0]):
        copy(i).start()
    factor = factor_column(place_ref, lines)

    def put(kx, value):
        grads[pl.ds(kx, lines, MODES), :] = value * factor

    x_forward(lines_ref, cos_ref, sin_ref, put, owners, lines, width)
    lane = iota((count, 2 * width), 1)
    own = iota((16, 8 * width), 1) // width == iota((16, 8 * width), 0) % 8

    def mix(i, carry):
        copy(i).wait()
        base = pl.multiple_of(i * count, count)
        g = grads[pl.ds(base, count), :]
        g_turned = pltpu.roll(g, width, 1)
        high, low = halves(interleave(g, jnp.where(lane < width, g_turned, -g_turned)))
        products = []
        for batch in range(count // 8):
            rows = slice(batch * 16, (batch + 1) * 16)
            left = jnp.concatenate([high[rows], low[rows]], axis=0)
            left = jnp.concatenate([left, left], axis=1)
            products.append(dot(left, split_weights(spec_w, base + batch * 8, width), NT))
        outs = []
        for product in products:
            rows = jnp.where(own, product[:16] + product[16:], 0.0)
            while rows.shape[1] > 2 * width:
                half = rows.shape[1] // 2
                rows = rows[:, :half] + rows[:, half:]
            rows = rows + pltpu.roll(rows, width, 1)
            outs.append(jnp.where(lane[:8] < width, rows[:8], rows[8:]))
        back[pl.ds(base, count), :] = jnp.concatenate(outs, axis=0)
        return carry

    lax.fori_loop(0, copied.shape[0], mix, 0)

    def take(kx):
        return back[pl.ds(kx, lines, MODES), :]

    x_inverse(take, out_ref, owners, lines, width)


def spec_grad_kernel(rank_ref, *refs, shapes, width):
    mode_refs, grad_refs, (out, modes, grads) = refs[:shapes], refs[shapes : 2 * shapes], refs[-3:]
    for parts, held in ((mode_refs, modes), (grad_refs, grads)):
        for distance, part in enumerate(parts):
            held[rank_ref[0] ^ distance] = part[...]
    row = iota((8, 2 * width), 0)
    lane = iota((8, 2 * width), 1)
    own = iota((8, 4 * width), 1) // width == iota((8, 4 * width), 0) % 4
    lefts, rights = [], []
    for batch in range(out.shape[0] // 8):
        where = slice(batch * 8, (batch + 1) * 8)
        left, right = [], []
        for shape in range(shapes):
            u, g = modes[shape, where], grads[shape, where]
            u_turned, g_turned = pltpu.roll(u, width, 1), pltpu.roll(g, width, 1)
            for part in (jnp.where(lane < width, u, u_turned), jnp.where(lane < width, u_turned, u)):
                left.append(jnp.where(own, jnp.concatenate([part] * 2, axis=1), 0.0))
            for part in (g, jnp.where(lane < width, g_turned, -g_turned)):
                pair = [jnp.where(row < 4, part, 0.0), jnp.where(row < 4, 0.0, part)]
                right.append(jnp.concatenate(pair, axis=1))
        left_high, left_low = halves(jnp.concatenate(left, axis=0))
        right_high, right_low = halves(jnp.concatenate(right, axis=0))
        lefts.append(jnp.concatenate([left_high, left_low, left_high], axis=0))
        rights.append(jnp.concatenate([right_high, right_high, right_low], axis=0))
    products = [dot(left, right, TN) for left, right in zip(lefts, rights)]
    for batch, product in enumerate(products):
        out[batch * 8 : batch * 8 + 4] = product[:, : 2 * width].reshape(4, width, 2 * width)
        out[batch * 8 + 4 : batch * 8 + 8] = product[:, 2 * width :].reshape(4, width, 2 * width)


def cell_sums(total, rows_here, width):
    hidden_sums, weight_sums = [], []
    for row in range(rows_here):
        slab = total[row * PLANE : (row + 1) * PLANE]
        hidden_sums.append(slab[:, :width] + slab[:, width : 2 * width])
        weight = slab[:, 2 * width + 4 : 2 * width + 5] + slab[:, 2 * width + 12 : 2 * width + 13]
        weight_sums.append(jnp.broadcast_to(weight, (PLANE, width)))
    return jnp.concatenate(hidden_sums, axis=1), jnp.concatenate(weight_sums, axis=1)


def grid_kernel(
    lines_far, reach_far, skip_far, proj_w, inverse_far, plane_far, after, plane_out, pre_bar_far, latent_far,
    lines, inverse, skip, reach, plane, latent, pre_bar, copied, *, rows_here,
):
    ends = [
        (lines_far, lines),
        (inverse_far, inverse),
        (skip_far, skip),
        (reach_far, reach),
        (plane_far, plane),
        (latent, latent_far),
        (pre_bar, pre_bar_far),
    ]
    copies = [pltpu.make_async_copy(*pair, copied.at[i]) for i, pair in enumerate(ends)]
    for copy in copies[:5]:
        copy.start()
    copies[0].wait()
    copies[1].wait()
    spectral = times_field(inverse, lines[...])
    copies[2].wait()
    value, slope = gelu_both(spectral + skip[...])
    latent[...] = value
    copies[5].start()
    copies[3].wait()
    bar = reach[...] * tile_lanes(proj_w[...], rows_here) * slope
    pre_bar[...] = bar
    copies[6].start()
    copies[4].wait()
    plane_out[...] = times_field(plane, bar)
    copies[5].wait()
    copies[6].wait()


def grid_grads_kernel(
    lat, pre_bar, latent, reach, sums, skip_w, dec_w2, dec_b2, proj_w,
    skip_w_grad, dec_w2_grad, rows_out, table, skip_back, *, rows_here, width,
):
    skip_back[...] = dot3(pre_bar[...], spread(skip_w[...], rows_here), NT)
    skip_w_grad[...] = gather_blocks(dot3(lat[...], pre_bar[...], TN), rows_here, width, width)
    scaled = latent[...] * tile_lanes(proj_w[...], rows_here)
    dec_w2_grad[...] = gather_blocks(dot3(sums[0], scaled, TN), rows_here, width, width)

    def column_sum(value):
        return fold_lanes(jnp.sum(value, axis=0, keepdims=True), rows_here, width)

    rows = [column_sum(pre_bar[...]), column_sum(sums[1] * scaled), column_sum(reach[...] * latent[...])]
    rows_out[...] = jnp.concatenate(rows + [jnp.zeros((5, width), F32)], axis=0)
    cell_kernel = dot3(scaled, spread(dec_w2[...], rows_here), NT)
    offset = scaled * tile_lanes(dec_b2[...], rows_here)
    cells = rows_here * PLANE
    table[cells:] = jnp.zeros((PAD, table.shape[1]), BF16)
    for row in range(rows_here):
        lanes = slice(row * width, (row + 1) * width)
        where = slice(row * PLANE, (row + 1) * PLANE)
        constant = jnp.sum(offset[:, lanes], axis=1, keepdims=True)
        high, low = halves(cell_kernel[:, lanes])
        c_high, c_low = halves(constant)
        lane = iota((PLANE, LANES), 1)
        tail = jnp.where(lane == 0, c_high.astype(F32), jnp.where(lane == 1, c_low.astype(F32), 0.0))
        table[where, : 2 * width] = jnp.concatenate([high.astype(F32), low.astype(F32)], axis=1).astype(BF16)
        table[where, 2 * width :] = tail.astype(BF16)


def input_columns(feats, cell, first_row):
    high, low = halves(feats)
    place = place_rows(cell, first_row)
    return jnp.concatenate([high.astype(F32), low.astype(F32), place, place], axis=0).astype(BF16)


def dec_edges_kernel(
    place_ref, bounds, keys, inverse_degree, saved, table, pred_out, w1_out, b1_out,
    found_scratch, pred_total, grad_total, *, owners, cells, width,
):
    step = pl.program_id(0)
    rows_here = cells // PLANE
    group = found_scratch.shape[1] // CHUNK
    first_row = place_ref[0] * rows_here
    shift = log2(owners * LANES)
    count8 = max(owners, 8)

    @pl.when(step == 0)
    def _():
        pred_total[...] = jnp.zeros_like(pred_total)
        grad_total[...] = jnp.zeros_like(grad_total)

    chunk = step * group
    per = CHUNK // keys.shape[1]

    def body(count):
        rows, key = joined_keys(keys, chunk, count)
        run = slice(0, count * CHUNK)
        gather_windows(
            found_scratch, keys, rows, table, bounds, 2, chunk, count, DEC_WINDOW, shift, 2 * width + 16
        )
        point = key & (owners * LANES - 1)
        found = found_scratch[:width, run] + found_scratch[width : 2 * width, run]
        constant = found_scratch[2 * width : 2 * width + 1, run] + found_scratch[2 * width + 1 : 2 * width + 2, run]
        edge = jnp.sum(saved[:width, run] * found, axis=0, keepdims=True) + constant
        owner = iota((count8, key.shape[1]), 0)
        high, low = halves(jnp.where(owner == (point >> 7), edge, 0.0))
        values = jnp.concatenate([high.astype(F32), low.astype(F32)], axis=0).astype(BF16)
        pred_total[...] += dot(values, one_hot(point & (LANES - 1), 0, LANES), NT)
        left = jnp.concatenate(halves(saved[width : 2 * width, run] * found), axis=0)
        right = input_columns(saved[2 * width :, run], key >> shift, first_row)
        grad_total[...] += dot(left, right, NT)

    each_size(bounds, 2, chunk, group, per, cells, body)

    @pl.when(step == pl.num_programs(0) - 1)
    def _():
        pred_out[...] = (pred_total[:owners] + pred_total[count8 : count8 + owners]) * inverse_degree[...]
        grad = grad_total[:width] + grad_total[width:]
        feats = (grad[:, :8] + grad[:, 8:16]).T
        places = grad[:, 16:24].T / (RES - 1.0)
        w1_out[...] = jnp.concatenate([feats[:3], places[:3]], axis=0)
        b1_out[...] = feats[3:4]


GRAD_ROWS = 108
PACKED_ROWS = 120


def enc_back_kernel(
    place_ref, bounds, keys, saved_hbm, lines_far, skip_far, scale_far, w2, lift_w, pred_bar,
    skip_w_grad, dec_w2_grad, row_grads, pred_part, dec_w1_grad, dec_b1_grad, inverse_hbm,
    *refs, owners, cells, width,
):
    packed, table, found_scratch, second, lifts, feat_total, grad_total, inverse, lines, skip, scale, copied, slots, loaded = refs[-14:]
    rows_here = cells // PLANE
    group = found_scratch.shape[1] // CHUNK
    first_row = place_ref[0] * rows_here
    shift = log2(owners * LANES)
    count8 = max(owners, 8)
    per = CHUNK // keys.shape[1]
    load = slot_copies(saved_hbm, slots, loaded, out=False)
    steps = keys.shape[0] * keys.shape[1] // slots.shape[2]

    def load_used(at):
        @pl.when(at < steps)
        def _():
            first_cell, _ = cell_range(bounds, 0, jnp.minimum(at, steps - 1) * group, per)

            @pl.when(first_cell < cells)
            def _():
                load(at).start()

    def begin():
        used = pl.ds(0, ENC_CELLS)
        ends = [(lines_far, lines), (inverse_hbm.at[:, used], inverse), (skip_far.at[used], skip), (scale_far, scale)]
        copies = [pltpu.make_async_copy(*pair, copied.at[i]) for i, pair in enumerate(ends)]
        for copy in copies:
            copy.start()
        feat_total[...] = jnp.zeros_like(feat_total)
        grad_total[...] = jnp.zeros_like(grad_total)
        second[...] = weights3(w2[...])
        high, low = halves(jnp.concatenate([lift_w[...], jnp.zeros((4, width), F32)], axis=0))
        rows = jnp.concatenate([high.astype(F32), low.astype(F32)], axis=0)
        lifts[...] = jnp.concatenate([rows, rows], axis=1).astype(BF16)
        copies[0].wait()
        copies[1].wait()
        load_used(0)
        field = times_field(inverse, lines[...])
        copies[2].wait()
        copies[3].wait()
        field = (field + skip[...]) * scale[...]
        table[cells:] = jnp.zeros((PAD, 2 * width), BF16)
        for row in range(rows_here):
            high, low = halves(field[:, row * width : (row + 1) * width])
            both = jnp.concatenate([high.astype(F32), low.astype(F32)], axis=1).astype(BF16)
            table[row * PLANE : row * PLANE + ENC_CELLS] = both
            table[row * PLANE + ENC_CELLS : (row + 1) * PLANE] = jnp.zeros((PLANE - ENC_CELLS, 2 * width), BF16)
        load_used(1)

    def run_step(step, carry):
        chunk = step * group

        def body(count):
            rows, key = joined_keys(keys, chunk, count)
            run = slice(0, count * CHUNK)
            gather_windows(
                found_scratch, keys, rows, table, bounds, 0, chunk, count, ENC_WINDOW, shift, 2 * width
            )
            load(step).wait()
            saved = slots.at[step % 2]
            point = key & (owners * LANES - 1)
            found = found_scratch[:width, run] + found_scratch[width:, run]
            source_bar = found * saved[3 * width : 4 * width, run]
            k_high, k_low = halves(found * saved[2 * width : 3 * width, run])
            hidden_bar = dot(second[...], jnp.concatenate([k_high, k_low, k_high], axis=0))
            pre_edge = hidden_bar * saved[width : 2 * width, run]
            source_parts = halves(source_bar)
            parts = [*halves(saved[:width, run]), *halves(pre_edge), *source_parts]
            left = jnp.concatenate(parts + [jnp.ones((16, count * CHUNK), BF16)], axis=0)
            tail = input_columns(saved[4 * width :, run], key >> shift, first_row)
            grad_total[...] += dot(left, jnp.concatenate([k_high, k_low, tail], axis=0), NT)
            owner_hot = iota((count8, count * CHUNK), 0) == (point >> 7)
            both = dot(lifts[...], jnp.concatenate(source_parts, axis=0))
            both = both[:8] + both[8:]
            edges = [jnp.where(owner_hot, both[feat : feat + 1], 0.0) for feat in range(4)]
            values = jnp.concatenate(halves(jnp.concatenate(edges, axis=0)), axis=0)
            feat_total[...] += dot(values, one_hot(point & (LANES - 1), 0, LANES), NT)
            load_used(step + 2)

        each_size(bounds, 0, chunk, group, per, cells, body)
        return carry

    begin()
    lax.fori_loop(0, used_steps(bounds, 0, group, per, cells, steps), run_step, 0)
    def end():
        w2_part = grad_total[:width, : 2 * width] + grad_total[width : 2 * width, : 2 * width]
        w2_grad = w2_part[:, :width] + w2_part[:, width:]
        b2_part = grad_total[6 * width : 6 * width + 1, : 2 * width]
        b2_grad = b2_part[:, :width] + b2_part[:, width:]
        pre_part = grad_total[2 * width : 3 * width, 2 * width :] + grad_total[3 * width : 4 * width, 2 * width :]
        feats = (pre_part[:, :8] + pre_part[:, 8:16]).T
        places = pre_part[:, 16:24].T / (RES - 1.0)
        lift_part = grad_total[4 * width : 5 * width, 2 * width :] + grad_total[5 * width : 6 * width, 2 * width :]
        lifts = (lift_part[:, :8] + lift_part[:, 8:16]).T
        pair = partial(jnp.concatenate, axis=1)
        stack = partial(jnp.concatenate, axis=0)
        half = width // 2
        bar_sum = jnp.broadcast_to(jnp.sum(pred_bar[...], axis=1, keepdims=True), (1, width))
        fixed = stack(
            [
                pair([w2_grad, dec_w2_grad[...]]),
                pair([skip_w_grad[:half], skip_w_grad[half:]]),
                pair([stack([places[:3], feats[:3]]), dec_w1_grad[...]]),
                pair([feats[3:4], dec_b1_grad[...]]),
                pair([b2_grad, row_grads[1:2]]),
                pair([lifts[4:8], stack([lifts[3:4], row_grads[0:1], row_grads[2:3], bar_sum])]),
            ]
        )
        both = feat_total[: 4 * count8] + feat_total[4 * count8 :]
        empty = jnp.zeros((PACKED_ROWS - GRAD_ROWS - 5, LANES), F32)
        for owner in range(owners):
            rows = [both[feat * count8 + owner : feat * count8 + owner + 1] for feat in range(4)]
            packed[owner] = stack([fixed] + rows + [pred_part[owner : owner + 1], empty])

    end()


def arrive_kernel(arrived, proj_b, after, grads, feat_grad, pred, *, owners):
    total = arrived[0]
    for owner in range(1, owners):
        total = total + arrived[owner]
    grads[...] = total[:GRAD_ROWS]
    feat_grad[...] = total[GRAD_ROWS : GRAD_ROWS + 4]
    pred[...] = total[GRAD_ROWS + 4 : GRAD_ROWS + 5] + proj_b[...]


def leave_kernel(*refs, shapes, width):
    half = width // 2
    terms = [ref[...] for ref in refs[:shapes]]
    while len(terms) > 1:
        terms = [terms[i] + terms[i + 1] for i in range(0, len(terms), 2)]
    left, right = terms[0][:, :width], terms[0][:, width:]
    outs = refs[shapes:]
    at = width + half
    enc_w1, enc_b1, enc_w2, enc_b2, lift_w, lift_b, skip_w, skip_b, dec_w1, dec_b1, dec_w2, dec_b2, proj_w, proj_b = outs
    enc_w2[...] = left[:width]
    dec_w2[...] = right[:width]
    skip_w[:half] = left[width:at]
    skip_w[half:] = right[width:at]
    enc_w1[...] = left[at : at + 6]
    dec_w1[...] = right[at : at + 6]
    enc_b1[...] = left[at + 6 : at + 7]
    dec_b1[...] = right[at + 6 : at + 7]
    enc_b2[...] = left[at + 7 : at + 8]
    dec_b2[...] = right[at + 7 : at + 8]
    lift_w[...] = left[at + 8 : at + 12]
    lift_b[...] = right[at + 8 : at + 9]
    skip_b[...] = right[at + 9 : at + 10]
    proj_w[...] = right[at + 10 : at + 11]
    proj_b[...] = right[at + 11 : at + 12, :1]


def shape(*dims, dtype=F32):
    return jax.ShapeDtypeStruct(dims, dtype)


def whole(array):
    zeros = (0,) * array.ndim
    return pl.BlockSpec(array.shape, lambda i: zeros, pipeline_mode=pl.Buffered(1))


HELD = VMEM
VMEM_BYTES = 65280 << 10
FAR = pl.BlockSpec(memory_space=pl.ANY)


def kernel_call(kernel, name, steps, operands, out_shape, out_specs, scratch=(), micros=10, **more):
    arrays = [array for array, _ in operands]
    specs = [whole(array) if spec is None else spec for array, spec in operands]
    return pl.pallas_call(
        kernel,
        grid=(steps,),
        in_specs=specs,
        out_specs=out_specs,
        out_shape=out_shape,
        scratch_shapes=list(scratch),
        compiler_params=pltpu.CompilerParams(vmem_limit_bytes=VMEM_BYTES),
        cost_estimate=pl.CostEstimate(flops=0, bytes_accessed=micros * 2_000_000, transcendentals=0),
        name=name,
        **more,
    )(*arrays)


def on_device(
    mesh_feat,
    mesh_pos,
    query_pos,
    enc_cell,
    enc_point,
    enc_count,
    dec_cell,
    dec_query,
    dec_count,
    enc_w1,
    enc_b1,
    enc_w2,
    enc_b2,
    lift_w,
    lift_b,
    spec_w,
    skip_w,
    skip_b,
    dec_w1,
    dec_b1,
    dec_w2,
    dec_b2,
    proj_w,
    proj_b,
    pred_bar,
):
    width = lift_w.shape[1]
    owners = lax.axis_size("wide")
    shapes = lax.axis_size("grid")
    rows_here = RES // owners
    cells = rows_here * PLANE
    modes_here = spec_w.shape[0]
    lines = modes_here // MODES
    enc_blocks, dec_blocks = enc_cell.shape[1], dec_cell.shape[1]
    enc_edges, dec_edges = enc_blocks * LANES, dec_blocks * LANES
    enc_span, dec_span = ENC_GROUP * CHUNK, DEC_GROUP * CHUNK
    lanes = rows_here * width
    place = lax.axis_index("wide").astype(jnp.int32).reshape(1)
    plane_np = plane_matrix(owners)
    plane = jnp.asarray(np.stack(halves_np(plane_np)))
    inverse = jnp.asarray(np.stack(halves_np(np.ascontiguousarray(plane_np.T))))
    cos_x, sin_x = (jnp.asarray(part) for part in x_tables(rows_here, width))
    rows = [value.reshape(1, -1) for value in (enc_b1, enc_b2, lift_b, skip_b, dec_b1, dec_b2, proj_w, proj_b)]
    enc_b1, enc_b2, lift_b, skip_b, dec_b1, dec_b2, proj_w, proj_b = rows
    sizes = dict(owners=owners, cells=cells, width=width)
    dma = pltpu.SemaphoreType.DMA

    def exchange(value):
        return lax.all_to_all(value, "wide", 0, 0, tiled=True)

    payload = kernel_call(
        partial(share_kernel, owners=owners),
        "share_points",
        1,
        [
            (value, None)
            for value in (
                mesh_feat, mesh_pos.transpose(1, 0, 2), query_pos.transpose(1, 0, 2), pred_bar, dec_query[0], dec_count
            )
        ],
        shape(owners, 2 * FEAT_ROWS + owners, LANES),
        HELD,
    )
    shared = exchange(payload)
    local = [enc_cell[0], enc_point[0], enc_count, dec_cell[0], dec_query[0], dec_count]
    enc_keys, dec_keys, bounds = kernel_call(
        partial(sort_kernel, owners=owners, cells=cells),
        "sort_edges",
        1,
        [(value, None) for value in local] + [(payload, FAR)],
        [
            shape(LANES, enc_blocks, dtype=jnp.int32),
            shape(LANES, dec_blocks, dtype=jnp.int32),
            shape(8, LANES, dtype=jnp.int32),
        ],
        [HELD] * 3,
    )

    fixed = owners * FEAT_ROWS
    saved_rows = 4 * width + FEAT_ROWS
    plane_scratch = pltpu.VMEM((2, 2 * MODES * MODES, PLANE), BF16)
    inverse_scratch = pltpu.VMEM((2, PLANE, 2 * MODES * MODES), BF16)
    saved, lat, scale, plane_lat = kernel_call(
        partial(enc_forward_kernel, **sizes),
        "encode",
        1,
        [(place, SMEM), (bounds, SMEM), (enc_keys, HELD), (shared, HELD)]
        + [(value, None) for value in (enc_w1, enc_b1, enc_w2, enc_b2, lift_w, lift_b)]
        + [(plane, FAR)],
        [
            shape(saved_rows, enc_edges),
            shape(PLANE, lanes),
            shape(ENC_CELLS, lanes),
            shape(2 * MODES * MODES, lanes),
        ],
        [FAR, FAR, FAR, HELD],
        [
            pltpu.VMEM((cells + PAD, 2 * LANES), F32),
            pltpu.VMEM((2 * fixed, LANES), BF16),
            pltpu.VMEM((2 * width, INPUT_ROWS), BF16),
            pltpu.VMEM((width, 3 * width), BF16),
            pltpu.VMEM((2 * width + 16, enc_span), BF16),
            plane_scratch,
            pltpu.VMEM((PLANE, lanes), F32),
            pltpu.VMEM((ENC_CELLS, lanes), F32),
            dma((3,)),
            pltpu.VMEM((2, saved_rows, enc_span), F32),
            dma((2,)),
        ],
    )
    modes_lines = exchange(plane_lat.reshape(owners, 2 * lines, lanes))

    dec_rows = 2 * width + FEAT_ROWS
    dec_steps = dec_edges // dec_span
    half_steps = dec_steps // 2

    def dec_sums(first_step, steps, before, saved_before, after, more, out_shape, scratch, name):
        return kernel_call(
            partial(dec_sums_kernel, first_step=first_step, **sizes),
            name,
            steps,
            [
                (place, SMEM), (bounds, SMEM), (dec_keys, HELD), (shared, HELD), (dec_w1, None), (dec_b1, None),
                (before, HELD if first_step else FAR), (saved_before, FAR), (after, FAR),
            ]
            + more,
            [shape(dec_rows, dec_edges)] + out_shape,
            [pl.BlockSpec((dec_rows, dec_span), lambda i: (0, i + first_step))] + [HELD] * len(out_shape),
            scratch
            + [
                pltpu.VMEM((2 * fixed, LANES), BF16),
                pltpu.VMEM((width, INPUT_ROWS), BF16),
                pltpu.VMEM((2 * width + 16, dec_span), BF16),
            ],
            input_output_aliases={7: 0} if first_step else {},
        )

    dec_saved, dec_total, inverse_degree, skip = dec_sums(
        0, half_steps, plane_lat, plane_lat, plane_lat, [(lat, HELD), (skip_w, None), (skip_b, None)],
        [shape(cells + PAD, 2 * LANES), shape(owners, LANES), shape(PLANE, lanes)], [], "decode_sums_a",
    )

    mix_step, grad_step = min(MIX_STEP, modes_here), min(GRAD_STEP, modes_here)

    def spec_block(step):
        return pl.BlockSpec((step, width, 2 * width), lambda i: (i, 0, 0))

    def mode_pass(kernel, lines_in, after, name):
        return kernel_call(
            partial(kernel, owners=owners, width=width),
            name,
            1,
            [(place, SMEM), (lines_in, HELD), (cos_x, None), (sin_x, None), (spec_w, FAR)]
            + [(value, FAR) for value in after],
            [shape(modes_here, 2 * width), shape(owners, 2 * lines, lanes)],
            [HELD, HELD],
            [
                pltpu.VMEM((modes_here, 2 * width), F32),
                pltpu.VMEM((modes_here, width, 2 * width), F32),
                dma((modes_here // mix_step,)),
            ],
        )

    modes, back_lines = mode_pass(mix_kernel, modes_lines, [inverse_degree], "mix_modes")
    def from_shapes(value, staged=True):
        parts, step = {0: value}, shapes // 2
        if staged:
            while step:
                pairs = [(i, i ^ step) for i in range(shapes)]
                parts.update({d ^ step: lax.ppermute(part, "grid", pairs) for d, part in parts.items()})
                step //= 2
        else:
            for step in range(1, shapes):
                parts[step] = lax.ppermute(value, "grid", [(i, i ^ step) for i in range(shapes)])
        return [parts[d] for d in range(shapes)]

    all_modes = from_shapes(modes)
    grid_lines = exchange(back_lines).reshape(2 * MODES * MODES, lanes)
    dec_saved, sums, reach = dec_sums(
        half_steps, dec_steps - half_steps, dec_total, dec_saved, back_lines,
        [(dec_w2, None), (dec_b2, None)],
        [shape(2, PLANE, lanes), shape(PLANE, lanes)],
        [pltpu.VMEM((cells + PAD, 2 * LANES), F32)],
        "decode_sums_b",
    )

    plane_bar, pre_bar, latent = kernel_call(
        partial(grid_kernel, rows_here=rows_here),
        "grid_fields",
        1,
        [(grid_lines, FAR), (reach, FAR), (skip, FAR), (proj_w, None), (inverse, FAR), (plane, FAR)]
        + [(value, FAR) for value in all_modes[shapes // 2 :][:1]],
        [shape(2 * MODES * MODES, lanes)] + [shape(PLANE, lanes)] * 2,
        [HELD, FAR, FAR],
        [
            pltpu.VMEM((2 * MODES * MODES, lanes), F32),
            inverse_scratch,
            pltpu.VMEM((PLANE, lanes), F32),
            pltpu.VMEM((PLANE, lanes), F32),
            plane_scratch,
            pltpu.VMEM((PLANE, lanes), F32),
            pltpu.VMEM((PLANE, lanes), F32),
            dma((7,)),
        ],
    )
    bar_lines = exchange(plane_bar.reshape(owners, 2 * lines, lanes))

    skip_w_grad, dec_w2_grad, row_grads, dec_table, skip_back = kernel_call(
        partial(grid_grads_kernel, rows_here=rows_here, width=width),
        "grid_grads",
        1,
        [(value, HELD) for value in (lat, pre_bar, latent, reach, sums)]
        + [(value, None) for value in (skip_w, dec_w2, dec_b2, proj_w)],
        [
            shape(width, width),
            shape(width, width),
            shape(8, width),
            shape(cells + PAD, 2 * LANES, dtype=BF16),
            shape(PLANE, lanes),
        ],
        [HELD] * 5,
    )

    mixed_bar, bar_back = mode_pass(mix_back_kernel, bar_lines, [row_grads] + all_modes[1:], "mix_back")
    bar_grid_lines = exchange(bar_back).reshape(2 * MODES * MODES, lanes)

    all_grads = from_shapes(mixed_bar)

    count8 = max(owners, 8)
    pred_part, dec_w1_grad, dec_b1_grad = kernel_call(
        partial(dec_edges_kernel, **sizes),
        "decode_edges",
        dec_steps,
        [
            (place, SMEM), (bounds, SMEM), (dec_keys, HELD), (inverse_degree, HELD),
            (dec_saved, pl.BlockSpec((dec_rows, dec_span), lambda i: (0, i))), (dec_table, HELD),
        ],
        [shape(owners, LANES), shape(6, width), shape(1, width)],
        [HELD] * 3,
        [
            pltpu.VMEM((2 * width + 16, dec_span), F32),
            pltpu.VMEM((2 * count8, LANES), F32),
            pltpu.VMEM((2 * width, 32), F32),
        ],
    )

    packed = kernel_call(
        partial(enc_back_kernel, **sizes),
        "encode_back",
        1,
        [(place, SMEM), (bounds, SMEM), (enc_keys, HELD), (saved, FAR)]
        + [(value, FAR) for value in (bar_grid_lines, skip_back, scale)]
        + [(value, None) for value in (enc_w2, lift_w, pred_bar)]
        + [(value, HELD) for value in (skip_w_grad, dec_w2_grad, row_grads, pred_part, dec_w1_grad, dec_b1_grad)]
        + [(inverse, FAR)]
        + [(value, FAR) for value in all_grads[shapes // 2 :][:1]],
        shape(owners, PACKED_ROWS, LANES),
        HELD,
        [
            pltpu.VMEM((cells + PAD, 2 * width), BF16),
            pltpu.VMEM((2 * width, enc_span), F32),
            pltpu.VMEM((width, 3 * width), BF16),
            pltpu.VMEM((16, 2 * width), BF16),
            pltpu.VMEM((8 * count8, LANES), F32),
            pltpu.VMEM((6 * width + 16, 2 * width + 32), F32),
            pltpu.VMEM((2, ENC_CELLS, 2 * MODES * MODES), BF16),
            pltpu.VMEM((2 * MODES * MODES, lanes), F32),
            pltpu.VMEM((ENC_CELLS, lanes), F32),
            pltpu.VMEM((ENC_CELLS, lanes), F32),
            dma((4,)),
            pltpu.VMEM((2, saved_rows, enc_span), F32),
            dma((2,)),
        ],
    )
    arrived = exchange(packed)

    rank = lax.axis_index("grid").astype(jnp.int32).reshape(1)
    spec_grad = kernel_call(
        partial(spec_grad_kernel, shapes=shapes, width=width),
        "spec_grad",
        modes_here // grad_step,
        [(rank, SMEM)]
        + [
            (value, pl.BlockSpec((grad_step, 2 * width), lambda i: (i, 0)))
            for value in all_modes + all_grads
        ]
        + [(packed, FAR)],
        shape(modes_here, width, 2 * width),
        spec_block(grad_step),
        [pltpu.VMEM((shapes, grad_step, 2 * width), F32)] * 2,
    )

    grads, feat_grad, pred = kernel_call(
        partial(arrive_kernel, owners=owners),
        "arrive",
        1,
        [(arrived, HELD), (proj_b, None), (spec_grad, FAR)],
        [shape(GRAD_ROWS, LANES), shape(4, LANES), shape(1, LANES)],
        [HELD] * 3,
    )
    terms = from_shapes(grads, staged=False)
    vector = shape(1, width)
    square = shape(width, width)
    first = shape(6, width)
    outs = kernel_call(
        partial(leave_kernel, shapes=shapes, width=width),
        "leave",
        1,
        [(term, HELD) for term in terms],
        [
            first, vector, square, vector, shape(4, width), vector,
            square, vector, first, vector, square, vector, vector, shape(1, 1),
        ],
        [HELD] * 14,
    )
    outs = [out.reshape(-1) if out.shape[0] == 1 else out for out in outs]
    return (pred, feat_grad[None], *outs[:6], spec_grad, *outs[6:])


def solution(mesh):
    placed = (
        P("grid", None, "wide"),
        P("grid", None, "wide"),
        P("grid", None, "wide"),
        P("grid", "wide", None),
        P("grid", "wide", None),
        P("grid", "wide"),
        P("grid", "wide", None),
        P("grid", "wide", None),
        P("grid", "wide"),
        P(),
        P(),
        P(),
        P(),
        P(),
        P(),
        P("wide", None, None),
        P(),
        P(),
        P(),
        P(),
        P(),
        P(),
        P(),
        P(),
        P("grid", "wide"),
    )
    return jax.shard_map(
        on_device,
        mesh=mesh,
        in_specs=placed,
        out_specs=(
            P("grid", "wide"),
            P("grid", None, "wide"),
            P(),
            P(),
            P(),
            P(),
            P(),
            P(),
            P("wide", None, None),
            P(),
            P(),
            P(),
            P(),
            P(),
            P(),
            P(),
            P(),
        ),
        check_vma=False,
    )
```

```python
from functools import partial
import math

import jax
import jax.numpy as jnp
import ml_dtypes
import numpy as np
from jax import lax
from jax.experimental import pallas as pl
from jax.experimental.pallas import tpu as pltpu
from jax.sharding import PartitionSpec as P

MODES = 16
RES = 32
PLANE = RES * RES
ENC_CELLS = RES * (RES - RES // 4)
CHUNK = 256
LANES = 128
ENC_GROUP = 16
DEC_GROUP = 16
FEW = 4
FEAT_ROWS = 8
INPUT_ROWS = 48
ENC_WINDOW = 64
DEC_WINDOW = 128
PAD = 256
MIX_STEP = 64
GRAD_STEP = 128
F32 = jnp.float32
BF16 = jnp.bfloat16
GELU_A = 0.7978845608028654
GELU_B = 0.044715

NN = (((1,), (0,)), ((), ()))
NT = (((1,), (1,)), ((), ()))
TN = (((0,), (0,)), ((), ()))

VMEM = pl.BlockSpec(memory_space=pltpu.VMEM)
SMEM = pl.BlockSpec(memory_space=pltpu.SMEM)


def kept_freqs():
    half = MODES // 2
    return np.concatenate([np.arange(half), np.arange(RES - half, RES)])


def plane_matrix(owners):
    lines = MODES * MODES // owners
    line = np.arange(MODES * MODES)
    freq_y, freq_z = kept_freqs()[line // MODES], line % MODES
    cell = np.arange(PLANE)
    turns = (freq_y[:, None] * (cell // RES) + freq_z[:, None] * (cell % RES)) % RES
    angle = turns * (2.0 * math.pi / RES)
    both = np.stack([np.cos(angle), -np.sin(angle)]).reshape(2, owners, lines, PLANE)
    matrix = both.transpose(1, 0, 2, 3).reshape(2 * MODES * MODES, PLANE)
    return matrix.astype(np.float32)


def halves_np(matrix):
    high = matrix.astype(ml_dtypes.bfloat16)
    low = (matrix - high.astype(np.float32)).astype(ml_dtypes.bfloat16)
    return high, low


def line_angles():
    turns = (kept_freqs()[:, None] * np.arange(RES)[None, :]) % RES
    return turns * (2.0 * math.pi / RES)


def x_tables(rows_here, width):
    angle = line_angles().reshape(MODES, RES // rows_here, rows_here, 1)
    angle = np.broadcast_to(angle, (MODES, RES // rows_here, rows_here, width))
    angle = angle.reshape(MODES, RES // rows_here, rows_here * width)
    return np.cos(angle).astype(np.float32), np.sin(angle).astype(np.float32)


def log2(number):
    return number.bit_length() - 1


def iota(shape, axis):
    return lax.broadcasted_iota(jnp.int32, shape, axis)


def halves(value):
    high = value.astype(BF16)
    low = (value - high.astype(F32)).astype(BF16)
    return high, low


def dot(a, b, dims=NN):
    return lax.dot_general(a, b, dims, preferred_element_type=F32)


def dot3(a, b, dims=NN):
    a_high, a_low = halves(a)
    b_high, b_low = halves(b)
    return dot(a_high, b_high, dims) + dot(a_low, b_high, dims) + dot(a_high, b_low, dims)


def one_hot(index, first, rows):
    places = iota((rows, index.shape[1]), 0)
    return jnp.where(places == index - first, 1.0, 0.0).astype(BF16)


def gelu_both(value):
    square = value * value
    half = 0.5 + 0.5 * jnp.tanh(value * (GELU_A + (GELU_A * GELU_B) * square))
    out = value * half
    return out, half + (out - out * half) * (2.0 * GELU_A + (6.0 * GELU_A * GELU_B) * square)


def sort_columns(values):
    rows = values.shape[0]
    regs = rows // 8
    low = log2(regs)
    total = low + 3 + 7
    sub = iota((8, LANES), 0)
    lane = iota((8, LANES), 1)
    x = values.reshape(regs, 8, LANES)

    def flip(x, bit):
        if bit >= total:
            return x
        if bit < low:
            y = x.reshape(regs >> (bit + 1), 2, 1 << bit, 8, LANES)
            return jnp.stack([y[:, 0], -y[:, 1]], axis=1).reshape(regs, 8, LANES)
        if bit < low + 3:
            sign = 1 - 2 * ((sub >> (bit - low)) & 1)
        else:
            sign = 1 - 2 * ((lane >> (bit - low - 3)) & 1)
        return x * sign.astype(F32)[None]

    def exchange(x, bit):
        if bit < low:
            y = x.reshape(regs >> (bit + 1), 2, 1 << bit, 8, LANES)
            one, two = y[:, 0], y[:, 1]
            pair = [jnp.minimum(one, two), jnp.maximum(one, two)]
            return jnp.stack(pair, axis=1).reshape(regs, 8, LANES)
        if bit < low + 3:
            axis, dist, size, place = 1, 1 << (bit - low), 8, sub
        else:
            axis, dist, size, place = 2, 1 << (bit - low - 3), LANES, lane
        after = pltpu.roll(x, size - dist, axis)
        before = after if 2 * dist == size else pltpu.roll(x, dist, axis)
        first = ((place & dist) == 0)[None]
        return jnp.where(first, jnp.minimum(x, after), jnp.maximum(x, before))

    for phase in range(1, total + 1):
        x = flip(x, phase)
        for bit in reversed(range(phase)):
            x = exchange(x, bit)
        x = flip(x, phase)
    return x.reshape(rows, LANES)


def layer_matrix(feat_rows, cell_rows):
    feat_high, feat_low = halves(feat_rows)
    cell_high, cell_low = halves(cell_rows)
    parts = [feat_high, feat_high, feat_low, cell_high, cell_low]
    parts = [part.astype(F32) for part in parts] + [jnp.zeros((LANES - 40, feat_rows.shape[1]), F32)]
    return jnp.concatenate(parts, axis=0).T[:, :INPUT_ROWS].astype(BF16)


def place_rows(cell, first_row):
    row = iota((8, cell.shape[1]), 0)
    shifts = jnp.where(row == 0, 2 * log2(RES), jnp.where(row == 1, log2(RES), 0))
    place = (cell >> shifts) & jnp.where(row < 3, RES - 1, 0)
    return (place + jnp.where(row == 0, first_row, 0)).astype(F32)


def edge_feats(key, table, owners):
    point = key & (owners * LANES - 1)
    found = dot(table, one_hot(point & (LANES - 1), 0, LANES))
    owner = (iota(found.shape, 0) >> 3) & (owners - 1)
    found = jnp.where(owner == (point >> 7), found, 0.0)
    return jnp.sum(found.reshape(2 * owners, FEAT_ROWS, key.shape[1]), axis=0)


def stack_inputs(feats, place):
    high, low = halves(feats)
    parts = [high.astype(F32), low.astype(F32), high.astype(F32), place, place, jnp.zeros_like(place)]
    return jnp.concatenate(parts, axis=0).astype(BF16)


def stack3(value):
    high, low = halves(value)
    return jnp.concatenate([high, low, high], axis=0)


def weights3(matrix):
    high, low = halves(matrix)
    return jnp.concatenate([high, high, low], axis=1)


def key_row(keys_ref, chunk):
    per = CHUNK // keys_ref.shape[1]
    rows = [keys_ref[pl.ds(chunk * per + i, 1), :] for i in range(per)]
    return rows[0] if per == 1 else jnp.concatenate(rows, axis=1)


def cell_range(bounds_ref, line, chunk, per):
    return bounds_ref[line, chunk * per], bounds_ref[line + 1, chunk * per + per - 1]


def spread(block, copies):
    rows, columns = block.shape
    tiled = jnp.concatenate([jnp.concatenate([block] * copies, axis=1)] * copies, axis=0)
    return jnp.where(
        iota(tiled.shape, 0) // rows == iota(tiled.shape, 1) // columns, tiled, 0.0
    )


def gather_blocks(product, copies, rows, columns):
    total = product[:rows, :columns]
    for i in range(1, copies):
        total = total + product[i * rows : (i + 1) * rows, i * columns : (i + 1) * columns]
    return total


def tile_lanes(row, copies):
    return row if copies == 1 else jnp.concatenate([row] * copies, axis=1)


def fold_lanes(row, copies, width):
    total = row[:, :width]
    for i in range(1, copies):
        total = total + row[:, i * width : (i + 1) * width]
    return total


def column(counts):
    return jnp.broadcast_to(counts, (8, counts.shape[1])).T[:, :1]


def share_kernel(feat, pos, query_pos, pred_bar, dec_query, dec_count, payload, *, owners):
    blocks = dec_query.shape[0]
    lane_valid = jnp.where(
        iota((blocks, LANES), 1) < column(dec_count[...]), dec_query[...], owners * LANES
    )
    ones = jnp.zeros((max(owners, 16), LANES), F32)
    degree = ones
    for block in range(0, blocks, 2):
        row = jnp.concatenate([lane_valid[block : block + 1], lane_valid[block + 1 : block + 2]], axis=1)
        high = one_hot(row >> 7, 0, ones.shape[0])
        low = one_hot(row & (LANES - 1), 0, LANES)
        degree = degree + dot(high, low, NT)
    filled = jnp.ones((1, LANES), F32)
    empty = jnp.zeros((3, LANES), F32)
    places = [pos[i] for i in range(3)]
    queries = [query_pos[i] for i in range(3)]
    rows = places + [filled, feat[0]] + queries + [filled, pred_bar[...], empty, degree[:owners]]
    mine = jnp.concatenate(rows, axis=0)
    for owner in range(owners):
        payload[owner] = mine


def sort_kernel(
    enc_cell, enc_point, enc_count, dec_cell, dec_query, dec_count, after,
    enc_keys, dec_keys, bounds, *, owners, cells,
):
    shift = log2(owners * LANES)

    def keys(cell, point, count):
        lane = iota(cell.shape, 1)
        key = jnp.where(lane < column(count), (cell << shift) | point, cells << shift)
        return sort_columns(key.astype(F32)).astype(jnp.int32)

    enc = keys(enc_cell[...], enc_point[...], enc_count[...])
    dec = keys(dec_cell[...], dec_query[...], dec_count[...])
    enc_keys[...] = enc.T
    dec_keys[...] = dec.T
    ends = [enc[:1], enc[-1:], dec[:1], dec[-1:]]
    bounds[...] = jnp.concatenate(ends + [jnp.zeros((4, LANES), jnp.int32)], axis=0) >> shift


def joined_keys(keys, chunk, group):
    rows = [key_row(keys, chunk + i) for i in range(group)]
    return rows, jnp.concatenate(rows, axis=1)


def later_windows(windows, size, visit):
    most = windows[0][1]
    for _, count in windows[1:]:
        most = jnp.maximum(most, count)

    @pl.when(most > 1)
    def _():
        for i, (begin, count) in enumerate(windows):

            def more(j, carry):
                visit(i, begin + j * size)
                return carry

            lax.fori_loop(1, count, more, 0)


def scatter_windows(total, keys, cell, message, bounds, line, chunk, group, size, shift, columns):
    per = CHUNK // keys.shape[1]
    windows, parts = [], []
    for i in range(group):
        begin, end = cell_range(bounds, line, chunk + i, per)
        begin = pl.multiple_of(begin & -8, 8)
        lanes = slice(i * CHUNK, (i + 1) * CHUNK)
        parts.append(dot(one_hot(cell[:, lanes], begin, size), message[:, lanes], NT))
        windows.append((begin, (end - begin) // size + 1))
    for (begin, _), part in zip(windows, parts):
        total[pl.ds(begin, size), :columns] += part

    def visit(i, start):
        start = pl.multiple_of(start, 8)
        hot = one_hot(key_row(keys, chunk + i) >> shift, start, size)
        part = dot(hot, message[:, i * CHUNK : (i + 1) * CHUNK], NT)
        total[pl.ds(start, size), :columns] += part

    later_windows(windows, size, visit)


def gather_windows(found, keys, rows, table, bounds, line, chunk, group, size, shift, columns):
    per = CHUNK // keys.shape[1]
    windows = []
    for i in range(group):
        begin, end = cell_range(bounds, line, chunk + i, per)
        begin = pl.multiple_of(begin & -16, 16)
        hot = one_hot(rows[i] >> shift, begin, size)
        found[:, i * CHUNK : (i + 1) * CHUNK] = dot(table[pl.ds(begin, size), :columns], hot, TN)
        windows.append((begin, (end - begin) // size + 1))

    def visit(i, start):
        start = pl.multiple_of(start, 16)
        hot = one_hot(key_row(keys, chunk + i) >> shift, start, size)
        part = dot(table[pl.ds(start, size), :columns], hot, TN)
        found[:, i * CHUNK : (i + 1) * CHUNK] += part

    later_windows(windows, size, visit)


def slot_copies(far, slots, semaphores, out):
    span = slots.shape[2]

    def copy(step):
        slot = step % 2
        columns = far.at[:, pl.ds(pl.multiple_of(step * span, span), span)]
        ends = (slots.at[slot], columns) if out else (columns, slots.at[slot])
        return pltpu.make_async_copy(*ends, semaphores.at[slot])

    return copy


def used_steps(bounds, line, group, per, cells, steps):
    used = 0
    for step in range(steps):
        used = used + jnp.where(bounds[line, step * group * per] < cells, 1, 0)
    return used


def each_size(bounds, line, chunk, group, per, cells, body):
    few = min(FEW, group)
    some = bounds[line, chunk * per] < cells
    if few == group:
        pl.when(some)(lambda: body(group))
        return
    many = bounds[line, (chunk + few) * per] < cells
    pl.when(many)(lambda: body(group))
    pl.when(some & jnp.logical_not(many))(lambda: body(few))


def enc_forward_kernel(
    place_ref, bounds, keys, shared, w1, b1, w2, b2, lift_w, lift_b, plane_hbm,
    saved_hbm, lat_far, scale_far, plane_out,
    total, table, first, second, message, plane, lat, scale, copied, slots, stored,
    *, owners, cells, width,
):
    rows_here = cells // PLANE
    group = message.shape[1] // CHUNK
    shift = log2(owners * LANES)
    first_row = place_ref[0] * rows_here
    copy = pltpu.make_async_copy(plane_hbm, plane, copied.at[0])
    save = slot_copies(saved_hbm, slots, stored, out=True)

    def begin():
        copy.start()
        total[...] = jnp.zeros_like(total)
        feats = jnp.concatenate([shared[i, :FEAT_ROWS] for i in range(owners)], axis=0)
        table[...] = jnp.concatenate(halves(feats), axis=0)
        empty = jnp.zeros((3, width), F32)
        pre_rows = jnp.concatenate([w1[3:6], b1[...], jnp.zeros((4, width), F32)], axis=0)
        lift_rows = jnp.concatenate([empty, lift_b[...], lift_w[...]], axis=0)
        cell_rows = jnp.concatenate([w1[0:3] / (RES - 1.0), jnp.zeros((5, width), F32)], axis=0)
        first[...] = layer_matrix(
            jnp.concatenate([pre_rows, lift_rows], axis=1),
            jnp.concatenate([cell_rows, jnp.zeros((8, width), F32)], axis=1),
        )
        second[...] = weights3(w2[...].T)

    def run_step(step, carry):
        chunk = step * group
        per = CHUNK // keys.shape[1]

        def body(count):
            bias = jnp.broadcast_to(b2[...], (8, width)).T[:, :1]
            _, key = joined_keys(keys, chunk, count)
            cell = key >> shift

            @pl.when(step >= 2)
            def _():
                save(step - 2).wait()

            saved = slots.at[step % 2]
            run = slice(0, count * CHUNK)
            feats = edge_feats(key, table[...], owners)
            both = dot(first[...], stack_inputs(feats, place_rows(cell, first_row)))
            lifted = both[width:]
            hidden, slope = gelu_both(both[:width])
            kernel = dot(second[...], stack3(hidden)) + bias
            saved[0 * width : 1 * width, run] = hidden
            saved[1 * width : 2 * width, run] = slope
            saved[2 * width : 3 * width, run] = lifted
            saved[3 * width : 4 * width, run] = kernel
            saved[4 * width :, run] = feats
            high, low = halves(kernel * lifted)
            message[:, run] = jnp.concatenate([high, low, jnp.ones((16, count * CHUNK), BF16)], axis=0)
            save(step).start()
            scatter_windows(
                total, keys, cell, message, bounds, 0, chunk, count, ENC_WINDOW, shift, 2 * width + 16
            )

        each_size(bounds, 0, chunk, group, per, cells, body)
        return carry

    begin()
    steps = keys.shape[0] * keys.shape[1] // slots.shape[2]
    used = used_steps(bounds, 0, group, CHUNK // keys.shape[1], cells, steps)
    lax.fori_loop(0, used, run_step, 0)
    def end():
        fields, scales = [], []
        for row in range(rows_here):
            slab = total[row * PLANE : row * PLANE + ENC_CELLS]
            inverse = 1.0 / jnp.maximum(slab[:, 2 * width : 2 * width + 1], 1.0)
            fields.append((slab[:, :width] + slab[:, width : 2 * width]) * inverse)
            scales.append(jnp.broadcast_to(inverse, (ENC_CELLS, width)))
        field = jnp.concatenate(fields, axis=1)
        lat[:ENC_CELLS] = field
        lat[ENC_CELLS:] = jnp.zeros((PLANE - ENC_CELLS, field.shape[1]), F32)
        scale[...] = jnp.concatenate(scales, axis=1)
        leaving = [
            pltpu.make_async_copy(lat, lat_far, copied.at[1]),
            pltpu.make_async_copy(scale, scale_far, copied.at[2]),
        ]
        for out in leaving:
            out.start()
        copy.wait()
        plane_out[...] = times_field(plane.at[:, :, pl.ds(0, ENC_CELLS)], field)
        for out in leaving:
            out.wait()

        @pl.when(used >= 2)
        def _():
            save(used - 2).wait()

        @pl.when(used >= 1)
        def _():
            save(used - 1).wait()

    end()


def times_field(matrix, field):
    high, low = halves(field)
    first, second = matrix[0], matrix[1]
    return dot(first, high) + dot(second, high) + dot(first, low)


def dec_sums_kernel(
    place_ref, bounds, keys, shared, w1, b1, before, saved_before, after, *refs,
    owners, cells, width, first_step,
):
    if first_step == 0:
        lat, skip_w, skip_b, saved, total, inverse_out, skip, table, first, message = refs
    else:
        dec_w2, dec_b2, saved, sums, reach, total, table, first, message = refs
    step = pl.program_id(0)
    rows_here = cells // PLANE
    group = message.shape[1] // CHUNK
    shift = log2(owners * LANES)
    first_row = place_ref[0] * rows_here

    @pl.when(step == 0)
    def _():
        total[...] = jnp.zeros_like(total) if first_step == 0 else before[...]
        degree = shared[0, 2 * FEAT_ROWS :]
        for i in range(1, owners):
            degree = degree + shared[i, 2 * FEAT_ROWS :]
        inverse = 1.0 / jnp.maximum(degree, 1.0)
        if first_step == 0:
            inverse_out[...] = inverse
        feats = []
        for i in range(owners):
            rows = shared[i, FEAT_ROWS : 2 * FEAT_ROWS]
            weighted = rows * inverse[i : i + 1]
            feats.append(jnp.where(iota(rows.shape, 0) == 4, weighted, rows))
        table[...] = jnp.concatenate(halves(jnp.concatenate(feats, axis=0)), axis=0)
        feat_rows = jnp.concatenate([w1[0:3], b1[...], jnp.zeros((4, width), F32)], axis=0)
        cell_rows = jnp.concatenate([w1[3:6] / (RES - 1.0), jnp.zeros((5, width), F32)], axis=0)
        first[...] = layer_matrix(feat_rows, cell_rows)

    chunk = (step + first_step) * group
    per = CHUNK // keys.shape[1]

    def body(count):
        _, key = joined_keys(keys, chunk, count)
        run = slice(0, count * CHUNK)
        cell = key >> shift
        feats = edge_feats(key, table[...], owners)
        hidden, slope = gelu_both(dot(first[...], stack_inputs(feats, place_rows(cell, first_row))))
        weight = feats[4:5]
        saved[0 * width : 1 * width, run] = hidden
        saved[1 * width : 2 * width, run] = slope * weight
        saved[2 * width :, run] = feats
        high, low = halves(hidden * weight)
        w_high, w_low = halves(feats)
        tail = jnp.concatenate([w_high.astype(F32), w_low.astype(F32)], axis=0).astype(BF16)
        message[:, run] = jnp.concatenate([high, low, tail], axis=0)
        scatter_windows(
            total, keys, cell, message, bounds, 2, chunk, count, DEC_WINDOW, shift, 2 * width + 16
        )

    each_size(bounds, 2, chunk, group, per, cells, body)

    @pl.when(step == pl.num_programs(0) - 1)
    def _():
        if first_step == 0:
            skipped = dot3(lat[...], spread(skip_w[...], rows_here))
            skip[...] = skipped + tile_lanes(skip_b[...], rows_here)
            return
        sums[0], sums[1] = cell_sums(total, rows_here, width)
        reached = dot3(sums[0], spread(dec_w2[...], rows_here))
        reach[...] = reached + sums[1] * tile_lanes(dec_b2[...], rows_here)


def x_forward(lines_ref, cos_ref, sin_ref, put, owners, lines, width):
    lanes = lines_ref.shape[2]

    def fold(value):
        if lanes == width:
            return value
        while value.shape[1] > 2 * width:
            half = value.shape[1] // 2
            value = value[:, :half] + value[:, half:]
        return value + pltpu.roll(value, width, 1)

    def join(real, imag):
        if lanes == width:
            return jnp.concatenate([real, imag], axis=1)
        return jnp.where(iota(real.shape, 1) < width, real, imag)

    for kx in range(MODES // 2 + 1):
        cos_real = cos_imag = sin_real = sin_imag = jnp.zeros((lines, lanes), F32)
        for owner in range(owners):
            cos, sin = cos_ref[kx, owner : owner + 1], sin_ref[kx, owner : owner + 1]
            line_real, line_imag = lines_ref[owner, :lines], lines_ref[owner, lines:]
            cos_real, cos_imag = cos_real + cos * line_real, cos_imag + cos * line_imag
            if kx > 0:
                sin_real, sin_imag = sin_real + sin * line_real, sin_imag + sin * line_imag
        put(kx, join(fold(cos_real + sin_imag), fold(cos_imag - sin_real)))
        if 0 < kx < MODES // 2:
            put(MODES - kx, join(fold(cos_real - sin_imag), fold(cos_imag + sin_real)))


def x_inverse(take, out_ref, owners, lines, width):
    rows_here = RES // owners
    half = MODES // 2
    modes = [take(kx) for kx in range(MODES)]
    lane = iota(modes[0].shape, 1)

    def turn(mode):
        turned = pltpu.roll(mode, width, 1)
        return jnp.where(lane < width, -turned, turned)

    even = [modes[0]] + [modes[k] + modes[MODES - k] for k in range(1, half)] + [modes[half]]
    odd = [None] + [turn(modes[k] - modes[MODES - k]) for k in range(1, half)] + [-turn(modes[half])]

    def weighted(values, factors):
        total = None
        for value, factor in zip(values, factors):
            if value is None or abs(factor) < 1e-9:
                continue
            factor = float(np.float32(factor))
            term = value if factor == 1.0 else value * factor
            total = term if total is None else total + term
        return total

    rows = {}
    for x in range(RES // 2 + 1):
        angles = np.arange(half + 1) * x % RES * (2.0 * math.pi / RES)
        cos_part, sin_part = weighted(even, np.cos(angles)), weighted(odd, np.sin(angles))
        rows[x] = cos_part if sin_part is None else cos_part + sin_part
        if 0 < x < RES // 2:
            rows[RES - x] = cos_part - sin_part
        for owner in {x // rows_here, (RES - x) % RES // rows_here}:
            here = [rows.get(owner * rows_here + i) for i in range(rows_here)]
            if any(value is None for value in here):
                continue
            if rows_here == 1:
                out_ref[owner, :lines] = here[0][:, :width]
                out_ref[owner, lines:] = here[0][:, width:]
                continue
            for pair in range(rows_here // 2):
                one, two = here[2 * pair], here[2 * pair + 1]
                one_turned, two_turned = pltpu.roll(one, width, 1), pltpu.roll(two, width, 1)
                where = slice(2 * pair * width, (2 * pair + 2) * width)
                out_ref[owner, :lines, where] = jnp.where(lane < width, one, two_turned)
                out_ref[owner, lines:, where] = jnp.where(lane < width, one_turned, two)


def factor_column(place_ref, lines):
    line = place_ref[0] * lines + iota((lines, 1), 0)
    return jnp.where((line & (MODES - 1)) == 0, 1.0, 2.0) / float(RES**3)


def split_weights(spec_w, base, width):
    block = spec_w[pl.ds(base, 8)].reshape(8 * width, 2 * width)
    return jnp.concatenate(halves(block), axis=1)


def interleave(one, two):
    parts = []
    for at in range(0, one.shape[0], 8):
        parts += [one[at : at + 8], two[at : at + 8]]
    return jnp.concatenate(parts, axis=0)


def fetch_weights(spec_hbm, spec_w, copied):
    count = spec_w.shape[0] // copied.shape[0]

    def copy(i):
        where = pl.ds(i * count, count)
        return pltpu.make_async_copy(spec_hbm.at[where], spec_w.at[where], copied.at[i])

    return count, copy


def mix_kernel(
    place_ref, lines_ref, cos_ref, sin_ref, spec_hbm, *refs, owners, width,
):
    modes, out_ref, mixed, spec_w, copied = refs[-5:]
    lines = MODES * MODES // owners
    count, copy = fetch_weights(spec_hbm, spec_w, copied)
    for i in range(copied.shape[0]):
        copy(i).start()

    def put(kx, value):
        modes[pl.ds(kx, lines, MODES), :] = value

    x_forward(lines_ref, cos_ref, sin_ref, put, owners, lines, width)
    lane = iota((count, 2 * width), 1)

    def mix(i, carry):
        copy(i).wait()
        base = pl.multiple_of(i * count, count)
        u = modes[pl.ds(base, count), :]
        u_turned = pltpu.roll(u, width, 1)
        both = interleave(jnp.where(lane < width, u, u_turned), jnp.where(lane < width, u_turned, u))
        both = jnp.concatenate([both] * 4, axis=1)
        own = iota(both.shape, 1) // width == iota(both.shape, 0) % 8
        high, low = halves(jnp.where(own, both, 0.0))
        products = []
        for batch in range(count // 8):
            rows = slice(batch * 16, (batch + 1) * 16)
            left = jnp.concatenate([high[rows], low[rows]], axis=0)
            products.append(dot(left, split_weights(spec_w, base + batch * 8, width)))
        outs = []
        for product in products:
            product = product[:, : 2 * width] + product[:, 2 * width :]
            product = product[:16] + product[16:]
            turned = pltpu.roll(product[8:], width, 1)
            outs.append(product[:8] + jnp.where(lane[:8] < width, -turned, turned))
        mixed[pl.ds(base, count), :] = jnp.concatenate(outs, axis=0)
        return carry

    lax.fori_loop(0, copied.shape[0], mix, 0)
    factor = factor_column(place_ref, lines)

    def take(kx):
        return mixed[pl.ds(kx, lines, MODES), :] * factor

    x_inverse(take, out_ref, owners, lines, width)


def mix_back_kernel(
    place_ref, lines_ref, cos_ref, sin_ref, spec_hbm, *refs, owners, width,
):
    grads, out_ref, back, spec_w, copied = refs[-5:]
    lines = MODES * MODES // owners
    count, copy = fetch_weights(spec_hbm, spec_w, copied)
    for i in range(copied.shape[0]):
        copy(i).start()
    factor = factor_column(place_ref, lines)

    def put(kx, value):
        grads[pl.ds(kx, lines, MODES), :] = value * factor

    x_forward(lines_ref, cos_ref, sin_ref, put, owners, lines, width)
    lane = iota((count, 2 * width), 1)
    own = iota((16, 8 * width), 1) // width == iota((16, 8 * width), 0) % 8

    def mix(i, carry):
        copy(i).wait()
        base = pl.multiple_of(i * count, count)
        g = grads[pl.ds(base, count), :]
        g_turned = pltpu.roll(g, width, 1)
        high, low = halves(interleave(g, jnp.where(lane < width, g_turned, -g_turned)))
        products = []
        for batch in range(count // 8):
            rows = slice(batch * 16, (batch + 1) * 16)
            left = jnp.concatenate([high[rows], low[rows]], axis=0)
            left = jnp.concatenate([left, left], axis=1)
            products.append(dot(left, split_weights(spec_w, base + batch * 8, width), NT))
        outs = []
        for product in products:
            rows = jnp.where(own, product[:16] + product[16:], 0.0)
            while rows.shape[1] > 2 * width:
                half = rows.shape[1] // 2
                rows = rows[:, :half] + rows[:, half:]
            rows = rows + pltpu.roll(rows, width, 1)
            outs.append(jnp.where(lane[:8] < width, rows[:8], rows[8:]))
        back[pl.ds(base, count), :] = jnp.concatenate(outs, axis=0)
        return carry

    lax.fori_loop(0, copied.shape[0], mix, 0)

    def take(kx):
        return back[pl.ds(kx, lines, MODES), :]

    x_inverse(take, out_ref, owners, lines, width)


def spec_grad_kernel(rank_ref, *refs, shapes, width):
    mode_refs, grad_refs, (out, modes, grads) = refs[:shapes], refs[shapes : 2 * shapes], refs[-3:]
    for parts, held in ((mode_refs, modes), (grad_refs, grads)):
        for distance, part in enumerate(parts):
            held[rank_ref[0] ^ distance] = part[...]
    row = iota((8, 2 * width), 0)
    lane = iota((8, 2 * width), 1)
    own = iota((8, 4 * width), 1) // width == iota((8, 4 * width), 0) % 4
    lefts, rights = [], []
    for batch in range(out.shape[0] // 8):
        where = slice(batch * 8, (batch + 1) * 8)
        left, right = [], []
        for shape in range(shapes):
            u, g = modes[shape, where], grads[shape, where]
            u_turned, g_turned = pltpu.roll(u, width, 1), pltpu.roll(g, width, 1)
            for part in (jnp.where(lane < width, u, u_turned), jnp.where(lane < width, u_turned, u)):
                left.append(jnp.where(own, jnp.concatenate([part] * 2, axis=1), 0.0))
            for part in (g, jnp.where(lane < width, g_turned, -g_turned)):
                pair = [jnp.where(row < 4, part, 0.0), jnp.where(row < 4, 0.0, part)]
                right.append(jnp.concatenate(pair, axis=1))
        left_high, left_low = halves(jnp.concatenate(left, axis=0))
        right_high, right_low = halves(jnp.concatenate(right, axis=0))
        lefts.append(jnp.concatenate([left_high, left_low, left_high], axis=0))
        rights.append(jnp.concatenate([right_high, right_high, right_low], axis=0))
    products = [dot(left, right, TN) for left, right in zip(lefts, rights)]
    for batch, product in enumerate(products):
        out[batch * 8 : batch * 8 + 4] = product[:, : 2 * width].reshape(4, width, 2 * width)
        out[batch * 8 + 4 : batch * 8 + 8] = product[:, 2 * width :].reshape(4, width, 2 * width)


def cell_sums(total, rows_here, width):
    hidden_sums, weight_sums = [], []
    for row in range(rows_here):
        slab = total[row * PLANE : (row + 1) * PLANE]
        hidden_sums.append(slab[:, :width] + slab[:, width : 2 * width])
        weight = slab[:, 2 * width + 4 : 2 * width + 5] + slab[:, 2 * width + 12 : 2 * width + 13]
        weight_sums.append(jnp.broadcast_to(weight, (PLANE, width)))
    return jnp.concatenate(hidden_sums, axis=1), jnp.concatenate(weight_sums, axis=1)


def grid_kernel(
    lines_far, reach_far, skip_far, proj_w, inverse_far, plane_far, after, plane_out, pre_bar_far, latent_far,
    lines, inverse, skip, reach, plane, latent, pre_bar, copied, *, rows_here,
):
    ends = [
        (lines_far, lines),
        (inverse_far, inverse),
        (skip_far, skip),
        (reach_far, reach),
        (plane_far, plane),
        (latent, latent_far),
        (pre_bar, pre_bar_far),
    ]
    copies = [pltpu.make_async_copy(*pair, copied.at[i]) for i, pair in enumerate(ends)]
    for copy in copies[:5]:
        copy.start()
    copies[0].wait()
    copies[1].wait()
    spectral = times_field(inverse, lines[...])
    copies[2].wait()
    value, slope = gelu_both(spectral + skip[...])
    latent[...] = value
    copies[5].start()
    copies[3].wait()
    bar = reach[...] * tile_lanes(proj_w[...], rows_here) * slope
    pre_bar[...] = bar
    copies[6].start()
    copies[4].wait()
    plane_out[...] = times_field(plane, bar)
    copies[5].wait()
    copies[6].wait()


def grid_grads_kernel(
    lat, pre_bar, latent, reach, sums, skip_w, dec_w2, dec_b2, proj_w,
    skip_w_grad, dec_w2_grad, rows_out, table, skip_back, *, rows_here, width,
):
    skip_back[...] = dot3(pre_bar[...], spread(skip_w[...], rows_here), NT)
    skip_w_grad[...] = gather_blocks(dot3(lat[...], pre_bar[...], TN), rows_here, width, width)
    scaled = latent[...] * tile_lanes(proj_w[...], rows_here)
    dec_w2_grad[...] = gather_blocks(dot3(sums[0], scaled, TN), rows_here, width, width)

    def column_sum(value):
        return fold_lanes(jnp.sum(value, axis=0, keepdims=True), rows_here, width)

    rows = [column_sum(pre_bar[...]), column_sum(sums[1] * scaled), column_sum(reach[...] * latent[...])]
    rows_out[...] = jnp.concatenate(rows + [jnp.zeros((5, width), F32)], axis=0)
    cell_kernel = dot3(scaled, spread(dec_w2[...], rows_here), NT)
    offset = scaled * tile_lanes(dec_b2[...], rows_here)
    cells = rows_here * PLANE
    table[cells:] = jnp.zeros((PAD, table.shape[1]), BF16)
    for row in range(rows_here):
        lanes = slice(row * width, (row + 1) * width)
        where = slice(row * PLANE, (row + 1) * PLANE)
        constant = jnp.sum(offset[:, lanes], axis=1, keepdims=True)
        high, low = halves(cell_kernel[:, lanes])
        c_high, c_low = halves(constant)
        lane = iota((PLANE, LANES), 1)
        tail = jnp.where(lane == 0, c_high.astype(F32), jnp.where(lane == 1, c_low.astype(F32), 0.0))
        table[where, : 2 * width] = jnp.concatenate([high.astype(F32), low.astype(F32)], axis=1).astype(BF16)
        table[where, 2 * width :] = tail.astype(BF16)


def input_columns(feats, cell, first_row):
    high, low = halves(feats)
    place = place_rows(cell, first_row)
    return jnp.concatenate([high.astype(F32), low.astype(F32), place, place], axis=0).astype(BF16)


def dec_edges_kernel(
    place_ref, bounds, keys, inverse_degree, saved, table, pred_out, w1_out, b1_out,
    found_scratch, pred_total, grad_total, *, owners, cells, width,
):
    step = pl.program_id(0)
    rows_here = cells // PLANE
    group = found_scratch.shape[1] // CHUNK
    first_row = place_ref[0] * rows_here
    shift = log2(owners * LANES)
    count8 = max(owners, 8)

    @pl.when(step == 0)
    def _():
        pred_total[...] = jnp.zeros_like(pred_total)
        grad_total[...] = jnp.zeros_like(grad_total)

    chunk = step * group
    per = CHUNK // keys.shape[1]

    def body(count):
        rows, key = joined_keys(keys, chunk, count)
        run = slice(0, count * CHUNK)
        gather_windows(
            found_scratch, keys, rows, table, bounds, 2, chunk, count, DEC_WINDOW, shift, 2 * width + 16
        )
        point = key & (owners * LANES - 1)
        found = found_scratch[:width, run] + found_scratch[width : 2 * width, run]
        constant = found_scratch[2 * width : 2 * width + 1, run] + found_scratch[2 * width + 1 : 2 * width + 2, run]
        edge = jnp.sum(saved[:width, run] * found, axis=0, keepdims=True) + constant
        owner = iota((count8, key.shape[1]), 0)
        high, low = halves(jnp.where(owner == (point >> 7), edge, 0.0))
        values = jnp.concatenate([high.astype(F32), low.astype(F32)], axis=0).astype(BF16)
        pred_total[...] += dot(values, one_hot(point & (LANES - 1), 0, LANES), NT)
        left = jnp.concatenate(halves(saved[width : 2 * width, run] * found), axis=0)
        right = input_columns(saved[2 * width :, run], key >> shift, first_row)
        grad_total[...] += dot(left, right, NT)

    each_size(bounds, 2, chunk, group, per, cells, body)

    @pl.when(step == pl.num_programs(0) - 1)
    def _():
        pred_out[...] = (pred_total[:owners] + pred_total[count8 : count8 + owners]) * inverse_degree[...]
        grad = grad_total[:width] + grad_total[width:]
        feats = (grad[:, :8] + grad[:, 8:16]).T
        places = grad[:, 16:24].T / (RES - 1.0)
        w1_out[...] = jnp.concatenate([feats[:3], places[:3]], axis=0)
        b1_out[...] = feats[3:4]


GRAD_ROWS = 108
PACKED_ROWS = 120


def enc_back_kernel(
    place_ref, bounds, keys, saved_hbm, lines_far, skip_far, scale_far, w2, lift_w, pred_bar,
    skip_w_grad, dec_w2_grad, row_grads, pred_part, dec_w1_grad, dec_b1_grad, inverse_hbm,
    *refs, owners, cells, width,
):
    packed, table, found_scratch, second, lifts, feat_total, grad_total, inverse, lines, skip, scale, copied, slots, loaded = refs[-14:]
    rows_here = cells // PLANE
    group = found_scratch.shape[1] // CHUNK
    first_row = place_ref[0] * rows_here
    shift = log2(owners * LANES)
    count8 = max(owners, 8)
    per = CHUNK // keys.shape[1]
    load = slot_copies(saved_hbm, slots, loaded, out=False)
    steps = keys.shape[0] * keys.shape[1] // slots.shape[2]

    def load_used(at):
        @pl.when(at < steps)
        def _():
            first_cell, _ = cell_range(bounds, 0, jnp.minimum(at, steps - 1) * group, per)

            @pl.when(first_cell < cells)
            def _():
                load(at).start()

    def begin():
        used = pl.ds(0, ENC_CELLS)
        ends = [(lines_far, lines), (inverse_hbm.at[:, used], inverse), (skip_far.at[used], skip), (scale_far, scale)]
        copies = [pltpu.make_async_copy(*pair, copied.at[i]) for i, pair in enumerate(ends)]
        for copy in copies:
            copy.start()
        feat_total[...] = jnp.zeros_like(feat_total)
        grad_total[...] = jnp.zeros_like(grad_total)
        second[...] = weights3(w2[...])
        high, low = halves(jnp.concatenate([lift_w[...], jnp.zeros((4, width), F32)], axis=0))
        rows = jnp.concatenate([high.astype(F32), low.astype(F32)], axis=0)
        lifts[...] = jnp.concatenate([rows, rows], axis=1).astype(BF16)
        copies[0].wait()
        copies[1].wait()
        load_used(0)
        field = times_field(inverse, lines[...])
        copies[2].wait()
        copies[3].wait()
        field = (field + skip[...]) * scale[...]
        table[cells:] = jnp.zeros((PAD, 2 * width), BF16)
        for row in range(rows_here):
            high, low = halves(field[:, row * width : (row + 1) * width])
            both = jnp.concatenate([high.astype(F32), low.astype(F32)], axis=1).astype(BF16)
            table[row * PLANE : row * PLANE + ENC_CELLS] = both
            table[row * PLANE + ENC_CELLS : (row + 1) * PLANE] = jnp.zeros((PLANE - ENC_CELLS, 2 * width), BF16)
        load_used(1)

    def run_step(step, carry):
        chunk = step * group

        def body(count):
            rows, key = joined_keys(keys, chunk, count)
            run = slice(0, count * CHUNK)
            gather_windows(
                found_scratch, keys, rows, table, bounds, 0, chunk, count, ENC_WINDOW, shift, 2 * width
            )
            load(step).wait()
            saved = slots.at[step % 2]
            point = key & (owners * LANES - 1)
            found = found_scratch[:width, run] + found_scratch[width:, run]
            source_bar = found * saved[3 * width : 4 * width, run]
            k_high, k_low = halves(found * saved[2 * width : 3 * width, run])
            hidden_bar = dot(second[...], jnp.concatenate([k_high, k_low, k_high], axis=0))
            pre_edge = hidden_bar * saved[width : 2 * width, run]
            source_parts = halves(source_bar)
            parts = [*halves(saved[:width, run]), *halves(pre_edge), *source_parts]
            left = jnp.concatenate(parts + [jnp.ones((16, count * CHUNK), BF16)], axis=0)
            tail = input_columns(saved[4 * width :, run], key >> shift, first_row)
            grad_total[...] += dot(left, jnp.concatenate([k_high, k_low, tail], axis=0), NT)
            owner_hot = iota((count8, count * CHUNK), 0) == (point >> 7)
            both = dot(lifts[...], jnp.concatenate(source_parts, axis=0))
            both = both[:8] + both[8:]
            edges = [jnp.where(owner_hot, both[feat : feat + 1], 0.0) for feat in range(4)]
            values = jnp.concatenate(halves(jnp.concatenate(edges, axis=0)), axis=0)
            feat_total[...] += dot(values, one_hot(point & (LANES - 1), 0, LANES), NT)
            load_used(step + 2)

        each_size(bounds, 0, chunk, group, per, cells, body)
        return carry

    begin()
    lax.fori_loop(0, used_steps(bounds, 0, group, per, cells, steps), run_step, 0)
    def end():
        w2_part = grad_total[:width, : 2 * width] + grad_total[width : 2 * width, : 2 * width]
        w2_grad = w2_part[:, :width] + w2_part[:, width:]
        b2_part = grad_total[6 * width : 6 * width + 1, : 2 * width]
        b2_grad = b2_part[:, :width] + b2_part[:, width:]
        pre_part = grad_total[2 * width : 3 * width, 2 * width :] + grad_total[3 * width : 4 * width, 2 * width :]
        feats = (pre_part[:, :8] + pre_part[:, 8:16]).T
        places = pre_part[:, 16:24].T / (RES - 1.0)
        lift_part = grad_total[4 * width : 5 * width, 2 * width :] + grad_total[5 * width : 6 * width, 2 * width :]
        lifts = (lift_part[:, :8] + lift_part[:, 8:16]).T
        pair = partial(jnp.concatenate, axis=1)
        stack = partial(jnp.concatenate, axis=0)
        half = width // 2
        bar_sum = jnp.broadcast_to(jnp.sum(pred_bar[...], axis=1, keepdims=True), (1, width))
        fixed = stack(
            [
                pair([w2_grad, dec_w2_grad[...]]),
                pair([skip_w_grad[:half], skip_w_grad[half:]]),
                pair([stack([places[:3], feats[:3]]), dec_w1_grad[...]]),
                pair([feats[3:4], dec_b1_grad[...]]),
                pair([b2_grad, row_grads[1:2]]),
                pair([lifts[4:8], stack([lifts[3:4], row_grads[0:1], row_grads[2:3], bar_sum])]),
            ]
        )
        both = feat_total[: 4 * count8] + feat_total[4 * count8 :]
        empty = jnp.zeros((PACKED_ROWS - GRAD_ROWS - 5, LANES), F32)
        for owner in range(owners):
            rows = [both[feat * count8 + owner : feat * count8 + owner + 1] for feat in range(4)]
            packed[owner] = stack([fixed] + rows + [pred_part[owner : owner + 1], empty])

    end()


def arrive_kernel(arrived, proj_b, after, grads, feat_grad, pred, *, owners):
    total = arrived[0]
    for owner in range(1, owners):
        total = total + arrived[owner]
    grads[...] = total[:GRAD_ROWS]
    feat_grad[...] = total[GRAD_ROWS : GRAD_ROWS + 4]
    pred[...] = total[GRAD_ROWS + 4 : GRAD_ROWS + 5] + proj_b[...]


def leave_kernel(*refs, shapes, width):
    half = width // 2
    terms = [ref[...] for ref in refs[:shapes]]
    while len(terms) > 1:
        terms = [terms[i] + terms[i + 1] for i in range(0, len(terms), 2)]
    left, right = terms[0][:, :width], terms[0][:, width:]
    outs = refs[shapes:]
    at = width + half
    enc_w1, enc_b1, enc_w2, enc_b2, lift_w, lift_b, skip_w, skip_b, dec_w1, dec_b1, dec_w2, dec_b2, proj_w, proj_b = outs
    enc_w2[...] = left[:width]
    dec_w2[...] = right[:width]
    skip_w[:half] = left[width:at]
    skip_w[half:] = right[width:at]
    enc_w1[...] = left[at : at + 6]
    dec_w1[...] = right[at : at + 6]
    enc_b1[...] = left[at + 6 : at + 7]
    dec_b1[...] = right[at + 6 : at + 7]
    enc_b2[...] = left[at + 7 : at + 8]
    dec_b2[...] = right[at + 7 : at + 8]
    lift_w[...] = left[at + 8 : at + 12]
    lift_b[...] = right[at + 8 : at + 9]
    skip_b[...] = right[at + 9 : at + 10]
    proj_w[...] = right[at + 10 : at + 11]
    proj_b[...] = right[at + 11 : at + 12, :1]


def shape(*dims, dtype=F32):
    return jax.ShapeDtypeStruct(dims, dtype)


def whole(array):
    zeros = (0,) * array.ndim
    return pl.BlockSpec(array.shape, lambda i: zeros, pipeline_mode=pl.Buffered(1))


HELD = VMEM
VMEM_BYTES = 64 << 20
FAR = pl.BlockSpec(memory_space=pl.ANY)


def kernel_call(kernel, name, steps, operands, out_shape, out_specs, scratch=(), micros=10, **more):
    arrays = [array for array, _ in operands]
    specs = [whole(array) if spec is None else spec for array, spec in operands]
    return pl.pallas_call(
        kernel,
        grid=(steps,),
        in_specs=specs,
        out_specs=out_specs,
        out_shape=out_shape,
        scratch_shapes=list(scratch),
        compiler_params=pltpu.CompilerParams(vmem_limit_bytes=VMEM_BYTES),
        cost_estimate=pl.CostEstimate(flops=0, bytes_accessed=micros * 2_000_000, transcendentals=0),
        name=name,
        **more,
    )(*arrays)


def on_device(
    mesh_feat,
    mesh_pos,
    query_pos,
    enc_cell,
    enc_point,
    enc_count,
    dec_cell,
    dec_query,
    dec_count,
    enc_w1,
    enc_b1,
    enc_w2,
    enc_b2,
    lift_w,
    lift_b,
    spec_w,
    skip_w,
    skip_b,
    dec_w1,
    dec_b1,
    dec_w2,
    dec_b2,
    proj_w,
    proj_b,
    pred_bar,
):
    width = lift_w.shape[1]
    owners = lax.axis_size("wide")
    shapes = lax.axis_size("grid")
    rows_here = RES // owners
    cells = rows_here * PLANE
    modes_here = spec_w.shape[0]
    lines = modes_here // MODES
    enc_blocks, dec_blocks = enc_cell.shape[1], dec_cell.shape[1]
    enc_edges, dec_edges = enc_blocks * LANES, dec_blocks * LANES
    enc_span, dec_span = ENC_GROUP * CHUNK, DEC_GROUP * CHUNK
    lanes = rows_here * width
    place = lax.axis_index("wide").astype(jnp.int32).reshape(1)
    plane_np = plane_matrix(owners)
    plane = jnp.asarray(np.stack(halves_np(plane_np)))
    inverse = jnp.asarray(np.stack(halves_np(np.ascontiguousarray(plane_np.T))))
    cos_x, sin_x = (jnp.asarray(part) for part in x_tables(rows_here, width))
    rows = [value.reshape(1, -1) for value in (enc_b1, enc_b2, lift_b, skip_b, dec_b1, dec_b2, proj_w, proj_b)]
    enc_b1, enc_b2, lift_b, skip_b, dec_b1, dec_b2, proj_w, proj_b = rows
    sizes = dict(owners=owners, cells=cells, width=width)
    dma = pltpu.SemaphoreType.DMA

    def exchange(value):
        return lax.all_to_all(value, "wide", 0, 0, tiled=True)

    payload = kernel_call(
        partial(share_kernel, owners=owners),
        "share_points",
        1,
        [
            (value, None)
            for value in (
                mesh_feat, mesh_pos.transpose(1, 0, 2), query_pos.transpose(1, 0, 2), pred_bar, dec_query[0], dec_count
            )
        ],
        shape(owners, 2 * FEAT_ROWS + owners, LANES),
        HELD,
    )
    shared = exchange(payload)
    local = [enc_cell[0], enc_point[0], enc_count, dec_cell[0], dec_query[0], dec_count]
    enc_keys, dec_keys, bounds = kernel_call(
        partial(sort_kernel, owners=owners, cells=cells),
        "sort_edges",
        1,
        [(value, None) for value in local] + [(payload, FAR)],
        [
            shape(LANES, enc_blocks, dtype=jnp.int32),
            shape(LANES, dec_blocks, dtype=jnp.int32),
            shape(8, LANES, dtype=jnp.int32),
        ],
        [HELD] * 3,
    )

    fixed = owners * FEAT_ROWS
    saved_rows = 4 * width + FEAT_ROWS
    plane_scratch = pltpu.VMEM((2, 2 * MODES * MODES, PLANE), BF16)
    inverse_scratch = pltpu.VMEM((2, PLANE, 2 * MODES * MODES), BF16)
    saved, lat, scale, plane_lat = kernel_call(
        partial(enc_forward_kernel, **sizes),
        "encode",
        1,
        [(place, SMEM), (bounds, SMEM), (enc_keys, HELD), (shared, HELD)]
        + [(value, None) for value in (enc_w1, enc_b1, enc_w2, enc_b2, lift_w, lift_b)]
        + [(plane, FAR)],
        [
            shape(saved_rows, enc_edges),
            shape(PLANE, lanes),
            shape(ENC_CELLS, lanes),
            shape(2 * MODES * MODES, lanes),
        ],
        [FAR, FAR, FAR, HELD],
        [
            pltpu.VMEM((cells + PAD, 2 * LANES), F32),
            pltpu.VMEM((2 * fixed, LANES), BF16),
            pltpu.VMEM((2 * width, INPUT_ROWS), BF16),
            pltpu.VMEM((width, 3 * width), BF16),
            pltpu.VMEM((2 * width + 16, enc_span), BF16),
            plane_scratch,
            pltpu.VMEM((PLANE, lanes), F32),
            pltpu.VMEM((ENC_CELLS, lanes), F32),
            dma((3,)),
            pltpu.VMEM((2, saved_rows, enc_span), F32),
            dma((2,)),
        ],
    )
    modes_lines = exchange(plane_lat.reshape(owners, 2 * lines, lanes))

    dec_rows = 2 * width + FEAT_ROWS
    dec_steps = dec_edges // dec_span
    half_steps = dec_steps // 2

    def dec_sums(first_step, steps, before, saved_before, after, more, out_shape, scratch, name):
        return kernel_call(
            partial(dec_sums_kernel, first_step=first_step, **sizes),
            name,
            steps,
            [
                (place, SMEM), (bounds, SMEM), (dec_keys, HELD), (shared, HELD), (dec_w1, None), (dec_b1, None),
                (before, HELD if first_step else FAR), (saved_before, FAR), (after, FAR),
            ]
            + more,
            [shape(dec_rows, dec_edges)] + out_shape,
            [pl.BlockSpec((dec_rows, dec_span), lambda i: (0, i + first_step))] + [HELD] * len(out_shape),
            scratch
            + [
                pltpu.VMEM((2 * fixed, LANES), BF16),
                pltpu.VMEM((width, INPUT_ROWS), BF16),
                pltpu.VMEM((2 * width + 16, dec_span), BF16),
            ],
            input_output_aliases={7: 0} if first_step else {},
        )

    dec_saved, dec_total, inverse_degree, skip = dec_sums(
        0, half_steps, plane_lat, plane_lat, plane_lat, [(lat, HELD), (skip_w, None), (skip_b, None)],
        [shape(cells + PAD, 2 * LANES), shape(owners, LANES), shape(PLANE, lanes)], [], "decode_sums_a",
    )

    mix_step, grad_step = min(MIX_STEP, modes_here), min(GRAD_STEP, modes_here)

    def spec_block(step):
        return pl.BlockSpec((step, width, 2 * width), lambda i: (i, 0, 0))

    def mode_pass(kernel, lines_in, after, name):
        return kernel_call(
            partial(kernel, owners=owners, width=width),
            name,
            1,
            [(place, SMEM), (lines_in, HELD), (cos_x, None), (sin_x, None), (spec_w, FAR)]
            + [(value, FAR) for value in after],
            [shape(modes_here, 2 * width), shape(owners, 2 * lines, lanes)],
            [HELD, HELD],
            [
                pltpu.VMEM((modes_here, 2 * width), F32),
                pltpu.VMEM((modes_here, width, 2 * width), F32),
                dma((modes_here // mix_step,)),
            ],
        )

    modes, back_lines = mode_pass(mix_kernel, modes_lines, [inverse_degree], "mix_modes")
    def from_shapes(value, staged=True):
        parts, step = {0: value}, shapes // 2
        if staged:
            while step:
                pairs = [(i, i ^ step) for i in range(shapes)]
                parts.update({d ^ step: lax.ppermute(part, "grid", pairs) for d, part in parts.items()})
                step //= 2
        else:
            for step in range(1, shapes):
                parts[step] = lax.ppermute(value, "grid", [(i, i ^ step) for i in range(shapes)])
        return [parts[d] for d in range(shapes)]

    all_modes = from_shapes(modes)
    grid_lines = exchange(back_lines).reshape(2 * MODES * MODES, lanes)
    dec_saved, sums, reach = dec_sums(
        half_steps, dec_steps - half_steps, dec_total, dec_saved, back_lines,
        [(dec_w2, None), (dec_b2, None)],
        [shape(2, PLANE, lanes), shape(PLANE, lanes)],
        [pltpu.VMEM((cells + PAD, 2 * LANES), F32)],
        "decode_sums_b",
    )

    plane_bar, pre_bar, latent = kernel_call(
        partial(grid_kernel, rows_here=rows_here),
        "grid_fields",
        1,
        [(grid_lines, FAR), (reach, FAR), (skip, FAR), (proj_w, None), (inverse, FAR), (plane, FAR)]
        + [(value, FAR) for value in all_modes[shapes // 2 :][:1]],
        [shape(2 * MODES * MODES, lanes)] + [shape(PLANE, lanes)] * 2,
        [HELD, FAR, FAR],
        [
            pltpu.VMEM((2 * MODES * MODES, lanes), F32),
            inverse_scratch,
            pltpu.VMEM((PLANE, lanes), F32),
            pltpu.VMEM((PLANE, lanes), F32),
            plane_scratch,
            pltpu.VMEM((PLANE, lanes), F32),
            pltpu.VMEM((PLANE, lanes), F32),
            dma((7,)),
        ],
    )
    bar_lines = exchange(plane_bar.reshape(owners, 2 * lines, lanes))

    skip_w_grad, dec_w2_grad, row_grads, dec_table, skip_back = kernel_call(
        partial(grid_grads_kernel, rows_here=rows_here, width=width),
        "grid_grads",
        1,
        [(value, HELD) for value in (lat, pre_bar, latent, reach, sums)]
        + [(value, None) for value in (skip_w, dec_w2, dec_b2, proj_w)],
        [
            shape(width, width),
            shape(width, width),
            shape(8, width),
            shape(cells + PAD, 2 * LANES, dtype=BF16),
            shape(PLANE, lanes),
        ],
        [HELD] * 5,
    )

    mixed_bar, bar_back = mode_pass(mix_back_kernel, bar_lines, [row_grads] + all_modes[1:], "mix_back")
    bar_grid_lines = exchange(bar_back).reshape(2 * MODES * MODES, lanes)

    all_grads = from_shapes(mixed_bar)

    count8 = max(owners, 8)
    pred_part, dec_w1_grad, dec_b1_grad = kernel_call(
        partial(dec_edges_kernel, **sizes),
        "decode_edges",
        dec_steps,
        [
            (place, SMEM), (bounds, SMEM), (dec_keys, HELD), (inverse_degree, HELD),
            (dec_saved, pl.BlockSpec((dec_rows, dec_span), lambda i: (0, i))), (dec_table, HELD),
        ],
        [shape(owners, LANES), shape(6, width), shape(1, width)],
        [HELD] * 3,
        [
            pltpu.VMEM((2 * width + 16, dec_span), F32),
            pltpu.VMEM((2 * count8, LANES), F32),
            pltpu.VMEM((2 * width, 32), F32),
        ],
    )

    packed = kernel_call(
        partial(enc_back_kernel, **sizes),
        "encode_back",
        1,
        [(place, SMEM), (bounds, SMEM), (enc_keys, HELD), (saved, FAR)]
        + [(value, FAR) for value in (bar_grid_lines, skip_back, scale)]
        + [(value, None) for value in (enc_w2, lift_w, pred_bar)]
        + [(value, HELD) for value in (skip_w_grad, dec_w2_grad, row_grads, pred_part, dec_w1_grad, dec_b1_grad)]
        + [(inverse, FAR)]
        + [(value, FAR) for value in all_grads[shapes // 2 :][:1]],
        shape(owners, PACKED_ROWS, LANES),
        HELD,
        [
            pltpu.VMEM((cells + PAD, 2 * width), BF16),
            pltpu.VMEM((2 * width, enc_span), F32),
            pltpu.VMEM((width, 3 * width), BF16),
            pltpu.VMEM((16, 2 * width), BF16),
            pltpu.VMEM((8 * count8, LANES), F32),
            pltpu.VMEM((6 * width + 16, 2 * width + 32), F32),
            pltpu.VMEM((2, ENC_CELLS, 2 * MODES * MODES), BF16),
            pltpu.VMEM((2 * MODES * MODES, lanes), F32),
            pltpu.VMEM((ENC_CELLS, lanes), F32),
            pltpu.VMEM((ENC_CELLS, lanes), F32),
            dma((4,)),
            pltpu.VMEM((2, saved_rows, enc_span), F32),
            dma((2,)),
        ],
    )
    arrived = exchange(packed)

    rank = lax.axis_index("grid").astype(jnp.int32).reshape(1)
    spec_grad = kernel_call(
        partial(spec_grad_kernel, shapes=shapes, width=width),
        "spec_grad",
        modes_here // grad_step,
        [(rank, SMEM)]
        + [
            (value, pl.BlockSpec((grad_step, 2 * width), lambda i: (i, 0)))
            for value in all_modes + all_grads
        ]
        + [(packed, FAR)],
        shape(modes_here, width, 2 * width),
        spec_block(grad_step),
        [pltpu.VMEM((shapes, grad_step, 2 * width), F32)] * 2,
    )

    grads, feat_grad, pred = kernel_call(
        partial(arrive_kernel, owners=owners),
        "arrive",
        1,
        [(arrived, HELD), (proj_b, None), (spec_grad, FAR)],
        [shape(GRAD_ROWS, LANES), shape(4, LANES), shape(1, LANES)],
        [HELD] * 3,
    )
    terms = from_shapes(grads, staged=False)
    vector = shape(1, width)
    square = shape(width, width)
    first = shape(6, width)
    outs = kernel_call(
        partial(leave_kernel, shapes=shapes, width=width),
        "leave",
        1,
        [(term, HELD) for term in terms],
        [
            first, vector, square, vector, shape(4, width), vector,
            square, vector, first, vector, square, vector, vector, shape(1, 1),
        ],
        [HELD] * 14,
    )
    outs = [out.reshape(-1) if out.shape[0] == 1 else out for out in outs]
    return (pred, feat_grad[None], *outs[:6], spec_grad, *outs[6:])


def solution(mesh):
    placed = (
        P("grid", None, "wide"),
        P("grid", None, "wide"),
        P("grid", None, "wide"),
        P("grid", "wide", None),
        P("grid", "wide", None),
        P("grid", "wide"),
        P("grid", "wide", None),
        P("grid", "wide", None),
        P("grid", "wide"),
        P(),
        P(),
        P(),
        P(),
        P(),
        P(),
        P("wide", None, None),
        P(),
        P(),
        P(),
        P(),
        P(),
        P(),
        P(),
        P(),
        P("grid", "wide"),
    )
    return jax.shard_map(
        on_device,
        mesh=mesh,
        in_specs=placed,
        out_specs=(
            P("grid", "wide"),
            P("grid", None, "wide"),
            P(),
            P(),
            P(),
            P(),
            P(),
            P(),
            P("wide", None, None),
            P(),
            P(),
            P(),
            P(),
            P(),
            P(),
            P(),
            P(),
        ),
        check_vma=False,
    )
```

```python
from functools import partial
import math

import jax
import jax.numpy as jnp
import ml_dtypes
import numpy as np
from jax import lax
from jax.experimental import pallas as pl
from jax.experimental.pallas import tpu as pltpu
from jax.sharding import PartitionSpec as P

MODES = 16
RES = 32
PLANE = RES * RES
ENC_CELLS = RES * (RES - RES // 4)
CHUNK = 256
LANES = 128
ENC_GROUP = 16
DEC_GROUP = 16
FEW = 4
FEAT_ROWS = 8
INPUT_ROWS = 48
ENC_WINDOW = 64
DEC_WINDOW = 128
PAD = 256
MIX_STEP = 64
GRAD_STEP = 128
F32 = jnp.float32
BF16 = jnp.bfloat16
GELU_A = 0.7978845608028654
GELU_B = 0.044715

NN = (((1,), (0,)), ((), ()))
NT = (((1,), (1,)), ((), ()))
TN = (((0,), (0,)), ((), ()))

VMEM = pl.BlockSpec(memory_space=pltpu.VMEM)
SMEM = pl.BlockSpec(memory_space=pltpu.SMEM)


def kept_freqs():
    half = MODES // 2
    return np.concatenate([np.arange(half), np.arange(RES - half, RES)])


def plane_matrix(owners):
    lines = MODES * MODES // owners
    line = np.arange(MODES * MODES)
    freq_y, freq_z = kept_freqs()[line // MODES], line % MODES
    cell = np.arange(PLANE)
    turns = (freq_y[:, None] * (cell // RES) + freq_z[:, None] * (cell % RES)) % RES
    angle = turns * (2.0 * math.pi / RES)
    both = np.stack([np.cos(angle), -np.sin(angle)]).reshape(2, owners, lines, PLANE)
    matrix = both.transpose(1, 0, 2, 3).reshape(2 * MODES * MODES, PLANE)
    return matrix.astype(np.float32)


def halves_np(matrix):
    high = matrix.astype(ml_dtypes.bfloat16)
    low = (matrix - high.astype(np.float32)).astype(ml_dtypes.bfloat16)
    return high, low


def line_angles():
    turns = (kept_freqs()[:, None] * np.arange(RES)[None, :]) % RES
    return turns * (2.0 * math.pi / RES)


def x_tables(rows_here, width):
    angle = line_angles().reshape(MODES, RES // rows_here, rows_here, 1)
    angle = np.broadcast_to(angle, (MODES, RES // rows_here, rows_here, width))
    angle = angle.reshape(MODES, RES // rows_here, rows_here * width)
    return np.cos(angle).astype(np.float32), np.sin(angle).astype(np.float32)


def log2(number):
    return number.bit_length() - 1


def iota(shape, axis):
    return lax.broadcasted_iota(jnp.int32, shape, axis)


def halves(value):
    high = value.astype(BF16)
    low = (value - high.astype(F32)).astype(BF16)
    return high, low


def dot(a, b, dims=NN):
    return lax.dot_general(a, b, dims, preferred_element_type=F32)


def dot3(a, b, dims=NN):
    a_high, a_low = halves(a)
    b_high, b_low = halves(b)
    return dot(a_high, b_high, dims) + dot(a_low, b_high, dims) + dot(a_high, b_low, dims)


def one_hot(index, first, rows):
    places = iota((rows, index.shape[1]), 0)
    return jnp.where(places == index - first, 1.0, 0.0).astype(BF16)


def gelu_both(value):
    square = value * value
    half = 0.5 + 0.5 * jnp.tanh(value * (GELU_A + (GELU_A * GELU_B) * square))
    out = value * half
    return out, half + (out - out * half) * (2.0 * GELU_A + (6.0 * GELU_A * GELU_B) * square)


def sort_steps(values):
    rows = values.shape[0]
    regs = rows // 8
    low = log2(regs)
    total = low + 3 + 7
    sub = iota((8, LANES), 0)
    lane = iota((8, LANES), 1)
    x = values.reshape(regs, 8, LANES)

    def flip(x, bit):
        if bit >= total:
            return x
        if bit < low:
            y = x.reshape(regs >> (bit + 1), 2, 1 << bit, 8, LANES)
            return jnp.stack([y[:, 0], -y[:, 1]], axis=1).reshape(regs, 8, LANES)
        if bit < low + 3:
            sign = 1 - 2 * ((sub >> (bit - low)) & 1)
        else:
            sign = 1 - 2 * ((lane >> (bit - low - 3)) & 1)
        return x * sign.astype(F32)[None]

    def exchange(x, bit):
        if bit < low:
            y = x.reshape(regs >> (bit + 1), 2, 1 << bit, 8, LANES)
            one, two = y[:, 0], y[:, 1]
            pair = [jnp.minimum(one, two), jnp.maximum(one, two)]
            return jnp.stack(pair, axis=1).reshape(regs, 8, LANES)
        if bit < low + 3:
            axis, dist, size, place = 1, 1 << (bit - low), 8, sub
        else:
            axis, dist, size, place = 2, 1 << (bit - low - 3), LANES, lane
        after = pltpu.roll(x, size - dist, axis)
        before = after if 2 * dist == size else pltpu.roll(x, dist, axis)
        first = ((place & dist) == 0)[None]
        return jnp.where(first, jnp.minimum(x, after), jnp.maximum(x, before))

    for phase in range(1, total + 1):
        x = flip(x, phase)
        for bit in reversed(range(phase)):
            x = exchange(x, bit)
            yield x
        x = flip(x, phase)
    yield x.reshape(rows, LANES)


def sort_together(arrays):
    running = [(i, sort_steps(array)) for i, array in enumerate(arrays)]
    held = list(arrays)
    while running:
        left = []
        for i, steps in running:
            value = next(steps, None)
            if value is not None:
                held[i] = value
                left.append((i, steps))
        running = left
    return held


def layer_matrix(feat_rows, cell_rows):
    feat_high, feat_low = halves(feat_rows)
    cell_high, cell_low = halves(cell_rows)
    parts = [feat_high, feat_high, feat_low, cell_high, cell_low]
    parts = [part.astype(F32) for part in parts] + [jnp.zeros((LANES - 40, feat_rows.shape[1]), F32)]
    return jnp.concatenate(parts, axis=0).T[:, :INPUT_ROWS].astype(BF16)


def place_rows(cell, first_row):
    row = iota((8, cell.shape[1]), 0)
    shifts = jnp.where(row == 0, 2 * log2(RES), jnp.where(row == 1, log2(RES), 0))
    place = (cell >> shifts) & jnp.where(row < 3, RES - 1, 0)
    return (place + jnp.where(row == 0, first_row, 0)).astype(F32)


def edge_feats(key, table, owners):
    point = key & (owners * LANES - 1)
    found = dot(table, one_hot(point & (LANES - 1), 0, LANES))
    owner = (iota(found.shape, 0) >> 3) & (owners - 1)
    found = jnp.where(owner == (point >> 7), found, 0.0)
    return jnp.sum(found.reshape(2 * owners, FEAT_ROWS, key.shape[1]), axis=0)


def stack_inputs(feats, place):
    high, low = halves(feats)
    parts = [high.astype(F32), low.astype(F32), high.astype(F32), place, place, jnp.zeros_like(place)]
    return jnp.concatenate(parts, axis=0).astype(BF16)


def stack3(value):
    high, low = halves(value)
    return jnp.concatenate([high, low, high], axis=0)


def weights3(matrix):
    high, low = halves(matrix)
    return jnp.concatenate([high, high, low], axis=1)


def key_row(keys_ref, chunk):
    per = CHUNK // keys_ref.shape[1]
    rows = [keys_ref[pl.ds(chunk * per + i, 1), :] for i in range(per)]
    return rows[0] if per == 1 else jnp.concatenate(rows, axis=1)


def cell_range(bounds_ref, line, chunk, per):
    return bounds_ref[line, chunk * per], bounds_ref[line + 1, chunk * per + per - 1]


def spread(block, copies):
    rows, columns = block.shape
    tiled = jnp.concatenate([jnp.concatenate([block] * copies, axis=1)] * copies, axis=0)
    return jnp.where(
        iota(tiled.shape, 0) // rows == iota(tiled.shape, 1) // columns, tiled, 0.0
    )


def gather_blocks(product, copies, rows, columns):
    total = product[:rows, :columns]
    for i in range(1, copies):
        total = total + product[i * rows : (i + 1) * rows, i * columns : (i + 1) * columns]
    return total


def tile_lanes(row, copies):
    return row if copies == 1 else jnp.concatenate([row] * copies, axis=1)


def fold_lanes(row, copies, width):
    total = row[:, :width]
    for i in range(1, copies):
        total = total + row[:, i * width : (i + 1) * width]
    return total


def column(counts):
    return jnp.broadcast_to(counts, (8, counts.shape[1])).T[:, :1]


def share_kernel(feat, pos, query_pos, pred_bar, dec_query, dec_count, payload, *, owners):
    blocks = dec_query.shape[0]
    lane_valid = jnp.where(
        iota((blocks, LANES), 1) < column(dec_count[...]), dec_query[...], owners * LANES
    )
    ones = jnp.zeros((max(owners, 16), LANES), F32)
    degree = ones
    for block in range(0, blocks, 2):
        row = jnp.concatenate([lane_valid[block : block + 1], lane_valid[block + 1 : block + 2]], axis=1)
        high = one_hot(row >> 7, 0, ones.shape[0])
        low = one_hot(row & (LANES - 1), 0, LANES)
        degree = degree + dot(high, low, NT)
    filled = jnp.ones((1, LANES), F32)
    empty = jnp.zeros((3, LANES), F32)
    places = [pos[i] for i in range(3)]
    queries = [query_pos[i] for i in range(3)]
    rows = places + [filled, feat[0]] + queries + [filled, pred_bar[...], empty, degree[:owners]]
    mine = jnp.concatenate(rows, axis=0)
    for owner in range(owners):
        payload[owner] = mine


def sort_kernel(
    enc_cell, enc_point, enc_count, dec_cell, dec_query, dec_count, after,
    enc_keys, dec_keys, bounds, *, owners, cells,
):
    shift = log2(owners * LANES)

    def keys(cell, point, count):
        lane = iota(cell.shape, 1)
        key = jnp.where(lane < column(count), (cell << shift) | point, cells << shift)
        return key.astype(F32)

    drawn = [
        keys(enc_cell[...], enc_point[...], enc_count[...]),
        keys(dec_cell[...], dec_query[...], dec_count[...]),
    ]
    enc, dec = (value.astype(jnp.int32) for value in sort_together(drawn))
    enc_keys[...] = enc.T
    dec_keys[...] = dec.T
    ends = [enc[:1], enc[-1:], dec[:1], dec[-1:]]
    bounds[...] = jnp.concatenate(ends + [jnp.zeros((4, LANES), jnp.int32)], axis=0) >> shift


def joined_keys(keys, chunk, group):
    rows = [key_row(keys, chunk + i) for i in range(group)]
    return rows, jnp.concatenate(rows, axis=1)


def later_windows(windows, size, visit):
    most = windows[0][1]
    for _, count in windows[1:]:
        most = jnp.maximum(most, count)

    @pl.when(most > 1)
    def _():
        for i, (begin, count) in enumerate(windows):

            def more(j, carry):
                visit(i, begin + j * size)
                return carry

            lax.fori_loop(1, count, more, 0)


def scatter_windows(total, keys, cell, message, bounds, line, chunk, group, size, shift, columns):
    per = CHUNK // keys.shape[1]
    windows, parts = [], []
    for i in range(group):
        begin, end = cell_range(bounds, line, chunk + i, per)
        begin = pl.multiple_of(begin & -8, 8)
        lanes = slice(i * CHUNK, (i + 1) * CHUNK)
        parts.append(dot(one_hot(cell[:, lanes], begin, size), message[:, lanes], NT))
        windows.append((begin, (end - begin) // size + 1))
    for (begin, _), part in zip(windows, parts):
        total[pl.ds(begin, size), :columns] += part

    def visit(i, start):
        start = pl.multiple_of(start, 8)
        hot = one_hot(key_row(keys, chunk + i) >> shift, start, size)
        part = dot(hot, message[:, i * CHUNK : (i + 1) * CHUNK], NT)
        total[pl.ds(start, size), :columns] += part

    later_windows(windows, size, visit)


def gather_windows(found, keys, rows, table, bounds, line, chunk, group, size, shift, columns):
    per = CHUNK // keys.shape[1]
    windows = []
    for i in range(group):
        begin, end = cell_range(bounds, line, chunk + i, per)
        begin = pl.multiple_of(begin & -16, 16)
        hot = one_hot(rows[i] >> shift, begin, size)
        found[:, i * CHUNK : (i + 1) * CHUNK] = dot(table[pl.ds(begin, size), :columns], hot, TN)
        windows.append((begin, (end - begin) // size + 1))

    def visit(i, start):
        start = pl.multiple_of(start, 16)
        hot = one_hot(key_row(keys, chunk + i) >> shift, start, size)
        part = dot(table[pl.ds(start, size), :columns], hot, TN)
        found[:, i * CHUNK : (i + 1) * CHUNK] += part

    later_windows(windows, size, visit)


def slot_copies(far, slots, semaphores, out):
    span = slots.shape[2]

    def copy(step):
        slot = step % 2
        columns = far.at[:, pl.ds(pl.multiple_of(step * span, span), span)]
        ends = (slots.at[slot], columns) if out else (columns, slots.at[slot])
        return pltpu.make_async_copy(*ends, semaphores.at[slot])

    return copy


def used_steps(bounds, line, group, per, cells, steps):
    used = 0
    for step in range(steps):
        used = used + jnp.where(bounds[line, step * group * per] < cells, 1, 0)
    return used


def each_size(bounds, line, chunk, group, per, cells, body):
    few = min(FEW, group)
    some = bounds[line, chunk * per] < cells
    if few == group:
        pl.when(some)(lambda: body(group))
        return
    many = bounds[line, (chunk + few) * per] < cells
    pl.when(many)(lambda: body(group))
    pl.when(some & jnp.logical_not(many))(lambda: body(few))


def enc_forward_kernel(
    place_ref, bounds, keys, shared, w1, b1, w2, b2, lift_w, lift_b, plane_hbm,
    saved_hbm, lat_far, scale_far, plane_out,
    total, table, first, second, message, plane, lat, scale, copied, slots, stored,
    *, owners, cells, width,
):
    rows_here = cells // PLANE
    group = message.shape[1] // CHUNK
    shift = log2(owners * LANES)
    first_row = place_ref[0] * rows_here
    copy = pltpu.make_async_copy(plane_hbm, plane, copied.at[0])
    save = slot_copies(saved_hbm, slots, stored, out=True)

    def begin():
        copy.start()
        total[...] = jnp.zeros_like(total)
        feats = jnp.concatenate([shared[i, :FEAT_ROWS] for i in range(owners)], axis=0)
        table[...] = jnp.concatenate(halves(feats), axis=0)
        empty = jnp.zeros((3, width), F32)
        pre_rows = jnp.concatenate([w1[3:6], b1[...], jnp.zeros((4, width), F32)], axis=0)
        lift_rows = jnp.concatenate([empty, lift_b[...], lift_w[...]], axis=0)
        cell_rows = jnp.concatenate([w1[0:3] / (RES - 1.0), jnp.zeros((5, width), F32)], axis=0)
        first[...] = layer_matrix(
            jnp.concatenate([pre_rows, lift_rows], axis=1),
            jnp.concatenate([cell_rows, jnp.zeros((8, width), F32)], axis=1),
        )
        second[...] = weights3(w2[...].T)

    def run_step(step, carry):
        chunk = step * group
        per = CHUNK // keys.shape[1]

        def body(count):
            bias = jnp.broadcast_to(b2[...], (8, width)).T[:, :1]
            _, key = joined_keys(keys, chunk, count)
            cell = key >> shift

            @pl.when(step >= 2)
            def _():
                save(step - 2).wait()

            saved = slots.at[step % 2]
            run = slice(0, count * CHUNK)
            feats = edge_feats(key, table[...], owners)
            both = dot(first[...], stack_inputs(feats, place_rows(cell, first_row)))
            lifted = both[width:]
            hidden, slope = gelu_both(both[:width])
            kernel = dot(second[...], stack3(hidden)) + bias
            saved[0 * width : 1 * width, run] = hidden
            saved[1 * width : 2 * width, run] = slope
            saved[2 * width : 3 * width, run] = lifted
            saved[3 * width : 4 * width, run] = kernel
            saved[4 * width :, run] = feats
            high, low = halves(kernel * lifted)
            message[:, run] = jnp.concatenate([high, low, jnp.ones((16, count * CHUNK), BF16)], axis=0)
            save(step).start()
            scatter_windows(
                total, keys, cell, message, bounds, 0, chunk, count, ENC_WINDOW, shift, 2 * width + 16
            )

        each_size(bounds, 0, chunk, group, per, cells, body)
        return carry

    begin()
    steps = keys.shape[0] * keys.shape[1] // slots.shape[2]
    used = used_steps(bounds, 0, group, CHUNK // keys.shape[1], cells, steps)
    lax.fori_loop(0, used, run_step, 0)
    def end():
        fields, scales = [], []
        for row in range(rows_here):
            slab = total[row * PLANE : row * PLANE + ENC_CELLS]
            inverse = 1.0 / jnp.maximum(slab[:, 2 * width : 2 * width + 1], 1.0)
            fields.append((slab[:, :width] + slab[:, width : 2 * width]) * inverse)
            scales.append(jnp.broadcast_to(inverse, (ENC_CELLS, width)))
        field = jnp.concatenate(fields, axis=1)
        lat[:ENC_CELLS] = field
        lat[ENC_CELLS:] = jnp.zeros((PLANE - ENC_CELLS, field.shape[1]), F32)
        scale[...] = jnp.concatenate(scales, axis=1)
        leaving = [
            pltpu.make_async_copy(lat, lat_far, copied.at[1]),
            pltpu.make_async_copy(scale, scale_far, copied.at[2]),
        ]
        for out in leaving:
            out.start()
        copy.wait()
        plane_out[...] = times_field(plane.at[:, :, pl.ds(0, ENC_CELLS)], field)
        for out in leaving:
            out.wait()

        @pl.when(used >= 2)
        def _():
            save(used - 2).wait()

        @pl.when(used >= 1)
        def _():
            save(used - 1).wait()

    end()


def times_field(matrix, field):
    high, low = halves(field)
    first, second = matrix[0], matrix[1]
    return dot(first, high) + dot(second, high) + dot(first, low)


def dec_sums_kernel(
    place_ref, bounds, keys, shared, w1, b1, before, saved_before, after, *refs,
    owners, cells, width, first_step,
):
    if first_step == 0:
        lat, skip_w, skip_b, saved, total, inverse_out, skip, table, first, message = refs
    else:
        dec_w2, dec_b2, saved, sums, reach, total, table, first, message = refs
    step = pl.program_id(0)
    rows_here = cells // PLANE
    group = message.shape[1] // CHUNK
    shift = log2(owners * LANES)
    first_row = place_ref[0] * rows_here

    @pl.when(step == 0)
    def _():
        total[...] = jnp.zeros_like(total) if first_step == 0 else before[...]
        degree = shared[0, 2 * FEAT_ROWS :]
        for i in range(1, owners):
            degree = degree + shared[i, 2 * FEAT_ROWS :]
        inverse = 1.0 / jnp.maximum(degree, 1.0)
        if first_step == 0:
            inverse_out[...] = inverse
        feats = []
        for i in range(owners):
            rows = shared[i, FEAT_ROWS : 2 * FEAT_ROWS]
            weighted = rows * inverse[i : i + 1]
            feats.append(jnp.where(iota(rows.shape, 0) == 4, weighted, rows))
        table[...] = jnp.concatenate(halves(jnp.concatenate(feats, axis=0)), axis=0)
        feat_rows = jnp.concatenate([w1[0:3], b1[...], jnp.zeros((4, width), F32)], axis=0)
        cell_rows = jnp.concatenate([w1[3:6] / (RES - 1.0), jnp.zeros((5, width), F32)], axis=0)
        first[...] = layer_matrix(feat_rows, cell_rows)

    chunk = (step + first_step) * group
    per = CHUNK // keys.shape[1]

    def body(count):
        _, key = joined_keys(keys, chunk, count)
        run = slice(0, count * CHUNK)
        cell = key >> shift
        feats = edge_feats(key, table[...], owners)
        hidden, slope = gelu_both(dot(first[...], stack_inputs(feats, place_rows(cell, first_row))))
        weight = feats[4:5]
        saved[0 * width : 1 * width, run] = hidden
        saved[1 * width : 2 * width, run] = slope * weight
        saved[2 * width :, run] = feats
        high, low = halves(hidden * weight)
        w_high, w_low = halves(feats)
        tail = jnp.concatenate([w_high.astype(F32), w_low.astype(F32)], axis=0).astype(BF16)
        message[:, run] = jnp.concatenate([high, low, tail], axis=0)
        scatter_windows(
            total, keys, cell, message, bounds, 2, chunk, count, DEC_WINDOW, shift, 2 * width + 16
        )

    each_size(bounds, 2, chunk, group, per, cells, body)

    @pl.when(step == pl.num_programs(0) - 1)
    def _():
        if first_step == 0:
            skipped = dot3(lat[...], spread(skip_w[...], rows_here))
            skip[...] = skipped + tile_lanes(skip_b[...], rows_here)
            return
        sums[0], sums[1] = cell_sums(total, rows_here, width)
        reached = dot3(sums[0], spread(dec_w2[...], rows_here))
        reach[...] = reached + sums[1] * tile_lanes(dec_b2[...], rows_here)


def x_forward(lines_ref, cos_ref, sin_ref, put, owners, lines, width):
    lanes = lines_ref.shape[2]

    def fold(value):
        if lanes == width:
            return value
        while value.shape[1] > 2 * width:
            half = value.shape[1] // 2
            value = value[:, :half] + value[:, half:]
        return value + pltpu.roll(value, width, 1)

    def join(real, imag):
        if lanes == width:
            return jnp.concatenate([real, imag], axis=1)
        return jnp.where(iota(real.shape, 1) < width, real, imag)

    for kx in range(MODES // 2 + 1):
        cos_real = cos_imag = sin_real = sin_imag = jnp.zeros((lines, lanes), F32)
        for owner in range(owners):
            cos, sin = cos_ref[kx, owner : owner + 1], sin_ref[kx, owner : owner + 1]
            line_real, line_imag = lines_ref[owner, :lines], lines_ref[owner, lines:]
            cos_real, cos_imag = cos_real + cos * line_real, cos_imag + cos * line_imag
            if kx > 0:
                sin_real, sin_imag = sin_real + sin * line_real, sin_imag + sin * line_imag
        put(kx, join(fold(cos_real + sin_imag), fold(cos_imag - sin_real)))
        if 0 < kx < MODES // 2:
            put(MODES - kx, join(fold(cos_real - sin_imag), fold(cos_imag + sin_real)))


def x_inverse(take, out_ref, owners, lines, width):
    rows_here = RES // owners
    half = MODES // 2
    modes = [take(kx) for kx in range(MODES)]
    lane = iota(modes[0].shape, 1)

    def turn(mode):
        turned = pltpu.roll(mode, width, 1)
        return jnp.where(lane < width, -turned, turned)

    even = [modes[0]] + [modes[k] + modes[MODES - k] for k in range(1, half)] + [modes[half]]
    odd = [None] + [turn(modes[k] - modes[MODES - k]) for k in range(1, half)] + [-turn(modes[half])]

    def weighted(values, factors):
        total = None
        for value, factor in zip(values, factors):
            if value is None or abs(factor) < 1e-9:
                continue
            factor = float(np.float32(factor))
            term = value if factor == 1.0 else value * factor
            total = term if total is None else total + term
        return total

    rows = {}
    for x in range(RES // 2 + 1):
        angles = np.arange(half + 1) * x % RES * (2.0 * math.pi / RES)
        cos_part, sin_part = weighted(even, np.cos(angles)), weighted(odd, np.sin(angles))
        rows[x] = cos_part if sin_part is None else cos_part + sin_part
        if 0 < x < RES // 2:
            rows[RES - x] = cos_part - sin_part
        for owner in {x // rows_here, (RES - x) % RES // rows_here}:
            here = [rows.get(owner * rows_here + i) for i in range(rows_here)]
            if any(value is None for value in here):
                continue
            if rows_here == 1:
                out_ref[owner, :lines] = here[0][:, :width]
                out_ref[owner, lines:] = here[0][:, width:]
                continue
            for pair in range(rows_here // 2):
                one, two = here[2 * pair], here[2 * pair + 1]
                one_turned, two_turned = pltpu.roll(one, width, 1), pltpu.roll(two, width, 1)
                where = slice(2 * pair * width, (2 * pair + 2) * width)
                out_ref[owner, :lines, where] = jnp.where(lane < width, one, two_turned)
                out_ref[owner, lines:, where] = jnp.where(lane < width, one_turned, two)


def factor_column(place_ref, lines):
    line = place_ref[0] * lines + iota((lines, 1), 0)
    return jnp.where((line & (MODES - 1)) == 0, 1.0, 2.0) / float(RES**3)


def split_weights(spec_w, base, width):
    block = spec_w[pl.ds(base, 8)].reshape(8 * width, 2 * width)
    return jnp.concatenate(halves(block), axis=1)


def interleave(one, two):
    parts = []
    for at in range(0, one.shape[0], 8):
        parts += [one[at : at + 8], two[at : at + 8]]
    return jnp.concatenate(parts, axis=0)


def fetch_weights(spec_hbm, spec_w, copied):
    count = spec_w.shape[0] // copied.shape[0]

    def copy(i):
        where = pl.ds(i * count, count)
        return pltpu.make_async_copy(spec_hbm.at[where], spec_w.at[where], copied.at[i])

    return count, copy


def mix_kernel(
    place_ref, lines_ref, cos_ref, sin_ref, spec_hbm, *refs, owners, width,
):
    modes, out_ref, mixed, spec_w, copied = refs[-5:]
    lines = MODES * MODES // owners
    count, copy = fetch_weights(spec_hbm, spec_w, copied)
    for i in range(copied.shape[0]):
        copy(i).start()

    def put(kx, value):
        modes[pl.ds(kx, lines, MODES), :] = value

    x_forward(lines_ref, cos_ref, sin_ref, put, owners, lines, width)
    lane = iota((count, 2 * width), 1)

    def mix(i, carry):
        copy(i).wait()
        base = pl.multiple_of(i * count, count)
        u = modes[pl.ds(base, count), :]
        u_turned = pltpu.roll(u, width, 1)
        both = interleave(jnp.where(lane < width, u, u_turned), jnp.where(lane < width, u_turned, u))
        both = jnp.concatenate([both] * 4, axis=1)
        own = iota(both.shape, 1) // width == iota(both.shape, 0) % 8
        high, low = halves(jnp.where(own, both, 0.0))
        products = []
        for batch in range(count // 8):
            rows = slice(batch * 16, (batch + 1) * 16)
            left = jnp.concatenate([high[rows], low[rows]], axis=0)
            products.append(dot(left, split_weights(spec_w, base + batch * 8, width)))
        outs = []
        for product in products:
            product = product[:, : 2 * width] + product[:, 2 * width :]
            product = product[:16] + product[16:]
            turned = pltpu.roll(product[8:], width, 1)
            outs.append(product[:8] + jnp.where(lane[:8] < width, -turned, turned))
        mixed[pl.ds(base, count), :] = jnp.concatenate(outs, axis=0)
        return carry

    lax.fori_loop(0, copied.shape[0], mix, 0)
    factor = factor_column(place_ref, lines)

    def take(kx):
        return mixed[pl.ds(kx, lines, MODES), :] * factor

    x_inverse(take, out_ref, owners, lines, width)


def mix_back_kernel(
    place_ref, lines_ref, cos_ref, sin_ref, spec_hbm, *refs, owners, width,
):
    grads, out_ref, back, spec_w, copied = refs[-5:]
    lines = MODES * MODES // owners
    count, copy = fetch_weights(spec_hbm, spec_w, copied)
    for i in range(copied.shape[0]):
        copy(i).start()
    factor = factor_column(place_ref, lines)

    def put(kx, value):
        grads[pl.ds(kx, lines, MODES), :] = value * factor

    x_forward(lines_ref, cos_ref, sin_ref, put, owners, lines, width)
    lane = iota((count, 2 * width), 1)
    own = iota((16, 8 * width), 1) // width == iota((16, 8 * width), 0) % 8

    def mix(i, carry):
        copy(i).wait()
        base = pl.multiple_of(i * count, count)
        g = grads[pl.ds(base, count), :]
        g_turned = pltpu.roll(g, width, 1)
        high, low = halves(interleave(g, jnp.where(lane < width, g_turned, -g_turned)))
        products = []
        for batch in range(count // 8):
            rows = slice(batch * 16, (batch + 1) * 16)
            left = jnp.concatenate([high[rows], low[rows]], axis=0)
            left = jnp.concatenate([left, left], axis=1)
            products.append(dot(left, split_weights(spec_w, base + batch * 8, width), NT))
        outs = []
        for product in products:
            rows = jnp.where(own, product[:16] + product[16:], 0.0)
            while rows.shape[1] > 2 * width:
                half = rows.shape[1] // 2
                rows = rows[:, :half] + rows[:, half:]
            rows = rows + pltpu.roll(rows, width, 1)
            outs.append(jnp.where(lane[:8] < width, rows[:8], rows[8:]))
        back[pl.ds(base, count), :] = jnp.concatenate(outs, axis=0)
        return carry

    lax.fori_loop(0, copied.shape[0], mix, 0)

    def take(kx):
        return back[pl.ds(kx, lines, MODES), :]

    x_inverse(take, out_ref, owners, lines, width)


def spec_grad_kernel(rank_ref, *refs, shapes, width):
    mode_refs, grad_refs, (out, modes, grads) = refs[:shapes], refs[shapes : 2 * shapes], refs[-3:]
    for parts, held in ((mode_refs, modes), (grad_refs, grads)):
        for distance, part in enumerate(parts):
            held[rank_ref[0] ^ distance] = part[...]
    row = iota((8, 2 * width), 0)
    lane = iota((8, 2 * width), 1)
    own = iota((8, 4 * width), 1) // width == iota((8, 4 * width), 0) % 4
    lefts, rights = [], []
    for batch in range(out.shape[0] // 8):
        where = slice(batch * 8, (batch + 1) * 8)
        left, right = [], []
        for shape in range(shapes):
            u, g = modes[shape, where], grads[shape, where]
            u_turned, g_turned = pltpu.roll(u, width, 1), pltpu.roll(g, width, 1)
            for part in (jnp.where(lane < width, u, u_turned), jnp.where(lane < width, u_turned, u)):
                left.append(jnp.where(own, jnp.concatenate([part] * 2, axis=1), 0.0))
            for part in (g, jnp.where(lane < width, g_turned, -g_turned)):
                pair = [jnp.where(row < 4, part, 0.0), jnp.where(row < 4, 0.0, part)]
                right.append(jnp.concatenate(pair, axis=1))
        left_high, left_low = halves(jnp.concatenate(left, axis=0))
        right_high, right_low = halves(jnp.concatenate(right, axis=0))
        lefts.append(jnp.concatenate([left_high, left_low, left_high], axis=0))
        rights.append(jnp.concatenate([right_high, right_high, right_low], axis=0))
    products = [dot(left, right, TN) for left, right in zip(lefts, rights)]
    for batch, product in enumerate(products):
        out[batch * 8 : batch * 8 + 4] = product[:, : 2 * width].reshape(4, width, 2 * width)
        out[batch * 8 + 4 : batch * 8 + 8] = product[:, 2 * width :].reshape(4, width, 2 * width)


def cell_sums(total, rows_here, width):
    hidden_sums, weight_sums = [], []
    for row in range(rows_here):
        slab = total[row * PLANE : (row + 1) * PLANE]
        hidden_sums.append(slab[:, :width] + slab[:, width : 2 * width])
        weight = slab[:, 2 * width + 4 : 2 * width + 5] + slab[:, 2 * width + 12 : 2 * width + 13]
        weight_sums.append(jnp.broadcast_to(weight, (PLANE, width)))
    return jnp.concatenate(hidden_sums, axis=1), jnp.concatenate(weight_sums, axis=1)


def grid_kernel(
    lines_far, reach_far, skip_far, proj_w, inverse_far, plane_far, after, plane_out, pre_bar_far, latent_far,
    lines, inverse, skip, reach, plane, latent, pre_bar, copied, *, rows_here,
):
    ends = [
        (lines_far, lines),
        (inverse_far, inverse),
        (skip_far, skip),
        (reach_far, reach),
        (plane_far, plane),
        (latent, latent_far),
        (pre_bar, pre_bar_far),
    ]
    copies = [pltpu.make_async_copy(*pair, copied.at[i]) for i, pair in enumerate(ends)]
    for copy in copies[:5]:
        copy.start()
    copies[0].wait()
    copies[1].wait()
    spectral = times_field(inverse, lines[...])
    copies[2].wait()
    value, slope = gelu_both(spectral + skip[...])
    latent[...] = value
    copies[5].start()
    copies[3].wait()
    bar = reach[...] * tile_lanes(proj_w[...], rows_here) * slope
    pre_bar[...] = bar
    copies[6].start()
    copies[4].wait()
    plane_out[...] = times_field(plane, bar)
    copies[5].wait()
    copies[6].wait()


def grid_grads_kernel(
    lat, pre_bar, latent, reach, sums, skip_w, dec_w2, dec_b2, proj_w,
    skip_w_grad, dec_w2_grad, rows_out, table, skip_back, *, rows_here, width,
):
    skip_back[...] = dot3(pre_bar[...], spread(skip_w[...], rows_here), NT)
    skip_w_grad[...] = gather_blocks(dot3(lat[...], pre_bar[...], TN), rows_here, width, width)
    scaled = latent[...] * tile_lanes(proj_w[...], rows_here)
    dec_w2_grad[...] = gather_blocks(dot3(sums[0], scaled, TN), rows_here, width, width)

    def column_sum(value):
        return fold_lanes(jnp.sum(value, axis=0, keepdims=True), rows_here, width)

    rows = [column_sum(pre_bar[...]), column_sum(sums[1] * scaled), column_sum(reach[...] * latent[...])]
    rows_out[...] = jnp.concatenate(rows + [jnp.zeros((5, width), F32)], axis=0)
    cell_kernel = dot3(scaled, spread(dec_w2[...], rows_here), NT)
    offset = scaled * tile_lanes(dec_b2[...], rows_here)
    cells = rows_here * PLANE
    table[cells:] = jnp.zeros((PAD, table.shape[1]), BF16)
    for row in range(rows_here):
        lanes = slice(row * width, (row + 1) * width)
        where = slice(row * PLANE, (row + 1) * PLANE)
        constant = jnp.sum(offset[:, lanes], axis=1, keepdims=True)
        high, low = halves(cell_kernel[:, lanes])
        c_high, c_low = halves(constant)
        lane = iota((PLANE, LANES), 1)
        tail = jnp.where(lane == 0, c_high.astype(F32), jnp.where(lane == 1, c_low.astype(F32), 0.0))
        table[where, : 2 * width] = jnp.concatenate([high.astype(F32), low.astype(F32)], axis=1).astype(BF16)
        table[where, 2 * width :] = tail.astype(BF16)


def input_columns(feats, cell, first_row):
    high, low = halves(feats)
    place = place_rows(cell, first_row)
    return jnp.concatenate([high.astype(F32), low.astype(F32), place, place], axis=0).astype(BF16)


def dec_edges_kernel(
    place_ref, bounds, keys, inverse_degree, saved, table, pred_out, w1_out, b1_out,
    found_scratch, pred_total, grad_total, *, owners, cells, width,
):
    step = pl.program_id(0)
    rows_here = cells // PLANE
    group = found_scratch.shape[1] // CHUNK
    first_row = place_ref[0] * rows_here
    shift = log2(owners * LANES)
    count8 = max(owners, 8)

    @pl.when(step == 0)
    def _():
        pred_total[...] = jnp.zeros_like(pred_total)
        grad_total[...] = jnp.zeros_like(grad_total)

    chunk = step * group
    per = CHUNK // keys.shape[1]

    def body(count):
        rows, key = joined_keys(keys, chunk, count)
        run = slice(0, count * CHUNK)
        gather_windows(
            found_scratch, keys, rows, table, bounds, 2, chunk, count, DEC_WINDOW, shift, 2 * width + 16
        )
        point = key & (owners * LANES - 1)
        found = found_scratch[:width, run] + found_scratch[width : 2 * width, run]
        constant = found_scratch[2 * width : 2 * width + 1, run] + found_scratch[2 * width + 1 : 2 * width + 2, run]
        edge = jnp.sum(saved[:width, run] * found, axis=0, keepdims=True) + constant
        owner = iota((count8, key.shape[1]), 0)
        high, low = halves(jnp.where(owner == (point >> 7), edge, 0.0))
        values = jnp.concatenate([high.astype(F32), low.astype(F32)], axis=0).astype(BF16)
        pred_total[...] += dot(values, one_hot(point & (LANES - 1), 0, LANES), NT)
        left = jnp.concatenate(halves(saved[width : 2 * width, run] * found), axis=0)
        right = input_columns(saved[2 * width :, run], key >> shift, first_row)
        grad_total[...] += dot(left, right, NT)

    each_size(bounds, 2, chunk, group, per, cells, body)

    @pl.when(step == pl.num_programs(0) - 1)
    def _():
        pred_out[...] = (pred_total[:owners] + pred_total[count8 : count8 + owners]) * inverse_degree[...]
        grad = grad_total[:width] + grad_total[width:]
        feats = (grad[:, :8] + grad[:, 8:16]).T
        places = grad[:, 16:24].T / (RES - 1.0)
        w1_out[...] = jnp.concatenate([feats[:3], places[:3]], axis=0)
        b1_out[...] = feats[3:4]


GRAD_ROWS = 108
PACKED_ROWS = 120


def enc_back_kernel(
    place_ref, bounds, keys, saved_hbm, lines_far, skip_far, scale_far, w2, lift_w, pred_bar,
    skip_w_grad, dec_w2_grad, row_grads, pred_part, dec_w1_grad, dec_b1_grad, inverse_hbm,
    *refs, owners, cells, width,
):
    packed, table, found_scratch, second, lifts, feat_total, grad_total, inverse, lines, skip, scale, copied, slots, loaded = refs[-14:]
    rows_here = cells // PLANE
    group = found_scratch.shape[1] // CHUNK
    first_row = place_ref[0] * rows_here
    shift = log2(owners * LANES)
    count8 = max(owners, 8)
    per = CHUNK // keys.shape[1]
    load = slot_copies(saved_hbm, slots, loaded, out=False)
    steps = keys.shape[0] * keys.shape[1] // slots.shape[2]

    def load_used(at):
        @pl.when(at < steps)
        def _():
            first_cell, _ = cell_range(bounds, 0, jnp.minimum(at, steps - 1) * group, per)

            @pl.when(first_cell < cells)
            def _():
                load(at).start()

    def begin():
        used = pl.ds(0, ENC_CELLS)
        ends = [(lines_far, lines), (inverse_hbm.at[:, used], inverse), (skip_far.at[used], skip), (scale_far, scale)]
        copies = [pltpu.make_async_copy(*pair, copied.at[i]) for i, pair in enumerate(ends)]
        for copy in copies:
            copy.start()
        feat_total[...] = jnp.zeros_like(feat_total)
        grad_total[...] = jnp.zeros_like(grad_total)
        second[...] = weights3(w2[...])
        high, low = halves(jnp.concatenate([lift_w[...], jnp.zeros((4, width), F32)], axis=0))
        rows = jnp.concatenate([high.astype(F32), low.astype(F32)], axis=0)
        lifts[...] = jnp.concatenate([rows, rows], axis=1).astype(BF16)
        copies[0].wait()
        copies[1].wait()
        load_used(0)
        field = times_field(inverse, lines[...])
        copies[2].wait()
        copies[3].wait()
        field = (field + skip[...]) * scale[...]
        table[cells:] = jnp.zeros((PAD, 2 * width), BF16)
        for row in range(rows_here):
            high, low = halves(field[:, row * width : (row + 1) * width])
            both = jnp.concatenate([high.astype(F32), low.astype(F32)], axis=1).astype(BF16)
            table[row * PLANE : row * PLANE + ENC_CELLS] = both
            table[row * PLANE + ENC_CELLS : (row + 1) * PLANE] = jnp.zeros((PLANE - ENC_CELLS, 2 * width), BF16)
        load_used(1)

    def run_step(step, carry):
        chunk = step * group

        def body(count):
            rows, key = joined_keys(keys, chunk, count)
            run = slice(0, count * CHUNK)
            gather_windows(
                found_scratch, keys, rows, table, bounds, 0, chunk, count, ENC_WINDOW, shift, 2 * width
            )
            load(step).wait()
            saved = slots.at[step % 2]
            point = key & (owners * LANES - 1)
            found = found_scratch[:width, run] + found_scratch[width:, run]
            source_bar = found * saved[3 * width : 4 * width, run]
            k_high, k_low = halves(found * saved[2 * width : 3 * width, run])
            hidden_bar = dot(second[...], jnp.concatenate([k_high, k_low, k_high], axis=0))
            pre_edge = hidden_bar * saved[width : 2 * width, run]
            source_parts = halves(source_bar)
            parts = [*halves(saved[:width, run]), *halves(pre_edge), *source_parts]
            left = jnp.concatenate(parts + [jnp.ones((16, count * CHUNK), BF16)], axis=0)
            tail = input_columns(saved[4 * width :, run], key >> shift, first_row)
            grad_total[...] += dot(left, jnp.concatenate([k_high, k_low, tail], axis=0), NT)
            owner_hot = iota((count8, count * CHUNK), 0) == (point >> 7)
            both = dot(lifts[...], jnp.concatenate(source_parts, axis=0))
            both = both[:8] + both[8:]
            edges = [jnp.where(owner_hot, both[feat : feat + 1], 0.0) for feat in range(4)]
            values = jnp.concatenate(halves(jnp.concatenate(edges, axis=0)), axis=0)
            feat_total[...] += dot(values, one_hot(point & (LANES - 1), 0, LANES), NT)
            load_used(step + 2)

        each_size(bounds, 0, chunk, group, per, cells, body)
        return carry

    begin()
    lax.fori_loop(0, used_steps(bounds, 0, group, per, cells, steps), run_step, 0)
    def end():
        w2_part = grad_total[:width, : 2 * width] + grad_total[width : 2 * width, : 2 * width]
        w2_grad = w2_part[:, :width] + w2_part[:, width:]
        b2_part = grad_total[6 * width : 6 * width + 1, : 2 * width]
        b2_grad = b2_part[:, :width] + b2_part[:, width:]
        pre_part = grad_total[2 * width : 3 * width, 2 * width :] + grad_total[3 * width : 4 * width, 2 * width :]
        feats = (pre_part[:, :8] + pre_part[:, 8:16]).T
        places = pre_part[:, 16:24].T / (RES - 1.0)
        lift_part = grad_total[4 * width : 5 * width, 2 * width :] + grad_total[5 * width : 6 * width, 2 * width :]
        lifts = (lift_part[:, :8] + lift_part[:, 8:16]).T
        pair = partial(jnp.concatenate, axis=1)
        stack = partial(jnp.concatenate, axis=0)
        half = width // 2
        bar_sum = jnp.broadcast_to(jnp.sum(pred_bar[...], axis=1, keepdims=True), (1, width))
        fixed = stack(
            [
                pair([w2_grad, dec_w2_grad[...]]),
                pair([skip_w_grad[:half], skip_w_grad[half:]]),
                pair([stack([places[:3], feats[:3]]), dec_w1_grad[...]]),
                pair([feats[3:4], dec_b1_grad[...]]),
                pair([b2_grad, row_grads[1:2]]),
                pair([lifts[4:8], stack([lifts[3:4], row_grads[0:1], row_grads[2:3], bar_sum])]),
            ]
        )
        both = feat_total[: 4 * count8] + feat_total[4 * count8 :]
        empty = jnp.zeros((PACKED_ROWS - GRAD_ROWS - 5, LANES), F32)
        for owner in range(owners):
            rows = [both[feat * count8 + owner : feat * count8 + owner + 1] for feat in range(4)]
            packed[owner] = stack([fixed] + rows + [pred_part[owner : owner + 1], empty])

    end()


def arrive_kernel(arrived, proj_b, after, grads, feat_grad, pred, *, owners):
    total = arrived[0]
    for owner in range(1, owners):
        total = total + arrived[owner]
    grads[...] = total[:GRAD_ROWS]
    feat_grad[...] = total[GRAD_ROWS : GRAD_ROWS + 4]
    pred[...] = total[GRAD_ROWS + 4 : GRAD_ROWS + 5] + proj_b[...]


def leave_kernel(*refs, shapes, width):
    half = width // 2
    terms = [ref[...] for ref in refs[:shapes]]
    while len(terms) > 1:
        terms = [terms[i] + terms[i + 1] for i in range(0, len(terms), 2)]
    left, right = terms[0][:, :width], terms[0][:, width:]
    outs = refs[shapes:]
    at = width + half
    enc_w1, enc_b1, enc_w2, enc_b2, lift_w, lift_b, skip_w, skip_b, dec_w1, dec_b1, dec_w2, dec_b2, proj_w, proj_b = outs
    enc_w2[...] = left[:width]
    dec_w2[...] = right[:width]
    skip_w[:half] = left[width:at]
    skip_w[half:] = right[width:at]
    enc_w1[...] = left[at : at + 6]
    dec_w1[...] = right[at : at + 6]
    enc_b1[...] = left[at + 6 : at + 7]
    dec_b1[...] = right[at + 6 : at + 7]
    enc_b2[...] = left[at + 7 : at + 8]
    dec_b2[...] = right[at + 7 : at + 8]
    lift_w[...] = left[at + 8 : at + 12]
    lift_b[...] = right[at + 8 : at + 9]
    skip_b[...] = right[at + 9 : at + 10]
    proj_w[...] = right[at + 10 : at + 11]
    proj_b[...] = right[at + 11 : at + 12, :1]


def shape(*dims, dtype=F32):
    return jax.ShapeDtypeStruct(dims, dtype)


def whole(array):
    zeros = (0,) * array.ndim
    return pl.BlockSpec(array.shape, lambda i: zeros, pipeline_mode=pl.Buffered(1))


HELD = VMEM
VMEM_BYTES = 65280 << 10
FAR = pl.BlockSpec(memory_space=pl.ANY)


def kernel_call(kernel, name, steps, operands, out_shape, out_specs, scratch=(), micros=10, **more):
    arrays = [array for array, _ in operands]
    specs = [whole(array) if spec is None else spec for array, spec in operands]
    return pl.pallas_call(
        kernel,
        grid=(steps,),
        in_specs=specs,
        out_specs=out_specs,
        out_shape=out_shape,
        scratch_shapes=list(scratch),
        compiler_params=pltpu.CompilerParams(vmem_limit_bytes=VMEM_BYTES),
        cost_estimate=pl.CostEstimate(flops=0, bytes_accessed=micros * 2_000_000, transcendentals=0),
        name=name,
        **more,
    )(*arrays)


def on_device(
    mesh_feat,
    mesh_pos,
    query_pos,
    enc_cell,
    enc_point,
    enc_count,
    dec_cell,
    dec_query,
    dec_count,
    enc_w1,
    enc_b1,
    enc_w2,
    enc_b2,
    lift_w,
    lift_b,
    spec_w,
    skip_w,
    skip_b,
    dec_w1,
    dec_b1,
    dec_w2,
    dec_b2,
    proj_w,
    proj_b,
    pred_bar,
):
    width = lift_w.shape[1]
    owners = lax.axis_size("wide")
    shapes = lax.axis_size("grid")
    rows_here = RES // owners
    cells = rows_here * PLANE
    modes_here = spec_w.shape[0]
    lines = modes_here // MODES
    enc_blocks, dec_blocks = enc_cell.shape[1], dec_cell.shape[1]
    enc_edges, dec_edges = enc_blocks * LANES, dec_blocks * LANES
    enc_span, dec_span = ENC_GROUP * CHUNK, DEC_GROUP * CHUNK
    lanes = rows_here * width
    place = lax.axis_index("wide").astype(jnp.int32).reshape(1)
    plane_np = plane_matrix(owners)
    plane = jnp.asarray(np.stack(halves_np(plane_np)))
    inverse = jnp.asarray(np.stack(halves_np(np.ascontiguousarray(plane_np.T))))
    cos_x, sin_x = (jnp.asarray(part) for part in x_tables(rows_here, width))
    rows = [value.reshape(1, -1) for value in (enc_b1, enc_b2, lift_b, skip_b, dec_b1, dec_b2, proj_w, proj_b)]
    enc_b1, enc_b2, lift_b, skip_b, dec_b1, dec_b2, proj_w, proj_b = rows
    sizes = dict(owners=owners, cells=cells, width=width)
    dma = pltpu.SemaphoreType.DMA

    def exchange(value):
        return lax.all_to_all(value, "wide", 0, 0, tiled=True)

    payload = kernel_call(
        partial(share_kernel, owners=owners),
        "share_points",
        1,
        [
            (value, None)
            for value in (
                mesh_feat, mesh_pos.transpose(1, 0, 2), query_pos.transpose(1, 0, 2), pred_bar, dec_query[0], dec_count
            )
        ],
        shape(owners, 2 * FEAT_ROWS + owners, LANES),
        HELD,
    )
    shared = exchange(payload)
    local = [enc_cell[0], enc_point[0], enc_count, dec_cell[0], dec_query[0], dec_count]
    enc_keys, dec_keys, bounds = kernel_call(
        partial(sort_kernel, owners=owners, cells=cells),
        "sort_edges",
        1,
        [(value, None) for value in local] + [(payload, FAR)],
        [
            shape(LANES, enc_blocks, dtype=jnp.int32),
            shape(LANES, dec_blocks, dtype=jnp.int32),
            shape(8, LANES, dtype=jnp.int32),
        ],
        [HELD] * 3,
    )

    fixed = owners * FEAT_ROWS
    saved_rows = 4 * width + FEAT_ROWS
    plane_scratch = pltpu.VMEM((2, 2 * MODES * MODES, PLANE), BF16)
    inverse_scratch = pltpu.VMEM((2, PLANE, 2 * MODES * MODES), BF16)
    saved, lat, scale, plane_lat = kernel_call(
        partial(enc_forward_kernel, **sizes),
        "encode",
        1,
        [(place, SMEM), (bounds, SMEM), (enc_keys, HELD), (shared, HELD)]
        + [(value, None) for value in (enc_w1, enc_b1, enc_w2, enc_b2, lift_w, lift_b)]
        + [(plane, FAR)],
        [
            shape(saved_rows, enc_edges),
            shape(PLANE, lanes),
            shape(ENC_CELLS, lanes),
            shape(2 * MODES * MODES, lanes),
        ],
        [FAR, FAR, FAR, HELD],
        [
            pltpu.VMEM((cells + PAD, 2 * LANES), F32),
            pltpu.VMEM((2 * fixed, LANES), BF16),
            pltpu.VMEM((2 * width, INPUT_ROWS), BF16),
            pltpu.VMEM((width, 3 * width), BF16),
            pltpu.VMEM((2 * width + 16, enc_span), BF16),
            plane_scratch,
            pltpu.VMEM((PLANE, lanes), F32),
            pltpu.VMEM((ENC_CELLS, lanes), F32),
            dma((3,)),
            pltpu.VMEM((2, saved_rows, enc_span), F32),
            dma((2,)),
        ],
    )
    modes_lines = exchange(plane_lat.reshape(owners, 2 * lines, lanes))

    dec_rows = 2 * width + FEAT_ROWS
    dec_steps = dec_edges // dec_span
    half_steps = dec_steps // 2

    def dec_sums(first_step, steps, before, saved_before, after, more, out_shape, scratch, name):
        return kernel_call(
            partial(dec_sums_kernel, first_step=first_step, **sizes),
            name,
            steps,
            [
                (place, SMEM), (bounds, SMEM), (dec_keys, HELD), (shared, HELD), (dec_w1, None), (dec_b1, None),
                (before, HELD if first_step else FAR), (saved_before, FAR), (after, FAR),
            ]
            + more,
            [shape(dec_rows, dec_edges)] + out_shape,
            [pl.BlockSpec((dec_rows, dec_span), lambda i: (0, i + first_step))] + [HELD] * len(out_shape),
            scratch
            + [
                pltpu.VMEM((2 * fixed, LANES), BF16),
                pltpu.VMEM((width, INPUT_ROWS), BF16),
                pltpu.VMEM((2 * width + 16, dec_span), BF16),
            ],
            input_output_aliases={7: 0} if first_step else {},
        )

    dec_saved, dec_total, inverse_degree, skip = dec_sums(
        0, half_steps, plane_lat, plane_lat, plane_lat, [(lat, HELD), (skip_w, None), (skip_b, None)],
        [shape(cells + PAD, 2 * LANES), shape(owners, LANES), shape(PLANE, lanes)], [], "decode_sums_a",
    )

    mix_step, grad_step = min(MIX_STEP, modes_here), min(GRAD_STEP, modes_here)

    def spec_block(step):
        return pl.BlockSpec((step, width, 2 * width), lambda i: (i, 0, 0))

    def mode_pass(kernel, lines_in, after, name):
        return kernel_call(
            partial(kernel, owners=owners, width=width),
            name,
            1,
            [(place, SMEM), (lines_in, HELD), (cos_x, None), (sin_x, None), (spec_w, FAR)]
            + [(value, FAR) for value in after],
            [shape(modes_here, 2 * width), shape(owners, 2 * lines, lanes)],
            [HELD, HELD],
            [
                pltpu.VMEM((modes_here, 2 * width), F32),
                pltpu.VMEM((modes_here, width, 2 * width), F32),
                dma((modes_here // mix_step,)),
            ],
        )

    modes, back_lines = mode_pass(mix_kernel, modes_lines, [inverse_degree], "mix_modes")
    def from_shapes(value, staged=True):
        parts, step = {0: value}, shapes // 2
        if staged:
            while step:
                pairs = [(i, i ^ step) for i in range(shapes)]
                parts.update({d ^ step: lax.ppermute(part, "grid", pairs) for d, part in parts.items()})
                step //= 2
        else:
            for step in range(1, shapes):
                parts[step] = lax.ppermute(value, "grid", [(i, i ^ step) for i in range(shapes)])
        return [parts[d] for d in range(shapes)]

    all_modes = from_shapes(modes)
    grid_lines = exchange(back_lines).reshape(2 * MODES * MODES, lanes)
    dec_saved, sums, reach = dec_sums(
        half_steps, dec_steps - half_steps, dec_total, dec_saved, back_lines,
        [(dec_w2, None), (dec_b2, None)],
        [shape(2, PLANE, lanes), shape(PLANE, lanes)],
        [pltpu.VMEM((cells + PAD, 2 * LANES), F32)],
        "decode_sums_b",
    )

    plane_bar, pre_bar, latent = kernel_call(
        partial(grid_kernel, rows_here=rows_here),
        "grid_fields",
        1,
        [(grid_lines, FAR), (reach, FAR), (skip, FAR), (proj_w, None), (inverse, FAR), (plane, FAR)]
        + [(value, FAR) for value in all_modes[shapes // 2 :][:1]],
        [shape(2 * MODES * MODES, lanes)] + [shape(PLANE, lanes)] * 2,
        [HELD, FAR, FAR],
        [
            pltpu.VMEM((2 * MODES * MODES, lanes), F32),
            inverse_scratch,
            pltpu.VMEM((PLANE, lanes), F32),
            pltpu.VMEM((PLANE, lanes), F32),
            plane_scratch,
            pltpu.VMEM((PLANE, lanes), F32),
            pltpu.VMEM((PLANE, lanes), F32),
            dma((7,)),
        ],
    )
    bar_lines = exchange(plane_bar.reshape(owners, 2 * lines, lanes))

    skip_w_grad, dec_w2_grad, row_grads, dec_table, skip_back = kernel_call(
        partial(grid_grads_kernel, rows_here=rows_here, width=width),
        "grid_grads",
        1,
        [(value, HELD) for value in (lat, pre_bar, latent, reach, sums)]
        + [(value, None) for value in (skip_w, dec_w2, dec_b2, proj_w)],
        [
            shape(width, width),
            shape(width, width),
            shape(8, width),
            shape(cells + PAD, 2 * LANES, dtype=BF16),
            shape(PLANE, lanes),
        ],
        [HELD] * 5,
    )

    mixed_bar, bar_back = mode_pass(mix_back_kernel, bar_lines, [row_grads] + all_modes[1:], "mix_back")
    bar_grid_lines = exchange(bar_back).reshape(2 * MODES * MODES, lanes)

    all_grads = from_shapes(mixed_bar)

    count8 = max(owners, 8)
    pred_part, dec_w1_grad, dec_b1_grad = kernel_call(
        partial(dec_edges_kernel, **sizes),
        "decode_edges",
        dec_steps,
        [
            (place, SMEM), (bounds, SMEM), (dec_keys, HELD), (inverse_degree, HELD),
            (dec_saved, pl.BlockSpec((dec_rows, dec_span), lambda i: (0, i))), (dec_table, HELD),
        ],
        [shape(owners, LANES), shape(6, width), shape(1, width)],
        [HELD] * 3,
        [
            pltpu.VMEM((2 * width + 16, dec_span), F32),
            pltpu.VMEM((2 * count8, LANES), F32),
            pltpu.VMEM((2 * width, 32), F32),
        ],
    )

    packed = kernel_call(
        partial(enc_back_kernel, **sizes),
        "encode_back",
        1,
        [(place, SMEM), (bounds, SMEM), (enc_keys, HELD), (saved, FAR)]
        + [(value, FAR) for value in (bar_grid_lines, skip_back, scale)]
        + [(value, None) for value in (enc_w2, lift_w, pred_bar)]
        + [(value, HELD) for value in (skip_w_grad, dec_w2_grad, row_grads, pred_part, dec_w1_grad, dec_b1_grad)]
        + [(inverse, FAR)]
        + [(value, FAR) for value in all_grads[shapes // 2 :][:1]],
        shape(owners, PACKED_ROWS, LANES),
        HELD,
        [
            pltpu.VMEM((cells + PAD, 2 * width), BF16),
            pltpu.VMEM((2 * width, enc_span), F32),
            pltpu.VMEM((width, 3 * width), BF16),
            pltpu.VMEM((16, 2 * width), BF16),
            pltpu.VMEM((8 * count8, LANES), F32),
            pltpu.VMEM((6 * width + 16, 2 * width + 32), F32),
            pltpu.VMEM((2, ENC_CELLS, 2 * MODES * MODES), BF16),
            pltpu.VMEM((2 * MODES * MODES, lanes), F32),
            pltpu.VMEM((ENC_CELLS, lanes), F32),
            pltpu.VMEM((ENC_CELLS, lanes), F32),
            dma((4,)),
            pltpu.VMEM((2, saved_rows, enc_span), F32),
            dma((2,)),
        ],
    )
    arrived = exchange(packed)

    rank = lax.axis_index("grid").astype(jnp.int32).reshape(1)
    spec_grad = kernel_call(
        partial(spec_grad_kernel, shapes=shapes, width=width),
        "spec_grad",
        modes_here // grad_step,
        [(rank, SMEM)]
        + [
            (value, pl.BlockSpec((grad_step, 2 * width), lambda i: (i, 0)))
            for value in all_modes + all_grads
        ]
        + [(packed, FAR)],
        shape(modes_here, width, 2 * width),
        spec_block(grad_step),
        [pltpu.VMEM((shapes, grad_step, 2 * width), F32)] * 2,
    )

    grads, feat_grad, pred = kernel_call(
        partial(arrive_kernel, owners=owners),
        "arrive",
        1,
        [(arrived, HELD), (proj_b, None), (spec_grad, FAR)],
        [shape(GRAD_ROWS, LANES), shape(4, LANES), shape(1, LANES)],
        [HELD] * 3,
    )
    terms = from_shapes(grads, staged=False)
    vector = shape(1, width)
    square = shape(width, width)
    first = shape(6, width)
    outs = kernel_call(
        partial(leave_kernel, shapes=shapes, width=width),
        "leave",
        1,
        [(term, HELD) for term in terms],
        [
            first, vector, square, vector, shape(4, width), vector,
            square, vector, first, vector, square, vector, vector, shape(1, 1),
        ],
        [HELD] * 14,
    )
    outs = [out.reshape(-1) if out.shape[0] == 1 else out for out in outs]
    return (pred, feat_grad[None], *outs[:6], spec_grad, *outs[6:])


def solution(mesh):
    placed = (
        P("grid", None, "wide"),
        P("grid", None, "wide"),
        P("grid", None, "wide"),
        P("grid", "wide", None),
        P("grid", "wide", None),
        P("grid", "wide"),
        P("grid", "wide", None),
        P("grid", "wide", None),
        P("grid", "wide"),
        P(),
        P(),
        P(),
        P(),
        P(),
        P(),
        P("wide", None, None),
        P(),
        P(),
        P(),
        P(),
        P(),
        P(),
        P(),
        P(),
        P("grid", "wide"),
    )
    return jax.shard_map(
        on_device,
        mesh=mesh,
        in_specs=placed,
        out_specs=(
            P("grid", "wide"),
            P("grid", None, "wide"),
            P(),
            P(),
            P(),
            P(),
            P(),
            P(),
            P("wide", None, None),
            P(),
            P(),
            P(),
            P(),
            P(),
            P(),
            P(),
            P(),
        ),
        check_vma=False,
    )
```
